32 devices in a mesh: dp: 4 (over y, core), mp: 8 (over z, x).
Axes of the slice: x: 2, y: 2, z: 4, core: 2. Of those that a mesh axis runs over, the one named last changes fastest.
Arguments:
- inputs: bfloat16 [32768, 768], P(('dp', 'mp')), may hold values from -6 to 6
- segments: int32 [32, 1024], P('dp'), may hold values from 0 to 3, never falling along the last dimension, each value on 1 to 384 neighbouring positions
- ln1_gain: float32 [768], replicated, may hold values from 0.1 to 1.9
- ln1_bias: float32 [768], replicated, may hold values from -3 to 3
- w_query: bfloat16 [768, 768], P(None, 'mp'), may hold values from -0.3125 to 0.3125
- w_key: bfloat16 [768, 768], P(None, 'mp'), may hold values from -0.21875 to 0.21875
- w_value: bfloat16 [768, 768], P(None, 'mp'), may hold values from -0.21875 to 0.21875
- w_output: bfloat16 [768, 768], P('mp'), may hold values from -3.5 to 3.5
- ln2_gain: float32 [768], replicated, may hold values from 0.1 to 1.9
- ln2_bias: float32 [768], replicated, may hold values from -3 to 3
- w_up: bfloat16 [768, 3072], P(None, 'mp'), may hold values from -0.21875 to 0.21875
- w_down: bfloat16 [3072, 768], P('mp'), may hold values from -0.109375 to 0.109375
- cotangent: bfloat16 [32768, 768], P(('dp', 'mp')), may hold values from -6 to 6
Outputs:
- output: bfloat16 [32768, 768], P(('dp', 'mp'))
- in_grad: bfloat16 [32768, 768], P(('dp', 'mp'))
- grad_ln1_gain: float32 [768], P('mp')
- grad_ln1_bias: float32 [768], P('mp')
- grad_w_query: float32 [768, 768], P(None, 'mp')
- grad_w_key: float32 [768, 768], P(None, 'mp')
- grad_w_value: float32 [768, 768], P(None, 'mp')
- grad_w_output: float32 [768, 768], P('mp')
- grad_ln2_gain: float32 [768], P('mp')
- grad_ln2_bias: float32 [768], P('mp')
- grad_w_up: float32 [768, 3072], P(None, 'mp')
- grad_w_down: float32 [3072, 768], P('mp')
The draws below stay inside these ranges and needn't reach their ends.
Inputs may be any that keep to these rules, and one draw needn't show every extreme that they name: `segments`: within each sequence the image numbers never fall, every image 0 to 3 holds 1 to 384 tokens, and one image of each sequence holds exactly 384.
All inputs are finite; a program needn't handle non-finite values.
Results may differ from the reference program's by a relative error of at most 0.012.
The reference program's roundings to bfloat16 on the way count: a program that leaves them out, or rounds other values in their place, can miss the bound.
Values may be sent and summed in bfloat16 or wider, within the bound.
No kernel may reach another device: no remote copies, remote signals or barrier semaphores. Data moves between devices by JAX's collectives and lax.ppermute only.
A program may use at most 256 MiB of HBM per device.

```python
import math
import jax
import jax.numpy as jnp
import numpy as np
from jax import lax

D = 768
HEADS = 16
HEAD_DIM = 48
FF = 3072
SEQ_LEN = 1024
IMAGES = 4
IMAGE_MOST = 384
SEQS = 32
TOKENS = 32768


def shard_levels(stream_key, dims, split, low, largest):
    loudness = 1.0
    for position, blocks in split:
        heights = jax.random.uniform(jax.random.fold_in(jax.random.fold_in(stream_key, 6), position), (blocks,), jnp.float32, low / len(split), largest / len(split))
        loudness = loudness * jnp.repeat(jnp.exp(heights), dims[position] // blocks).reshape((-1,) + (1,) * (len(dims) - 1 - position))
    return loudness


def profile(count, total, most, slope):
    weights = [(1 << 20) // math.isqrt(rank ** slope) + 1 for rank in range(2, count + 1)]
    rest, holding = total - most - (count - 1), [1] * (count - 1)
    while rest > 0:
        free = [i for i in range(count - 1) if holding[i] < most]
        pool, budget = sum([weights[i] for i in free]), rest
        for i in free:
            addition = min(most - holding[i], max(1, budget * weights[i] // pool), rest)
            holding[i] = holding[i] + addition
            rest = rest - addition
    return np.array([most] + holding)


def ragged_sizes(rng, amount, total, reach, lean):
    if amount == 2:
        one = jax.random.randint(rng, (), max(1, total - reach), min(reach, total - 1) + 1)
        return jnp.stack([one, total - one])
    sizes = jnp.asarray(profile(amount, total, reach, lean), jnp.int32)
    pairs = (amount - 1) // 2
    source_of, taker = sizes[1:1 + 2 * pairs:2], sizes[2:2 + 2 * pairs:2]
    slack = jnp.minimum(source_of - 1, reach - taker)
    moved = jax.random.randint(jax.random.fold_in(rng, 1), (pairs,), 0, 1 << 20) % (slack + 1)
    sizes = sizes.at[1:1 + 2 * pairs:2].set(source_of - moved).at[2:2 + 2 * pairs:2].set(taker + moved)
    return sizes[jax.random.permutation(jax.random.fold_in(rng, 2), amount)]


def bell_draw(own_key, extent, scale, most, split=(), kind=jnp.bfloat16):
    level = shard_levels(own_key, extent, split, -0.22, 0.18) if split else 1.0
    entries = jax.random.normal(own_key, extent, jnp.float32) * scale * level
    return jnp.minimum(jnp.maximum(entries, -most), most).astype(kind)


def setup_inputs(seed: int = 0) -> dict:
    arg_keys = jax.random.split(jax.random.key(seed), 14)
    return {
        "inputs": bell_draw(arg_keys[0], (TOKENS, D), 1.0, 6.0, ((0, 32),)),
        "segments": jax.vmap(lambda own: jnp.searchsorted(jnp.cumsum(ragged_sizes(own, IMAGES, SEQ_LEN, IMAGE_MOST, 1)), jnp.arange(SEQ_LEN), side="right"))(jax.random.split(arg_keys[1], SEQS)).reshape((SEQS, SEQ_LEN)).astype(jnp.int32),
        "ln1_gain": jnp.clip(1.0 + 0.18 * jax.random.normal(arg_keys[2], (D,), jnp.float32), 0.1, 1.9),
        "ln1_bias": bell_draw(arg_keys[3], (D,), 0.5, 3.0, (), jnp.float32),
        "w_query": bell_draw(arg_keys[4], (D, D), (D // 2) ** -0.5, 0.3125, ((1, 8),)),
        "w_key": bell_draw(arg_keys[5], (D, D), D ** -0.5, 0.21875, ((1, 8),)),
        "w_value": bell_draw(arg_keys[6], (D, D), D ** -0.5, 0.21875, ((1, 8),)),
        "w_output": bell_draw(arg_keys[7], (D, D), (max(D // 256, 1)) ** -0.5, 3.5, ((0, 8),)),
        "ln2_gain": jnp.clip(1.0 + 0.18 * jax.random.normal(arg_keys[8], (D,), jnp.float32), 0.1, 1.9),
        "ln2_bias": bell_draw(arg_keys[9], (D,), 0.5, 3.0, (), jnp.float32),
        "w_up": bell_draw(arg_keys[10], (D, FF), D ** -0.5, 0.21875, ((1, 8),)),
        "w_down": bell_draw(arg_keys[11], (FF, D), FF ** -0.5, 0.109375, ((0, 8),)),
        "cotangent": bell_draw(arg_keys[12], (TOKENS, D), 1.0, 6.0, ((0, 32),)),
    }


norm_eps = 1e-06
negative_fill = -1e+30

@jax.custom_vjp
def low(v):
    return lax.optimization_barrier(v.astype(jnp.bfloat16)).astype(jnp.float32)

@jax.custom_vjp
def low_back(v):
    return v

def low_keep(v):
    return (low(v), None)

def low_pass(kept, grad):
    return (grad,)

def back_keep(v):
    return (v, None)

def back_low(kept, grad):
    return (low(grad),)
low.defvjp(low_keep, low_pass)
low_back.defvjp(back_keep, back_low)

def layer_norm(values, gain, bias):
    center = lax.optimization_barrier(jnp.mean(values, axis=-1, keepdims=True))
    shifted = values - center
    spread = lax.optimization_barrier(jnp.mean(shifted * shifted, axis=-1, keepdims=True))
    return shifted * lax.rsqrt(spread + norm_eps) * gain + bias

def high_dot(left, right):
    return jnp.dot(left, right, precision=lax.Precision.HIGHEST, preferred_element_type=jnp.float32)

def attend_one(operands):
    query, key_rows, value, same_image = operands
    scores = jnp.einsum('qhd,khd->hqk', query, key_rows, precision=lax.Precision.HIGHEST) * HEAD_DIM ** (-0.5)
    scores = low_back(scores)
    masked = jnp.where(same_image[None], scores, negative_fill)
    top_score = lax.optimization_barrier(jnp.max(masked, axis=-1, keepdims=True))
    expo = jnp.exp(masked - top_score)
    probs = expo / lax.optimization_barrier(jnp.sum(expo, axis=-1, keepdims=True))
    return jnp.einsum('hqk,khd->qhd', low(probs), value, precision=lax.Precision.HIGHEST)

def layer(rows, same_image, gain_one, bias_one, w_query, w_key, w_value, w_output, gain_two, bias_two, w_up, w_down):
    group = same_image.shape[0]
    norm_one = low(layer_norm(rows, gain_one, bias_one))
    query = low(low_back(high_dot(norm_one, w_query))).reshape(group, SEQ_LEN, HEADS, HEAD_DIM)
    key_rows = low(low_back(high_dot(norm_one, w_key))).reshape(group, SEQ_LEN, HEADS, HEAD_DIM)
    value = low(low_back(high_dot(norm_one, w_value))).reshape(group, SEQ_LEN, HEADS, HEAD_DIM)
    attended = lax.map(jax.checkpoint(attend_one), (query, key_rows, value, same_image))
    attended = low(low_back(attended.reshape(group * SEQ_LEN, D)))
    residual = rows + low_back(high_dot(attended, w_output))
    norm_two = low(layer_norm(residual, gain_two, bias_two))
    pre_act = low_back(high_dot(norm_two, w_up))
    activation = low(jax.nn.gelu(pre_act, approximate=False))
    return residual + low_back(high_dot(activation, w_down))

def reference(inputs, segments, ln1_gain, ln1_bias, w_query, w_key, w_value, w_output, ln2_gain, ln2_bias, w_up, w_down, cotangent):
    per_group = 4 if SEQS % 4 == 0 else 2 if SEQS % 2 == 0 else 1
    groups = SEQS // per_group
    params = tuple((item.astype(jnp.float32) for item in (ln1_gain, ln1_bias, w_query, w_key, w_value, w_output, ln2_gain, ln2_bias, w_up, w_down)))
    rows_all = inputs.astype(jnp.float32).reshape(groups, per_group * SEQ_LEN, D)
    grads_all = cotangent.astype(jnp.float32).reshape(groups, per_group * SEQ_LEN, D)
    segs_all = segments.reshape(groups, per_group, SEQ_LEN)

    def one_group(totals, operands):
        rows, grad_rows, seg_rows = operands
        same_image = seg_rows[:, :, None] == seg_rows[:, None, :]

        def forward(values, *weights):
            return layer(values, same_image, *weights)
        result, backward = jax.vjp(forward, rows, *params)
        gradients = backward(grad_rows)
        totals = tuple((total + grad for total, grad in zip(totals, gradients[1:])))
        return (totals, (result.astype(jnp.bfloat16), gradients[0].astype(jnp.bfloat16)))
    zero_grads = tuple((jnp.zeros_like(item) for item in params))
    totals, (outputs, in_grads) = lax.scan(one_group, zero_grads, (rows_all, grads_all, segs_all))
    return (outputs.reshape(TOKENS, D), in_grads.reshape(TOKENS, D), totals[0], totals[1], totals[2], totals[3], totals[4], totals[5], totals[6], totals[7], totals[8], totals[9])
```

```python
import functools
import math

import jax
import jax.numpy as jnp
from jax import lax
from jax.experimental import pallas as pl
from jax.experimental.pallas import tpu as pltpu
from jax.sharding import PartitionSpec as P

HEAD_DIM = 48
PAIR = 2 * HEAD_DIM
IMAGES = 4
TILE = 128
norm_eps = 1e-06
negative_fill = -1e30
SCALE = HEAD_DIM ** (-0.5)
SCALE_LOG2 = SCALE * math.log2(math.e)
BF16 = jnp.bfloat16
F32 = jnp.float32


def layer_norm(values, gain, bias):
    center = jnp.mean(values, axis=-1, keepdims=True)
    shifted = values - center
    spread = jnp.mean(shifted * shifted, axis=-1, keepdims=True)
    return shifted * lax.rsqrt(spread + norm_eps) * gain + bias


def dot(left, right, dims):
    return lax.dot_general(left, right, (dims, ((), ())), preferred_element_type=F32)


NN = ((1,), (0,))
NT = ((1,), (1,))
TN = ((0,), (0,))


def window_kinds(tiles):
    return tuple(n for n in (2, 3, 4, 5) if n < tiles) + (tiles,)


def image_rows(segs, length):
    row = lax.broadcasted_iota(jnp.int32, (TILE - PAIR, length), 0)
    here = row == segs
    one_hot = jnp.where(here, 1.0, 0.0).astype(BF16)
    fill = jnp.where(jnp.logical_or(here, row >= IMAGES), 0.0, negative_fill).astype(BF16)
    return one_hot, fill


def side_by_side(pair, extra):
    blank = jnp.zeros((HEAD_DIM, TILE), BF16)
    left = jnp.concatenate([pair[:HEAD_DIM], blank, extra], axis=0)
    right = jnp.concatenate([blank, pair[HEAD_DIM:], extra], axis=0)
    return jnp.concatenate([left, right], axis=1)


def attend_forward_kernel(
    first_ref, kind_ref, segs_ref, q_ref, k_ref, v_ref, out_ref, lse_ref, hot_ref, keys_ref, vals_ref
):
    length = q_ref.shape[1]
    pairs = q_ref.shape[0] // PAIR
    one_hot, fill = image_rows(segs_ref[...], length)
    hot_ref[...] = one_hot
    for j in range(pairs):
        rows = slice(PAIR * j, PAIR * (j + 1))
        keys_ref[j] = jnp.concatenate([k_ref[rows, :], fill], axis=0).T
        vals_ref[j] = jnp.concatenate([v_ref[rows, :], jnp.ones((16, length), BF16)], axis=0)

    def block(b, carry):
        at = pl.ds(pl.multiple_of(b * TILE, TILE), TILE)
        first = pl.multiple_of(first_ref[b] * TILE, TILE)

        def variant(tiles):
            span = pl.ds(first, tiles * TILE)
            for j in range(pairs):
                top = PAIR * j
                query = side_by_side(q_ref[top : top + PAIR, at], hot_ref[:, at])
                scores = dot(keys_ref[j, span, :], query, NN)
                most = jnp.max(scores, axis=0, keepdims=True)
                expo = jnp.exp2((scores - most) * SCALE_LOG2).astype(BF16)
                mixed = dot(vals_ref[j, :, span], expo, NN)
                total = mixed[PAIR : PAIR + 1, :]
                inverse = 1.0 / total
                out_ref[top : top + HEAD_DIM, at] = (
                    mixed[:HEAD_DIM, :TILE] * inverse[:, :TILE]
                ).astype(BF16)
                out_ref[top + HEAD_DIM : top + PAIR, at] = (
                    mixed[HEAD_DIM:PAIR, TILE:] * inverse[:, TILE:]
                ).astype(BF16)
                lse_ref[j, pl.ds(b, 1), :] = most * SCALE_LOG2 + jnp.log2(total)

        for tiles in window_kinds(length // TILE):
            pl.when(kind_ref[b] == tiles)(functools.partial(variant, tiles))
        return carry

    lax.fori_loop(0, length // TILE, block, 0)


def attend_backward_kernel(
    first_ref,
    kind_ref,
    segs_ref,
    q_ref,
    k_ref,
    v_ref,
    att_ref,
    grad_ref,
    lse_ref,
    dq_ref,
    dk_ref,
    dv_ref,
    hot_ref,
    keys_ref,
    vals_ref,
    queries_ref,
    grads_ref,
    key_sum_ref,
    val_sum_ref,
):
    length = q_ref.shape[1]
    pairs = q_ref.shape[0] // PAIR
    one_hot, fill = image_rows(segs_ref[...], length)
    hot_ref[...] = one_hot
    pad = jnp.zeros((TILE - PAIR, length), BF16)
    for j in range(pairs):
        rows = slice(PAIR * j, PAIR * (j + 1))
        keys_ref[j] = jnp.concatenate([k_ref[rows, :], fill], axis=0).T
        vals_ref[j] = jnp.concatenate([v_ref[rows, :], pad], axis=0).T
        queries_ref[j] = jnp.concatenate([q_ref[rows, :], pad], axis=0).T
        grads_ref[j] = jnp.concatenate([grad_ref[rows, :], pad], axis=0).T
    key_sum_ref[...] = jnp.zeros(key_sum_ref.shape, F32)
    val_sum_ref[...] = jnp.zeros(val_sum_ref.shape, F32)
    no_rows = jnp.zeros((TILE - PAIR, TILE), BF16)
    lane = lax.broadcasted_iota(jnp.int32, (TILE, TILE), 1)
    in_first = lane < HEAD_DIM

    def stacked(both):
        blank = jnp.zeros_like(both)
        return jnp.concatenate(
            [jnp.where(in_first, both, blank), jnp.where(in_first, blank, both)], axis=0
        )

    def block(b, carry):
        at = pl.ds(pl.multiple_of(b * TILE, TILE), TILE)
        first = pl.multiple_of(first_ref[b] * TILE, TILE)

        def variant(tiles):
            span = pl.ds(first, tiles * TILE)
            for j in range(pairs):
                top = PAIR * j
                query = side_by_side(q_ref[top : top + PAIR, at], hot_ref[:, at])
                grad = grad_ref[top : top + PAIR, at]
                agree = grad.astype(F32) * att_ref[top : top + PAIR, at].astype(F32)
                delta = jnp.concatenate(
                    [
                        jnp.sum(agree[:HEAD_DIM], axis=0, keepdims=True),
                        jnp.sum(agree[HEAD_DIM:], axis=0, keepdims=True),
                    ],
                    axis=1,
                )
                scores = dot(keys_ref[j, span, :], query, NN)
                probs = jnp.exp2(scores * SCALE_LOG2 - lse_ref[j, pl.ds(b, 1), :])
                prob_grad = dot(vals_ref[j, span, :], side_by_side(grad, no_rows), NN)
                score_grad = (probs * (prob_grad - delta)).astype(BF16)
                val_sum_ref[j, span, :] += dot(
                    probs.astype(BF16), stacked(grads_ref[j, at, :]), NN
                )
                key_sum_ref[j, span, :] += dot(score_grad, stacked(queries_ref[j, at, :]), NN)
                query_grad = dot(k_ref[top : top + PAIR, span], score_grad, NN) * SCALE
                dq_ref[top : top + HEAD_DIM, at] = query_grad[:HEAD_DIM, :TILE].astype(BF16)
                dq_ref[top + HEAD_DIM : top + PAIR, at] = query_grad[HEAD_DIM:, TILE:].astype(BF16)

        for tiles in window_kinds(length // TILE):
            pl.when(kind_ref[b] == tiles)(functools.partial(variant, tiles))
        return carry

    lax.fori_loop(0, length // TILE, block, 0)
    for j in range(pairs):
        rows = slice(PAIR * j, PAIR * (j + 1))
        dk_ref[rows, :] = (key_sum_ref[j] * SCALE).T[:PAIR].astype(BF16)
        dv_ref[rows, :] = val_sum_ref[j].T[:PAIR].astype(BF16)


def windows(segs):
    length = segs.shape[0]
    tiles = length // TILE
    by_tile = segs.reshape(tiles, TILE)
    begin = jnp.sum(segs[None, :] < by_tile[:, :1], axis=1)
    end = jnp.sum(segs[None, :] <= by_tile[:, -1:], axis=1)
    first = begin // TILE
    need = (end + TILE - 1) // TILE - first
    kinds = jnp.asarray(window_kinds(tiles), jnp.int32)
    kind = jnp.min(jnp.where(kinds[None, :] >= need[:, None], kinds[None, :], tiles), axis=1)
    return jnp.minimum(first, tiles - kind).astype(jnp.int32), kind.astype(jnp.int32)


def attention_specs(heads, length):
    pairs = heads // 2
    step = 2 if pairs % 2 == 0 else 1
    rows = pl.BlockSpec((step * PAIR, length), lambda i, *_: (i, 0))
    segs = pl.BlockSpec((1, length), lambda i, *_: (0, 0))
    lse = pl.BlockSpec((step, length // TILE, 2 * TILE), lambda i, *_: (i, 0, 0))
    return pairs, step, rows, segs, lse


def attend_forward(query, keys, value, segs, first, kind):
    length = segs.shape[0]
    heads = query.shape[0] // HEAD_DIM
    pairs, step, rows, segs_spec, lse = attention_specs(heads, length)
    work = heads * length * length * HEAD_DIM
    return pl.pallas_call(
        attend_forward_kernel,
        grid_spec=pltpu.PrefetchScalarGridSpec(
            num_scalar_prefetch=2,
            grid=(pairs // step,),
            in_specs=[segs_spec, rows, rows, rows],
            out_specs=[rows, lse],
            scratch_shapes=[
                pltpu.VMEM((TILE - PAIR, length), BF16),
                pltpu.VMEM((step, length, TILE), BF16),
                pltpu.VMEM((step, PAIR + 16, length), BF16),
            ],
        ),
        out_shape=[
            jax.ShapeDtypeStruct(query.shape, BF16),
            jax.ShapeDtypeStruct((pairs, length // TILE, 2 * TILE), F32),
        ],
        compiler_params=pltpu.CompilerParams(vmem_limit_bytes=40 << 20),
        cost_estimate=pl.CostEstimate(
            flops=8 * work, bytes_accessed=8 * query.size, transcendentals=heads * length * length // 2
        ),
        name="attend_forward",
    )(first, kind, segs[None, :], query, keys, value)


def attend_backward(query, keys, value, attended, grad, lse, segs, first, kind):
    length = segs.shape[0]
    heads = query.shape[0] // HEAD_DIM
    pairs, step, rows, segs_spec, lse_spec = attention_specs(heads, length)
    work = heads * length * length * HEAD_DIM
    wide = pltpu.VMEM((step, length, TILE), BF16)
    total = pltpu.VMEM((step, length, TILE), F32)
    return pl.pallas_call(
        attend_backward_kernel,
        grid_spec=pltpu.PrefetchScalarGridSpec(
            num_scalar_prefetch=2,
            grid=(pairs // step,),
            in_specs=[segs_spec, rows, rows, rows, rows, rows, lse_spec],
            out_specs=[rows, rows, rows],
            scratch_shapes=[
                pltpu.VMEM((TILE - PAIR, length), BF16),
                wide,
                wide,
                wide,
                wide,
                total,
                total,
            ],
        ),
        out_shape=[jax.ShapeDtypeStruct(query.shape, BF16)] * 3,
        compiler_params=pltpu.CompilerParams(vmem_limit_bytes=40 << 20),
        cost_estimate=pl.CostEstimate(
            flops=20 * work, bytes_accessed=16 * query.size, transcendentals=heads * length * length // 2
        ),
        name="attend_backward",
    )(first, kind, segs[None, :], query, keys, value, attended, grad, lse)


def gelu_parts(values):
    below = 0.5 * (1.0 + lax.erf(values * (0.5 ** 0.5)))
    density = jnp.exp(values * values * -0.5) * ((2.0 * math.pi) ** -0.5)
    return values * below, below + values * density


def feed_forward_kernel(
    norm_ref, cot_ref, up_ref, down_ref, mlp_ref, back_ref, up_grad_ref, down_grad_ref, act_ref, pre_ref
):
    rows = norm_ref.shape[0]
    chunk = min(rows, 256)

    @pl.when(pl.program_id(0) == 0)
    def _():
        mlp_ref[...] = jnp.zeros(mlp_ref.shape, F32)
        back_ref[...] = jnp.zeros(back_ref.shape, F32)

    for start in range(0, rows, chunk):
        at = slice(start, start + chunk)
        pre_act = dot(norm_ref[at, :], up_ref[...], NT)
        act_grad = dot(cot_ref[at, :], down_ref[...], NT)
        activation, slope = gelu_parts(pre_act)
        activation = activation.astype(BF16)
        pre_grad = (act_grad * slope).astype(BF16)
        act_ref[at, :] = activation
        pre_ref[at, :] = pre_grad
        mlp_ref[at, :] += dot(activation, down_ref[...], NN)
        back_ref[at, :] += dot(pre_grad, up_ref[...], NN)
    down_grad_ref[...] = dot(act_ref[...], cot_ref[...], TN).astype(BF16)
    up_grad_ref[...] = dot(pre_ref[...], norm_ref[...], TN).astype(BF16)


def feed_forward(norm, cot, up, down):
    rows, width = norm.shape
    hidden = up.shape[0]
    part = 512 if hidden % 512 == 0 else hidden
    whole = pl.BlockSpec((rows, width), lambda i: (0, 0))
    block = pl.BlockSpec((part, width), lambda i: (i, 0))
    return pl.pallas_call(
        feed_forward_kernel,
        grid=(hidden // part,),
        in_specs=[whole, whole, block, block],
        out_specs=[whole, whole, block, block],
        out_shape=[
            jax.ShapeDtypeStruct((rows, width), F32),
            jax.ShapeDtypeStruct((rows, width), F32),
            jax.ShapeDtypeStruct((hidden, width), BF16),
            jax.ShapeDtypeStruct((hidden, width), BF16),
        ],
        scratch_shapes=[pltpu.VMEM((rows, part), BF16), pltpu.VMEM((rows, part), BF16)],
        compiler_params=pltpu.CompilerParams(vmem_limit_bytes=56 << 20),
        cost_estimate=pl.CostEstimate(
            flops=12 * rows * width * hidden,
            bytes_accessed=8 * hidden * width + 12 * rows * width,
            transcendentals=2 * rows * hidden,
        ),
        name="feed_forward",
    )(norm, cot, up, down)


def shards(
    dp_size,
    mp_size,
    inputs,
    segments,
    ln1_gain,
    ln1_bias,
    w_query,
    w_key,
    w_value,
    w_output,
    ln2_gain,
    ln2_bias,
    w_up,
    w_down,
    cotangent,
):
    rows, width = inputs.shape
    seq_count, seq_length = segments.shape
    local = w_query.shape[1]
    shared_by = seq_length // rows
    at_mp = lax.axis_index("mp")
    at_dp = lax.axis_index("dp")
    split = dp_size == 4

    def gather(parts):
        count = parts.shape[1]
        if split:
            mine = lax.dynamic_index_in_dim(parts, at_dp, 0, keepdims=False)
            return lax.all_gather(mine, ("dp", "mp"), axis=0, tiled=True).reshape(
                4, mp_size * count, width
            )
        return lax.all_gather(parts, "mp", axis=1, tiled=True)

    def reduce(parts):
        if split:
            mine = lax.psum_scatter(
                parts.reshape(-1, width), ("dp", "mp"), scatter_dimension=0, tiled=True
            )
            return lax.all_gather(mine, "dp", axis=0, tiled=False)
        return lax.psum(lax.psum_scatter(parts, "mp", scatter_dimension=1, tiled=True), "dp")

    groups = [
        [start + i for i in range(shared_by)] for start in range(0, mp_size, shared_by)
    ]

    def to_heads(values):
        if shared_by == 1:
            return values
        return lax.all_to_all(values, "mp", 0, 1, axis_index_groups=groups, tiled=True)

    def to_tokens(values):
        if shared_by == 1:
            return values
        return lax.all_to_all(values, "mp", 1, 0, axis_index_groups=groups, tiled=True)

    attn_weights = gather(jnp.stack([w_query.T, w_key.T, w_value.T, w_output]))
    up = gather(w_up.T.reshape(4, -1, width)).reshape(-1, width)
    down = gather(w_down.reshape(4, -1, width)).reshape(-1, width)
    w_project = attn_weights[:3].reshape(3 * width, width)
    w_out = attn_weights[3]

    segs = lax.dynamic_index_in_dim(segments, at_mp // shared_by, 0, keepdims=False)
    first, kind = windows(segs)

    resid_in = inputs.astype(F32)
    norm_one = layer_norm(resid_in, ln1_gain, ln1_bias).astype(BF16)
    projected = dot(w_project, norm_one, NT).astype(BF16)
    query, keys, value = [to_heads(projected[i * width : (i + 1) * width]) for i in range(3)]
    attended_heads, lse = attend_forward(query, keys, value, segs, first, kind)
    attended = to_tokens(attended_heads)
    residual = resid_in + dot(attended, w_out, TN)
    norm_two = layer_norm(residual, ln2_gain, ln2_bias).astype(BF16)

    mlp_branch, norm_two_grad, grad_up, grad_down = feed_forward(norm_two, cotangent, up, down)
    output = (residual + mlp_branch).astype(BF16)
    up_sum = reduce(grad_up.reshape(4, -1, width)).reshape(-1, width)
    down_sum = reduce(grad_down.reshape(4, -1, width)).reshape(-1, width)

    norm_two_back = jax.vjp(layer_norm, residual, ln2_gain, ln2_bias)[1]
    resid_part, gain_two_grad, bias_two_grad = norm_two_back(norm_two_grad)
    res_grad = cotangent.astype(F32) + resid_part
    branch_grad = res_grad.astype(BF16)
    grad_out = dot(attended, branch_grad, NN).astype(BF16)
    att_grad = to_heads(dot(w_out, branch_grad, NT).astype(BF16))
    proj_grad = jnp.concatenate(
        [
            to_tokens(item)
            for item in attend_backward(
                query, keys, value, attended_heads, att_grad, lse, segs, first, kind
            )
        ],
        axis=0,
    )
    grad_project = dot(proj_grad, norm_one, NN).astype(BF16)
    attn_sum = reduce(
        jnp.concatenate([grad_project, grad_out], axis=0).reshape(4, width, width)
    ).astype(F32)
    norm_one_grad = dot(proj_grad, w_project, TN)
    norm_one_back = jax.vjp(layer_norm, resid_in, ln1_gain, ln1_bias)[1]
    input_part, gain_one_grad, bias_one_grad = norm_one_back(norm_one_grad)
    in_grad = (res_grad + input_part).astype(BF16)

    norm_parts = jnp.stack([gain_one_grad, bias_one_grad, gain_two_grad, bias_two_grad])
    norm_sums = lax.dynamic_slice_in_dim(
        lax.psum(norm_parts, ("dp", "mp")), at_mp * (width // mp_size), width // mp_size, 1
    )
    return (
        output,
        in_grad,
        norm_sums[0],
        norm_sums[1],
        attn_sum[0].T,
        attn_sum[1].T,
        attn_sum[2].T,
        attn_sum[3],
        norm_sums[2],
        norm_sums[3],
        up_sum.astype(F32).T,
        down_sum.astype(F32),
    )


def solution(mesh):
    return jax.shard_map(
        functools.partial(shards, mesh.shape["dp"], mesh.shape["mp"]),
        mesh=mesh,
        in_specs=(
            P(("dp", "mp"), None),
            P("dp", None),
            P(),
            P(),
            P(None, "mp"),
            P(None, "mp"),
            P(None, "mp"),
            P("mp", None),
            P(),
            P(),
            P(None, "mp"),
            P("mp", None),
            P(("dp", "mp"), None),
        ),
        out_specs=(
            P(("dp", "mp"), None),
            P(("dp", "mp"), None),
            P("mp"),
            P("mp"),
            P(None, "mp"),
            P(None, "mp"),
            P(None, "mp"),
            P("mp", None),
            P("mp"),
            P("mp"),
            P(None, "mp"),
            P("mp", None),
        ),
        check_vma=False,
    )
```

```python
import functools
import math

import jax
import jax.numpy as jnp
from jax import lax
from jax.experimental import pallas as pl
from jax.experimental.pallas import tpu as pltpu
from jax.sharding import PartitionSpec as P

HEAD_DIM = 48
PAIR = 2 * HEAD_DIM
IMAGES = 4
TILE = 128
norm_eps = 1e-06
negative_fill = -1e30
SCALE = HEAD_DIM ** (-0.5)
SCALE_LOG2 = SCALE * math.log2(math.e)
BF16 = jnp.bfloat16
F32 = jnp.float32


def layer_norm(values, gain, bias):
    center = jnp.mean(values, axis=-1, keepdims=True)
    shifted = values - center
    spread = jnp.mean(shifted * shifted, axis=-1, keepdims=True)
    return shifted * lax.rsqrt(spread + norm_eps) * gain + bias


def dot(left, right, dims):
    return lax.dot_general(left, right, (dims, ((), ())), preferred_element_type=F32)


NN = ((1,), (0,))
NT = ((1,), (1,))
TN = ((0,), (0,))


def window_kinds(tiles):
    return tuple(n for n in (2, 3, 4, 5) if n < tiles) + (tiles,)


def image_rows(segs, length):
    row = lax.broadcasted_iota(jnp.int32, (TILE - PAIR, length), 0)
    here = row == segs
    one_hot = jnp.where(here, 1.0, 0.0).astype(BF16)
    fill = jnp.where(jnp.logical_or(here, row >= IMAGES), 0.0, negative_fill).astype(BF16)
    return one_hot, fill


def side_by_side(pair, extra):
    blank = jnp.zeros((HEAD_DIM, TILE), BF16)
    left = jnp.concatenate([pair[:HEAD_DIM], blank, extra], axis=0)
    right = jnp.concatenate([blank, pair[HEAD_DIM:], extra], axis=0)
    return jnp.concatenate([left, right], axis=1)


def attend_forward_kernel(
    first_ref, kind_ref, segs_ref, qv_ref, k_ref, out_ref, lse_ref, hot_ref, keys_ref, vals_ref
):
    q_ref, v_ref = qv_ref.at[0], qv_ref.at[1]
    length = q_ref.shape[1]
    pairs = q_ref.shape[0] // PAIR
    one_hot, fill = image_rows(segs_ref[...], length)
    hot_ref[...] = one_hot
    for j in range(pairs):
        rows = slice(PAIR * j, PAIR * (j + 1))
        keys_ref[j] = jnp.concatenate([k_ref[rows, :], fill], axis=0).T
        vals_ref[j] = jnp.concatenate([v_ref[rows, :], jnp.ones((16, length), BF16)], axis=0)

    def block(b, carry):
        at = pl.ds(pl.multiple_of(b * TILE, TILE), TILE)
        first = pl.multiple_of(first_ref[b] * TILE, TILE)

        def variant(tiles):
            span = pl.ds(first, tiles * TILE)
            for j in range(pairs):
                top = PAIR * j
                query = side_by_side(q_ref[top : top + PAIR, at], hot_ref[:, at])
                scores = dot(keys_ref[j, span, :], query, NN)
                most = jnp.max(scores, axis=0, keepdims=True)
                expo = jnp.exp2((scores - most) * SCALE_LOG2).astype(BF16)
                mixed = dot(vals_ref[j, :, span], expo, NN)
                total = mixed[PAIR : PAIR + 1, :]
                inverse = 1.0 / total
                out_ref[top : top + HEAD_DIM, at] = (
                    mixed[:HEAD_DIM, :TILE] * inverse[:, :TILE]
                ).astype(BF16)
                out_ref[top + HEAD_DIM : top + PAIR, at] = (
                    mixed[HEAD_DIM:PAIR, TILE:] * inverse[:, TILE:]
                ).astype(BF16)
                lse_ref[j, pl.ds(b, 1), :] = most * SCALE_LOG2 + jnp.log2(total)

        for tiles in window_kinds(length // TILE):
            pl.when(kind_ref[b] == tiles)(functools.partial(variant, tiles))
        return carry

    lax.fori_loop(0, length // TILE, block, 0)


def attend_backward_kernel(
    first_ref,
    kind_ref,
    segs_ref,
    qv_ref,
    k_ref,
    att_ref,
    grad_ref,
    lse_ref,
    dqv_ref,
    dk_ref,
    hot_ref,
    keys_ref,
    vals_ref,
    queries_ref,
    grads_ref,
    key_sum_ref,
    val_sum_ref,
):
    q_ref, v_ref = qv_ref.at[0], qv_ref.at[1]
    dq_ref, dv_ref = dqv_ref.at[0], dqv_ref.at[1]
    length = q_ref.shape[1]
    pairs = q_ref.shape[0] // PAIR
    one_hot, fill = image_rows(segs_ref[...], length)
    hot_ref[...] = one_hot
    pad = jnp.zeros((TILE - PAIR, length), BF16)
    for j in range(pairs):
        rows = slice(PAIR * j, PAIR * (j + 1))
        keys_ref[j] = jnp.concatenate([k_ref[rows, :], fill], axis=0).T
        vals_ref[j] = jnp.concatenate([v_ref[rows, :], pad], axis=0).T
        queries_ref[j] = jnp.concatenate([q_ref[rows, :], pad], axis=0).T
        grads_ref[j] = jnp.concatenate([grad_ref[rows, :], pad], axis=0).T
    key_sum_ref[...] = jnp.zeros(key_sum_ref.shape, F32)
    val_sum_ref[...] = jnp.zeros(val_sum_ref.shape, F32)
    no_rows = jnp.zeros((TILE - PAIR, TILE), BF16)
    lane = lax.broadcasted_iota(jnp.int32, (TILE, TILE), 1)
    in_first = lane < HEAD_DIM

    def stacked(both):
        blank = jnp.zeros_like(both)
        return jnp.concatenate(
            [jnp.where(in_first, both, blank), jnp.where(in_first, blank, both)], axis=0
        )

    def block(b, carry):
        at = pl.ds(pl.multiple_of(b * TILE, TILE), TILE)
        first = pl.multiple_of(first_ref[b] * TILE, TILE)

        def variant(tiles):
            span = pl.ds(first, tiles * TILE)
            for j in range(pairs):
                top = PAIR * j
                query = side_by_side(q_ref[top : top + PAIR, at], hot_ref[:, at])
                grad = grad_ref[top : top + PAIR, at]
                agree = grad.astype(F32) * att_ref[top : top + PAIR, at].astype(F32)
                delta = jnp.concatenate(
                    [
                        jnp.sum(agree[:HEAD_DIM], axis=0, keepdims=True),
                        jnp.sum(agree[HEAD_DIM:], axis=0, keepdims=True),
                    ],
                    axis=1,
                )
                scores = dot(keys_ref[j, span, :], query, NN)
                probs = jnp.exp2(scores * SCALE_LOG2 - lse_ref[j, pl.ds(b, 1), :])
                prob_grad = dot(vals_ref[j, span, :], side_by_side(grad, no_rows), NN)
                score_grad = (probs * (prob_grad - delta)).astype(BF16)
                val_sum_ref[j, span, :] += dot(
                    probs.astype(BF16), stacked(grads_ref[j, at, :]), NN
                )
                key_sum_ref[j, span, :] += dot(score_grad, stacked(queries_ref[j, at, :]), NN)
                query_grad = dot(k_ref[top : top + PAIR, span], score_grad, NN) * SCALE
                dq_ref[top : top + HEAD_DIM, at] = query_grad[:HEAD_DIM, :TILE].astype(BF16)
                dq_ref[top + HEAD_DIM : top + PAIR, at] = query_grad[HEAD_DIM:, TILE:].astype(BF16)

        for tiles in window_kinds(length // TILE):
            pl.when(kind_ref[b] == tiles)(functools.partial(variant, tiles))
        return carry

    lax.fori_loop(0, length // TILE, block, 0)
    for j in range(pairs):
        rows = slice(PAIR * j, PAIR * (j + 1))
        dk_ref[rows, :] = (key_sum_ref[j] * SCALE).T[:PAIR].astype(BF16)
        dv_ref[rows, :] = val_sum_ref[j].T[:PAIR].astype(BF16)


def windows(segs):
    length = segs.shape[0]
    tiles = length // TILE
    by_tile = segs.reshape(tiles, TILE)
    begin = jnp.sum(segs[None, :] < by_tile[:, :1], axis=1)
    end = jnp.sum(segs[None, :] <= by_tile[:, -1:], axis=1)
    first = begin // TILE
    need = (end + TILE - 1) // TILE - first
    kinds = jnp.asarray(window_kinds(tiles), jnp.int32)
    kind = jnp.min(jnp.where(kinds[None, :] >= need[:, None], kinds[None, :], tiles), axis=1)
    return jnp.minimum(first, tiles - kind).astype(jnp.int32), kind.astype(jnp.int32)


def attention_specs(heads, length):
    pairs = heads // 2
    step = 2 if pairs % 2 == 0 else 1
    rows = pl.BlockSpec((step * PAIR, length), lambda i, *_: (i, 0))
    two = pl.BlockSpec((2, step * PAIR, length), lambda i, *_: (0, i, 0))
    segs = pl.BlockSpec((1, length), lambda i, *_: (0, 0))
    lse = pl.BlockSpec((step, length // TILE, 2 * TILE), lambda i, *_: (i, 0, 0))
    return pairs, step, rows, two, segs, lse


def attend_forward(query_value, keys, segs, first, kind):
    length = segs.shape[0]
    heads = keys.shape[0] // HEAD_DIM
    pairs, step, rows, two, segs_spec, lse = attention_specs(heads, length)
    work = heads * length * length * HEAD_DIM
    return pl.pallas_call(
        attend_forward_kernel,
        grid_spec=pltpu.PrefetchScalarGridSpec(
            num_scalar_prefetch=2,
            grid=(pairs // step,),
            in_specs=[segs_spec, two, rows],
            out_specs=[rows, lse],
            scratch_shapes=[
                pltpu.VMEM((TILE - PAIR, length), BF16),
                pltpu.VMEM((step, length, TILE), BF16),
                pltpu.VMEM((step, PAIR + 16, length), BF16),
            ],
        ),
        out_shape=[
            jax.ShapeDtypeStruct(keys.shape, BF16),
            jax.ShapeDtypeStruct((pairs, length // TILE, 2 * TILE), F32),
        ],
        compiler_params=pltpu.CompilerParams(vmem_limit_bytes=40 << 20),
        cost_estimate=pl.CostEstimate(
            flops=20 * work, bytes_accessed=8 * keys.size, transcendentals=heads * length * length // 2
        ),
        name="attend_forward",
    )(first, kind, segs[None, :], query_value, keys)


def attend_backward(query_value, keys, attended, grad, lse, segs, first, kind):
    length = segs.shape[0]
    heads = keys.shape[0] // HEAD_DIM
    pairs, step, rows, two, segs_spec, lse_spec = attention_specs(heads, length)
    work = heads * length * length * HEAD_DIM
    wide = pltpu.VMEM((step, length, TILE), BF16)
    total = pltpu.VMEM((step, length, TILE), F32)
    return pl.pallas_call(
        attend_backward_kernel,
        grid_spec=pltpu.PrefetchScalarGridSpec(
            num_scalar_prefetch=2,
            grid=(pairs // step,),
            in_specs=[segs_spec, two, rows, rows, rows, lse_spec],
            out_specs=[two, rows],
            scratch_shapes=[
                pltpu.VMEM((TILE - PAIR, length), BF16),
                wide,
                wide,
                wide,
                wide,
                total,
                total,
            ],
        ),
        out_shape=[
            jax.ShapeDtypeStruct(query_value.shape, BF16),
            jax.ShapeDtypeStruct(keys.shape, BF16),
        ],
        compiler_params=pltpu.CompilerParams(vmem_limit_bytes=40 << 20),
        cost_estimate=pl.CostEstimate(
            flops=20 * work, bytes_accessed=16 * keys.size, transcendentals=heads * length * length // 2
        ),
        name="attend_backward",
    )(first, kind, segs[None, :], query_value, keys, attended, grad, lse)


def gelu_parts(values):
    below = 0.5 * (1.0 + lax.erf(values * (0.5 ** 0.5)))
    density = jnp.exp(values * values * -0.5) * ((2.0 * math.pi) ** -0.5)
    return values * below, below + values * density


def feed_forward_kernel(norm_ref, cot_ref, *refs):
    parts = (len(refs) - 6) // 2
    up_refs, down_refs = refs[:parts], refs[parts : 2 * parts]
    mlp_ref, back_ref, up_grad_ref, down_grad_ref, act_ref, pre_ref = refs[2 * parts :]
    rows = norm_ref.shape[0]
    chunk = min(rows, 256)

    def part(g):
        up_ref, down_ref = up_refs[g], down_refs[g]
        for start in range(0, rows, chunk):
            at = slice(start, start + chunk)
            pre_act = dot(norm_ref[at, :], up_ref[...], NT)
            act_grad = dot(cot_ref[at, :], down_ref[...], NT)
            activation, slope = gelu_parts(pre_act)
            activation = activation.astype(BF16)
            pre_grad = (act_grad * slope).astype(BF16)
            act_ref[at, :] = activation
            pre_ref[at, :] = pre_grad
            mlp = dot(activation, down_ref[...], NN)
            back = dot(pre_grad, up_ref[...], NN)
            if g == 0:
                mlp_ref[at, :] = mlp
                back_ref[at, :] = back
            else:
                mlp_ref[at, :] += mlp
                back_ref[at, :] += back
        down_grad_ref[...] = dot(act_ref[...], cot_ref[...], TN).astype(BF16)
        up_grad_ref[...] = dot(pre_ref[...], norm_ref[...], TN).astype(BF16)

    for g in range(parts):
        pl.when(pl.program_id(0) == g)(functools.partial(part, g))


def feed_forward(norm, cot, ups, downs):
    rows, width = norm.shape
    parts = len(ups)
    hidden = ups[0].shape[0]
    whole = pl.BlockSpec((rows, width), lambda i: (0, 0))
    block = pl.BlockSpec((hidden, width), lambda i: (0, 0))
    grads = pl.BlockSpec((None, hidden, width), lambda i: (i, 0, 0))
    return pl.pallas_call(
        feed_forward_kernel,
        grid=(parts,),
        in_specs=[whole, whole] + [block] * (2 * parts),
        out_specs=[whole, whole, grads, grads],
        out_shape=[
            jax.ShapeDtypeStruct((rows, width), F32),
            jax.ShapeDtypeStruct((rows, width), F32),
            jax.ShapeDtypeStruct((parts, hidden, width), BF16),
            jax.ShapeDtypeStruct((parts, hidden, width), BF16),
        ],
        scratch_shapes=[pltpu.VMEM((rows, hidden), BF16), pltpu.VMEM((rows, hidden), BF16)],
        compiler_params=pltpu.CompilerParams(vmem_limit_bytes=56 << 20),
        cost_estimate=pl.CostEstimate(
            flops=12 * rows * width * hidden * parts,
            bytes_accessed=8 * hidden * parts * width + 12 * rows * width,
            transcendentals=2 * rows * hidden * parts,
        ),
        name="feed_forward",
    )(norm, cot, *ups, *downs)


def add(*terms):
    return functools.reduce(jnp.add, [item.astype(F32) for item in terms]).astype(BF16)


class Hypercube:
    def __init__(self, at_dp):
        self.at_y = at_dp // 2
        self.at_core = at_dp % 2

    def swap(self, values, axis):
        name, size, mask = {"core": ("dp", 4, 1), "y": ("dp", 4, 2), "x": ("mp", 8, 1)}[axis]
        return lax.ppermute(values, name, [(i, i ^ mask) for i in range(size)])

    def send_z(self, values, offset):
        return lax.ppermute(values, "mp", [(i, i ^ (2 * offset)) for i in range(8)])

    def order(self, at, mine, other):
        return jnp.where(at == 0, jnp.stack([mine, other]), jnp.stack([other, mine]))

    def gather(self, piece, fixed):
        _, count, width = piece.shape
        along_z = jnp.stack([piece] + [self.send_z(piece, offset) for offset in (1, 2, 3)])
        one = along_z[:, 0].reshape(4 * count, width)
        two = along_z[:, 1].reshape(4 * count, width)
        stack_y = functools.partial(self.order, self.at_y) if fixed else lambda a, b: jnp.stack([a, b])
        one = jnp.concatenate([one, self.swap(one, "x")], axis=0)
        two = stack_y(two, self.swap(two, "y"))
        one = stack_y(one, self.swap(one, "y"))
        two = jnp.concatenate([two, self.swap(two, "x")], axis=1)
        return (one, two), (self.swap(one, "core"), self.swap(two, "core"))

    def reduce(self, mine, other, fixed):
        one, two = [add(a, self.swap(b, "core")) for a, b in zip(mine, other)]
        half = one.shape[1] // 2
        count = half // 4

        def halve_y(values):
            if fixed:
                keep = lax.dynamic_index_in_dim(values, self.at_y, 0, keepdims=False)
                send = lax.dynamic_index_in_dim(values, 1 - self.at_y, 0, keepdims=False)
            else:
                keep, send = values[0], values[1]
            return add(keep, self.swap(send, "y"))

        one = halve_y(one)
        two = add(two[:, :half], self.swap(two[:, half:], "x"))
        one = add(one[:half], self.swap(one[half:], "x"))
        two = halve_y(two)
        along_z = jnp.stack([one.reshape(4, count, -1), two.reshape(4, count, -1)], axis=1)
        piece = add(along_z[0], *[self.send_z(along_z[offset], offset) for offset in (1, 2, 3)])
        pieces = self.order(self.at_y, piece, self.swap(piece, "y"))
        return self.order(self.at_core, pieces, self.swap(pieces, "core"))

    def total(self, values):
        for axis in ("core", "y", "x"):
            values = values + self.swap(values, axis)
        return values + self.send_z(values, 1) + self.send_z(values, 2) + self.send_z(values, 3)


class Plain:
    def __init__(self, mp_size):
        self.mp_size = mp_size

    def gather(self, parts):
        return lax.all_gather(parts, "mp", axis=1, tiled=True)

    def reduce(self, parts):
        return lax.psum(lax.psum_scatter(parts, "mp", scatter_dimension=1, tiled=True), "dp")

    def total(self, values):
        return lax.psum(values, ("dp", "mp"))


def shards(
    dp_size,
    mp_size,
    inputs,
    segments,
    ln1_gain,
    ln1_bias,
    w_query,
    w_key,
    w_value,
    w_output,
    ln2_gain,
    ln2_bias,
    w_up,
    w_down,
    cotangent,
):
    rows, width = inputs.shape
    seq_count, seq_length = segments.shape
    local = w_query.shape[1]
    shared_by = seq_length // rows
    at_mp = lax.axis_index("mp")
    at_dp = lax.axis_index("dp")
    cube = dp_size == 4 and mp_size == 8 and shared_by == 1
    comm = Hypercube(at_dp) if cube else Plain(mp_size)

    groups = [
        [start + i for i in range(shared_by)] for start in range(0, mp_size, shared_by)
    ]

    def to_heads(values):
        if shared_by == 1:
            return values
        axis = values.ndim - 2
        return lax.all_to_all(
            values, "mp", axis, axis + 1, axis_index_groups=groups, tiled=True
        )

    def to_tokens(values):
        if shared_by == 1:
            return values
        axis = values.ndim - 2
        return lax.all_to_all(
            values, "mp", axis + 1, axis, axis_index_groups=groups, tiled=True
        )

    attn_local = jnp.stack([w_query.T, w_key.T, w_value.T, w_output])
    mlp_local = jnp.stack([w_up.T, w_down])
    if cube:
        attn_pieces = attn_local.reshape(2, 2, 2, HEAD_DIM, width).transpose(0, 2, 1, 3, 4)
        attn_piece = lax.dynamic_index_in_dim(
            attn_pieces.reshape(4, 2, HEAD_DIM, width), at_dp, 0, keepdims=False
        )
        attn_weights = comm.gather(attn_piece, True)
        mlp_pieces = mlp_local.reshape(2, 2, 4, -1, width)
        mlp_mine = lax.dynamic_index_in_dim(mlp_pieces, at_dp, 2, keepdims=False)
        mlp_weights = [comm.gather(mlp_mine[:, half], False) for half in range(2)]
        mlp_weights = [
            [[kind.reshape(-1, width) for kind in group] for group in unit] for unit in mlp_weights
        ]
    else:
        everything = comm.gather(attn_local)
        attn_weights = [(everything[0::2], everything[1::2])]
        everything = comm.gather(mlp_local)
        mlp_weights = [[everything]]

    segs = lax.dynamic_index_in_dim(segments, at_mp // shared_by, 0, keepdims=False)
    first, kind = windows(segs)

    resid_in = inputs.astype(F32)
    norm_one = layer_norm(resid_in, ln1_gain, ln1_bias).astype(BF16)
    residual = resid_in
    saved = []
    for query_value_w, key_out_w in attn_weights:
        count = query_value_w.shape[1]
        query_value = dot(query_value_w.reshape(2 * count, width), norm_one, NT).astype(BF16)
        query_value = to_heads(query_value.reshape(2, count, rows))
        keys = to_heads(dot(key_out_w[0], norm_one, NT).astype(BF16))
        heads_out, lse = attend_forward(query_value, keys, segs, first, kind)
        attended = to_tokens(heads_out)
        residual = residual + dot(attended, key_out_w[1], TN)
        saved.append((query_value, keys, heads_out, lse, attended))
    norm_two = layer_norm(residual, ln2_gain, ln2_bias).astype(BF16)

    result = residual
    norm_two_grad = 0.0
    mlp_sums = []
    for unit in mlp_weights:
        ups, downs = [group[0] for group in unit], [group[1] for group in unit]
        mlp, back, up_grad, down_grad = feed_forward(norm_two, cotangent, ups, downs)
        result = result + mlp
        norm_two_grad = norm_two_grad + back
        if cube:
            mine, other = [
                [grad[g].reshape(2, -1, width) for grad in (up_grad, down_grad)] for g in range(2)
            ]
            mlp_sums.append(comm.reduce(mine, other, False))
        else:
            mlp_sums = comm.reduce(jnp.concatenate([up_grad, down_grad], axis=0))
    output = result.astype(BF16)

    norm_two_back = jax.vjp(layer_norm, residual, ln2_gain, ln2_bias)[1]
    resid_part, gain_two_grad, bias_two_grad = norm_two_back(norm_two_grad)
    norm_two_sums = comm.total(jnp.stack([gain_two_grad, bias_two_grad]))
    res_grad = cotangent.astype(F32) + resid_part
    branch_grad = res_grad.astype(BF16)

    norm_one_grad = 0.0
    attn_grads = []
    for (query_value_w, key_out_w), (query_value, keys, heads_out, lse, attended) in list(
        zip(attn_weights, saved)
    )[::-1]:
        count = query_value_w.shape[1]
        out_grad = dot(attended, branch_grad, NN).astype(BF16)
        att_grad = to_heads(dot(key_out_w[1], branch_grad, NT).astype(BF16))
        query_value_grad, key_grad = attend_backward(
            query_value, keys, heads_out, att_grad, lse, segs, first, kind
        )
        query_value_grad = to_tokens(query_value_grad).reshape(2 * count, rows)
        key_grad = to_tokens(key_grad)
        attn_grads.append(
            (
                dot(query_value_grad, norm_one, NN).astype(BF16).reshape(2, count, width),
                jnp.stack([dot(key_grad, norm_one, NN).astype(BF16), out_grad]),
            )
        )
        norm_one_grad = (
            norm_one_grad
            + dot(query_value_grad, query_value_w.reshape(2 * count, width), TN)
            + dot(key_grad, key_out_w[0], TN)
        )
    norm_one_back = jax.vjp(layer_norm, resid_in, ln1_gain, ln1_bias)[1]
    input_part, gain_one_grad, bias_one_grad = norm_one_back(norm_one_grad)
    norm_one_sums = comm.total(jnp.stack([gain_one_grad, bias_one_grad]))
    in_grad = (res_grad + input_part).astype(BF16)

    if cube:
        sums = comm.reduce(attn_grads[1], attn_grads[0], True)
        attn_sum = sums.transpose(1, 2, 0, 3, 4).reshape(4, local, width).astype(F32)
        sums = jnp.stack(mlp_sums)
        up_sum, down_sum = (
            sums.transpose(3, 0, 2, 1, 4, 5).reshape(2, -1, width).astype(F32)
        )
    else:
        query_value_sum, key_out_sum = [comm.reduce(item) for item in attn_grads[0]]
        attn_sum = jnp.stack(
            [query_value_sum[0], key_out_sum[0], query_value_sum[1], key_out_sum[1]]
        ).astype(F32)
        up_sum, down_sum = mlp_sums.astype(F32)

    norm_sums = lax.dynamic_slice_in_dim(
        jnp.concatenate([norm_one_sums, norm_two_sums]),
        at_mp * (width // mp_size),
        width // mp_size,
        1,
    )
    return (
        output,
        in_grad,
        norm_sums[0],
        norm_sums[1],
        attn_sum[0].T,
        attn_sum[1].T,
        attn_sum[2].T,
        attn_sum[3],
        norm_sums[2],
        norm_sums[3],
        up_sum.T,
        down_sum,
    )


def solution(mesh):
    return jax.shard_map(
        functools.partial(shards, mesh.shape["dp"], mesh.shape["mp"]),
        mesh=mesh,
        in_specs=(
            P(("dp", "mp"), None),
            P("dp", None),
            P(),
            P(),
            P(None, "mp"),
            P(None, "mp"),
            P(None, "mp"),
            P("mp", None),
            P(),
            P(),
            P(None, "mp"),
            P("mp", None),
            P(("dp", "mp"), None),
        ),
        out_specs=(
            P(("dp", "mp"), None),
            P(("dp", "mp"), None),
            P("mp"),
            P("mp"),
            P(None, "mp"),
            P(None, "mp"),
            P(None, "mp"),
            P("mp", None),
            P("mp"),
            P("mp"),
            P(None, "mp"),
            P("mp", None),
        ),
        check_vma=False,
    )
```

```python
import functools
import math

import jax
import jax.numpy as jnp
from jax import lax
from jax.experimental import pallas as pl
from jax.experimental.pallas import tpu as pltpu
from jax.sharding import PartitionSpec as P

HEAD_DIM = 48
PAIR = 2 * HEAD_DIM
IMAGES = 4
TILE = 128
norm_eps = 1e-06
negative_fill = -1e30
SCALE = HEAD_DIM ** (-0.5)
SCALE_LOG2 = SCALE * math.log2(math.e)
BF16 = jnp.bfloat16
F32 = jnp.float32


def layer_norm(values, gain, bias):
    center = jnp.mean(values, axis=-1, keepdims=True)
    shifted = values - center
    spread = jnp.mean(shifted * shifted, axis=-1, keepdims=True)
    return shifted * lax.rsqrt(spread + norm_eps) * gain + bias


def dot(left, right, dims):
    return lax.dot_general(left, right, (dims, ((), ())), preferred_element_type=F32)


NN = ((1,), (0,))
NT = ((1,), (1,))
TN = ((0,), (0,))


def window_kinds(tiles):
    return tuple(n for n in (2, 3, 4, 5) if n < tiles) + (tiles,)


def image_rows(segs, length):
    row = lax.broadcasted_iota(jnp.int32, (TILE - PAIR, length), 0)
    here = row == segs
    one_hot = jnp.where(here, 1.0, 0.0).astype(BF16)
    fill = jnp.where(jnp.logical_or(here, row >= IMAGES), 0.0, negative_fill).astype(BF16)
    return one_hot, fill


def side_by_side(pair, extra):
    blank = jnp.zeros((HEAD_DIM, TILE), BF16)
    left = jnp.concatenate([pair[:HEAD_DIM], blank, extra], axis=0)
    right = jnp.concatenate([blank, pair[HEAD_DIM:], extra], axis=0)
    return jnp.concatenate([left, right], axis=1)


def attend_forward_kernel(
    first_ref, kind_ref, segs_ref, qv_ref, k_ref, out_ref, lse_ref, hot_ref, keys_ref, vals_ref
):
    q_ref, v_ref = qv_ref.at[0], qv_ref.at[1]
    length = q_ref.shape[1]
    pairs = q_ref.shape[0] // PAIR
    one_hot, fill = image_rows(segs_ref[...], length)
    hot_ref[...] = one_hot
    for j in range(pairs):
        rows = slice(PAIR * j, PAIR * (j + 1))
        keys_ref[j] = jnp.concatenate([k_ref[rows, :], fill], axis=0).T
        vals_ref[j] = jnp.concatenate([v_ref[rows, :], jnp.ones((16, length), BF16)], axis=0)

    def block(b, carry):
        at = pl.ds(pl.multiple_of(b * TILE, TILE), TILE)
        first = pl.multiple_of(first_ref[b] * TILE, TILE)

        def variant(tiles):
            span = pl.ds(first, tiles * TILE)
            for j in range(pairs):
                top = PAIR * j
                query = side_by_side(q_ref[top : top + PAIR, at], hot_ref[:, at])
                scores = dot(keys_ref[j, span, :], query, NN)
                most = jnp.max(scores, axis=0, keepdims=True)
                expo = jnp.exp2((scores - most) * SCALE_LOG2).astype(BF16)
                mixed = dot(vals_ref[j, :, span], expo, NN)
                total = mixed[PAIR : PAIR + 1, :]
                inverse = 1.0 / total
                out_ref[top : top + HEAD_DIM, at] = (
                    mixed[:HEAD_DIM, :TILE] * inverse[:, :TILE]
                ).astype(BF16)
                out_ref[top + HEAD_DIM : top + PAIR, at] = (
                    mixed[HEAD_DIM:PAIR, TILE:] * inverse[:, TILE:]
                ).astype(BF16)
                lse_ref[j, pl.ds(b, 1), :] = most * SCALE_LOG2 + jnp.log2(total)

        for tiles in window_kinds(length // TILE):
            pl.when(kind_ref[b] == tiles)(functools.partial(variant, tiles))
        return carry

    lax.fori_loop(0, length // TILE, block, 0)


def attend_backward_kernel(
    first_ref,
    kind_ref,
    segs_ref,
    qv_ref,
    k_ref,
    att_ref,
    grad_ref,
    lse_ref,
    dqv_ref,
    dk_ref,
    hot_ref,
    keys_ref,
    vals_ref,
    queries_ref,
    grads_ref,
    key_sum_ref,
    val_sum_ref,
):
    q_ref, v_ref = qv_ref.at[0], qv_ref.at[1]
    dq_ref, dv_ref = dqv_ref.at[0], dqv_ref.at[1]
    length = q_ref.shape[1]
    pairs = q_ref.shape[0] // PAIR
    one_hot, fill = image_rows(segs_ref[...], length)
    hot_ref[...] = one_hot
    pad = jnp.zeros((TILE - PAIR, length), BF16)
    for j in range(pairs):
        rows = slice(PAIR * j, PAIR * (j + 1))
        keys_ref[j] = jnp.concatenate([k_ref[rows, :], fill], axis=0).T
        vals_ref[j] = jnp.concatenate([v_ref[rows, :], pad], axis=0).T
        queries_ref[j] = jnp.concatenate([q_ref[rows, :], pad], axis=0).T
        grads_ref[j] = jnp.concatenate([grad_ref[rows, :], pad], axis=0).T
    key_sum_ref[...] = jnp.zeros(key_sum_ref.shape, F32)
    val_sum_ref[...] = jnp.zeros(val_sum_ref.shape, F32)
    no_rows = jnp.zeros((TILE - PAIR, TILE), BF16)
    lane = lax.broadcasted_iota(jnp.int32, (TILE, TILE), 1)
    in_first = lane < HEAD_DIM

    def stacked(both):
        blank = jnp.zeros_like(both)
        return jnp.concatenate(
            [jnp.where(in_first, both, blank), jnp.where(in_first, blank, both)], axis=0
        )

    def block(b, carry):
        at = pl.ds(pl.multiple_of(b * TILE, TILE), TILE)
        first = pl.multiple_of(first_ref[b] * TILE, TILE)

        def variant(tiles):
            span = pl.ds(first, tiles * TILE)
            for j in range(pairs):
                top = PAIR * j
                query = side_by_side(q_ref[top : top + PAIR, at], hot_ref[:, at])
                grad = grad_ref[top : top + PAIR, at]
                agree = grad.astype(F32) * att_ref[top : top + PAIR, at].astype(F32)
                delta = jnp.concatenate(
                    [
                        jnp.sum(agree[:HEAD_DIM], axis=0, keepdims=True),
                        jnp.sum(agree[HEAD_DIM:], axis=0, keepdims=True),
                    ],
                    axis=1,
                )
                scores = dot(keys_ref[j, span, :], query, NN)
                probs = jnp.exp2(scores * SCALE_LOG2 - lse_ref[j, pl.ds(b, 1), :])
                prob_grad = dot(vals_ref[j, span, :], side_by_side(grad, no_rows), NN)
                score_grad = (probs * (prob_grad - delta)).astype(BF16)
                val_sum_ref[j, span, :] += dot(
                    probs.astype(BF16), stacked(grads_ref[j, at, :]), NN
                )
                key_sum_ref[j, span, :] += dot(score_grad, stacked(queries_ref[j, at, :]), NN)
                query_grad = dot(k_ref[top : top + PAIR, span], score_grad, NN) * SCALE
                dq_ref[top : top + HEAD_DIM, at] = query_grad[:HEAD_DIM, :TILE].astype(BF16)
                dq_ref[top + HEAD_DIM : top + PAIR, at] = query_grad[HEAD_DIM:, TILE:].astype(BF16)

        for tiles in window_kinds(length // TILE):
            pl.when(kind_ref[b] == tiles)(functools.partial(variant, tiles))
        return carry

    lax.fori_loop(0, length // TILE, block, 0)
    for j in range(pairs):
        rows = slice(PAIR * j, PAIR * (j + 1))
        dk_ref[rows, :] = (key_sum_ref[j] * SCALE).T[:PAIR].astype(BF16)
        dv_ref[rows, :] = val_sum_ref[j].T[:PAIR].astype(BF16)


def windows(segs):
    length = segs.shape[0]
    tiles = length // TILE
    by_tile = segs.reshape(tiles, TILE)
    begin = jnp.sum(segs[None, :] < by_tile[:, :1], axis=1)
    end = jnp.sum(segs[None, :] <= by_tile[:, -1:], axis=1)
    first = begin // TILE
    need = (end + TILE - 1) // TILE - first
    kinds = jnp.asarray(window_kinds(tiles), jnp.int32)
    kind = jnp.min(jnp.where(kinds[None, :] >= need[:, None], kinds[None, :], tiles), axis=1)
    return jnp.minimum(first, tiles - kind).astype(jnp.int32), kind.astype(jnp.int32)


def attention_specs(heads, length):
    pairs = heads // 2
    step = 2 if pairs % 2 == 0 else 1
    rows = pl.BlockSpec((step * PAIR, length), lambda i, *_: (i, 0))
    two = pl.BlockSpec((2, step * PAIR, length), lambda i, *_: (0, i, 0))
    segs = pl.BlockSpec((1, length), lambda i, *_: (0, 0))
    lse = pl.BlockSpec((step, length // TILE, 2 * TILE), lambda i, *_: (i, 0, 0))
    return pairs, step, rows, two, segs, lse


def attend_forward(query_value, keys, segs, first, kind):
    length = segs.shape[0]
    heads = keys.shape[0] // HEAD_DIM
    pairs, step, rows, two, segs_spec, lse = attention_specs(heads, length)
    work = heads * length * length * HEAD_DIM
    return pl.pallas_call(
        attend_forward_kernel,
        grid_spec=pltpu.PrefetchScalarGridSpec(
            num_scalar_prefetch=2,
            grid=(pairs // step,),
            in_specs=[segs_spec, two, rows],
            out_specs=[rows, lse],
            scratch_shapes=[
                pltpu.VMEM((TILE - PAIR, length), BF16),
                pltpu.VMEM((step, length, TILE), BF16),
                pltpu.VMEM((step, PAIR + 16, length), BF16),
            ],
        ),
        out_shape=[
            jax.ShapeDtypeStruct(keys.shape, BF16),
            jax.ShapeDtypeStruct((pairs, length // TILE, 2 * TILE), F32),
        ],
        compiler_params=pltpu.CompilerParams(vmem_limit_bytes=40 << 20),
        cost_estimate=pl.CostEstimate(
            flops=20 * work, bytes_accessed=8 * keys.size, transcendentals=heads * length * length // 2
        ),
        name="attend_forward",
    )(first, kind, segs[None, :], query_value, keys)


def attend_backward(query_value, keys, attended, grad, lse, segs, first, kind):
    length = segs.shape[0]
    heads = keys.shape[0] // HEAD_DIM
    pairs, step, rows, two, segs_spec, lse_spec = attention_specs(heads, length)
    work = heads * length * length * HEAD_DIM
    wide = pltpu.VMEM((step, length, TILE), BF16)
    total = pltpu.VMEM((step, length, TILE), F32)
    return pl.pallas_call(
        attend_backward_kernel,
        grid_spec=pltpu.PrefetchScalarGridSpec(
            num_scalar_prefetch=2,
            grid=(pairs // step,),
            in_specs=[segs_spec, two, rows, rows, rows, lse_spec],
            out_specs=[two, rows],
            scratch_shapes=[
                pltpu.VMEM((TILE - PAIR, length), BF16),
                wide,
                wide,
                wide,
                wide,
                total,
                total,
            ],
        ),
        out_shape=[
            jax.ShapeDtypeStruct(query_value.shape, BF16),
            jax.ShapeDtypeStruct(keys.shape, BF16),
        ],
        compiler_params=pltpu.CompilerParams(vmem_limit_bytes=40 << 20),
        cost_estimate=pl.CostEstimate(
            flops=20 * work, bytes_accessed=16 * keys.size, transcendentals=heads * length * length // 2
        ),
        name="attend_backward",
    )(first, kind, segs[None, :], query_value, keys, attended, grad, lse)


def gelu_parts(values):
    below = 0.5 * (1.0 + lax.erf(values * (0.5 ** 0.5)))
    density = jnp.exp(values * values * -0.5) * ((2.0 * math.pi) ** -0.5)
    return values * below, below + values * density


def feed_forward_kernel(norm_ref, cot_ref, up_ref, down_ref, mlp_ref, back_ref, grad_ref, act_ref, pre_ref):
    rows = norm_ref.shape[0]
    chunk = min(rows, 256)

    @pl.when(pl.program_id(0) == 0)
    def _():
        mlp_ref[...] = jnp.zeros(mlp_ref.shape, F32)
        back_ref[...] = jnp.zeros(back_ref.shape, F32)

    for start in range(0, rows, chunk):
        at = slice(start, start + chunk)
        pre_act = dot(norm_ref[at, :], up_ref[...], NT)
        act_grad = dot(cot_ref[at, :], down_ref[...], NT)
        activation, slope = gelu_parts(pre_act)
        activation = activation.astype(BF16)
        pre_grad = (act_grad * slope).astype(BF16)
        act_ref[at, :] = activation
        pre_ref[at, :] = pre_grad
        mlp_ref[at, :] += dot(activation, down_ref[...], NN)
        back_ref[at, :] += dot(pre_grad, up_ref[...], NN)
    grad_ref[0] = dot(pre_ref[...], norm_ref[...], TN).astype(BF16)
    grad_ref[1] = dot(act_ref[...], cot_ref[...], TN).astype(BF16)


def feed_forward(norm, cot, up, down):
    rows, width = norm.shape
    hidden = up.shape[0]
    part = 512 if hidden % 512 == 0 else hidden
    whole = pl.BlockSpec((rows, width), lambda i: (0, 0))
    block = pl.BlockSpec((part, width), lambda i: (i, 0))
    return pl.pallas_call(
        feed_forward_kernel,
        grid=(hidden // part,),
        in_specs=[whole, whole, block, block],
        out_specs=[whole, whole, pl.BlockSpec((2, part, width), lambda i: (0, i, 0))],
        out_shape=[
            jax.ShapeDtypeStruct((rows, width), F32),
            jax.ShapeDtypeStruct((rows, width), F32),
            jax.ShapeDtypeStruct((2, hidden, width), BF16),
        ],
        scratch_shapes=[pltpu.VMEM((rows, part), BF16), pltpu.VMEM((rows, part), BF16)],
        compiler_params=pltpu.CompilerParams(vmem_limit_bytes=56 << 20),
        cost_estimate=pl.CostEstimate(
            flops=12 * rows * width * hidden,
            bytes_accessed=8 * hidden * width + 12 * rows * width,
            transcendentals=2 * rows * hidden,
        ),
        name="feed_forward",
    )(norm, cot, up, down)


def add(*terms):
    return functools.reduce(jnp.add, [item.astype(F32) for item in terms]).astype(BF16)


def after(values, *earlier):
    return lax.optimization_barrier((values,) + earlier)[0]


def swap(values, axis):
    name, size, mask = {"core": ("dp", 4, 1), "y": ("dp", 4, 2), "x": ("mp", 8, 1)}[axis]
    return lax.ppermute(values, name, [(i, i ^ mask) for i in range(size)])


def send_z(parts):
    return [
        lax.ppermute(part, "mp", [(i, i ^ (2 * (offset + 1))) for i in range(8)])
        for offset, part in enumerate(parts)
    ]


def order(at, mine, other):
    return jnp.where(at == 0, jnp.stack([mine, other]), jnp.stack([other, mine]))


def pair(mine, other):
    return jnp.stack([mine, other])


def gather_z(piece, received):
    count, width = piece.shape[1:]
    along_z = jnp.stack([piece] + received)
    return along_z[:, 0].reshape(4 * count, width), along_z[:, 1].reshape(4 * count, width)


def gather_first(one, two):
    return swap(one, "x"), swap(two, "y")


def gather_second(chunks, received, stack):
    one = jnp.concatenate([chunks[0], received[0]], axis=0)
    two = stack(chunks[1], received[1])
    return (one, two), (swap(one, "y"), swap(two, "x"))


def gather_last(chunks, received, stack):
    return stack(chunks[0], received[0]), jnp.concatenate([chunks[1], received[1]], axis=1)


def reduce_first(mine, received, split):
    keep, send = split(mine[0]), split(received[0])
    half = mine[1].shape[1] // 2
    one = add(keep[0], send[0])
    two = add(mine[1][:, :half], received[1][:, :half])
    return (one, two), (add(keep[1], send[1]), add(mine[1][:, half:], received[1][:, half:]))


def reduce_second(mine, received, split):
    half = mine[0].shape[0] // 2
    keep, send = split(mine[1]), split(received[1])
    one = add(mine[0][:half], received[0][:half])
    two = add(keep[0], send[0])
    return (one, two), (add(mine[0][half:], received[0][half:]), add(keep[1], send[1]))


def reduce_z(mine, received):
    count = mine[0].shape[0] // 4
    parts = [
        jnp.stack([add(a[i * count : (i + 1) * count], b[i * count : (i + 1) * count]) for a, b in zip(mine, received)])
        for i in range(4)
    ]
    return parts[0], parts[1:]


def reduce_last(piece, at_y, at_core):
    pieces = order(at_y, piece, swap(piece, "y"))
    return order(at_core, pieces, swap(pieces, "core"))


def norm_back(values, gain, bias, grad):
    return jax.vjp(layer_norm, values, gain, bias)[1](grad)


def on_cube(
    inputs,
    segments,
    ln1_gain,
    ln1_bias,
    w_query,
    w_key,
    w_value,
    w_output,
    ln2_gain,
    ln2_bias,
    w_up,
    w_down,
    cotangent,
):
    rows, width = inputs.shape
    local = w_query.shape[1]
    at_dp, at_mp = lax.axis_index("dp"), lax.axis_index("mp")
    at_y, at_core = at_dp // 2, at_dp % 2
    order_y = functools.partial(order, at_y)

    def halve_y(values):
        return tuple(
            lax.dynamic_index_in_dim(values, at, 0, keepdims=False) for at in (at_y, 1 - at_y)
        )

    def halve_pair(values):
        return values[0], values[1]

    attn_local = jnp.stack([w_query.T, w_key.T, w_value.T, w_output])
    attn_pieces = attn_local.reshape(2, 2, 2, HEAD_DIM, width).transpose(0, 2, 1, 3, 4)
    attn_piece = lax.dynamic_index_in_dim(
        attn_pieces.reshape(4, 2, HEAD_DIM, width), at_dp, 0, keepdims=False
    )
    mlp_pieces = jnp.stack([w_up.T, w_down]).reshape(2, 4, -1, width)
    mlp_piece = lax.dynamic_index_in_dim(mlp_pieces, at_dp, 1, keepdims=False)

    attn_z = send_z([attn_piece] * 3)
    attn_chunks = gather_z(attn_piece, attn_z)
    attn_got = gather_first(*attn_chunks)
    mlp_piece = after(mlp_piece, *attn_z)
    mlp_z = send_z([mlp_piece] * 3)
    attn_chunks, attn_got = gather_second(attn_chunks, attn_got, order_y)
    mlp_chunks = after(gather_z(mlp_piece, mlp_z), *attn_got)
    mlp_first = gather_first(*mlp_chunks)
    weights = gather_last(attn_chunks, attn_got, order_y)
    attn_weights = [weights, tuple(swap(item, "core") for item in weights)]

    segs = lax.dynamic_index_in_dim(segments, at_mp, 0, keepdims=False)
    first, kind = windows(segs)
    resid_in = inputs.astype(F32)
    norm_one = layer_norm(resid_in, ln1_gain, ln1_bias).astype(BF16)
    residual = resid_in
    saved = []
    for (query_value_w, key_out_w), earlier in zip(attn_weights, (mlp_z, mlp_first)):
        count = query_value_w.shape[1]
        query_value = dot(query_value_w.reshape(2 * count, width), norm_one, NT).astype(BF16)
        keys = after(dot(key_out_w[0], norm_one, NT).astype(BF16), *earlier)
        attended, lse = attend_forward(query_value.reshape(2, count, rows), keys, segs, first, kind)
        residual = residual + dot(attended, key_out_w[1], TN)
        saved.append((query_value.reshape(2, count, rows), keys, attended, lse))
    norm_two = layer_norm(residual, ln2_gain, ln2_bias).astype(BF16)

    mlp_first = after(mlp_first, saved[0][2])
    mlp_chunks, mlp_got = gather_second(mlp_chunks, mlp_first, pair)
    mlp_got = after(mlp_got, saved[1][2])
    mine = [item.reshape(-1, width) for item in gather_last(mlp_chunks, mlp_got, pair)]
    other = [swap(item, "core") for item in mine]
    mlp_one, back_one, mlp_mine = feed_forward(norm_two, cotangent, *mine)
    mlp_two, back_two, mlp_other = feed_forward(after(norm_two, mlp_mine), cotangent, *other)
    output = (residual + mlp_one + mlp_two).astype(BF16)
    mlp_mine = mlp_mine.reshape(2, 2, -1, width)
    mlp_got = swap(mlp_other.reshape(2, 2, -1, width), "core")

    resid_part, gain_two_grad, bias_two_grad = norm_back(
        residual, ln2_gain, ln2_bias, back_one + back_two
    )
    res_grad = cotangent.astype(F32) + resid_part
    branch_grad = res_grad.astype(BF16)

    norm_one_grad = 0.0
    attn_grads = []
    for g in (1, 0):
        query_value_w, key_out_w = attn_weights[g]
        query_value, keys, attended, lse = saved[g]
        count = query_value_w.shape[1]
        out_grad = dot(attended, branch_grad, NN).astype(BF16)
        att_grad = dot(key_out_w[1], branch_grad, NT).astype(BF16)
        if g == 1:
            att_grad = after(att_grad, mlp_got)
            mlp_mine, sends = reduce_first(mlp_mine, mlp_got, halve_pair)
            mlp_got = swap(sends[0], "y"), swap(sends[1], "x")
        else:
            att_grad = after(att_grad, *mlp_got)
            mlp_mine, sends = reduce_second(mlp_mine, mlp_got, halve_pair)
            mlp_got = swap(sends[0], "x"), swap(sends[1], "y")
        query_value_grad, key_grad = attend_backward(
            query_value, keys, attended, att_grad, lse, segs, first, kind
        )
        query_value_grad = query_value_grad.reshape(2 * count, rows)
        if g == 0:
            query_value_grad, key_grad = after((query_value_grad, key_grad), *mlp_got)
        grads = (
            dot(query_value_grad, norm_one, NN).astype(BF16).reshape(2, count, width),
            jnp.stack([dot(key_grad, norm_one, NN).astype(BF16), out_grad]),
        )
        if g == 1:
            attn_got = [swap(item, "core") for item in grads]
        attn_grads.append((query_value_grad, key_grad))
    attn_mine, attn_sends = reduce_first(grads, attn_got, halve_y)
    attn_got = swap(attn_sends[0], "y"), swap(attn_sends[1], "x")
    mlp_mine, mlp_sends = reduce_z(mlp_mine, mlp_got)
    mlp_got = send_z(mlp_sends)

    for g, (query_value_grad, key_grad) in zip((1, 0), attn_grads):
        query_value_w, key_out_w = attn_weights[g]
        if g == 0:
            query_value_grad, key_grad = after(
                (query_value_grad, key_grad), *attn_sends, *mlp_sends
            )
        norm_one_grad = (
            norm_one_grad
            + dot(query_value_grad, query_value_w.reshape(-1, width), TN)
            + dot(key_grad, key_out_w[0], TN)
        )
    input_part, gain_one_grad, bias_one_grad = norm_back(resid_in, ln1_gain, ln1_bias, norm_one_grad)
    in_grad = (res_grad + input_part).astype(BF16)
    norm_parts = jnp.stack([gain_one_grad, bias_one_grad, gain_two_grad, bias_two_grad])
    norm_sums = lax.dynamic_slice_in_dim(
        jnp.sum(lax.all_gather(norm_parts, ("dp", "mp"), axis=0, tiled=False), axis=0),
        at_mp * (width // 8),
        width // 8,
        1,
    )

    attn_got = after(attn_got, norm_parts)
    attn_mine, sends = reduce_second(attn_mine, attn_got, halve_y)
    attn_got = swap(sends[0], "x"), swap(sends[1], "y")
    mlp_sum = reduce_last(add(mlp_mine, *mlp_got), at_y, at_core)
    attn_mine, sends = reduce_z(attn_mine, attn_got)
    attn_got = send_z(sends)
    attn_sum = reduce_last(add(attn_mine, *attn_got), at_y, at_core)
    attn_sum = attn_sum.transpose(1, 2, 0, 3, 4).reshape(4, local, width).astype(F32)
    up_sum, down_sum = mlp_sum.transpose(2, 1, 0, 3, 4).reshape(2, -1, width).astype(F32)
    return (
        output,
        in_grad,
        norm_sums[0],
        norm_sums[1],
        attn_sum[0].T,
        attn_sum[1].T,
        attn_sum[2].T,
        attn_sum[3],
        norm_sums[2],
        norm_sums[3],
        up_sum.T,
        down_sum,
    )


def on_any(
    mp_size,
    inputs,
    segments,
    ln1_gain,
    ln1_bias,
    w_query,
    w_key,
    w_value,
    w_output,
    ln2_gain,
    ln2_bias,
    w_up,
    w_down,
    cotangent,
):
    rows, width = inputs.shape
    seq_length = segments.shape[1]
    shared_by = seq_length // rows
    at_mp = lax.axis_index("mp")
    groups = [[start + i for i in range(shared_by)] for start in range(0, mp_size, shared_by)]

    def exchange(values, split, join):
        if shared_by == 1:
            return values
        return lax.all_to_all(values, "mp", split, join, axis_index_groups=groups, tiled=True)

    def gather(parts):
        return lax.all_gather(parts, "mp", axis=1, tiled=True)

    def reduce(parts):
        return lax.psum(lax.psum_scatter(parts, "mp", scatter_dimension=1, tiled=True), "dp")

    attn_w = gather(jnp.stack([w_query.T, w_value.T, w_key.T, w_output]))
    up, down = gather(jnp.stack([w_up.T, w_down]))
    project, w_out = attn_w[:3].reshape(3 * width, width), attn_w[3]

    segs = lax.dynamic_index_in_dim(segments, at_mp // shared_by, 0, keepdims=False)
    first, kind = windows(segs)
    resid_in = inputs.astype(F32)
    norm_one = layer_norm(resid_in, ln1_gain, ln1_bias).astype(BF16)
    projected = dot(project, norm_one, NT).astype(BF16).reshape(3, width, rows)
    projected = exchange(projected, 1, 2)
    query_value, keys = projected[:2], projected[2]
    heads_out, lse = attend_forward(query_value, keys, segs, first, kind)
    attended = exchange(heads_out, 1, 0)
    residual = resid_in + dot(attended, w_out, TN)
    norm_two = layer_norm(residual, ln2_gain, ln2_bias).astype(BF16)
    mlp_branch, norm_two_grad, mlp_grads = feed_forward(norm_two, cotangent, up, down)
    output = (residual + mlp_branch).astype(BF16)
    up_sum, down_sum = reduce(mlp_grads).astype(F32)

    resid_part, gain_two_grad, bias_two_grad = norm_back(residual, ln2_gain, ln2_bias, norm_two_grad)
    res_grad = cotangent.astype(F32) + resid_part
    branch_grad = res_grad.astype(BF16)
    out_grad = dot(attended, branch_grad, NN).astype(BF16)
    att_grad = exchange(dot(w_out, branch_grad, NT).astype(BF16), 0, 1)
    query_value_grad, key_grad = attend_backward(
        query_value, keys, heads_out, att_grad, lse, segs, first, kind
    )
    proj_grad = exchange(jnp.concatenate([query_value_grad, key_grad[None]]), 2, 1)
    proj_grad = proj_grad.reshape(3 * width, rows)
    project_grad = dot(proj_grad, norm_one, NN).astype(BF16).reshape(3, width, width)
    attn_sum = reduce(jnp.concatenate([project_grad, out_grad[None]])).astype(F32)
    input_part, gain_one_grad, bias_one_grad = norm_back(
        resid_in, ln1_gain, ln1_bias, dot(proj_grad, project, TN)
    )
    in_grad = (res_grad + input_part).astype(BF16)
    norm_parts = jnp.stack([gain_one_grad, bias_one_grad, gain_two_grad, bias_two_grad])
    norm_sums = lax.dynamic_slice_in_dim(
        lax.psum(norm_parts, ("dp", "mp")), at_mp * (width // mp_size), width // mp_size, 1
    )
    return (
        output,
        in_grad,
        norm_sums[0],
        norm_sums[1],
        attn_sum[0].T,
        attn_sum[2].T,
        attn_sum[1].T,
        attn_sum[3],
        norm_sums[2],
        norm_sums[3],
        up_sum.T,
        down_sum,
    )


def shards(dp_size, mp_size, inputs, segments, *rest):
    if dp_size == 4 and mp_size == 8 and inputs.shape[0] == segments.shape[1]:
        return on_cube(inputs, segments, *rest)
    return on_any(mp_size, inputs, segments, *rest)


def solution(mesh):
    return jax.shard_map(
        functools.partial(shards, mesh.shape["dp"], mesh.shape["mp"]),
        mesh=mesh,
        in_specs=(
            P(("dp", "mp"), None),
            P("dp", None),
            P(),
            P(),
            P(None, "mp"),
            P(None, "mp"),
            P(None, "mp"),
            P("mp", None),
            P(),
            P(),
            P(None, "mp"),
            P("mp", None),
            P(("dp", "mp"), None),
        ),
        out_specs=(
            P(("dp", "mp"), None),
            P(("dp", "mp"), None),
            P("mp"),
            P("mp"),
            P(None, "mp"),
            P(None, "mp"),
            P(None, "mp"),
            P("mp", None),
            P("mp"),
            P("mp"),
            P(None, "mp"),
            P("mp", None),
        ),
        check_vma=False,
    )
```

```python
import functools
import math

import jax
import jax.numpy as jnp
from jax import lax
from jax.experimental import pallas as pl
from jax.experimental.pallas import tpu as pltpu
from jax.sharding import PartitionSpec as P

HEAD_DIM = 48
PAIR = 2 * HEAD_DIM
IMAGES = 4
TILE = 128
norm_eps = 1e-06
negative_fill = -1e30
SCALE = HEAD_DIM ** (-0.5)
SCALE_LOG2 = SCALE * math.log2(math.e)
BF16 = jnp.bfloat16
F32 = jnp.float32


def layer_norm(values, gain, bias):
    center = jnp.mean(values, axis=-1, keepdims=True)
    shifted = values - center
    spread = jnp.mean(shifted * shifted, axis=-1, keepdims=True)
    return shifted * lax.rsqrt(spread + norm_eps) * gain + bias


def dot(left, right, dims):
    return lax.dot_general(left, right, (dims, ((), ())), preferred_element_type=F32)


NN = ((1,), (0,))
NT = ((1,), (1,))
TN = ((0,), (0,))


def window_kinds(tiles):
    return tuple(n for n in (2, 3, 4, 5, 6) if n < tiles) + (tiles,)


def image_rows(segs, length):
    row = lax.broadcasted_iota(jnp.int32, (TILE - PAIR, length), 0)
    here = row == segs
    one_hot = jnp.where(here, 1.0, 0.0).astype(BF16)
    fill = jnp.where(jnp.logical_or(here, row >= IMAGES), 0.0, negative_fill).astype(BF16)
    return one_hot, fill


def side_by_side(pair, extra):
    blank = jnp.zeros((HEAD_DIM, TILE), BF16)
    left = jnp.concatenate([pair[:HEAD_DIM], blank, extra], axis=0)
    right = jnp.concatenate([blank, pair[HEAD_DIM:], extra], axis=0)
    return jnp.concatenate([left, right], axis=1)


def attend_forward_kernel(
    first_ref, kind_ref, segs_ref, qv_ref, k_ref, out_ref, lse_ref, hot_ref, keys_ref, vals_ref
):
    q_ref, v_ref = qv_ref.at[0], qv_ref.at[1]
    length = q_ref.shape[1]
    pairs = q_ref.shape[0] // PAIR
    one_hot, fill = image_rows(segs_ref[...], length)
    hot_ref[...] = one_hot
    for j in range(pairs):
        rows = slice(PAIR * j, PAIR * (j + 1))
        keys_ref[j] = jnp.concatenate([k_ref[rows, :], fill], axis=0).T
        vals_ref[j] = jnp.concatenate([v_ref[rows, :], jnp.ones((16, length), BF16)], axis=0)

    def block(b, carry):
        at = pl.ds(pl.multiple_of(b * TILE, TILE), TILE)
        first = pl.multiple_of(first_ref[b] * TILE, TILE)

        def variant(tiles):
            span = pl.ds(first, tiles * TILE)
            scores = [
                dot(
                    keys_ref[j, span, :],
                    side_by_side(q_ref[PAIR * j : PAIR * (j + 1), at], hot_ref[:, at]),
                    NN,
                )
                for j in range(pairs)
            ]
            for j in range(pairs):
                top = PAIR * j
                most = jnp.max(scores[j], axis=0, keepdims=True)
                expo = jnp.exp2((scores[j] - most) * SCALE_LOG2).astype(BF16)
                mixed = dot(vals_ref[j, :, span], expo, NN)
                total = mixed[PAIR : PAIR + 1, :]
                inverse = 1.0 / total
                out_ref[top : top + HEAD_DIM, at] = (
                    mixed[:HEAD_DIM, :TILE] * inverse[:, :TILE]
                ).astype(BF16)
                out_ref[top + HEAD_DIM : top + PAIR, at] = (
                    mixed[HEAD_DIM:PAIR, TILE:] * inverse[:, TILE:]
                ).astype(BF16)
                lse_ref[j, pl.ds(b, 1), :] = most * SCALE_LOG2 + jnp.log2(total)

        for tiles in window_kinds(length // TILE):
            pl.when(kind_ref[b] == tiles)(functools.partial(variant, tiles))
        return carry

    lax.fori_loop(0, length // TILE, block, 0)


def attend_backward_kernel(
    first_ref,
    kind_ref,
    segs_ref,
    qv_ref,
    k_ref,
    att_ref,
    grad_ref,
    lse_ref,
    dqv_ref,
    dk_ref,
    hot_ref,
    keys_ref,
    vals_ref,
    queries_ref,
    grads_ref,
    key_sum_ref,
    val_sum_ref,
):
    q_ref, v_ref = qv_ref.at[0], qv_ref.at[1]
    dq_ref, dv_ref = dqv_ref.at[0], dqv_ref.at[1]
    length = q_ref.shape[1]
    pairs = q_ref.shape[0] // PAIR
    one_hot, fill = image_rows(segs_ref[...], length)
    hot_ref[...] = one_hot
    pad = jnp.zeros((TILE - PAIR, length), BF16)
    for j in range(pairs):
        rows = slice(PAIR * j, PAIR * (j + 1))
        keys_ref[j] = jnp.concatenate([k_ref[rows, :], fill], axis=0).T
        vals_ref[j] = jnp.concatenate([v_ref[rows, :], pad], axis=0).T
        queries_ref[j] = jnp.concatenate([q_ref[rows, :], pad], axis=0).T
        grads_ref[j] = jnp.concatenate([grad_ref[rows, :], pad], axis=0).T
    key_sum_ref[...] = jnp.zeros(key_sum_ref.shape, F32)
    val_sum_ref[...] = jnp.zeros(val_sum_ref.shape, F32)
    no_rows = jnp.zeros((TILE - PAIR, TILE), BF16)
    lane = lax.broadcasted_iota(jnp.int32, (TILE, TILE), 1)
    in_first = lane < HEAD_DIM

    def stacked(both):
        blank = jnp.zeros_like(both)
        return jnp.concatenate(
            [jnp.where(in_first, both, blank), jnp.where(in_first, blank, both)], axis=0
        )

    def block(b, carry):
        at = pl.ds(pl.multiple_of(b * TILE, TILE), TILE)
        first = pl.multiple_of(first_ref[b] * TILE, TILE)

        def variant(tiles):
            span = pl.ds(first, tiles * TILE)
            scores = [
                dot(
                    keys_ref[j, span, :],
                    side_by_side(q_ref[PAIR * j : PAIR * (j + 1), at], hot_ref[:, at]),
                    NN,
                )
                for j in range(pairs)
            ]
            prob_grads = [
                dot(
                    vals_ref[j, span, :],
                    side_by_side(grad_ref[PAIR * j : PAIR * (j + 1), at], no_rows),
                    NN,
                )
                for j in range(pairs)
            ]
            for j in range(pairs):
                top = PAIR * j
                grad = grad_ref[top : top + PAIR, at]
                agree = grad.astype(F32) * att_ref[top : top + PAIR, at].astype(F32)
                delta = jnp.concatenate(
                    [
                        jnp.sum(agree[:HEAD_DIM], axis=0, keepdims=True),
                        jnp.sum(agree[HEAD_DIM:], axis=0, keepdims=True),
                    ],
                    axis=1,
                )
                probs = jnp.exp2(scores[j] * SCALE_LOG2 - lse_ref[j, pl.ds(b, 1), :])
                score_grad = (probs * (prob_grads[j] - delta)).astype(BF16)
                val_sum_ref[j, span, :] += dot(
                    probs.astype(BF16), stacked(grads_ref[j, at, :]), NN
                )
                key_sum_ref[j, span, :] += dot(score_grad, stacked(queries_ref[j, at, :]), NN)
                query_grad = dot(k_ref[top : top + PAIR, span], score_grad, NN) * SCALE
                dq_ref[top : top + HEAD_DIM, at] = query_grad[:HEAD_DIM, :TILE].astype(BF16)
                dq_ref[top + HEAD_DIM : top + PAIR, at] = query_grad[HEAD_DIM:, TILE:].astype(BF16)

        for tiles in window_kinds(length // TILE):
            pl.when(kind_ref[b] == tiles)(functools.partial(variant, tiles))
        return carry

    lax.fori_loop(0, length // TILE, block, 0)
    for j in range(pairs):
        rows = slice(PAIR * j, PAIR * (j + 1))
        dk_ref[rows, :] = (key_sum_ref[j] * SCALE).T[:PAIR].astype(BF16)
        dv_ref[rows, :] = val_sum_ref[j].T[:PAIR].astype(BF16)


def windows(segs):
    length = segs.shape[0]
    tiles = length // TILE
    by_tile = segs.reshape(tiles, TILE)
    begin = jnp.sum(segs[None, :] < by_tile[:, :1], axis=1)
    end = jnp.sum(segs[None, :] <= by_tile[:, -1:], axis=1)
    first = begin // TILE
    need = (end + TILE - 1) // TILE - first
    kinds = jnp.asarray(window_kinds(tiles), jnp.int32)
    kind = jnp.min(jnp.where(kinds[None, :] >= need[:, None], kinds[None, :], tiles), axis=1)
    return jnp.minimum(first, tiles - kind).astype(jnp.int32), kind.astype(jnp.int32)


def attention_specs(heads, length):
    pairs = heads // 2
    step = 4 if pairs % 4 == 0 else pairs if pairs < 4 else 1
    rows = pl.BlockSpec((step * PAIR, length), lambda i, *_: (i, 0))
    two = pl.BlockSpec((2, step * PAIR, length), lambda i, *_: (0, i, 0))
    segs = pl.BlockSpec((1, length), lambda i, *_: (0, 0))
    lse = pl.BlockSpec((step, length // TILE, 2 * TILE), lambda i, *_: (i, 0, 0))
    return pairs, step, rows, two, segs, lse


def attend_forward(query_value, keys, segs, first, kind):
    length = segs.shape[0]
    heads = keys.shape[0] // HEAD_DIM
    pairs, step, rows, two, segs_spec, lse = attention_specs(heads, length)
    work = heads * length * length * HEAD_DIM
    return pl.pallas_call(
        attend_forward_kernel,
        grid_spec=pltpu.PrefetchScalarGridSpec(
            num_scalar_prefetch=2,
            grid=(pairs // step,),
            in_specs=[segs_spec, two, rows],
            out_specs=[rows, lse],
            scratch_shapes=[
                pltpu.VMEM((TILE - PAIR, length), BF16),
                pltpu.VMEM((step, length, TILE), BF16),
                pltpu.VMEM((step, PAIR + 16, length), BF16),
            ],
        ),
        out_shape=[
            jax.ShapeDtypeStruct(keys.shape, BF16),
            jax.ShapeDtypeStruct((pairs, length // TILE, 2 * TILE), F32),
        ],
        compiler_params=pltpu.CompilerParams(vmem_limit_bytes=40 << 20),
        cost_estimate=pl.CostEstimate(
            flops=20 * work, bytes_accessed=8 * keys.size, transcendentals=heads * length * length // 2
        ),
        name="attend_forward",
    )(first, kind, segs[None, :], query_value, keys)


def attend_backward(query_value, keys, attended, grad, lse, segs, first, kind):
    length = segs.shape[0]
    heads = keys.shape[0] // HEAD_DIM
    pairs, step, rows, two, segs_spec, lse_spec = attention_specs(heads, length)
    work = heads * length * length * HEAD_DIM
    wide = pltpu.VMEM((step, length, TILE), BF16)
    total = pltpu.VMEM((step, length, TILE), F32)
    return pl.pallas_call(
        attend_backward_kernel,
        grid_spec=pltpu.PrefetchScalarGridSpec(
            num_scalar_prefetch=2,
            grid=(pairs // step,),
            in_specs=[segs_spec, two, rows, rows, rows, lse_spec],
            out_specs=[two, rows],
            scratch_shapes=[
                pltpu.VMEM((TILE - PAIR, length), BF16),
                wide,
                wide,
                wide,
                wide,
                total,
                total,
            ],
        ),
        out_shape=[
            jax.ShapeDtypeStruct(query_value.shape, BF16),
            jax.ShapeDtypeStruct(keys.shape, BF16),
        ],
        compiler_params=pltpu.CompilerParams(vmem_limit_bytes=40 << 20),
        cost_estimate=pl.CostEstimate(
            flops=20 * work, bytes_accessed=16 * keys.size, transcendentals=heads * length * length // 2
        ),
        name="attend_backward",
    )(first, kind, segs[None, :], query_value, keys, attended, grad, lse)


def gelu_parts(values):
    below = 0.5 * (1.0 + lax.erf(values * (0.5 ** 0.5)))
    density = jnp.exp(values * values * -0.5) * ((2.0 * math.pi) ** -0.5)
    return values * below, below + values * density


def feed_forward_kernel(norm_ref, cot_ref, up_ref, down_ref, mlp_ref, back_ref, grad_ref, act_ref, pre_ref):
    rows = norm_ref.shape[0]
    chunk = min(rows, 256)

    @pl.when(pl.program_id(0) == 0)
    def _():
        mlp_ref[...] = jnp.zeros(mlp_ref.shape, F32)
        back_ref[...] = jnp.zeros(back_ref.shape, F32)

    for start in range(0, rows, chunk):
        at = slice(start, start + chunk)
        pre_act = dot(norm_ref[at, :], up_ref[...], NT)
        act_grad = dot(cot_ref[at, :], down_ref[...], NT)
        activation, slope = gelu_parts(pre_act)
        activation = activation.astype(BF16)
        pre_grad = (act_grad * slope).astype(BF16)
        act_ref[at, :] = activation
        pre_ref[at, :] = pre_grad
        mlp_ref[at, :] += dot(activation, down_ref[...], NN)
        back_ref[at, :] += dot(pre_grad, up_ref[...], NN)
    grad_ref[0] = dot(pre_ref[...], norm_ref[...], TN).astype(BF16)
    grad_ref[1] = dot(act_ref[...], cot_ref[...], TN).astype(BF16)


def feed_forward(norm, cot, up, down):
    rows, width = norm.shape
    hidden = up.shape[0]
    part = 512 if hidden % 512 == 0 else hidden
    whole = pl.BlockSpec((rows, width), lambda i: (0, 0))
    block = pl.BlockSpec((part, width), lambda i: (i, 0))
    return pl.pallas_call(
        feed_forward_kernel,
        grid=(hidden // part,),
        in_specs=[whole, whole, block, block],
        out_specs=[whole, whole, pl.BlockSpec((2, part, width), lambda i: (0, i, 0))],
        out_shape=[
            jax.ShapeDtypeStruct((rows, width), F32),
            jax.ShapeDtypeStruct((rows, width), F32),
            jax.ShapeDtypeStruct((2, hidden, width), BF16),
        ],
        scratch_shapes=[pltpu.VMEM((rows, part), BF16), pltpu.VMEM((rows, part), BF16)],
        compiler_params=pltpu.CompilerParams(vmem_limit_bytes=56 << 20),
        cost_estimate=pl.CostEstimate(
            flops=12 * rows * width * hidden,
            bytes_accessed=8 * hidden * width + 12 * rows * width,
            transcendentals=2 * rows * hidden,
        ),
        name="feed_forward",
    )(norm, cot, up, down)


def add(*terms):
    return functools.reduce(jnp.add, [item.astype(F32) for item in terms]).astype(BF16)


def after(values, *earlier):
    return lax.optimization_barrier((values,) + earlier)[0]


def swap(values, axis):
    name, size, mask = {"core": ("dp", 4, 1), "y": ("dp", 4, 2), "x": ("mp", 8, 1)}[axis]
    return lax.ppermute(values, name, [(i, i ^ mask) for i in range(size)])


def send_z(parts):
    return [
        lax.ppermute(part, "mp", [(i, i ^ (2 * (offset + 1))) for i in range(8)])
        for offset, part in enumerate(parts)
    ]


def order(at, mine, other):
    return jnp.where(at == 0, jnp.stack([mine, other]), jnp.stack([other, mine]))


def pair(mine, other):
    return jnp.stack([mine, other])


def gather_z(piece, received):
    count, width = piece.shape[1:]
    along_z = jnp.stack([piece] + received)
    return along_z[:, 0].reshape(4 * count, width), along_z[:, 1].reshape(4 * count, width)


def gather_first(one, two):
    return swap(one, "x"), swap(two, "y")


def gather_second(chunks, received, stack):
    one = jnp.concatenate([chunks[0], received[0]], axis=0)
    two = stack(chunks[1], received[1])
    return (one, two), (swap(one, "y"), swap(two, "x"))


def gather_last(chunks, received, stack):
    return stack(chunks[0], received[0]), jnp.concatenate([chunks[1], received[1]], axis=1)


def reduce_first(mine, received, split):
    keep, send = split(mine[0]), split(received[0])
    half = mine[1].shape[1] // 2
    one = add(keep[0], send[0])
    two = add(mine[1][:, :half], received[1][:, :half])
    return (one, two), (add(keep[1], send[1]), add(mine[1][:, half:], received[1][:, half:]))


def reduce_second(mine, received, split):
    half = mine[0].shape[0] // 2
    keep, send = split(mine[1]), split(received[1])
    one = add(mine[0][:half], received[0][:half])
    two = add(keep[0], send[0])
    return (one, two), (add(mine[0][half:], received[0][half:]), add(keep[1], send[1]))


def reduce_z(mine, received):
    count = mine[0].shape[0] // 4
    parts = [
        jnp.stack([add(a[i * count : (i + 1) * count], b[i * count : (i + 1) * count]) for a, b in zip(mine, received)])
        for i in range(4)
    ]
    return parts[0], parts[1:]


def reduce_last(piece, at_y, at_core):
    pieces = order(at_y, piece, swap(piece, "y"))
    return order(at_core, pieces, swap(pieces, "core"))


def total(values):
    for axis in ("core", "y", "x"):
        values = values + swap(values, axis)
    return functools.reduce(jnp.add, send_z([values] * 3), values)


def norm_back(values, gain, bias, grad):
    return jax.vjp(layer_norm, values, gain, bias)[1](grad)


def on_cube(
    inputs,
    segments,
    ln1_gain,
    ln1_bias,
    w_query,
    w_key,
    w_value,
    w_output,
    ln2_gain,
    ln2_bias,
    w_up,
    w_down,
    cotangent,
):
    rows, width = inputs.shape
    local = w_query.shape[1]
    at_dp, at_mp = lax.axis_index("dp"), lax.axis_index("mp")
    at_y, at_core = at_dp // 2, at_dp % 2
    order_y = functools.partial(order, at_y)

    def halve_y(values):
        return tuple(
            lax.dynamic_index_in_dim(values, at, 0, keepdims=False) for at in (at_y, 1 - at_y)
        )

    def halve_pair(values):
        return values[0], values[1]

    attn_local = jnp.stack([w_query.T, w_key.T, w_value.T, w_output])
    attn_pieces = attn_local.reshape(2, 2, 2, HEAD_DIM, width).transpose(0, 2, 1, 3, 4)
    attn_piece = lax.dynamic_index_in_dim(
        attn_pieces.reshape(4, 2, HEAD_DIM, width), at_dp, 0, keepdims=False
    )
    mlp_pieces = jnp.stack([w_up.T, w_down]).reshape(2, 4, -1, width)
    mlp_piece = lax.dynamic_index_in_dim(mlp_pieces, at_dp, 1, keepdims=False)

    attn_z = send_z([attn_piece] * 3)
    attn_chunks = gather_z(attn_piece, attn_z)
    attn_got = gather_first(*attn_chunks)
    mlp_piece = after(mlp_piece, *attn_z)
    mlp_z = send_z([mlp_piece] * 3)
    attn_chunks, attn_got = gather_second(attn_chunks, attn_got, order_y)
    weights = gather_last(attn_chunks, attn_got, order_y)
    attn_weights = [weights, tuple(swap(item, "core") for item in weights)]

    segs = lax.dynamic_index_in_dim(segments, at_mp, 0, keepdims=False)
    first, kind = windows(segs)
    resid_in = inputs.astype(F32)
    norm_one = layer_norm(resid_in, ln1_gain, ln1_bias).astype(BF16)
    residual = resid_in
    saved = []
    for g, (query_value_w, key_out_w) in enumerate(attn_weights):
        count = query_value_w.shape[1]
        query_value = dot(query_value_w.reshape(2 * count, width), norm_one, NT).astype(BF16)
        keys = dot(key_out_w[0], norm_one, NT).astype(BF16)
        if g == 0:
            mlp_z = after(mlp_z, query_value, keys)
            mlp_chunks = gather_z(mlp_piece, mlp_z)
            mlp_first = gather_first(*mlp_chunks)
            keys = after(keys, *mlp_z)
        else:
            keys = after(keys, *mlp_first)
        attended, lse = attend_forward(query_value.reshape(2, count, rows), keys, segs, first, kind)
        residual = residual + dot(attended, key_out_w[1], TN)
        saved.append((query_value.reshape(2, count, rows), keys, attended, lse))
    norm_two = layer_norm(residual, ln2_gain, ln2_bias).astype(BF16)

    mlp_first = after(mlp_first, saved[0][2])
    mlp_chunks, mlp_got = gather_second(mlp_chunks, mlp_first, pair)
    mlp_got = after(mlp_got, saved[1][2])
    mine = [item.reshape(-1, width) for item in gather_last(mlp_chunks, mlp_got, pair)]
    other = [swap(item, "core") for item in mine]
    mlp_one, back_one, mlp_mine = feed_forward(norm_two, cotangent, *mine)
    mlp_two, back_two, mlp_other = feed_forward(after(norm_two, mlp_mine), cotangent, *other)
    output = (residual + mlp_one + mlp_two).astype(BF16)
    mlp_mine = mlp_mine.reshape(2, 2, -1, width)
    mlp_got = swap(mlp_other.reshape(2, 2, -1, width), "core")

    resid_part, gain_two_grad, bias_two_grad = norm_back(
        residual, ln2_gain, ln2_bias, back_one + back_two
    )
    res_grad = cotangent.astype(F32) + resid_part
    branch_grad = res_grad.astype(BF16)

    norm_one_grad = 0.0
    attn_grads = []
    for g in (1, 0):
        query_value_w, key_out_w = attn_weights[g]
        query_value, keys, attended, lse = saved[g]
        count = query_value_w.shape[1]
        out_grad = dot(attended, branch_grad, NN).astype(BF16)
        att_grad = dot(key_out_w[1], branch_grad, NT).astype(BF16)
        if g == 1:
            att_grad = after(att_grad, mlp_got)
            mlp_mine, sends = reduce_first(mlp_mine, mlp_got, halve_pair)
            mlp_got = swap(sends[0], "y"), swap(sends[1], "x")
        else:
            att_grad = after(att_grad, *mlp_got)
            mlp_mine, sends = reduce_second(mlp_mine, mlp_got, halve_pair)
            mlp_got = swap(sends[0], "x"), swap(sends[1], "y")
        query_value_grad, key_grad = attend_backward(
            query_value, keys, attended, att_grad, lse, segs, first, kind
        )
        query_value_grad = query_value_grad.reshape(2 * count, rows)
        if g == 0:
            query_value_grad, key_grad = after((query_value_grad, key_grad), *mlp_got)
        grads = (
            dot(query_value_grad, norm_one, NN).astype(BF16).reshape(2, count, width),
            jnp.stack([dot(key_grad, norm_one, NN).astype(BF16), out_grad]),
        )
        if g == 1:
            attn_got = [swap(item, "core") for item in grads]
        attn_grads.append((query_value_grad, key_grad))
    attn_mine, attn_sends = reduce_first(grads, attn_got, halve_y)
    attn_got = swap(attn_sends[0], "y"), swap(attn_sends[1], "x")
    mlp_mine, mlp_sends = reduce_z(mlp_mine, mlp_got)
    mlp_got = send_z(mlp_sends)

    for g, (query_value_grad, key_grad) in zip((1, 0), attn_grads):
        query_value_w, key_out_w = attn_weights[g]
        if g == 0:
            query_value_grad, key_grad = after(
                (query_value_grad, key_grad), *attn_sends, *mlp_sends
            )
        norm_one_grad = (
            norm_one_grad
            + dot(query_value_grad, query_value_w.reshape(-1, width), TN)
            + dot(key_grad, key_out_w[0], TN)
        )
    input_part, gain_one_grad, bias_one_grad = norm_back(resid_in, ln1_gain, ln1_bias, norm_one_grad)
    in_grad = (res_grad + input_part).astype(BF16)
    norm_parts = jnp.stack([gain_one_grad, bias_one_grad, gain_two_grad, bias_two_grad])
    norm_sums = lax.dynamic_slice_in_dim(
        total(after(norm_parts, *attn_got)), at_mp * (width // 8), width // 8, 1
    )

    attn_got = after(attn_got, norm_parts)
    attn_mine, sends = reduce_second(attn_mine, attn_got, halve_y)
    attn_got = swap(sends[0], "x"), swap(sends[1], "y")
    mlp_sum = reduce_last(add(mlp_mine, *mlp_got), at_y, at_core)
    attn_mine, sends = reduce_z(attn_mine, attn_got)
    attn_got = send_z(sends)
    attn_sum = reduce_last(add(attn_mine, *attn_got), at_y, at_core)
    attn_sum = attn_sum.transpose(1, 2, 0, 3, 4).reshape(4, local, width).astype(F32)
    up_sum, down_sum = mlp_sum.transpose(2, 1, 0, 3, 4).reshape(2, -1, width).astype(F32)
    return (
        output,
        in_grad,
        norm_sums[0],
        norm_sums[1],
        attn_sum[0].T,
        attn_sum[1].T,
        attn_sum[2].T,
        attn_sum[3],
        norm_sums[2],
        norm_sums[3],
        up_sum.T,
        down_sum,
    )


def on_any(
    mp_size,
    inputs,
    segments,
    ln1_gain,
    ln1_bias,
    w_query,
    w_key,
    w_value,
    w_output,
    ln2_gain,
    ln2_bias,
    w_up,
    w_down,
    cotangent,
):
    rows, width = inputs.shape
    seq_length = segments.shape[1]
    shared_by = seq_length // rows
    at_mp = lax.axis_index("mp")
    groups = [[start + i for i in range(shared_by)] for start in range(0, mp_size, shared_by)]

    def exchange(values, split, join):
        if shared_by == 1:
            return values
        return lax.all_to_all(values, "mp", split, join, axis_index_groups=groups, tiled=True)

    def gather(parts):
        return lax.all_gather(parts, "mp", axis=1, tiled=True)

    def reduce(parts):
        return lax.psum(lax.psum_scatter(parts, "mp", scatter_dimension=1, tiled=True), "dp")

    attn_w = gather(jnp.stack([w_query.T, w_value.T, w_key.T, w_output]))
    up, down = gather(jnp.stack([w_up.T, w_down]))
    project, w_out = attn_w[:3].reshape(3 * width, width), attn_w[3]

    segs = lax.dynamic_index_in_dim(segments, at_mp // shared_by, 0, keepdims=False)
    first, kind = windows(segs)
    resid_in = inputs.astype(F32)
    norm_one = layer_norm(resid_in, ln1_gain, ln1_bias).astype(BF16)
    projected = dot(project, norm_one, NT).astype(BF16).reshape(3, width, rows)
    projected = exchange(projected, 1, 2)
    query_value, keys = projected[:2], projected[2]
    heads_out, lse = attend_forward(query_value, keys, segs, first, kind)
    attended = exchange(heads_out, 1, 0)
    residual = resid_in + dot(attended, w_out, TN)
    norm_two = layer_norm(residual, ln2_gain, ln2_bias).astype(BF16)
    mlp_branch, norm_two_grad, mlp_grads = feed_forward(norm_two, cotangent, up, down)
    output = (residual + mlp_branch).astype(BF16)
    up_sum, down_sum = reduce(mlp_grads).astype(F32)

    resid_part, gain_two_grad, bias_two_grad = norm_back(residual, ln2_gain, ln2_bias, norm_two_grad)
    res_grad = cotangent.astype(F32) + resid_part
    branch_grad = res_grad.astype(BF16)
    out_grad = dot(attended, branch_grad, NN).astype(BF16)
    att_grad = exchange(dot(w_out, branch_grad, NT).astype(BF16), 0, 1)
    query_value_grad, key_grad = attend_backward(
        query_value, keys, heads_out, att_grad, lse, segs, first, kind
    )
    proj_grad = exchange(jnp.concatenate([query_value_grad, key_grad[None]]), 2, 1)
    proj_grad = proj_grad.reshape(3 * width, rows)
    project_grad = dot(proj_grad, norm_one, NN).astype(BF16).reshape(3, width, width)
    attn_sum = reduce(jnp.concatenate([project_grad, out_grad[None]])).astype(F32)
    input_part, gain_one_grad, bias_one_grad = norm_back(
        resid_in, ln1_gain, ln1_bias, dot(proj_grad, project, TN)
    )
    in_grad = (res_grad + input_part).astype(BF16)
    norm_parts = jnp.stack([gain_one_grad, bias_one_grad, gain_two_grad, bias_two_grad])
    norm_sums = lax.dynamic_slice_in_dim(
        lax.psum(norm_parts, ("dp", "mp")), at_mp * (width // mp_size), width // mp_size, 1
    )
    return (
        output,
        in_grad,
        norm_sums[0],
        norm_sums[1],
        attn_sum[0].T,
        attn_sum[2].T,
        attn_sum[1].T,
        attn_sum[3],
        norm_sums[2],
        norm_sums[3],
        up_sum.T,
        down_sum,
    )


def shards(dp_size, mp_size, inputs, segments, *rest):
    if dp_size == 4 and mp_size == 8 and inputs.shape[0] == segments.shape[1]:
        return on_cube(inputs, segments, *rest)
    return on_any(mp_size, inputs, segments, *rest)


def solution(mesh):
    return jax.shard_map(
        functools.partial(shards, mesh.shape["dp"], mesh.shape["mp"]),
        mesh=mesh,
        in_specs=(
            P(("dp", "mp"), None),
            P("dp", None),
            P(),
            P(),
            P(None, "mp"),
            P(None, "mp"),
            P(None, "mp"),
            P("mp", None),
            P(),
            P(),
            P(None, "mp"),
            P("mp", None),
            P(("dp", "mp"), None),
        ),
        out_specs=(
            P(("dp", "mp"), None),
            P(("dp", "mp"), None),
            P("mp"),
            P("mp"),
            P(None, "mp"),
            P(None, "mp"),
            P(None, "mp"),
            P("mp", None),
            P("mp"),
            P("mp"),
            P(None, "mp"),
            P("mp", None),
        ),
        check_vma=False,
    )
```

```python
import functools
import math

import jax
import jax.numpy as jnp
from jax import lax
from jax.experimental import pallas as pl
from jax.experimental.pallas import tpu as pltpu
from jax.sharding import PartitionSpec as P

HEAD_DIM = 48
PAIR = 2 * HEAD_DIM
IMAGES = 4
TILE = 128
norm_eps = 1e-06
negative_fill = -1e30
SCALE = HEAD_DIM ** (-0.5)
SCALE_LOG2 = SCALE * math.log2(math.e)
BF16 = jnp.bfloat16
F32 = jnp.float32


def layer_norm(values, gain, bias):
    center = jnp.mean(values, axis=-1, keepdims=True)
    shifted = values - center
    spread = jnp.mean(shifted * shifted, axis=-1, keepdims=True)
    return shifted * lax.rsqrt(spread + norm_eps) * gain + bias


def dot(left, right, dims):
    return lax.dot_general(left, right, (dims, ((), ())), preferred_element_type=F32)


NN = ((1,), (0,))
NT = ((1,), (1,))
TN = ((0,), (0,))


def window_kinds(tiles):
    return tuple(n for n in (2, 3, 4, 5, 6) if n < tiles) + (tiles,)


def image_rows(segs, length):
    row = lax.broadcasted_iota(jnp.int32, (TILE - PAIR, length), 0)
    here = row == segs
    one_hot = jnp.where(here, 1.0, 0.0).astype(BF16)
    fill = jnp.where(jnp.logical_or(here, row >= IMAGES), 0.0, negative_fill).astype(BF16)
    return one_hot, fill


def side_by_side(pair, extra):
    blank = jnp.zeros((HEAD_DIM, TILE), BF16)
    left = jnp.concatenate([pair[:HEAD_DIM], blank, extra], axis=0)
    right = jnp.concatenate([blank, pair[HEAD_DIM:], extra], axis=0)
    return jnp.concatenate([left, right], axis=1)


def attend_forward_kernel(
    first_ref, kind_ref, segs_ref, qv_ref, k_ref, out_ref, lse_ref, hot_ref, keys_ref, vals_ref
):
    q_ref, v_ref = qv_ref.at[0], qv_ref.at[1]
    length = q_ref.shape[1]
    pairs = q_ref.shape[0] // PAIR
    one_hot, fill = image_rows(segs_ref[...], length)
    hot_ref[...] = one_hot
    for j in range(pairs):
        rows = slice(PAIR * j, PAIR * (j + 1))
        keys_ref[j] = jnp.concatenate([k_ref[rows, :], fill], axis=0).T
        vals_ref[j] = jnp.concatenate([v_ref[rows, :], jnp.ones((16, length), BF16)], axis=0)

    def block(b, carry):
        at = pl.ds(pl.multiple_of(b * TILE, TILE), TILE)
        first = pl.multiple_of(first_ref[b] * TILE, TILE)

        def variant(tiles):
            span = pl.ds(first, tiles * TILE)
            scores = [
                dot(
                    keys_ref[j, span, :],
                    side_by_side(q_ref[PAIR * j : PAIR * (j + 1), at], hot_ref[:, at]),
                    NN,
                )
                for j in range(pairs)
            ]
            for j in range(pairs):
                top = PAIR * j
                most = jnp.max(scores[j], axis=0, keepdims=True)
                expo = jnp.exp2((scores[j] - most) * SCALE_LOG2).astype(BF16)
                mixed = dot(vals_ref[j, :, span], expo, NN)
                total = mixed[PAIR : PAIR + 1, :]
                inverse = 1.0 / total
                out_ref[top : top + HEAD_DIM, at] = (
                    mixed[:HEAD_DIM, :TILE] * inverse[:, :TILE]
                ).astype(BF16)
                out_ref[top + HEAD_DIM : top + PAIR, at] = (
                    mixed[HEAD_DIM:PAIR, TILE:] * inverse[:, TILE:]
                ).astype(BF16)
                lse_ref[j, pl.ds(b, 1), :] = most * SCALE_LOG2 + jnp.log2(total)

        for tiles in window_kinds(length // TILE):
            pl.when(kind_ref[b] == tiles)(functools.partial(variant, tiles))
        return carry

    lax.fori_loop(0, length // TILE, block, 0)


def attend_backward_kernel(
    first_ref,
    kind_ref,
    segs_ref,
    qv_ref,
    k_ref,
    att_ref,
    grad_ref,
    lse_ref,
    dqv_ref,
    dk_ref,
    hot_ref,
    keys_ref,
    vals_ref,
    queries_ref,
    grads_ref,
    key_sum_ref,
    val_sum_ref,
):
    q_ref, v_ref = qv_ref.at[0], qv_ref.at[1]
    dq_ref, dv_ref = dqv_ref.at[0], dqv_ref.at[1]
    length = q_ref.shape[1]
    pairs = q_ref.shape[0] // PAIR
    one_hot, fill = image_rows(segs_ref[...], length)
    hot_ref[...] = one_hot
    pad = jnp.zeros((TILE - PAIR, length), BF16)
    for j in range(pairs):
        rows = slice(PAIR * j, PAIR * (j + 1))
        keys_ref[j] = jnp.concatenate([k_ref[rows, :], fill], axis=0).T
        vals_ref[j] = jnp.concatenate([v_ref[rows, :], pad], axis=0).T
        queries_ref[j] = jnp.concatenate([q_ref[rows, :], pad], axis=0).T
        grads_ref[j] = jnp.concatenate([grad_ref[rows, :], pad], axis=0).T
    key_sum_ref[...] = jnp.zeros(key_sum_ref.shape, F32)
    val_sum_ref[...] = jnp.zeros(val_sum_ref.shape, F32)
    no_rows = jnp.zeros((TILE - PAIR, TILE), BF16)
    lane = lax.broadcasted_iota(jnp.int32, (TILE, TILE), 1)
    in_first = lane < HEAD_DIM

    def stacked(both):
        blank = jnp.zeros_like(both)
        return jnp.concatenate(
            [jnp.where(in_first, both, blank), jnp.where(in_first, blank, both)], axis=0
        )

    def block(b, carry):
        at = pl.ds(pl.multiple_of(b * TILE, TILE), TILE)
        first = pl.multiple_of(first_ref[b] * TILE, TILE)

        def variant(tiles):
            span = pl.ds(first, tiles * TILE)
            scores = [
                dot(
                    keys_ref[j, span, :],
                    side_by_side(q_ref[PAIR * j : PAIR * (j + 1), at], hot_ref[:, at]),
                    NN,
                )
                for j in range(pairs)
            ]
            prob_grads = [
                dot(
                    vals_ref[j, span, :],
                    side_by_side(grad_ref[PAIR * j : PAIR * (j + 1), at], no_rows),
                    NN,
                )
                for j in range(pairs)
            ]
            for j in range(pairs):
                top = PAIR * j
                grad = grad_ref[top : top + PAIR, at]
                agree = grad.astype(F32) * att_ref[top : top + PAIR, at].astype(F32)
                delta = jnp.concatenate(
                    [
                        jnp.sum(agree[:HEAD_DIM], axis=0, keepdims=True),
                        jnp.sum(agree[HEAD_DIM:], axis=0, keepdims=True),
                    ],
                    axis=1,
                )
                probs = jnp.exp2(scores[j] * SCALE_LOG2 - lse_ref[j, pl.ds(b, 1), :])
                score_grad = (probs * (prob_grads[j] - delta)).astype(BF16)
                val_sum_ref[j, span, :] += dot(
                    probs.astype(BF16), stacked(grads_ref[j, at, :]), NN
                )
                key_sum_ref[j, span, :] += dot(score_grad, stacked(queries_ref[j, at, :]), NN)
                query_grad = dot(k_ref[top : top + PAIR, span], score_grad, NN) * SCALE
                dq_ref[top : top + HEAD_DIM, at] = query_grad[:HEAD_DIM, :TILE].astype(BF16)
                dq_ref[top + HEAD_DIM : top + PAIR, at] = query_grad[HEAD_DIM:, TILE:].astype(BF16)

        for tiles in window_kinds(length // TILE):
            pl.when(kind_ref[b] == tiles)(functools.partial(variant, tiles))
        return carry

    lax.fori_loop(0, length // TILE, block, 0)
    for j in range(pairs):
        rows = slice(PAIR * j, PAIR * (j + 1))
        dk_ref[rows, :] = (key_sum_ref[j] * SCALE).T[:PAIR].astype(BF16)
        dv_ref[rows, :] = val_sum_ref[j].T[:PAIR].astype(BF16)


def windows(segs):
    length = segs.shape[0]
    tiles = length // TILE
    by_tile = segs.reshape(tiles, TILE)
    begin = jnp.sum(segs[None, :] < by_tile[:, :1], axis=1)
    end = jnp.sum(segs[None, :] <= by_tile[:, -1:], axis=1)
    first = begin // TILE
    need = (end + TILE - 1) // TILE - first
    kinds = jnp.asarray(window_kinds(tiles), jnp.int32)
    kind = jnp.min(jnp.where(kinds[None, :] >= need[:, None], kinds[None, :], tiles), axis=1)
    return jnp.minimum(first, tiles - kind).astype(jnp.int32), kind.astype(jnp.int32)


def attention_specs(heads, length):
    pairs = heads // 2
    step = 4 if pairs % 4 == 0 else pairs if pairs < 4 else 1
    rows = pl.BlockSpec((step * PAIR, length), lambda i, *_: (i, 0))
    two = pl.BlockSpec((2, step * PAIR, length), lambda i, *_: (0, i, 0))
    segs = pl.BlockSpec((1, length), lambda i, *_: (0, 0))
    lse = pl.BlockSpec((step, length // TILE, 2 * TILE), lambda i, *_: (i, 0, 0))
    return pairs, step, rows, two, segs, lse


def attend_forward(query_value, keys, segs, first, kind):
    length = segs.shape[0]
    heads = keys.shape[0] // HEAD_DIM
    pairs, step, rows, two, segs_spec, lse = attention_specs(heads, length)
    work = heads * length * length * HEAD_DIM
    return pl.pallas_call(
        attend_forward_kernel,
        grid_spec=pltpu.PrefetchScalarGridSpec(
            num_scalar_prefetch=2,
            grid=(pairs // step,),
            in_specs=[segs_spec, two, rows],
            out_specs=[rows, lse],
            scratch_shapes=[
                pltpu.VMEM((TILE - PAIR, length), BF16),
                pltpu.VMEM((step, length, TILE), BF16),
                pltpu.VMEM((step, PAIR + 16, length), BF16),
            ],
        ),
        out_shape=[
            jax.ShapeDtypeStruct(keys.shape, BF16),
            jax.ShapeDtypeStruct((pairs, length // TILE, 2 * TILE), F32),
        ],
        compiler_params=pltpu.CompilerParams(vmem_limit_bytes=40 << 20),
        cost_estimate=pl.CostEstimate(
            flops=20 * work, bytes_accessed=8 * keys.size, transcendentals=heads * length * length // 2
        ),
        name="attend_forward",
    )(first, kind, segs[None, :], query_value, keys)


def attend_backward(query_value, keys, attended, grad, lse, segs, first, kind):
    length = segs.shape[0]
    heads = keys.shape[0] // HEAD_DIM
    pairs, step, rows, two, segs_spec, lse_spec = attention_specs(heads, length)
    work = heads * length * length * HEAD_DIM
    wide = pltpu.VMEM((step, length, TILE), BF16)
    total = pltpu.VMEM((step, length, TILE), F32)
    return pl.pallas_call(
        attend_backward_kernel,
        grid_spec=pltpu.PrefetchScalarGridSpec(
            num_scalar_prefetch=2,
            grid=(pairs // step,),
            in_specs=[segs_spec, two, rows, rows, rows, lse_spec],
            out_specs=[two, rows],
            scratch_shapes=[
                pltpu.VMEM((TILE - PAIR, length), BF16),
                wide,
                wide,
                wide,
                wide,
                total,
                total,
            ],
        ),
        out_shape=[
            jax.ShapeDtypeStruct(query_value.shape, BF16),
            jax.ShapeDtypeStruct(keys.shape, BF16),
        ],
        compiler_params=pltpu.CompilerParams(vmem_limit_bytes=40 << 20),
        cost_estimate=pl.CostEstimate(
            flops=20 * work, bytes_accessed=16 * keys.size, transcendentals=heads * length * length // 2
        ),
        name="attend_backward",
    )(first, kind, segs[None, :], query_value, keys, attended, grad, lse)


def gelu_parts(values):
    below = 0.5 * (1.0 + lax.erf(values * (0.5 ** 0.5)))
    density = jnp.exp(values * values * -0.5) * ((2.0 * math.pi) ** -0.5)
    return values * below, below + values * density


def feed_forward_kernel(norm_ref, cot_ref, *refs):
    parts = (len(refs) - 2) // 4
    weight_refs, (mlp_ref, back_ref) = refs[:parts], refs[parts : parts + 2]
    grad_refs = refs[parts + 2 : 2 * parts + 2]
    act_refs, pre_refs = refs[2 * parts + 2 : 3 * parts + 2], refs[3 * parts + 2 :]
    rows = norm_ref.shape[0]
    chunk = min(rows, 256)

    @pl.when(pl.program_id(0) == 0)
    def _():
        mlp_ref[...] = jnp.zeros(mlp_ref.shape, F32)
        back_ref[...] = jnp.zeros(back_ref.shape, F32)

    for start in range(0, rows, chunk):
        at = slice(start, start + chunk)
        mlp = back = 0.0
        for weight_ref, act_ref, pre_ref in zip(weight_refs, act_refs, pre_refs):
            pre_act = dot(norm_ref[at, :], weight_ref[0], NT)
            act_grad = dot(cot_ref[at, :], weight_ref[1], NT)
            activation, slope = gelu_parts(pre_act)
            activation = activation.astype(BF16)
            pre_grad = (act_grad * slope).astype(BF16)
            act_ref[at, :] = activation
            pre_ref[at, :] = pre_grad
            mlp = mlp + dot(activation, weight_ref[1], NN)
            back = back + dot(pre_grad, weight_ref[0], NN)
        mlp_ref[at, :] += mlp
        back_ref[at, :] += back
    for grad_ref, act_ref, pre_ref in zip(grad_refs, act_refs, pre_refs):
        grad_ref[0] = dot(pre_ref[...], norm_ref[...], TN).astype(BF16)
        grad_ref[1] = dot(act_ref[...], cot_ref[...], TN).astype(BF16)


def feed_forward(norm, cot, parts):
    rows, width = norm.shape
    hidden = parts[0].shape[1]
    step = 256 if hidden % 256 == 0 else hidden
    count = len(parts)
    whole = pl.BlockSpec((rows, width), lambda i: (0, 0))
    block = pl.BlockSpec((2, step, width), lambda i: (0, i, 0))
    sums = jax.ShapeDtypeStruct((rows, width), F32)
    mlp, back, *grads = pl.pallas_call(
        feed_forward_kernel,
        grid=(hidden // step,),
        in_specs=[whole, whole] + [block] * count,
        out_specs=[whole, whole] + [block] * count,
        out_shape=[sums, sums] + [jax.ShapeDtypeStruct(part.shape, BF16) for part in parts],
        scratch_shapes=[pltpu.VMEM((rows, step), BF16)] * (2 * count),
        compiler_params=pltpu.CompilerParams(vmem_limit_bytes=56 << 20),
        cost_estimate=pl.CostEstimate(
            flops=12 * rows * width * hidden * count,
            bytes_accessed=8 * hidden * width * count + 12 * rows * width,
            transcendentals=2 * rows * hidden * count,
        ),
        name="feed_forward",
    )(norm, cot, *parts)
    return mlp, back, grads


def add(*terms):
    return functools.reduce(jnp.add, [item.astype(F32) for item in terms]).astype(BF16)


def after(values, *earlier):
    return lax.optimization_barrier((values,) + earlier)[0]


def swap(values, axis):
    name, size, mask = {"core": ("dp", 4, 1), "y": ("dp", 4, 2), "x": ("mp", 8, 1)}[axis]
    return lax.ppermute(values, name, [(i, i ^ mask) for i in range(size)])


def send_z(parts):
    return [
        lax.ppermute(part, "mp", [(i, i ^ (2 * (offset + 1))) for i in range(8)])
        for offset, part in enumerate(parts)
    ]


def order(at, mine, other, axis=0):
    return jnp.where(
        at == 0, jnp.stack([mine, other], axis), jnp.stack([other, mine], axis)
    )


def total(values):
    for axis in ("core", "y", "x"):
        values = values + swap(values, axis)
    return functools.reduce(jnp.add, send_z([values] * 3), values)


def norm_back(values, gain, bias, grad):
    return jax.vjp(layer_norm, values, gain, bias)[1](grad)


def on_cube(
    inputs,
    segments,
    ln1_gain,
    ln1_bias,
    w_query,
    w_key,
    w_value,
    w_output,
    ln2_gain,
    ln2_bias,
    w_up,
    w_down,
    cotangent,
):
    rows, width = inputs.shape
    local = w_query.shape[1]
    at_dp, at_mp = lax.axis_index("dp"), lax.axis_index("mp")
    at_y, at_core = at_dp // 2, at_dp % 2

    def pick_y(values, axis, at):
        return lax.dynamic_index_in_dim(values, at, axis, keepdims=False)

    kinds = jnp.stack([jnp.stack([w_query.T, w_value.T]), jnp.stack([w_key.T, w_output])])
    own_w = order(at_core, kinds[:, :, :HEAD_DIM], kinds[:, :, HEAD_DIM:], 2)
    attn_piece = pick_y(own_w[:, :, 0], 1, at_y)
    own_w = own_w.reshape(2, 2, local, width)
    attn_z = send_z([attn_piece] * 3)
    mlp_pieces = jnp.stack([w_up.T, w_down]).reshape(2, 2, 4, -1, width)
    mlp_piece = lax.dynamic_index_in_dim(mlp_pieces, at_dp, 2, keepdims=False)

    segs = lax.dynamic_index_in_dim(segments, at_mp, 0, keepdims=False)
    first, kind = windows(segs)
    resid_in = inputs.astype(F32)
    norm_one = layer_norm(resid_in, ln1_gain, ln1_bias).astype(BF16)

    def project(weights):
        count = weights.shape[2]
        query_value = dot(weights[0].reshape(2 * count, width), norm_one, NT).astype(BF16)
        keys = dot(weights[1, 0], norm_one, NT).astype(BF16)
        return query_value.reshape(2, count, rows), keys

    def attend(projected, weights, earlier=()):
        query_value, keys = projected
        keys = after(keys, *earlier)
        attended, lse = attend_forward(query_value, keys, segs, first, kind)
        return (query_value, keys, attended, lse), dot(attended, weights[1, 1], TN)

    own, own_branch = attend(project(own_w), own_w)

    attn_z = after(attn_z, own[2])
    near = jnp.stack(attn_z, 1)
    far = jnp.concatenate([attn_piece[:, None], near], axis=1)
    near_got, far_got = swap(near, "y"), swap(far, "x")
    mlp_z = [send_z([after(mlp_piece[:, 0], *attn_z)] * 3)]

    near = order(at_y, near, near_got, 1)
    near_got = swap(near, "core")
    far = far_got
    far_got = swap(far, "y")
    near_w = jnp.stack([near, near_got], 2).reshape(2, 2, -1, width)
    near_parts = project(near_w)

    def along_z(half):
        piece = mlp_piece[:, half][:, None]
        return jnp.concatenate([piece] + [item[:, None] for item in mlp_z[half]], 1).reshape(
            2, -1, width
        )

    mlp_got = after(mlp_z[0], *near_parts)
    mlp_z = [mlp_got, send_z([after(mlp_piece[:, 1], *mlp_got)] * 3)]
    mlp_one = along_z(0)
    mlp_one_got = swap(mlp_one, "x")
    near, near_branch = attend(near_parts, near_w, tuple(mlp_got) + (far_got,))

    far = order(at_y, far, far_got, 1)
    far_got = swap(far, "core")
    mlp_one_got = after(mlp_one_got, near[2])
    mlp_one = jnp.concatenate([mlp_one, mlp_one_got], 1)
    mlp_one_got = swap(mlp_one, "y")
    mlp_z[1] = after(mlp_z[1], near[2])
    mlp_two = along_z(1)
    mlp_two_got = swap(mlp_two, "x")
    far_w = jnp.stack([far, far_got], 2).reshape(2, 2, -1, width)
    far_parts = project(far_w)
    far, far_branch = attend(far_parts, far_w, tuple(mlp_z[1]))

    residual = resid_in + own_branch + near_branch + far_branch
    norm_two = layer_norm(residual, ln2_gain, ln2_bias).astype(BF16)

    mlp_one = jnp.concatenate([mlp_one, mlp_one_got], 1)
    mlp_one_other = swap(mlp_one, "core")
    mlp_two = jnp.concatenate([mlp_two, after(mlp_two_got, mlp_one_got)], 1)
    mlp_two_got = swap(mlp_two, "y")
    branch_a, back_a, one_grads = feed_forward(norm_two, cotangent, [mlp_one, mlp_one_other])
    mlp_two_got = after(mlp_two_got, branch_a)
    mlp_two = jnp.concatenate([mlp_two, mlp_two_got], 1)
    mlp_two_other = swap(mlp_two, "core")
    one_got = swap(one_grads[1], "core")
    branch_b, back_b, two_grads = feed_forward(norm_two, cotangent, [mlp_two])
    one_got = after(one_got, branch_b)

    def halve(terms, keep, send):
        return [keep(item) for item in terms], add(*[send(item) for item in terms])

    quarter = 4 * mlp_piece.shape[2]
    one_terms, send = halve(
        [one_grads[0], one_got], lambda v: v[:, : 2 * quarter], lambda v: v[:, 2 * quarter :]
    )
    one_got = swap(send, "y")
    branch_c, back_c, two_other_grads = feed_forward(
        after(norm_two, send), cotangent, [mlp_two_other]
    )
    two_got = swap(two_other_grads[0], "core")
    output = (residual + branch_a + branch_b + branch_c).astype(BF16)

    resid_part, gain_two_grad, bias_two_grad = norm_back(
        residual, ln2_gain, ln2_bias, back_a + back_b + back_c
    )
    res_grad = cotangent.astype(F32) + resid_part
    branch_grad = res_grad.astype(BF16)

    def before_attention(saved, weights):
        out_grad = dot(saved[2], branch_grad, NN).astype(BF16)
        return out_grad, dot(weights[1, 1], branch_grad, NT).astype(BF16)

    def attend_back(saved, out_grad, att_grad, earlier=()):
        query_value, keys, attended, lse = saved
        count = keys.shape[0]
        query_value_grad, key_grad = attend_backward(
            query_value, keys, attended, after(att_grad, *earlier), lse, segs, first, kind
        )
        query_value_grad = query_value_grad.reshape(2 * count, rows)
        one = dot(query_value_grad, norm_one, NN).astype(BF16).reshape(2, 2, -1, width)
        key_w = dot(key_grad, norm_one, NN).astype(BF16).reshape(2, -1, width)
        out_w = out_grad.reshape(2, -1, width)
        grads = [jnp.stack([one[:, core], jnp.stack([key_w[core], out_w[core]])]) for core in (0, 1)]
        return (query_value_grad, key_grad), grads

    def project_back(projected, weights):
        return dot(projected[0], weights[0].reshape(-1, width), TN) + dot(
            projected[1], weights[1, 0], TN
        )

    def halve_y(terms):
        return halve(terms, lambda v: pick_y(v, 1, at_y), lambda v: pick_y(v, 1, 1 - at_y))

    far_out, far_att = before_attention(far, far_w)
    near_out, near_att = before_attention(near, near_w)
    own_out, own_att = before_attention(own, own_w)
    two_got = after(two_got, far_att, near_att)
    pairs = [item.reshape(2, 2, 2, -1, width) for item in (two_grads[0], two_got)]
    two_terms, send = halve(pairs, lambda v: v[:, :, 0], lambda v: v[:, :, 1])
    two_got = swap(send, "x")
    far_projected, far_grads = attend_back(far, far_out, far_att, (send,))
    far_got = swap(far_grads[1], "core")

    one_got = after(one_got, far_grads[0])
    one_terms, send = halve(
        one_terms + [one_got], lambda v: v[:, :quarter], lambda v: v[:, quarter:]
    )
    one_got = swap(send, "x")
    near_att = after(near_att, send)
    far_terms, send = halve_y([far_grads[0], far_got])
    far_got = swap(send, "y")
    near_projected, near_grads = attend_back(near, near_out, near_att, (send,))
    near_got = swap(near_grads[1], "core")
    far_got = after(far_got, near_grads[0])
    far_got = swap(add(*far_terms, far_got), "x")
    two_got = after(two_got, near_grads[0])
    two_terms, send = halve(two_terms + [two_got], lambda v: v[:, 0], lambda v: v[:, 1])
    two_got = swap(send, "y")
    own_att = after(own_att, send)
    near_terms, send = halve_y([near_grads[0], near_got])
    near_got = swap(send, "y")
    own_projected, own_grads = attend_back(own, own_out, own_att, (send,))
    own_got = swap(own_grads[1], "core")

    def part_z(values, at):
        return values.reshape(2, -1, HEAD_DIM, width)[:, at]

    def spread_z(terms):
        sends = [add(*[part_z(item, at) for item in terms]) for at in (1, 2, 3)]
        return [part_z(item, 0) for item in terms], sends

    one_terms, one_sends = spread_z(one_terms + [after(one_got, own_grads[0])])
    one_z = send_z(one_sends)
    own_terms, own_send = halve_y([own_grads[0], own_got])
    own_y = swap(own_send, "y")

    norm_one_grad = project_back(far_projected, far_w) + project_back(near_projected, near_w)
    norm_one_grad = norm_one_grad + project_back(
        after(own_projected, own_send, *one_sends), own_w
    )
    input_part, gain_one_grad, bias_one_grad = norm_back(
        resid_in, ln1_gain, ln1_bias, norm_one_grad
    )
    in_grad = (res_grad + input_part).astype(BF16)
    norm_parts = jnp.stack([gain_one_grad, bias_one_grad, gain_two_grad, bias_two_grad])

    far_got = after(far_got, norm_one_grad)
    got = [far_got.reshape(2, 4, HEAD_DIM, width)]
    near_sums = [
        item.reshape(2, 3, HEAD_DIM, width) for item in near_terms + [near_got]
    ] + [got[0][:, 1:]]
    sends = [add(*[item[:, at] for item in near_sums]) for at in range(3)]
    attn_z = send_z(sends)
    two_terms, two_sends = spread_z(two_terms + [after(two_got, *sends)])
    two_z = send_z(two_sends)
    norm_sums = lax.dynamic_slice_in_dim(
        total(after(norm_parts, *sends)), at_mp * (width // 8), width // 8, 1
    )

    def collect(terms):
        piece = add(*terms)
        pieces = order(at_y, piece, swap(piece, "y"))
        return order(at_core, pieces, swap(pieces, "core"))

    one_sum = collect(one_terms + one_z)
    attn_sum = collect(
        [item.reshape(2, HEAD_DIM, width) for item in own_terms + [own_y]] + [got[0][:, 0]] + attn_z
    )
    two_sum = collect(two_terms + two_z)
    attn_sum = attn_sum.transpose(1, 2, 0, 3, 4).reshape(4, local, width).astype(F32)
    mlp_sum = jnp.stack([one_sum, two_sum])
    up_sum, down_sum = mlp_sum.transpose(3, 0, 2, 1, 4, 5).reshape(2, -1, width).astype(F32)
    return (
        output,
        in_grad,
        norm_sums[0],
        norm_sums[1],
        attn_sum[0].T,
        attn_sum[1].T,
        attn_sum[2].T,
        attn_sum[3],
        norm_sums[2],
        norm_sums[3],
        up_sum.T,
        down_sum,
    )


def on_any(
    mp_size,
    inputs,
    segments,
    ln1_gain,
    ln1_bias,
    w_query,
    w_key,
    w_value,
    w_output,
    ln2_gain,
    ln2_bias,
    w_up,
    w_down,
    cotangent,
):
    rows, width = inputs.shape
    seq_length = segments.shape[1]
    shared_by = seq_length // rows
    at_mp = lax.axis_index("mp")
    groups = [[start + i for i in range(shared_by)] for start in range(0, mp_size, shared_by)]

    def exchange(values, split, join):
        if shared_by == 1:
            return values
        return lax.all_to_all(values, "mp", split, join, axis_index_groups=groups, tiled=True)

    def gather(parts):
        return lax.all_gather(parts, "mp", axis=1, tiled=True)

    def reduce(parts):
        return lax.psum(lax.psum_scatter(parts, "mp", scatter_dimension=1, tiled=True), "dp")

    attn_w = gather(jnp.stack([w_query.T, w_value.T, w_key.T, w_output]))
    mlp_w = gather(jnp.stack([w_up.T, w_down]))
    project, w_out = attn_w[:3].reshape(3 * width, width), attn_w[3]

    segs = lax.dynamic_index_in_dim(segments, at_mp // shared_by, 0, keepdims=False)
    first, kind = windows(segs)
    resid_in = inputs.astype(F32)
    norm_one = layer_norm(resid_in, ln1_gain, ln1_bias).astype(BF16)
    projected = dot(project, norm_one, NT).astype(BF16).reshape(3, width, rows)
    projected = exchange(projected, 1, 2)
    query_value, keys = projected[:2], projected[2]
    heads_out, lse = attend_forward(query_value, keys, segs, first, kind)
    attended = exchange(heads_out, 1, 0)
    residual = resid_in + dot(attended, w_out, TN)
    norm_two = layer_norm(residual, ln2_gain, ln2_bias).astype(BF16)
    mlp_branch, norm_two_grad, (mlp_grads,) = feed_forward(norm_two, cotangent, [mlp_w])
    output = (residual + mlp_branch).astype(BF16)
    up_sum, down_sum = reduce(mlp_grads).astype(F32)

    resid_part, gain_two_grad, bias_two_grad = norm_back(residual, ln2_gain, ln2_bias, norm_two_grad)
    res_grad = cotangent.astype(F32) + resid_part
    branch_grad = res_grad.astype(BF16)
    out_grad = dot(attended, branch_grad, NN).astype(BF16)
    att_grad = exchange(dot(w_out, branch_grad, NT).astype(BF16), 0, 1)
    query_value_grad, key_grad = attend_backward(
        query_value, keys, heads_out, att_grad, lse, segs, first, kind
    )
    proj_grad = exchange(jnp.concatenate([query_value_grad, key_grad[None]]), 2, 1)
    proj_grad = proj_grad.reshape(3 * width, rows)
    project_grad = dot(proj_grad, norm_one, NN).astype(BF16).reshape(3, width, width)
    attn_sum = reduce(jnp.concatenate([project_grad, out_grad[None]])).astype(F32)
    input_part, gain_one_grad, bias_one_grad = norm_back(
        resid_in, ln1_gain, ln1_bias, dot(proj_grad, project, TN)
    )
    in_grad = (res_grad + input_part).astype(BF16)
    norm_parts = jnp.stack([gain_one_grad, bias_one_grad, gain_two_grad, bias_two_grad])
    norm_sums = lax.dynamic_slice_in_dim(
        lax.psum(norm_parts, ("dp", "mp")), at_mp * (width // mp_size), width // mp_size, 1
    )
    return (
        output,
        in_grad,
        norm_sums[0],
        norm_sums[1],
        attn_sum[0].T,
        attn_sum[2].T,
        attn_sum[1].T,
        attn_sum[3],
        norm_sums[2],
        norm_sums[3],
        up_sum.T,
        down_sum,
    )


def shards(dp_size, mp_size, inputs, segments, *rest):
    if dp_size == 4 and mp_size == 8 and inputs.shape[0] == segments.shape[1]:
        return on_cube(inputs, segments, *rest)
    return on_any(mp_size, inputs, segments, *rest)


def solution(mesh):
    return jax.shard_map(
        functools.partial(shards, mesh.shape["dp"], mesh.shape["mp"]),
        mesh=mesh,
        in_specs=(
            P(("dp", "mp"), None),
            P("dp", None),
            P(),
            P(),
            P(None, "mp"),
            P(None, "mp"),
            P(None, "mp"),
            P("mp", None),
            P(),
            P(),
            P(None, "mp"),
            P("mp", None),
            P(("dp", "mp"), None),
        ),
        out_specs=(
            P(("dp", "mp"), None),
            P(("dp", "mp"), None),
            P("mp"),
            P("mp"),
            P(None, "mp"),
            P(None, "mp"),
            P(None, "mp"),
            P("mp", None),
            P("mp"),
            P("mp"),
            P(None, "mp"),
            P("mp", None),
        ),
        check_vma=False,
    )
```

```python
import functools
import math

import jax
import jax.numpy as jnp
from jax import lax
from jax.experimental import pallas as pl
from jax.experimental.pallas import tpu as pltpu
from jax.sharding import PartitionSpec as P

HEAD_DIM = 48
PAIR = 2 * HEAD_DIM
IMAGES = 4
TILE = 128
norm_eps = 1e-06
negative_fill = -1e30
SCALE = HEAD_DIM ** (-0.5)
SCALE_LOG2 = SCALE * math.log2(math.e)
BF16 = jnp.bfloat16
F32 = jnp.float32


def layer_norm(values, gain, bias):
    center = jnp.mean(values, axis=-1, keepdims=True)
    shifted = values - center
    spread = jnp.mean(shifted * shifted, axis=-1, keepdims=True)
    return shifted * lax.rsqrt(spread + norm_eps) * gain + bias


def dot(left, right, dims):
    return lax.dot_general(left, right, (dims, ((), ())), preferred_element_type=F32)


NN = ((1,), (0,))
NT = ((1,), (1,))
TN = ((0,), (0,))


def window_kinds(tiles):
    return tuple(n for n in (2, 3, 4, 5, 6) if n < tiles) + (tiles,)


def image_rows(segs, length):
    row = lax.broadcasted_iota(jnp.int32, (TILE - PAIR, length), 0)
    here = row == segs
    one_hot = jnp.where(here, 1.0, 0.0).astype(BF16)
    fill = jnp.where(jnp.logical_or(here, row >= IMAGES), 0.0, negative_fill).astype(BF16)
    return one_hot, fill


def side_by_side(pair, extra):
    blank = jnp.zeros((HEAD_DIM, TILE), BF16)
    left = jnp.concatenate([pair[:HEAD_DIM], blank, extra], axis=0)
    right = jnp.concatenate([blank, pair[HEAD_DIM:], extra], axis=0)
    return jnp.concatenate([left, right], axis=1)


def pair_places(ref):
    cores, count = ref.shape[0], ref.shape[1]
    return [(core, top) for core in range(cores) for top in range(0, count, PAIR)]


def attend_forward_kernel(
    first_ref, kind_ref, flip_ref, segs_ref, qv_ref, k_ref, out_ref, lse_ref, hot_ref, keys_ref, vals_ref
):
    length = k_ref.shape[-1]
    at_q = flip_ref[0]
    places = pair_places(k_ref)
    one_hot, fill = image_rows(segs_ref[...], length)
    hot_ref[...] = one_hot
    for j, (core, top) in enumerate(places):
        rows = slice(top, top + PAIR)
        keys_ref[j] = jnp.concatenate([k_ref[core, rows, :], fill], axis=0).T
        vals_ref[j] = jnp.concatenate(
            [qv_ref[core, 1 - at_q, rows, :], jnp.ones((16, length), BF16)], axis=0
        )

    def block(b, carry):
        at = pl.ds(pl.multiple_of(b * TILE, TILE), TILE)
        first = pl.multiple_of(first_ref[b] * TILE, TILE)

        def variant(tiles):
            span = pl.ds(first, tiles * TILE)
            scores = [
                dot(
                    keys_ref[j, span, :],
                    side_by_side(qv_ref[core, at_q, top : top + PAIR, at], hot_ref[:, at]),
                    NN,
                )
                for j, (core, top) in enumerate(places)
            ]
            for j, (core, top) in enumerate(places):
                most = jnp.max(scores[j], axis=0, keepdims=True)
                expo = jnp.exp2((scores[j] - most) * SCALE_LOG2).astype(BF16)
                mixed = dot(vals_ref[j, :, span], expo, NN)
                total = mixed[PAIR : PAIR + 1, :]
                inverse = 1.0 / total
                out_ref[core, top : top + HEAD_DIM, at] = (
                    mixed[:HEAD_DIM, :TILE] * inverse[:, :TILE]
                ).astype(BF16)
                out_ref[core, top + HEAD_DIM : top + PAIR, at] = (
                    mixed[HEAD_DIM:PAIR, TILE:] * inverse[:, TILE:]
                ).astype(BF16)
                lse_ref[j, pl.ds(b, 1), :] = most * SCALE_LOG2 + jnp.log2(total)

        for tiles in window_kinds(length // TILE):
            pl.when(kind_ref[b] == tiles)(functools.partial(variant, tiles))
        return carry

    lax.fori_loop(0, length // TILE, block, 0)


def attend_backward_kernel(
    first_ref,
    kind_ref,
    flip_ref,
    segs_ref,
    qv_ref,
    k_ref,
    att_ref,
    grad_ref,
    lse_ref,
    dqv_ref,
    dk_ref,
    hot_ref,
    keys_ref,
    vals_ref,
    queries_ref,
    grads_ref,
    key_sum_ref,
    val_sum_ref,
):
    length = k_ref.shape[-1]
    at_q = flip_ref[0]
    places = pair_places(k_ref)
    one_hot, fill = image_rows(segs_ref[...], length)
    hot_ref[...] = one_hot
    pad = jnp.zeros((TILE - PAIR, length), BF16)
    for j, (core, top) in enumerate(places):
        rows = slice(top, top + PAIR)
        keys_ref[j] = jnp.concatenate([k_ref[core, rows, :], fill], axis=0).T
        vals_ref[j] = jnp.concatenate([qv_ref[core, 1 - at_q, rows, :], pad], axis=0).T
        queries_ref[j] = jnp.concatenate([qv_ref[core, at_q, rows, :], pad], axis=0).T
        grads_ref[j] = jnp.concatenate([grad_ref[core, rows, :], pad], axis=0).T
    key_sum_ref[...] = jnp.zeros(key_sum_ref.shape, F32)
    val_sum_ref[...] = jnp.zeros(val_sum_ref.shape, F32)
    no_rows = jnp.zeros((TILE - PAIR, TILE), BF16)
    lane = lax.broadcasted_iota(jnp.int32, (TILE, TILE), 1)
    in_first = lane < HEAD_DIM

    def stacked(both):
        blank = jnp.zeros_like(both)
        return jnp.concatenate(
            [jnp.where(in_first, both, blank), jnp.where(in_first, blank, both)], axis=0
        )

    def block(b, carry):
        at = pl.ds(pl.multiple_of(b * TILE, TILE), TILE)
        first = pl.multiple_of(first_ref[b] * TILE, TILE)

        def variant(tiles):
            span = pl.ds(first, tiles * TILE)
            scores = [
                dot(
                    keys_ref[j, span, :],
                    side_by_side(qv_ref[core, at_q, top : top + PAIR, at], hot_ref[:, at]),
                    NN,
                )
                for j, (core, top) in enumerate(places)
            ]
            prob_grads = [
                dot(
                    vals_ref[j, span, :],
                    side_by_side(grad_ref[core, top : top + PAIR, at], no_rows),
                    NN,
                )
                for j, (core, top) in enumerate(places)
            ]
            for j, (core, top) in enumerate(places):
                rows = slice(top, top + PAIR)
                agree = grad_ref[core, rows, at].astype(F32) * att_ref[core, rows, at].astype(F32)
                delta = jnp.concatenate(
                    [
                        jnp.sum(agree[:HEAD_DIM], axis=0, keepdims=True),
                        jnp.sum(agree[HEAD_DIM:], axis=0, keepdims=True),
                    ],
                    axis=1,
                )
                probs = jnp.exp2(scores[j] * SCALE_LOG2 - lse_ref[j, pl.ds(b, 1), :])
                score_grad = (probs * (prob_grads[j] - delta)).astype(BF16)
                val_sum_ref[j, span, :] += dot(
                    probs.astype(BF16), stacked(grads_ref[j, at, :]), NN
                )
                key_sum_ref[j, span, :] += dot(score_grad, stacked(queries_ref[j, at, :]), NN)
                query_grad = dot(k_ref[core, rows, span], score_grad, NN) * SCALE
                dqv_ref[core, at_q, top : top + HEAD_DIM, at] = query_grad[
                    :HEAD_DIM, :TILE
                ].astype(BF16)
                dqv_ref[core, at_q, top + HEAD_DIM : top + PAIR, at] = query_grad[
                    HEAD_DIM:, TILE:
                ].astype(BF16)

        for tiles in window_kinds(length // TILE):
            pl.when(kind_ref[b] == tiles)(functools.partial(variant, tiles))
        return carry

    lax.fori_loop(0, length // TILE, block, 0)
    for j, (core, top) in enumerate(places):
        rows = slice(top, top + PAIR)
        dk_ref[core, rows, :] = (key_sum_ref[j] * SCALE).T[:PAIR].astype(BF16)
        dqv_ref[core, 1 - at_q, rows, :] = val_sum_ref[j].T[:PAIR].astype(BF16)


def windows(segs):
    length = segs.shape[0]
    tiles = length // TILE
    by_tile = segs.reshape(tiles, TILE)
    begin = jnp.sum(segs[None, :] < by_tile[:, :1], axis=1)
    end = jnp.sum(segs[None, :] <= by_tile[:, -1:], axis=1)
    first = begin // TILE
    need = (end + TILE - 1) // TILE - first
    kinds = jnp.asarray(window_kinds(tiles), jnp.int32)
    kind = jnp.min(jnp.where(kinds[None, :] >= need[:, None], kinds[None, :], tiles), axis=1)
    return jnp.minimum(first, tiles - kind).astype(jnp.int32), kind.astype(jnp.int32)


def attention_specs(keys):
    cores, count, length = keys.shape
    pairs = cores * count // PAIR
    step = pairs if pairs <= 4 else 4
    part = count * step // pairs
    rows = pl.BlockSpec((cores, part, length), lambda i, *_: (0, i, 0))
    two = pl.BlockSpec((cores, 2, part, length), lambda i, *_: (0, 0, i, 0))
    segs = pl.BlockSpec((1, length), lambda i, *_: (0, 0))
    lse = pl.BlockSpec((step, length // TILE, 2 * TILE), lambda i, *_: (i, 0, 0))
    return pairs, step, rows, two, segs, lse


def attend_forward(query_value, keys, place):
    first, kind, flip, segs = place
    length = segs.shape[0]
    pairs, step, rows, two, segs_spec, lse = attention_specs(keys)
    return pl.pallas_call(
        attend_forward_kernel,
        grid_spec=pltpu.PrefetchScalarGridSpec(
            num_scalar_prefetch=3,
            grid=(pairs // step,),
            in_specs=[segs_spec, two, rows],
            out_specs=[rows, lse],
            scratch_shapes=[
                pltpu.VMEM((TILE - PAIR, length), BF16),
                pltpu.VMEM((step, length, TILE), BF16),
                pltpu.VMEM((step, PAIR + 16, length), BF16),
            ],
        ),
        out_shape=[
            jax.ShapeDtypeStruct(keys.shape, BF16),
            jax.ShapeDtypeStruct((pairs, length // TILE, 2 * TILE), F32),
        ],
        compiler_params=pltpu.CompilerParams(vmem_limit_bytes=40 << 20),
        name="attend_forward",
    )(first, kind, flip, segs[None, :], query_value, keys)


def attend_backward(query_value, keys, attended, grad, lse, place):
    first, kind, flip, segs = place
    length = segs.shape[0]
    pairs, step, rows, two, segs_spec, lse_spec = attention_specs(keys)
    wide = pltpu.VMEM((step, length, TILE), BF16)
    total = pltpu.VMEM((step, length, TILE), F32)
    return pl.pallas_call(
        attend_backward_kernel,
        grid_spec=pltpu.PrefetchScalarGridSpec(
            num_scalar_prefetch=3,
            grid=(pairs // step,),
            in_specs=[segs_spec, two, rows, rows, rows, lse_spec],
            out_specs=[two, rows],
            scratch_shapes=[
                pltpu.VMEM((TILE - PAIR, length), BF16),
                wide,
                wide,
                wide,
                wide,
                total,
                total,
            ],
        ),
        out_shape=[
            jax.ShapeDtypeStruct(query_value.shape, BF16),
            jax.ShapeDtypeStruct(keys.shape, BF16),
        ],
        compiler_params=pltpu.CompilerParams(vmem_limit_bytes=40 << 20),
        name="attend_backward",
    )(first, kind, flip, segs[None, :], query_value, keys, attended, grad, lse)


def gelu_parts(values):
    below = 0.5 * (1.0 + lax.erf(values * (0.5 ** 0.5)))
    density = jnp.exp(values * values * -0.5) * ((2.0 * math.pi) ** -0.5)
    return values * below, below + values * density


def feed_forward_kernel(
    norm_ref, cot_ref, up_ref, down_ref, mlp_ref, back_ref, up_grad_ref, down_grad_ref, act_ref, pre_ref
):
    rows = norm_ref.shape[0]
    chunk = min(rows, 256)

    @pl.when(pl.program_id(0) == 0)
    def _():
        mlp_ref[...] = jnp.zeros(mlp_ref.shape, F32)
        back_ref[...] = jnp.zeros(back_ref.shape, F32)

    for start in range(0, rows, chunk):
        at = slice(start, start + chunk)
        pre_act = dot(norm_ref[at, :], up_ref[...], NT)
        act_grad = dot(cot_ref[at, :], down_ref[...], NT)
        activation, slope = gelu_parts(pre_act)
        activation = activation.astype(BF16)
        pre_grad = (act_grad * slope).astype(BF16)
        act_ref[at, :] = activation
        pre_ref[at, :] = pre_grad
        mlp_ref[at, :] += dot(activation, down_ref[...], NN)
        back_ref[at, :] += dot(pre_grad, up_ref[...], NN)
    up_grad_ref[...] = dot(pre_ref[...], norm_ref[...], TN).astype(BF16)
    down_grad_ref[...] = dot(act_ref[...], cot_ref[...], TN).astype(BF16)


def feed_forward(norm, cot, up, down):
    rows, width = norm.shape
    hidden = up.shape[0]
    part = 512 if hidden % 512 == 0 else hidden
    whole = pl.BlockSpec((rows, width), lambda i: (0, 0))
    block = pl.BlockSpec((part, width), lambda i: (i, 0))
    return pl.pallas_call(
        feed_forward_kernel,
        grid=(hidden // part,),
        in_specs=[whole, whole, block, block],
        out_specs=[whole, whole, block, block],
        out_shape=[
            jax.ShapeDtypeStruct((rows, width), F32),
            jax.ShapeDtypeStruct((rows, width), F32),
            jax.ShapeDtypeStruct((hidden, width), BF16),
            jax.ShapeDtypeStruct((hidden, width), BF16),
        ],
        scratch_shapes=[pltpu.VMEM((rows, part), BF16), pltpu.VMEM((rows, part), BF16)],
        compiler_params=pltpu.CompilerParams(vmem_limit_bytes=56 << 20),
        name="feed_forward",
    )(norm, cot, up, down)


def add(*terms):
    return functools.reduce(jnp.add, [item.astype(F32) for item in terms]).astype(BF16)


def after(values, *earlier):
    return lax.optimization_barrier((values,) + earlier)[0]


def swap(values, axis):
    name, size, mask = {"core": ("dp", 4, 1), "y": ("dp", 4, 2), "x": ("mp", 8, 1)}[axis]
    return lax.ppermute(values, name, [(i, i ^ mask) for i in range(size)])


def send_z(parts):
    return [
        lax.ppermute(part, "mp", [(i, i ^ (2 * (offset + 1))) for i in range(8)])
        for offset, part in enumerate(parts)
    ]


def order(at, mine, other):
    return jnp.where(at == 0, jnp.stack([mine, other]), jnp.stack([other, mine]))


class Line:
    def __init__(self):
        self.last = ()

    def __call__(self, step, *args):
        args, _ = lax.optimization_barrier((args, self.last))
        result = step(*args)
        self.last = tuple(jax.tree.leaves(result))
        return result


def total(values):
    for axis in ("core", "y", "x"):
        values = values + swap(values, axis)
    return functools.reduce(jnp.add, send_z([values] * 3), values)


def norm_back(values, gain, bias, grad):
    return jax.vjp(layer_norm, values, gain, bias)[1](grad)


def on_cube(
    inputs,
    segments,
    ln1_gain,
    ln1_bias,
    w_query,
    w_key,
    w_value,
    w_output,
    ln2_gain,
    ln2_bias,
    w_up,
    w_down,
    cotangent,
):
    rows, width = inputs.shape
    local = w_query.shape[1]
    at_dp, at_mp = lax.axis_index("dp"), lax.axis_index("mp")
    at_y, at_core = at_dp // 2, at_dp % 2
    line = Line()

    def pick(values, at):
        return lax.dynamic_index_in_dim(values, at, 0, keepdims=False)

    def cut_attention(query, key, value, out):
        kinds = jnp.stack([query.T, key.T, value.T, out]).reshape(2, 2, 2, HEAD_DIM, width)
        return pick(kinds.transpose(0, 2, 1, 3, 4).reshape(4, 2, HEAD_DIM, width), at_dp)

    def cut_mlp(up, down):
        pieces = jnp.stack([up.T, down]).reshape(2, 4, -1, width)
        return lax.dynamic_index_in_dim(pieces, at_dp, 1, keepdims=False)

    attn_piece = line(cut_attention, w_query, w_key, w_value, w_output)
    attn_z = send_z([attn_piece] * 3)
    mlp_piece = line(cut_mlp, w_up, w_down)

    def begin(rows_in):
        return layer_norm(rows_in.astype(F32), ln1_gain, ln1_bias).astype(BF16)

    norm_one = line(begin, inputs)
    segs = pick(segments, at_mp)
    place = windows(segs) + (at_y.reshape(1), segs)
    place = line(lambda item: item, place)

    near_z = line(lambda *parts: jnp.stack(parts), attn_piece, *attn_z)
    near_got = swap(near_z, "y")
    far_z = swap(near_z, "x")
    mlp_z = send_z([lax.optimization_barrier((mlp_piece, near_z))[0]] * 3)
    near_y = line(lambda mine, other, _: jnp.stack([mine, other]), near_z, near_got, far_z)
    near_got = swap(near_y, "core")
    far_got = swap(far_z, "y")

    def both_cores(mine, other):
        query_value, key_out = [jnp.stack([mine[:, :, i], other[:, :, i]]) for i in (0, 1)]
        key, out = [
            lax.dynamic_index_in_dim(key_out, at, 1, keepdims=False).reshape(-1, width)
            for at in (at_y, 1 - at_y)
        ]
        return query_value.reshape(-1, width), key, out

    def project(weights, norm):
        query_value = dot(weights[0], norm, NT).astype(BF16).reshape(2, 2, -1, rows)
        return query_value, dot(weights[1], norm, NT).astype(BF16).reshape(2, -1, rows)

    def attend(query_value, keys):
        return attend_forward(query_value, keys, place)

    def branch(base, attended, weights):
        return base + dot(attended.reshape(-1, rows), weights[2], TN)

    near_w = line(both_cores, near_y, near_got)
    near = line(project, near_w, norm_one)
    near += tuple(line(attend, *near))

    def mlp_along_z(piece, *others):
        return [
            jnp.concatenate([piece[i]] + [item[i] for item in others], 0) for i in (0, 1)
        ]

    up, down = line(mlp_along_z, mlp_piece, *mlp_z)
    up_got, down_got = swap(up, "x"), swap(down, "y")
    far_y = line(lambda *parts: jnp.stack(parts), far_z, far_got)
    far_got = swap(far_y, "core")
    residual = line(branch, inputs.astype(F32), near[2], near_w)
    far_w = line(both_cores, far_y, far_got)
    far = line(project, far_w, norm_one)
    far += tuple(line(attend, *far))

    def mlp_second(up, up_got, down, down_got):
        return jnp.concatenate([up, up_got], 0), jnp.stack([down, down_got])

    up, down = line(mlp_second, up, up_got, down, down_got)
    up_got, down_got = swap(up, "y"), swap(down, "x")

    def middle(residual, attended, weights):
        residual = branch(residual, attended, weights)
        return residual, layer_norm(residual, ln2_gain, ln2_bias).astype(BF16)

    residual, norm_two = line(middle, residual, far[2], far_w)

    def mlp_last(up, up_got, down, down_got):
        return jnp.concatenate([up, up_got], 0), jnp.concatenate([down, down_got], 1).reshape(-1, width)

    up, down = line(mlp_last, up, up_got, down, down_got)
    other_up, other_down = swap(up, "core"), swap(down, "core")
    mlp_a, back_a, up_mine, down_mine = line(feed_forward, norm_two, cotangent, up, down)
    mlp_b, back_b, *grads = line(feed_forward, norm_two, cotangent, other_up, other_down)
    up_got, down_got = [swap(item, "core") for item in grads]

    def end(residual, mlp_a, mlp_b, back_a, back_b):
        output = (residual + mlp_a + mlp_b).astype(BF16)
        resid_part, gain_grad, bias_grad = norm_back(residual, ln2_gain, ln2_bias, back_a + back_b)
        res_grad = cotangent.astype(F32) + resid_part
        return res_grad.astype(BF16), res_grad, gain_grad, bias_grad, output

    branch_grad, res_grad, gain_two_grad, bias_two_grad, output = line(
        end, residual, mlp_a, mlp_b, back_a, back_b
    )

    def before_attention(attended, weights, grad):
        att_grad = dot(weights[2], grad, NT).astype(BF16).reshape(attended.shape)
        return att_grad, dot(attended.reshape(-1, rows), grad, NN).astype(BF16)

    far_att, far_out = line(before_attention, far[2], far_w, branch_grad)

    quarter = up.shape[0] // 4

    def up_sum_of(terms, low, high):
        return add(*[item[low:high] for item in terms])

    def down_sum_of(terms, y, x, low=0, high=quarter):
        whole, by_y = terms[:2], terms[2:]
        whole = [item.reshape(2, 2, quarter, width)[y, x, low:high] for item in whole]
        return add(*whole, *[item.reshape(-1, quarter, width)[y, low:high] for item in by_y])

    def mlp_sum_first(up_terms, down_terms):
        return (
            up_sum_of(up_terms, 2 * quarter, 4 * quarter),
            jnp.stack([down_sum_of(down_terms, y, 1) for y in (0, 1)]),
        )

    up_terms, down_terms = (up_mine, up_got), (down_mine, down_got)
    sends = line(mlp_sum_first, up_terms, down_terms)
    up_terms += (swap(sends[0], "y"),)
    down_terms += (swap(sends[1], "x"),)

    def attend_back(saved, att_grad):
        return attend_backward(*saved[:3], att_grad, saved[3], place)

    def weight_grads(query_value_grad, key_grad, out_grad, norm):
        query_value = dot(query_value_grad.reshape(-1, rows), norm, NN).astype(BF16)
        keys = dot(key_grad.reshape(-1, rows), norm, NN).astype(BF16)
        sums = (
            query_value.reshape(2, 2, -1, width),
            keys.reshape(2, -1, width),
            out_grad.reshape(2, -1, width),
        )
        return sums, [item[1] for item in sums]

    def project_back(grads, weights):
        return dot(grads[0].reshape(-1, rows), weights[0], TN) + dot(
            grads[1].reshape(-1, rows), weights[1], TN
        )

    def attn_terms_of(mine, got, at):
        terms = [(mine[0][0, at], mine[1][0], mine[2][0]), (got[0][at], got[1], got[2])]
        first = at_y == at
        return [
            [item[0] for item in terms],
            [jnp.where(first, item[1], item[2]) for item in terms],
        ]

    def sum_other_y(mine, got):
        return jnp.stack([add(*terms) for terms in attn_terms_of(mine, got, 1)])

    def sum_this_y(mine, got, from_y):
        terms = attn_terms_of(mine, got, 0)
        return jnp.stack([add(*terms[i], from_y[i]) for i in (0, 1)])

    far_grads = line(attend_back, far, far_att)
    far_mine, sends = line(weight_grads, *far_grads, far_out, norm_one)
    far_got = [swap(item, "core") for item in sends]
    near_att, near_out = line(before_attention, near[2], near_w, branch_grad)
    norm_one_grad = line(project_back, far_grads, far_w)
    far_y = swap(line(sum_other_y, far_mine, far_got), "y")

    def mlp_sum_second(up_terms, down_terms):
        return up_sum_of(up_terms, quarter, 2 * quarter), down_sum_of(down_terms, 1, 0)

    sends = line(mlp_sum_second, up_terms, down_terms)
    up_terms += (swap(sends[0], "x"),)
    down_y = swap(sends[1], "y")

    near_grads = line(attend_back, near, near_att)
    near_mine, sends = line(weight_grads, *near_grads, near_out, norm_one)
    near_got = [swap(item, "core") for item in sends]
    far_x = swap(line(sum_this_y, far_mine, far_got, far_y), "x")
    part = quarter // 4

    def mlp_sum_of_z(up_terms, down_terms, down_y, z):
        low, high = z * part, (z + 1) * part
        return (
            up_sum_of(up_terms, low, high),
            down_sum_of(down_terms + (jnp.stack([down_y, down_y]),), 0, 0, low, high),
        )

    def mlp_sum_z(*terms):
        return [jnp.stack(mlp_sum_of_z(*terms, z)) for z in (1, 2, 3)]

    mlp_z = send_z(line(mlp_sum_z, up_terms, down_terms, down_y))
    near_y = swap(line(sum_other_y, near_mine, near_got), "y")

    def finish(norm_one_grad, grads, weights):
        norm_one_grad = norm_one_grad + project_back(grads, weights)
        input_part, gain_grad, bias_grad = norm_back(
            inputs.astype(F32), ln1_gain, ln1_bias, norm_one_grad
        )
        parts = jnp.stack([gain_grad, bias_grad, gain_two_grad, bias_two_grad])
        return parts, (res_grad + input_part).astype(BF16)

    norm_parts, in_grad = line(finish, norm_one_grad, near_grads, near_w)

    def attn_sum_z(mine, got, from_y, from_x):
        count = HEAD_DIM
        whole = sum_this_y(mine, got, from_y).astype(F32) + from_x.reshape(2, -1, width)
        return [whole[:, at * count : (at + 1) * count].astype(BF16) for at in (0, 1, 2, 3)]

    attn_mine, *sends = line(attn_sum_z, near_mine, near_got, near_y, far_x)
    attn_z = send_z(sends)
    norm_sums = lax.dynamic_slice_in_dim(
        total(lax.optimization_barrier((norm_parts, line.last))[0]),
        at_mp * (width // 8),
        width // 8,
        1,
    )

    def mlp_piece_sum(up_terms, down_terms, down_y, others):
        mine = mlp_sum_of_z(up_terms, down_terms, down_y, 0)
        return jnp.stack([add(item, *[other[i] for other in others]) for i, item in enumerate(mine)])

    def of_shard(piece):
        pieces = order(at_y, piece, swap(piece, "y"))
        return order(at_core, pieces, swap(pieces, "core"))

    mlp_sum = of_shard(line(mlp_piece_sum, up_terms, down_terms, down_y, mlp_z))
    attn_sum = of_shard(line(add, attn_mine, *attn_z))
    attn_sum = attn_sum.transpose(1, 2, 0, 3, 4).reshape(4, local, width).astype(F32)
    up_sum, down_sum = mlp_sum.transpose(2, 1, 0, 3, 4).reshape(2, -1, width).astype(F32)
    return (
        output,
        in_grad,
        norm_sums[0],
        norm_sums[1],
        attn_sum[0].T,
        attn_sum[1].T,
        attn_sum[2].T,
        attn_sum[3],
        norm_sums[2],
        norm_sums[3],
        up_sum.T,
        down_sum,
    )


def on_any(
    mp_size,
    inputs,
    segments,
    ln1_gain,
    ln1_bias,
    w_query,
    w_key,
    w_value,
    w_output,
    ln2_gain,
    ln2_bias,
    w_up,
    w_down,
    cotangent,
):
    rows, width = inputs.shape
    seq_length = segments.shape[1]
    shared_by = seq_length // rows
    at_mp = lax.axis_index("mp")
    groups = [[start + i for i in range(shared_by)] for start in range(0, mp_size, shared_by)]

    def exchange(values, split, join):
        if shared_by == 1:
            return values
        return lax.all_to_all(values, "mp", split, join, axis_index_groups=groups, tiled=True)

    def gather(parts):
        return lax.all_gather(parts, "mp", axis=1, tiled=True)

    def reduce(parts):
        return lax.psum(lax.psum_scatter(parts, "mp", scatter_dimension=1, tiled=True), "dp")

    attn_w = gather(jnp.stack([w_query.T, w_value.T, w_key.T, w_output]))
    up, down = gather(jnp.stack([w_up.T, w_down]))
    project, w_out = attn_w[:3].reshape(3 * width, width), attn_w[3]

    segs = lax.dynamic_index_in_dim(segments, at_mp // shared_by, 0, keepdims=False)
    place = windows(segs) + (jnp.zeros((1,), jnp.int32), segs)
    resid_in = inputs.astype(F32)
    norm_one = layer_norm(resid_in, ln1_gain, ln1_bias).astype(BF16)
    projected = dot(project, norm_one, NT).astype(BF16).reshape(3, width, rows)
    projected = exchange(projected, 1, 2)
    query_value, keys = projected[None, :2], projected[2:]
    heads_out, lse = attend_forward(query_value, keys, place)
    attended = exchange(heads_out[0], 1, 0)
    residual = resid_in + dot(attended, w_out, TN)
    norm_two = layer_norm(residual, ln2_gain, ln2_bias).astype(BF16)
    mlp_branch, norm_two_grad, *mlp_grads = feed_forward(norm_two, cotangent, up, down)
    output = (residual + mlp_branch).astype(BF16)
    up_sum, down_sum = reduce(jnp.stack(mlp_grads)).astype(F32)

    resid_part, gain_two_grad, bias_two_grad = norm_back(residual, ln2_gain, ln2_bias, norm_two_grad)
    res_grad = cotangent.astype(F32) + resid_part
    branch_grad = res_grad.astype(BF16)
    out_grad = dot(attended, branch_grad, NN).astype(BF16)
    att_grad = exchange(dot(w_out, branch_grad, NT).astype(BF16), 0, 1)
    query_value_grad, key_grad = attend_backward(
        query_value, keys, heads_out, att_grad[None], lse, place
    )
    proj_grad = exchange(jnp.concatenate([query_value_grad[0], key_grad]), 2, 1)
    proj_grad = proj_grad.reshape(3 * width, rows)
    project_grad = dot(proj_grad, norm_one, NN).astype(BF16).reshape(3, width, width)
    attn_sum = reduce(jnp.concatenate([project_grad, out_grad[None]])).astype(F32)
    input_part, gain_one_grad, bias_one_grad = norm_back(
        resid_in, ln1_gain, ln1_bias, dot(proj_grad, project, TN)
    )
    in_grad = (res_grad + input_part).astype(BF16)
    norm_parts = jnp.stack([gain_one_grad, bias_one_grad, gain_two_grad, bias_two_grad])
    norm_sums = lax.dynamic_slice_in_dim(
        lax.psum(norm_parts, ("dp", "mp")), at_mp * (width // mp_size), width // mp_size, 1
    )
    return (
        output,
        in_grad,
        norm_sums[0],
        norm_sums[1],
        attn_sum[0].T,
        attn_sum[2].T,
        attn_sum[1].T,
        attn_sum[3],
        norm_sums[2],
        norm_sums[3],
        up_sum.T,
        down_sum,
    )


def shards(dp_size, mp_size, inputs, segments, *rest):
    if dp_size == 4 and mp_size == 8 and inputs.shape[0] == segments.shape[1]:
        return on_cube(inputs, segments, *rest)
    return on_any(mp_size, inputs, segments, *rest)


def solution(mesh):
    return jax.shard_map(
        functools.partial(shards, mesh.shape["dp"], mesh.shape["mp"]),
        mesh=mesh,
        in_specs=(
            P(("dp", "mp"), None),
            P("dp", None),
            P(),
            P(),
            P(None, "mp"),
            P(None, "mp"),
            P(None, "mp"),
            P("mp", None),
            P(),
            P(),
            P(None, "mp"),
            P("mp", None),
            P(("dp", "mp"), None),
        ),
        out_specs=(
            P(("dp", "mp"), None),
            P(("dp", "mp"), None),
            P("mp"),
            P("mp"),
            P(None, "mp"),
            P(None, "mp"),
            P(None, "mp"),
            P("mp", None),
            P("mp"),
            P("mp"),
            P(None, "mp"),
            P("mp", None),
        ),
        check_vma=False,
    )
```

```python
import functools
import math

import jax
import jax.numpy as jnp
from jax import lax
from jax.experimental import pallas as pl
from jax.experimental.pallas import tpu as pltpu
from jax.sharding import PartitionSpec as P

HEAD_DIM = 48
PAIR = 2 * HEAD_DIM
IMAGES = 4
TILE = 128
norm_eps = 1e-06
negative_fill = -1e30
SCALE = HEAD_DIM ** (-0.5)
SCALE_LOG2 = SCALE * math.log2(math.e)
BF16 = jnp.bfloat16
F32 = jnp.float32


def layer_norm(values, gain, bias):
    center = jnp.mean(values, axis=-1, keepdims=True)
    shifted = values - center
    spread = jnp.mean(shifted * shifted, axis=-1, keepdims=True)
    return shifted * lax.rsqrt(spread + norm_eps) * gain + bias


def layer_norm_back(values, gain, grad):
    shifted = values - jnp.mean(values, axis=-1, keepdims=True)
    scale = lax.rsqrt(jnp.mean(shifted * shifted, axis=-1, keepdims=True) + norm_eps)
    unit = shifted * scale
    scaled = grad * gain
    back = scale * (
        scaled
        - jnp.mean(scaled, axis=-1, keepdims=True)
        - unit * jnp.mean(scaled * unit, axis=-1, keepdims=True)
    )
    return back, jnp.sum(grad * unit, axis=0, keepdims=True), jnp.sum(grad, axis=0, keepdims=True)


def dot(left, right, dims):
    return lax.dot_general(left, right, (dims, ((), ())), preferred_element_type=F32)


NN = ((1,), (0,))
NT = ((1,), (1,))
TN = ((0,), (0,))


def window_kinds(tiles):
    return tuple(n for n in (2, 3, 4, 5, 6) if n < tiles) + (tiles,)


def image_rows(segs, length):
    row = lax.broadcasted_iota(jnp.int32, (TILE - PAIR, length), 0)
    here = row == segs
    one_hot = jnp.where(here, 1.0, 0.0).astype(BF16)
    fill = jnp.where(jnp.logical_or(here, row >= IMAGES), 0.0, negative_fill).astype(BF16)
    return one_hot, fill


def side_by_side(pair, extra):
    blank = jnp.zeros((HEAD_DIM, TILE), BF16)
    left = jnp.concatenate([pair[:HEAD_DIM], blank, extra], axis=0)
    right = jnp.concatenate([blank, pair[HEAD_DIM:], extra], axis=0)
    return jnp.concatenate([left, right], axis=1)


def pair_places(ref):
    cores, count = ref.shape[0], ref.shape[1]
    return [(core, top) for core in range(cores) for top in range(0, count, PAIR)]


def attend_forward_kernel(
    first_ref, kind_ref, flip_ref, segs_ref, qv_ref, k_ref, out_ref, lse_ref, hot_ref, keys_ref, vals_ref
):
    length = k_ref.shape[-1]
    at_q = flip_ref[0]
    places = pair_places(k_ref)
    one_hot, fill = image_rows(segs_ref[...], length)
    hot_ref[...] = one_hot
    for j, (core, top) in enumerate(places):
        rows = slice(top, top + PAIR)
        keys_ref[j] = jnp.concatenate([k_ref[core, rows, :], fill], axis=0).T
        vals_ref[j] = jnp.concatenate(
            [qv_ref[core, 1 - at_q, rows, :], jnp.ones((16, length), BF16)], axis=0
        )

    def block(b, carry):
        at = pl.ds(pl.multiple_of(b * TILE, TILE), TILE)
        first = pl.multiple_of(first_ref[b] * TILE, TILE)

        def variant(tiles):
            span = pl.ds(first, tiles * TILE)
            scores = [
                dot(
                    keys_ref[j, span, :],
                    side_by_side(qv_ref[core, at_q, top : top + PAIR, at], hot_ref[:, at]),
                    NN,
                )
                for j, (core, top) in enumerate(places)
            ]
            for j, (core, top) in enumerate(places):
                most = jnp.max(scores[j], axis=0, keepdims=True)
                expo = jnp.exp2((scores[j] - most) * SCALE_LOG2).astype(BF16)
                mixed = dot(vals_ref[j, :, span], expo, NN)
                total = mixed[PAIR : PAIR + 1, :]
                inverse = 1.0 / total
                out_ref[core, top : top + HEAD_DIM, at] = (
                    mixed[:HEAD_DIM, :TILE] * inverse[:, :TILE]
                ).astype(BF16)
                out_ref[core, top + HEAD_DIM : top + PAIR, at] = (
                    mixed[HEAD_DIM:PAIR, TILE:] * inverse[:, TILE:]
                ).astype(BF16)
                lse_ref[j, pl.ds(b, 1), :] = most * SCALE_LOG2 + jnp.log2(total)

        for tiles in window_kinds(length // TILE):
            pl.when(kind_ref[b] == tiles)(functools.partial(variant, tiles))
        return carry

    lax.fori_loop(0, length // TILE, block, 0)


def attend_backward_kernel(
    first_ref,
    kind_ref,
    flip_ref,
    segs_ref,
    qv_ref,
    k_ref,
    att_ref,
    grad_ref,
    lse_ref,
    dqv_ref,
    dk_ref,
    hot_ref,
    keys_ref,
    vals_ref,
    queries_ref,
    grads_ref,
    key_sum_ref,
    val_sum_ref,
):
    length = k_ref.shape[-1]
    at_q = flip_ref[0]
    places = pair_places(k_ref)
    one_hot, fill = image_rows(segs_ref[...], length)
    hot_ref[...] = one_hot
    pad = jnp.zeros((TILE - PAIR, length), BF16)
    for j, (core, top) in enumerate(places):
        rows = slice(top, top + PAIR)
        keys_ref[j] = jnp.concatenate([k_ref[core, rows, :], fill], axis=0).T
        vals_ref[j] = jnp.concatenate([qv_ref[core, 1 - at_q, rows, :], pad], axis=0).T
        queries_ref[j] = jnp.concatenate([qv_ref[core, at_q, rows, :], pad], axis=0).T
        grads_ref[j] = jnp.concatenate([grad_ref[core, rows, :], pad], axis=0).T
    key_sum_ref[...] = jnp.zeros(key_sum_ref.shape, F32)
    val_sum_ref[...] = jnp.zeros(val_sum_ref.shape, F32)
    no_rows = jnp.zeros((TILE - PAIR, TILE), BF16)
    lane = lax.broadcasted_iota(jnp.int32, (TILE, TILE), 1)
    in_first = lane < HEAD_DIM

    def stacked(both):
        blank = jnp.zeros_like(both)
        return jnp.concatenate(
            [jnp.where(in_first, both, blank), jnp.where(in_first, blank, both)], axis=0
        )

    def block(b, carry):
        at = pl.ds(pl.multiple_of(b * TILE, TILE), TILE)
        first = pl.multiple_of(first_ref[b] * TILE, TILE)

        def variant(tiles):
            span = pl.ds(first, tiles * TILE)
            scores = [
                dot(
                    keys_ref[j, span, :],
                    side_by_side(qv_ref[core, at_q, top : top + PAIR, at], hot_ref[:, at]),
                    NN,
                )
                for j, (core, top) in enumerate(places)
            ]
            prob_grads = [
                dot(
                    vals_ref[j, span, :],
                    side_by_side(grad_ref[core, top : top + PAIR, at], no_rows),
                    NN,
                )
                for j, (core, top) in enumerate(places)
            ]
            for j, (core, top) in enumerate(places):
                rows = slice(top, top + PAIR)
                agree = grad_ref[core, rows, at].astype(F32) * att_ref[core, rows, at].astype(F32)
                delta = jnp.concatenate(
                    [
                        jnp.sum(agree[:HEAD_DIM], axis=0, keepdims=True),
                        jnp.sum(agree[HEAD_DIM:], axis=0, keepdims=True),
                    ],
                    axis=1,
                )
                probs = jnp.exp2(scores[j] * SCALE_LOG2 - lse_ref[j, pl.ds(b, 1), :])
                score_grad = (probs * (prob_grads[j] - delta)).astype(BF16)
                val_sum_ref[j, span, :] += dot(
                    probs.astype(BF16), stacked(grads_ref[j, at, :]), NN
                )
                key_sum_ref[j, span, :] += dot(score_grad, stacked(queries_ref[j, at, :]), NN)
                query_grad = dot(k_ref[core, rows, span], score_grad, NN) * SCALE
                dqv_ref[core, at_q, top : top + HEAD_DIM, at] = query_grad[
                    :HEAD_DIM, :TILE
                ].astype(BF16)
                dqv_ref[core, at_q, top + HEAD_DIM : top + PAIR, at] = query_grad[
                    HEAD_DIM:, TILE:
                ].astype(BF16)

        for tiles in window_kinds(length // TILE):
            pl.when(kind_ref[b] == tiles)(functools.partial(variant, tiles))
        return carry

    lax.fori_loop(0, length // TILE, block, 0)
    for j, (core, top) in enumerate(places):
        rows = slice(top, top + PAIR)
        dk_ref[core, rows, :] = (key_sum_ref[j] * SCALE).T[:PAIR].astype(BF16)
        dqv_ref[core, 1 - at_q, rows, :] = val_sum_ref[j].T[:PAIR].astype(BF16)


def windows(segs):
    length = segs.shape[0]
    tiles = length // TILE
    by_tile = segs.reshape(tiles, TILE)
    begin = jnp.sum(segs[None, :] < by_tile[:, :1], axis=1)
    end = jnp.sum(segs[None, :] <= by_tile[:, -1:], axis=1)
    first = begin // TILE
    need = (end + TILE - 1) // TILE - first
    kinds = jnp.asarray(window_kinds(tiles), jnp.int32)
    kind = jnp.min(jnp.where(kinds[None, :] >= need[:, None], kinds[None, :], tiles), axis=1)
    return jnp.minimum(first, tiles - kind).astype(jnp.int32), kind.astype(jnp.int32)


def attention_specs(keys):
    cores, count, length = keys.shape
    pairs = cores * count // PAIR
    step = pairs if pairs <= 4 else 4
    part = count * step // pairs
    rows = pl.BlockSpec((cores, part, length), lambda i, *_: (0, i, 0))
    two = pl.BlockSpec((cores, 2, part, length), lambda i, *_: (0, 0, i, 0))
    segs = pl.BlockSpec((1, length), lambda i, *_: (0, 0))
    lse = pl.BlockSpec((step, length // TILE, 2 * TILE), lambda i, *_: (i, 0, 0))
    return pairs, step, rows, two, segs, lse


def attend_forward(query_value, keys, place):
    first, kind, flip, segs = place
    length = segs.shape[0]
    pairs, step, rows, two, segs_spec, lse = attention_specs(keys)
    return pl.pallas_call(
        attend_forward_kernel,
        grid_spec=pltpu.PrefetchScalarGridSpec(
            num_scalar_prefetch=3,
            grid=(pairs // step,),
            in_specs=[segs_spec, two, rows],
            out_specs=[rows, lse],
            scratch_shapes=[
                pltpu.VMEM((TILE - PAIR, length), BF16),
                pltpu.VMEM((step, length, TILE), BF16),
                pltpu.VMEM((step, PAIR + 16, length), BF16),
            ],
        ),
        out_shape=[
            jax.ShapeDtypeStruct(keys.shape, BF16),
            jax.ShapeDtypeStruct((pairs, length // TILE, 2 * TILE), F32),
        ],
        compiler_params=pltpu.CompilerParams(vmem_limit_bytes=40 << 20),
        name="attend_forward",
    )(first, kind, flip, segs[None, :], query_value, keys)


def attend_backward(query_value, keys, attended, grad, lse, place):
    first, kind, flip, segs = place
    length = segs.shape[0]
    pairs, step, rows, two, segs_spec, lse_spec = attention_specs(keys)
    wide = pltpu.VMEM((step, length, TILE), BF16)
    total = pltpu.VMEM((step, length, TILE), F32)
    return pl.pallas_call(
        attend_backward_kernel,
        grid_spec=pltpu.PrefetchScalarGridSpec(
            num_scalar_prefetch=3,
            grid=(pairs // step,),
            in_specs=[segs_spec, two, rows, rows, rows, lse_spec],
            out_specs=[two, rows],
            scratch_shapes=[
                pltpu.VMEM((TILE - PAIR, length), BF16),
                wide,
                wide,
                wide,
                wide,
                total,
                total,
            ],
        ),
        out_shape=[
            jax.ShapeDtypeStruct(query_value.shape, BF16),
            jax.ShapeDtypeStruct(keys.shape, BF16),
        ],
        compiler_params=pltpu.CompilerParams(vmem_limit_bytes=40 << 20),
        name="attend_backward",
    )(first, kind, flip, segs[None, :], query_value, keys, attended, grad, lse)


def gelu_parts(values):
    below = 0.5 * (1.0 + lax.erf(values * (0.5 ** 0.5)))
    density = jnp.exp(values * values * -0.5) * ((2.0 * math.pi) ** -0.5)
    return values * below, below + values * density


def feed_forward_step(
    norm_ref, cot_ref, up_ref, down_ref, mlp_ref, back_ref, up_grad_ref, down_grad_ref, act_ref, pre_ref
):
    rows = norm_ref.shape[0]
    chunk = min(rows, 256)
    for start in range(0, rows, chunk):
        at = slice(start, start + chunk)
        pre_act = dot(norm_ref[at, :], up_ref[...], NT)
        act_grad = dot(cot_ref[at, :], down_ref[...], NT)
        activation, slope = gelu_parts(pre_act)
        activation = activation.astype(BF16)
        pre_grad = (act_grad * slope).astype(BF16)
        act_ref[at, :] = activation
        pre_ref[at, :] = pre_grad
        mlp_ref[at, :] += dot(activation, down_ref[...], NN)
        back_ref[at, :] += dot(pre_grad, up_ref[...], NN)
    up_grad_ref[...] = dot(pre_ref[...], norm_ref[...], TN).astype(BF16)
    down_grad_ref[...] = dot(act_ref[...], cot_ref[...], TN).astype(BF16)


def feed_forward_kernel(norm_ref, cot_ref, up_ref, down_ref, mlp_ref, back_ref, *refs):
    @pl.when(pl.program_id(0) == 0)
    def _():
        mlp_ref[...] = jnp.zeros(mlp_ref.shape, F32)
        back_ref[...] = jnp.zeros(back_ref.shape, F32)

    feed_forward_step(norm_ref, cot_ref, up_ref, down_ref, mlp_ref, back_ref, *refs)


def feed_forward_end_kernel(
    norm_ref,
    cot_ref,
    up_ref,
    down_ref,
    residual_ref,
    mlp_in_ref,
    back_in_ref,
    gain_ref,
    output_ref,
    res_grad_ref,
    branch_ref,
    norm_grad_ref,
    up_grad_ref,
    down_grad_ref,
    mlp_ref,
    back_ref,
    act_ref,
    pre_ref,
):
    @pl.when(pl.program_id(0) == 0)
    def _():
        mlp_ref[...] = mlp_in_ref[...]
        back_ref[...] = back_in_ref[...]

    feed_forward_step(
        norm_ref, cot_ref, up_ref, down_ref, mlp_ref, back_ref, up_grad_ref, down_grad_ref, act_ref, pre_ref
    )

    @pl.when(pl.program_id(0) == pl.num_programs(0) - 1)
    def _():
        rows = norm_ref.shape[0]
        chunk = min(rows, 128)
        gain = gain_ref[...]
        norm_grad_ref[...] = jnp.zeros(norm_grad_ref.shape, F32)

        def part(i, carry):
            at = pl.ds(pl.multiple_of(i * chunk, chunk), chunk)
            residual = residual_ref[at, :]
            output_ref[at, :] = (residual + mlp_ref[at, :]).astype(BF16)
            back, gain_grad, bias_grad = layer_norm_back(residual, gain, back_ref[at, :])
            res_grad = cot_ref[at, :].astype(F32) + back
            res_grad_ref[at, :] = res_grad
            branch_ref[at, :] = res_grad.astype(BF16)
            norm_grad_ref[0:1, :] += gain_grad
            norm_grad_ref[1:2, :] += bias_grad
            return carry

        lax.fori_loop(0, rows // chunk, part, 0)


def feed_forward(norm, cot, up, down, end=()):
    rows, width = norm.shape
    hidden = up.shape[0]
    part = 512 if hidden % 512 == 0 else hidden
    once = pl.Buffered(1)
    whole = pl.BlockSpec((rows, width), lambda i: (0, 0), pipeline_mode=once)
    block = pl.BlockSpec((part, width), lambda i: (i, 0))
    few = pl.BlockSpec((8, width), lambda i: (0, 0))
    sums = jax.ShapeDtypeStruct((rows, width), F32)
    low = jax.ShapeDtypeStruct((rows, width), BF16)
    grads = jax.ShapeDtypeStruct((hidden, width), BF16)
    parts = [pltpu.VMEM((rows, part), BF16)] * 2
    if end:
        kernel = feed_forward_end_kernel
        one = pl.BlockSpec((1, width), lambda i: (0, 0))
        end_specs, end = [whole, whole, whole, one], (*end[:3], end[3][None, :])
        out_specs = [whole, whole, whole, few, block, block]
        out_shape = [low, sums, low, jax.ShapeDtypeStruct((8, width), F32), grads, grads]
        parts = [pltpu.VMEM((rows, width), F32)] * 2 + parts
    else:
        kernel = feed_forward_kernel
        end_specs, out_specs, out_shape = [], [whole, whole, block, block], [sums, sums, grads, grads]
    return pl.pallas_call(
        kernel,
        grid=(hidden // part,),
        in_specs=[whole, whole, block, block] + end_specs,
        out_specs=out_specs,
        out_shape=out_shape,
        scratch_shapes=parts,
        compiler_params=pltpu.CompilerParams(vmem_limit_bytes=60 << 20),
        name="feed_forward",
    )(norm, cot, up, down, *end)


def add(*terms):
    return functools.reduce(jnp.add, [item.astype(F32) for item in terms]).astype(BF16)


def swap(values, axis):
    name, size, mask = {"core": ("dp", 4, 1), "y": ("dp", 4, 2), "x": ("mp", 8, 1)}[axis]
    return lax.ppermute(values, name, [(i, i ^ mask) for i in range(size)])


def send_z(parts):
    return [
        lax.ppermute(part, "mp", [(i, i ^ (2 * (offset + 1))) for i in range(8)])
        for offset, part in enumerate(parts)
    ]


def order(at, mine, other):
    return jnp.where(at == 0, jnp.stack([mine, other]), jnp.stack([other, mine]))


class Line:
    def __init__(self):
        self.last = ()

    def __call__(self, step, *args):
        args, _ = lax.optimization_barrier((args, self.last))
        result = step(*args)
        self.last = tuple(jax.tree.leaves(result))
        return result


def norm_back(values, gain, bias, grad):
    return jax.vjp(layer_norm, values, gain, bias)[1](grad)


def on_cube(
    inputs,
    segments,
    ln1_gain,
    ln1_bias,
    w_query,
    w_key,
    w_value,
    w_output,
    ln2_gain,
    ln2_bias,
    w_up,
    w_down,
    cotangent,
):
    rows, width = inputs.shape
    local = w_query.shape[1]
    at_dp, at_mp = lax.axis_index("dp"), lax.axis_index("mp")
    at_y, at_core = at_dp // 2, at_dp % 2
    line = Line()

    def pick(values, at):
        return lax.dynamic_index_in_dim(values, at, 0, keepdims=False)

    def cut_attention(query, key, value, out):
        kinds = jnp.stack([query.T, key.T, value.T, out]).reshape(2, 2, 2, HEAD_DIM, width)
        return pick(kinds.transpose(0, 2, 1, 3, 4).reshape(4, 2, HEAD_DIM, width), at_dp)

    def cut_mlp(up, down):
        pieces = jnp.stack([up.T, down]).reshape(2, 4, -1, width)
        return lax.dynamic_index_in_dim(pieces, at_dp, 1, keepdims=False)

    attn_piece = line(cut_attention, w_query, w_key, w_value, w_output)
    attn_z = send_z([attn_piece] * 3)
    mlp_piece = line(cut_mlp, w_up, w_down)
    mlp_z = send_z([mlp_piece] * 3)

    def begin(rows_in):
        return layer_norm(rows_in.astype(F32), ln1_gain, ln1_bias).astype(BF16)

    norm_one = line(begin, inputs)
    segs = pick(segments, at_mp)
    place = windows(segs) + (at_y.reshape(1), segs)
    place = line(lambda item: item, place)

    near_z = line(lambda *parts: jnp.stack(parts[:4]), attn_piece, *attn_z, mlp_z[0])
    near_got = swap(near_z, "y")
    far_z = swap(near_z, "x")
    near_y = line(lambda *parts: jnp.stack(parts[:2]), near_z, near_got, far_z, mlp_z[1])
    near_got = swap(near_y, "core")
    far_got = swap(far_z, "y")

    def both_cores(mine, other):
        query_value, key_out = [jnp.stack([mine[:, :, i], other[:, :, i]]) for i in (0, 1)]
        key, out = [
            lax.dynamic_index_in_dim(key_out, at, 1, keepdims=False).reshape(-1, width)
            for at in (at_y, 1 - at_y)
        ]
        return query_value.reshape(-1, width), key, out

    def project(weights, norm):
        query_value = dot(weights[0], norm, NT).astype(BF16).reshape(2, 2, -1, rows)
        return query_value, dot(weights[1], norm, NT).astype(BF16).reshape(2, -1, rows)

    def attend(query_value, keys):
        return attend_forward(query_value, keys, place)

    def branch(base, attended, weights):
        return base + dot(attended.reshape(-1, rows), weights[2], TN)

    def mlp_along_z(piece, *others):
        return [
            jnp.concatenate([piece[i]] + [item[i] for item in others], 0) for i in (0, 1)
        ]

    def mlp_second(up, up_got, down, down_got):
        return jnp.concatenate([up, up_got], 0), jnp.stack([down, down_got])

    near_w = line(both_cores, near_y, near_got)
    near = line(project, near_w, norm_one)
    up, down = line(mlp_along_z, mlp_piece, *mlp_z)
    up_got, down_got = swap(up, "x"), swap(down, "y")
    near += tuple(line(attend, *near))

    far_y = line(lambda *parts: jnp.stack(parts), far_z, far_got)
    far_got = swap(far_y, "core")
    up, down = line(mlp_second, up, up_got, down, down_got)
    up_got, down_got = swap(up, "y"), swap(down, "x")
    residual = line(branch, inputs.astype(F32), near[2], near_w)
    far_w = line(both_cores, far_y, far_got)
    far = line(project, far_w, norm_one)
    far += tuple(line(attend, *far))

    def middle(residual, attended, weights):
        residual = branch(residual, attended, weights)
        return residual, layer_norm(residual, ln2_gain, ln2_bias).astype(BF16)

    residual, norm_two = line(middle, residual, far[2], far_w)

    def mlp_last(up, up_got, down, down_got):
        return jnp.concatenate([up, up_got], 0), jnp.concatenate([down, down_got], 1).reshape(-1, width)

    up, down = line(mlp_last, up, up_got, down, down_got)
    other_up, other_down = swap(up, "core"), swap(down, "core")
    mlp_a, back_a, up_mine, down_mine = line(feed_forward, norm_two, cotangent, up, down)
    output, res_grad, branch_grad, norm_two_grads, *grads = line(
        feed_forward, norm_two, cotangent, other_up, other_down, (residual, mlp_a, back_a, ln2_gain)
    )
    up_got, down_got = [swap(item, "core") for item in grads]

    def before_attention(attended, weights, grad):
        att_grad = dot(weights[2], grad, NT).astype(BF16).reshape(attended.shape)
        return att_grad, dot(attended.reshape(-1, rows), grad, NN).astype(BF16)

    far_att, far_out = line(before_attention, far[2], far_w, branch_grad)
    near_att, near_out = line(before_attention, near[2], near_w, branch_grad)

    quarter = up.shape[0] // 4

    def up_sum_of(terms, low, high):
        return add(*[item[low:high] for item in terms])

    def down_sum_of(terms, y, x, low=0, high=quarter):
        whole, by_y = terms[:2], terms[2:]
        whole = [item.reshape(2, 2, quarter, width)[y, x, low:high] for item in whole]
        return add(*whole, *[item.reshape(-1, quarter, width)[y, low:high] for item in by_y])

    def mlp_sum_first(up_terms, down_terms):
        return (
            up_sum_of(up_terms, 2 * quarter, 4 * quarter),
            jnp.stack([down_sum_of(down_terms, y, 1) for y in (0, 1)]),
        )

    up_terms, down_terms = (up_mine, up_got), (down_mine, down_got)
    sends = line(mlp_sum_first, up_terms, down_terms)
    up_terms += (swap(sends[0], "y"),)
    down_terms += (swap(sends[1], "x"),)

    def attend_back(saved, att_grad):
        return attend_backward(*saved[:3], att_grad, saved[3], place)

    def weight_grads(query_value_grad, key_grad, out_grad, norm):
        query_value = dot(query_value_grad.reshape(-1, rows), norm, NN).astype(BF16)
        keys = dot(key_grad.reshape(-1, rows), norm, NN).astype(BF16)
        sums = (
            query_value.reshape(2, 2, -1, width),
            keys.reshape(2, -1, width),
            out_grad.reshape(2, -1, width),
        )
        return sums, [item[1] for item in sums]

    def project_back(grads, weights):
        return dot(grads[0].reshape(-1, rows), weights[0], TN) + dot(
            grads[1].reshape(-1, rows), weights[1], TN
        )

    def attn_terms_of(mine, got, at):
        terms = [(mine[0][0, at], mine[1][0], mine[2][0]), (got[0][at], got[1], got[2])]
        first = at_y == at
        return [
            [item[0] for item in terms],
            [jnp.where(first, item[1], item[2]) for item in terms],
        ]

    def sum_other_y(mine, got):
        return jnp.stack([add(*terms) for terms in attn_terms_of(mine, got, 1)])

    def sum_this_y(mine, got, from_y):
        terms = attn_terms_of(mine, got, 0)
        return jnp.stack([add(*terms[i], from_y[i]) for i in (0, 1)])

    far_grads = line(attend_back, far, far_att)
    far_mine, sends = line(weight_grads, *far_grads, far_out, norm_one)
    far_got = [swap(item, "core") for item in sends]
    norm_one_grad = line(project_back, far_grads, far_w)
    far_y = swap(line(sum_other_y, far_mine, far_got), "y")

    def mlp_sum_second(up_terms, down_terms):
        return up_sum_of(up_terms, quarter, 2 * quarter), down_sum_of(down_terms, 1, 0)

    sends = line(mlp_sum_second, up_terms, down_terms)
    up_terms += (swap(sends[0], "x"),)
    down_y = swap(sends[1], "y")

    near_grads = line(attend_back, near, near_att)
    near_mine, sends = line(weight_grads, *near_grads, near_out, norm_one)
    near_got = [swap(item, "core") for item in sends]
    far_x = swap(line(sum_this_y, far_mine, far_got, far_y), "x")
    part = quarter // 4

    def mlp_sum_of_z(up_terms, down_terms, down_y, z):
        low, high = z * part, (z + 1) * part
        return (
            up_sum_of(up_terms, low, high),
            down_sum_of(down_terms + (jnp.stack([down_y, down_y]),), 0, 0, low, high),
        )

    def mlp_sum_z(*terms):
        return [jnp.stack(mlp_sum_of_z(*terms, z)) for z in (1, 2, 3)]

    mlp_z = send_z(line(mlp_sum_z, up_terms, down_terms, down_y))
    near_y = swap(line(sum_other_y, near_mine, near_got), "y")

    def finish(norm_one_grad, grads, weights):
        norm_one_grad = norm_one_grad + project_back(grads, weights)
        input_part, gain_grad, bias_grad = layer_norm_back(
            inputs.astype(F32), ln1_gain, norm_one_grad
        )
        parts = jnp.concatenate([gain_grad, bias_grad, norm_two_grads[:2]])
        return parts, (res_grad + input_part).astype(BF16)

    norm_sums, in_grad = line(finish, norm_one_grad, near_grads, near_w)

    def mlp_piece_sum(up_terms, down_terms, down_y, others):
        mine = mlp_sum_of_z(up_terms, down_terms, down_y, 0)
        return jnp.stack([add(item, *[other[i] for other in others]) for i, item in enumerate(mine)])

    def in_order(piece, y, core, both):
        return order(at_core, order(at_y, piece, y), order(at_y, core, both))

    mlp_sum = line(mlp_piece_sum, up_terms, down_terms, down_y, mlp_z)
    mlp_got = swap(mlp_sum, "y")

    def attn_sum_z(mine, got, from_y, from_x):
        count = HEAD_DIM
        whole = sum_this_y(mine, got, from_y).astype(F32) + from_x.reshape(2, -1, width)
        return [whole[:, at * count : (at + 1) * count].astype(BF16) for at in (0, 1, 2, 3)]

    attn_mine, *sends = line(attn_sum_z, near_mine, near_got, near_y, far_x)
    attn_z = send_z(sends)
    got = swap(norm_sums, "core")
    norm_sums = line(jnp.add, norm_sums, got)
    got = swap(norm_sums, "y")
    mlp_sum = line(functools.partial(order, at_y), mlp_sum, mlp_got)
    mlp_got = swap(mlp_sum, "core")
    norm_sums = line(jnp.add, norm_sums, got)
    got = swap(norm_sums, "x")
    attn_sum = line(add, attn_mine, *attn_z)
    attn_got = [
        lax.ppermute(attn_sum, "dp", [(i, i ^ mask) for i in range(4)]) for mask in (2, 1, 3)
    ]
    norm_sums = line(jnp.add, norm_sums, got)
    got = send_z([norm_sums] * 3)
    mlp_sum = line(functools.partial(order, at_core), mlp_sum, mlp_got)
    up_sum, down_sum = line(
        lambda item: tuple(item.transpose(2, 1, 0, 3, 4).reshape(2, -1, width).astype(F32)), mlp_sum
    )
    up_sum = line(jnp.transpose, up_sum)
    attn_sum = line(in_order, attn_sum, *attn_got)
    norm_sums = line(lambda *terms: sum(terms[1:], terms[0]), norm_sums, *got)
    norm_sums = lax.dynamic_slice_in_dim(norm_sums, at_mp * (width // 8), width // 8, 1)
    attn_sum = attn_sum.transpose(1, 2, 0, 3, 4).reshape(4, local, width).astype(F32)
    return (
        output,
        in_grad,
        norm_sums[0],
        norm_sums[1],
        attn_sum[0].T,
        attn_sum[1].T,
        attn_sum[2].T,
        attn_sum[3],
        norm_sums[2],
        norm_sums[3],
        up_sum,
        down_sum,
    )


def on_any(
    mp_size,
    inputs,
    segments,
    ln1_gain,
    ln1_bias,
    w_query,
    w_key,
    w_value,
    w_output,
    ln2_gain,
    ln2_bias,
    w_up,
    w_down,
    cotangent,
):
    rows, width = inputs.shape
    seq_length = segments.shape[1]
    shared_by = seq_length // rows
    at_mp = lax.axis_index("mp")
    groups = [[start + i for i in range(shared_by)] for start in range(0, mp_size, shared_by)]

    def exchange(values, split, join):
        if shared_by == 1:
            return values
        return lax.all_to_all(values, "mp", split, join, axis_index_groups=groups, tiled=True)

    def gather(parts):
        return lax.all_gather(parts, "mp", axis=1, tiled=True)

    def reduce(parts):
        return lax.psum(lax.psum_scatter(parts, "mp", scatter_dimension=1, tiled=True), "dp")

    attn_w = gather(jnp.stack([w_query.T, w_value.T, w_key.T, w_output]))
    up, down = gather(jnp.stack([w_up.T, w_down]))
    project, w_out = attn_w[:3].reshape(3 * width, width), attn_w[3]

    segs = lax.dynamic_index_in_dim(segments, at_mp // shared_by, 0, keepdims=False)
    place = windows(segs) + (jnp.zeros((1,), jnp.int32), segs)
    resid_in = inputs.astype(F32)
    norm_one = layer_norm(resid_in, ln1_gain, ln1_bias).astype(BF16)
    projected = dot(project, norm_one, NT).astype(BF16).reshape(3, width, rows)
    projected = exchange(projected, 1, 2)
    query_value, keys = projected[None, :2], projected[2:]
    heads_out, lse = attend_forward(query_value, keys, place)
    attended = exchange(heads_out[0], 1, 0)
    residual = resid_in + dot(attended, w_out, TN)
    norm_two = layer_norm(residual, ln2_gain, ln2_bias).astype(BF16)
    mlp_branch, norm_two_grad, *mlp_grads = feed_forward(norm_two, cotangent, up, down)
    output = (residual + mlp_branch).astype(BF16)
    up_sum, down_sum = reduce(jnp.stack(mlp_grads)).astype(F32)

    resid_part, gain_two_grad, bias_two_grad = norm_back(residual, ln2_gain, ln2_bias, norm_two_grad)
    res_grad = cotangent.astype(F32) + resid_part
    branch_grad = res_grad.astype(BF16)
    out_grad = dot(attended, branch_grad, NN).astype(BF16)
    att_grad = exchange(dot(w_out, branch_grad, NT).astype(BF16), 0, 1)
    query_value_grad, key_grad = attend_backward(
        query_value, keys, heads_out, att_grad[None], lse, place
    )
    proj_grad = exchange(jnp.concatenate([query_value_grad[0], key_grad]), 2, 1)
    proj_grad = proj_grad.reshape(3 * width, rows)
    project_grad = dot(proj_grad, norm_one, NN).astype(BF16).reshape(3, width, width)
    attn_sum = reduce(jnp.concatenate([project_grad, out_grad[None]])).astype(F32)
    input_part, gain_one_grad, bias_one_grad = norm_back(
        resid_in, ln1_gain, ln1_bias, dot(proj_grad, project, TN)
    )
    in_grad = (res_grad + input_part).astype(BF16)
    norm_parts = jnp.stack([gain_one_grad, bias_one_grad, gain_two_grad, bias_two_grad])
    norm_sums = lax.dynamic_slice_in_dim(
        lax.psum(norm_parts, ("dp", "mp")), at_mp * (width // mp_size), width // mp_size, 1
    )
    return (
        output,
        in_grad,
        norm_sums[0],
        norm_sums[1],
        attn_sum[0].T,
        attn_sum[2].T,
        attn_sum[1].T,
        attn_sum[3],
        norm_sums[2],
        norm_sums[3],
        up_sum.T,
        down_sum,
    )


def shards(dp_size, mp_size, inputs, segments, *rest):
    if dp_size == 4 and mp_size == 8 and inputs.shape[0] == segments.shape[1]:
        return on_cube(inputs, segments, *rest)
    return on_any(mp_size, inputs, segments, *rest)


def solution(mesh):
    return jax.shard_map(
        functools.partial(shards, mesh.shape["dp"], mesh.shape["mp"]),
        mesh=mesh,
        in_specs=(
            P(("dp", "mp"), None),
            P("dp", None),
            P(),
            P(),
            P(None, "mp"),
            P(None, "mp"),
            P(None, "mp"),
            P("mp", None),
            P(),
            P(),
            P(None, "mp"),
            P("mp", None),
            P(("dp", "mp"), None),
        ),
        out_specs=(
            P(("dp", "mp"), None),
            P(("dp", "mp"), None),
            P("mp"),
            P("mp"),
            P(None, "mp"),
            P(None, "mp"),
            P(None, "mp"),
            P("mp", None),
            P("mp"),
            P("mp"),
            P(None, "mp"),
            P("mp", None),
        ),
        check_vma=False,
    )
```

```python
import functools
import math

import jax
import jax.numpy as jnp
from jax import lax
from jax.experimental import pallas as pl
from jax.experimental.pallas import tpu as pltpu
from jax.sharding import PartitionSpec as P

HEAD_DIM = 48
PAIR = 2 * HEAD_DIM
IMAGES = 4
TILE = 128
norm_eps = 1e-06
negative_fill = -1e30
SCALE = HEAD_DIM ** (-0.5)
SCALE_LOG2 = SCALE * math.log2(math.e)
BF16 = jnp.bfloat16
F32 = jnp.float32


def layer_norm(values, gain, bias):
    center = jnp.mean(values, axis=-1, keepdims=True)
    shifted = values - center
    spread = jnp.mean(shifted * shifted, axis=-1, keepdims=True)
    return shifted * lax.rsqrt(spread + norm_eps) * gain + bias


def layer_norm_back(values, gain, grad):
    shifted = values - jnp.mean(values, axis=-1, keepdims=True)
    scale = lax.rsqrt(jnp.mean(shifted * shifted, axis=-1, keepdims=True) + norm_eps)
    unit = shifted * scale
    scaled = grad * gain
    back = scale * (
        scaled
        - jnp.mean(scaled, axis=-1, keepdims=True)
        - unit * jnp.mean(scaled * unit, axis=-1, keepdims=True)
    )
    return back, jnp.sum(grad * unit, axis=0, keepdims=True), jnp.sum(grad, axis=0, keepdims=True)


def dot(left, right, dims):
    return lax.dot_general(left, right, (dims, ((), ())), preferred_element_type=F32)


NN = ((1,), (0,))
NT = ((1,), (1,))
TN = ((0,), (0,))


def window_kinds(tiles):
    return tuple(n for n in (2, 3, 4, 5, 6) if n < tiles) + (tiles,)


def image_rows(segs, length):
    row = lax.broadcasted_iota(jnp.int32, (TILE - PAIR, length), 0)
    here = row == segs
    one_hot = jnp.where(here, 1.0, 0.0).astype(BF16)
    fill = jnp.where(jnp.logical_or(here, row >= IMAGES), 0.0, negative_fill).astype(BF16)
    return one_hot, fill


def side_by_side(pair, extra):
    blank = jnp.zeros((HEAD_DIM, TILE), BF16)
    left = jnp.concatenate([pair[:HEAD_DIM], blank, extra], axis=0)
    right = jnp.concatenate([blank, pair[HEAD_DIM:], extra], axis=0)
    return jnp.concatenate([left, right], axis=1)


def pair_places(ref):
    cores, count = ref.shape[0], ref.shape[1]
    return [(core, top) for core in range(cores) for top in range(0, count, PAIR)]


def attend_forward_kernel(
    first_ref, kind_ref, flip_ref, segs_ref, qv_ref, k_ref, out_ref, lse_ref, hot_ref, keys_ref, vals_ref
):
    length = k_ref.shape[-1]
    at_q = flip_ref[0]
    places = pair_places(k_ref)
    one_hot, fill = image_rows(segs_ref[...], length)
    hot_ref[...] = one_hot
    for j, (core, top) in enumerate(places):
        rows = slice(top, top + PAIR)
        keys_ref[j] = jnp.concatenate([k_ref[core, rows, :], fill], axis=0).T
        vals_ref[j] = jnp.concatenate(
            [qv_ref[core, 1 - at_q, rows, :], jnp.ones((16, length), BF16)], axis=0
        )

    def block(b, carry):
        at = pl.ds(pl.multiple_of(b * TILE, TILE), TILE)
        first = pl.multiple_of(first_ref[b] * TILE, TILE)

        def variant(tiles):
            span = pl.ds(first, tiles * TILE)
            scores = [
                dot(
                    keys_ref[j, span, :],
                    side_by_side(qv_ref[core, at_q, top : top + PAIR, at], hot_ref[:, at]),
                    NN,
                )
                for j, (core, top) in enumerate(places)
            ]
            for j, (core, top) in enumerate(places):
                most = jnp.max(scores[j], axis=0, keepdims=True)
                expo = jnp.exp2((scores[j] - most) * SCALE_LOG2).astype(BF16)
                mixed = dot(vals_ref[j, :, span], expo, NN)
                total = mixed[PAIR : PAIR + 1, :]
                inverse = 1.0 / total
                out_ref[core, top : top + HEAD_DIM, at] = (
                    mixed[:HEAD_DIM, :TILE] * inverse[:, :TILE]
                ).astype(BF16)
                out_ref[core, top + HEAD_DIM : top + PAIR, at] = (
                    mixed[HEAD_DIM:PAIR, TILE:] * inverse[:, TILE:]
                ).astype(BF16)
                lse_ref[j, pl.ds(b, 1), :] = most * SCALE_LOG2 + jnp.log2(total)

        for tiles in window_kinds(length // TILE):
            pl.when(kind_ref[b] == tiles)(functools.partial(variant, tiles))
        return carry

    lax.fori_loop(0, length // TILE, block, 0)


def attend_backward_kernel(
    first_ref,
    kind_ref,
    flip_ref,
    segs_ref,
    qv_ref,
    k_ref,
    att_ref,
    grad_ref,
    lse_ref,
    dqv_ref,
    dk_ref,
    hot_ref,
    keys_ref,
    vals_ref,
    queries_ref,
    grads_ref,
    key_sum_ref,
    val_sum_ref,
):
    length = k_ref.shape[-1]
    at_q = flip_ref[0]
    places = pair_places(k_ref)
    one_hot, fill = image_rows(segs_ref[...], length)
    hot_ref[...] = one_hot
    pad = jnp.zeros((TILE - PAIR, length), BF16)
    for j, (core, top) in enumerate(places):
        rows = slice(top, top + PAIR)
        keys_ref[j] = jnp.concatenate([k_ref[core, rows, :], fill], axis=0).T
        vals_ref[j] = jnp.concatenate([qv_ref[core, 1 - at_q, rows, :], pad], axis=0).T
        queries_ref[j] = jnp.concatenate([qv_ref[core, at_q, rows, :], pad], axis=0).T
        grads_ref[j] = jnp.concatenate([grad_ref[core, rows, :], pad], axis=0).T
    key_sum_ref[...] = jnp.zeros(key_sum_ref.shape, F32)
    val_sum_ref[...] = jnp.zeros(val_sum_ref.shape, F32)
    no_rows = jnp.zeros((TILE - PAIR, TILE), BF16)
    lane = lax.broadcasted_iota(jnp.int32, (TILE, TILE), 1)
    in_first = lane < HEAD_DIM

    def stacked(both):
        blank = jnp.zeros_like(both)
        return jnp.concatenate(
            [jnp.where(in_first, both, blank), jnp.where(in_first, blank, both)], axis=0
        )

    def block(b, carry):
        at = pl.ds(pl.multiple_of(b * TILE, TILE), TILE)
        first = pl.multiple_of(first_ref[b] * TILE, TILE)

        def variant(tiles):
            span = pl.ds(first, tiles * TILE)
            scores = [
                dot(
                    keys_ref[j, span, :],
                    side_by_side(qv_ref[core, at_q, top : top + PAIR, at], hot_ref[:, at]),
                    NN,
                )
                for j, (core, top) in enumerate(places)
            ]
            prob_grads = [
                dot(
                    vals_ref[j, span, :],
                    side_by_side(grad_ref[core, top : top + PAIR, at], no_rows),
                    NN,
                )
                for j, (core, top) in enumerate(places)
            ]
            for j, (core, top) in enumerate(places):
                rows = slice(top, top + PAIR)
                agree = grad_ref[core, rows, at].astype(F32) * att_ref[core, rows, at].astype(F32)
                delta = jnp.concatenate(
                    [
                        jnp.sum(agree[:HEAD_DIM], axis=0, keepdims=True),
                        jnp.sum(agree[HEAD_DIM:], axis=0, keepdims=True),
                    ],
                    axis=1,
                )
                probs = jnp.exp2(scores[j] * SCALE_LOG2 - lse_ref[j, pl.ds(b, 1), :])
                score_grad = (probs * (prob_grads[j] - delta)).astype(BF16)
                val_sum_ref[j, span, :] += dot(
                    probs.astype(BF16), stacked(grads_ref[j, at, :]), NN
                )
                key_sum_ref[j, span, :] += dot(score_grad, stacked(queries_ref[j, at, :]), NN)
                query_grad = dot(k_ref[core, rows, span], score_grad, NN) * SCALE
                dqv_ref[core, at_q, top : top + HEAD_DIM, at] = query_grad[
                    :HEAD_DIM, :TILE
                ].astype(BF16)
                dqv_ref[core, at_q, top + HEAD_DIM : top + PAIR, at] = query_grad[
                    HEAD_DIM:, TILE:
                ].astype(BF16)

        for tiles in window_kinds(length // TILE):
            pl.when(kind_ref[b] == tiles)(functools.partial(variant, tiles))
        return carry

    lax.fori_loop(0, length // TILE, block, 0)
    for j, (core, top) in enumerate(places):
        rows = slice(top, top + PAIR)
        dk_ref[core, rows, :] = (key_sum_ref[j] * SCALE).T[:PAIR].astype(BF16)
        dqv_ref[core, 1 - at_q, rows, :] = val_sum_ref[j].T[:PAIR].astype(BF16)


def windows(segs):
    length = segs.shape[0]
    tiles = length // TILE
    by_tile = segs.reshape(tiles, TILE)
    begin = jnp.sum(segs[None, :] < by_tile[:, :1], axis=1)
    end = jnp.sum(segs[None, :] <= by_tile[:, -1:], axis=1)
    first = begin // TILE
    need = (end + TILE - 1) // TILE - first
    kinds = jnp.asarray(window_kinds(tiles), jnp.int32)
    kind = jnp.min(jnp.where(kinds[None, :] >= need[:, None], kinds[None, :], tiles), axis=1)
    return jnp.minimum(first, tiles - kind).astype(jnp.int32), kind.astype(jnp.int32)


def attention_specs(keys):
    cores, count, length = keys.shape
    pairs = cores * count // PAIR
    step = pairs if pairs <= 4 else 4
    part = count * step // pairs
    rows = pl.BlockSpec((cores, part, length), lambda i, *_: (0, i, 0))
    two = pl.BlockSpec((cores, 2, part, length), lambda i, *_: (0, 0, i, 0))
    segs = pl.BlockSpec((1, length), lambda i, *_: (0, 0))
    lse = pl.BlockSpec((step, length // TILE, 2 * TILE), lambda i, *_: (i, 0, 0))
    return pairs, step, rows, two, segs, lse


def attend_forward(query_value, keys, place):
    first, kind, flip, segs = place
    length = segs.shape[0]
    pairs, step, rows, two, segs_spec, lse = attention_specs(keys)
    return pl.pallas_call(
        attend_forward_kernel,
        grid_spec=pltpu.PrefetchScalarGridSpec(
            num_scalar_prefetch=3,
            grid=(pairs // step,),
            in_specs=[segs_spec, two, rows],
            out_specs=[rows, lse],
            scratch_shapes=[
                pltpu.VMEM((TILE - PAIR, length), BF16),
                pltpu.VMEM((step, length, TILE), BF16),
                pltpu.VMEM((step, PAIR + 16, length), BF16),
            ],
        ),
        out_shape=[
            jax.ShapeDtypeStruct(keys.shape, BF16),
            jax.ShapeDtypeStruct((pairs, length // TILE, 2 * TILE), F32),
        ],
        compiler_params=pltpu.CompilerParams(vmem_limit_bytes=40 << 20),
        name="attend_forward",
    )(first, kind, flip, segs[None, :], query_value, keys)


def attend_backward(query_value, keys, attended, grad, lse, place):
    first, kind, flip, segs = place
    length = segs.shape[0]
    pairs, step, rows, two, segs_spec, lse_spec = attention_specs(keys)
    wide = pltpu.VMEM((step, length, TILE), BF16)
    total = pltpu.VMEM((step, length, TILE), F32)
    return pl.pallas_call(
        attend_backward_kernel,
        grid_spec=pltpu.PrefetchScalarGridSpec(
            num_scalar_prefetch=3,
            grid=(pairs // step,),
            in_specs=[segs_spec, two, rows, rows, rows, lse_spec],
            out_specs=[two, rows],
            scratch_shapes=[
                pltpu.VMEM((TILE - PAIR, length), BF16),
                wide,
                wide,
                wide,
                wide,
                total,
                total,
            ],
        ),
        out_shape=[
            jax.ShapeDtypeStruct(query_value.shape, BF16),
            jax.ShapeDtypeStruct(keys.shape, BF16),
        ],
        compiler_params=pltpu.CompilerParams(vmem_limit_bytes=40 << 20),
        name="attend_backward",
    )(first, kind, flip, segs[None, :], query_value, keys, attended, grad, lse)


def gelu_parts(values):
    below = 0.5 * (1.0 + lax.erf(values * (0.5 ** 0.5)))
    density = jnp.exp(values * values * -0.5) * ((2.0 * math.pi) ** -0.5)
    return values * below, below + values * density


def feed_forward_kernel(
    norm_ref, cot_ref, up_ref, down_ref, mlp_ref, back_ref, up_grad_ref, down_grad_ref, act_ref, pre_ref
):
    rows = norm_ref.shape[0]
    chunk = min(rows, 256)

    @pl.when(pl.program_id(0) == 0)
    def _():
        mlp_ref[...] = jnp.zeros(mlp_ref.shape, F32)
        back_ref[...] = jnp.zeros(back_ref.shape, F32)

    for start in range(0, rows, chunk):
        at = slice(start, start + chunk)
        pre_act = dot(norm_ref[at, :], up_ref[...], NT)
        act_grad = dot(cot_ref[at, :], down_ref[...], NT)
        activation, slope = gelu_parts(pre_act)
        activation = activation.astype(BF16)
        pre_grad = (act_grad * slope).astype(BF16)
        act_ref[at, :] = activation
        pre_ref[at, :] = pre_grad
        mlp_ref[at, :] += dot(activation, down_ref[...], NN)
        back_ref[at, :] += dot(pre_grad, up_ref[...], NN)
    up_grad_ref[...] = dot(pre_ref[...], norm_ref[...], TN).astype(BF16)
    down_grad_ref[...] = dot(act_ref[...], cot_ref[...], TN).astype(BF16)


def feed_forward(norm, cot, up, down):
    rows, width = norm.shape
    hidden = up.shape[0]
    part = 512 if hidden % 512 == 0 else hidden
    whole = pl.BlockSpec((rows, width), lambda i: (0, 0))
    block = pl.BlockSpec((part, width), lambda i: (i, 0))
    sums = jax.ShapeDtypeStruct((rows, width), F32)
    grads = jax.ShapeDtypeStruct((hidden, width), BF16)
    return pl.pallas_call(
        feed_forward_kernel,
        grid=(hidden // part,),
        in_specs=[whole, whole, block, block],
        out_specs=[whole, whole, block, block],
        out_shape=[sums, sums, grads, grads],
        scratch_shapes=[pltpu.VMEM((rows, part), BF16)] * 2,
        compiler_params=pltpu.CompilerParams(vmem_limit_bytes=56 << 20),
        name="feed_forward",
    )(norm, cot, up, down)


def middle_kernel(parts, residual_ref, cot_ref, gain_ref, *refs):
    mlp_refs, back_refs = refs[:parts], refs[parts : 2 * parts]
    output_ref, res_grad_ref, branch_ref, norm_grad_ref = refs[2 * parts :]

    @pl.when(pl.program_id(0) == 0)
    def _():
        norm_grad_ref[...] = jnp.zeros(norm_grad_ref.shape, F32)

    residual = residual_ref[...]
    output_ref[...] = sum([ref[...] for ref in mlp_refs], residual).astype(BF16)
    grad = functools.reduce(jnp.add, [ref[...] for ref in back_refs])
    back, gain_grad, bias_grad = layer_norm_back(residual, gain_ref[...], grad)
    res_grad = cot_ref[...].astype(F32) + back
    res_grad_ref[...] = res_grad
    branch_ref[...] = res_grad.astype(BF16)
    norm_grad_ref[0:1, :] += gain_grad
    norm_grad_ref[1:2, :] += bias_grad


def middle(residual, cot, gain, mlps, backs):
    rows, width = residual.shape
    parts = len(mlps)
    step = 128
    block = pl.BlockSpec((step, width), lambda i: (i, 0))
    sums = jax.ShapeDtypeStruct((rows, width), F32)
    low = jax.ShapeDtypeStruct((rows, width), BF16)
    return pl.pallas_call(
        functools.partial(middle_kernel, parts),
        grid=(rows // step,),
        in_specs=[block, block, pl.BlockSpec((1, width), lambda i: (0, 0))] + [block] * (2 * parts),
        out_specs=[block, block, block, pl.BlockSpec((8, width), lambda i: (0, 0))],
        out_shape=[low, sums, low, jax.ShapeDtypeStruct((8, width), F32)],
        name="middle",
    )(residual, cot, gain[None, :], *mlps, *backs)


def add(*terms):
    return functools.reduce(jnp.add, [item.astype(F32) for item in terms]).astype(BF16)


def swap(values, axis):
    name, size, mask = {
        "core": ("dp", 4, 1),
        "y": ("dp", 4, 2),
        "x": ("mp", 8, 1),
        "z1": ("mp", 8, 2),
        "z2": ("mp", 8, 4),
    }[axis]
    return lax.ppermute(values, name, [(i, i ^ mask) for i in range(size)])


def order(at, mine, other):
    return jnp.where(at == 0, jnp.stack([mine, other]), jnp.stack([other, mine]))


class Line:
    def __init__(self):
        self.last = ()

    def __call__(self, step, *args):
        args, _ = lax.optimization_barrier((args, self.last))
        result = step(*args)
        self.last = tuple(jax.tree.leaves(result))
        return result


def on_cube(
    inputs,
    segments,
    ln1_gain,
    ln1_bias,
    w_query,
    w_key,
    w_value,
    w_output,
    ln2_gain,
    ln2_bias,
    w_up,
    w_down,
    cotangent,
):
    rows, width = inputs.shape
    local = w_query.shape[1]
    at_dp, at_mp = lax.axis_index("dp"), lax.axis_index("mp")
    at_y, at_core = at_dp // 2, at_dp % 2
    line = Line()

    def pick(values, at):
        return lax.dynamic_index_in_dim(values, at, 0, keepdims=False)

    def cut_attention(query, key, value, out):
        kinds = jnp.stack([query.T, key.T, value.T, out]).reshape(2, 2, 2, HEAD_DIM, width)
        return pick(kinds.transpose(0, 2, 1, 3, 4).reshape(4, 2, HEAD_DIM, width), at_dp)

    def cut_mlp(up, down):
        pieces = jnp.stack([up.T, down]).reshape(2, 4, -1, width)
        return lax.dynamic_index_in_dim(pieces, at_dp, 1, keepdims=False)

    def join(*parts):
        return jnp.concatenate(parts, 0)

    attn_piece = line(cut_attention, w_query, w_key, w_value, w_output)[None]
    attn_got = swap(attn_piece, "z2")
    mlp_piece = line(cut_mlp, w_up, w_down)[None]
    mlp_got = swap(mlp_piece, "z2")

    def begin(rows_in):
        return layer_norm(rows_in.astype(F32), ln1_gain, ln1_bias).astype(BF16)

    norm_one = line(begin, inputs)
    segs = pick(segments, at_mp)
    place = windows(segs) + (at_y.reshape(1), segs)
    place = line(lambda item: item, place)

    attn_pair = line(join, attn_piece, attn_got)
    attn_got = swap(attn_pair, "z1")
    mlp_pair = line(join, mlp_piece, mlp_got)
    mlp_got = swap(mlp_pair, "z1")
    near_z = line(join, attn_pair, attn_got)
    near_got = swap(near_z, "y")
    far_z = swap(near_z, "x")
    near_y = line(lambda *parts: jnp.stack(parts[:2]), near_z, near_got, far_z, mlp_got)
    near_got = swap(near_y, "core")
    far_got = swap(far_z, "y")

    def both_cores(mine, other):
        query_value, key_out = [jnp.stack([mine[:, :, i], other[:, :, i]]) for i in (0, 1)]
        key, out = [
            lax.dynamic_index_in_dim(key_out, at, 1, keepdims=False).reshape(-1, width)
            for at in (at_y, 1 - at_y)
        ]
        return query_value.reshape(-1, width), key, out

    def project(weights, norm):
        query_value = dot(weights[0], norm, NT).astype(BF16).reshape(2, 2, -1, rows)
        return query_value, dot(weights[1], norm, NT).astype(BF16).reshape(2, -1, rows)

    def attend(query_value, keys):
        return attend_forward(query_value, keys, place)

    def branch(base, attended, weights):
        return base + dot(attended.reshape(-1, rows), weights[2], TN)

    def mlp_along_z(pair, got):
        return [jnp.concatenate([pair[:, i], got[:, i]], 0).reshape(-1, width) for i in (0, 1)]

    def mlp_second(up, up_got, down, down_got):
        return jnp.concatenate([up, up_got], 0), jnp.stack([down, down_got])

    near_w = line(both_cores, near_y, near_got)
    near = line(project, near_w, norm_one)
    up, down = line(mlp_along_z, mlp_pair, mlp_got)
    up_got, down_got = swap(up, "x"), swap(down, "y")
    near += tuple(line(attend, *near))

    far_y = line(lambda *parts: jnp.stack(parts), far_z, far_got)
    far_got = swap(far_y, "core")
    up, down = line(mlp_second, up, up_got, down, down_got)
    up_got, down_got = swap(up, "y"), swap(down, "x")
    residual = line(branch, inputs.astype(F32), near[2], near_w)
    far_w = line(both_cores, far_y, far_got)
    far = line(project, far_w, norm_one)
    far += tuple(line(attend, *far))

    def second_norm(residual, attended, weights):
        residual = branch(residual, attended, weights)
        return residual, layer_norm(residual, ln2_gain, ln2_bias).astype(BF16)

    residual, norm_two = line(second_norm, residual, far[2], far_w)

    def mlp_last(up, up_got, down, down_got):
        return jnp.concatenate([up, up_got], 0), jnp.concatenate([down, down_got], 1).reshape(-1, width)

    up, down = line(mlp_last, up, up_got, down, down_got)
    other_up, other_down = swap(up, "core"), swap(down, "core")
    mlp_a, back_a, up_mine, down_mine = line(feed_forward, norm_two, cotangent, up, down)
    mlp_b, back_b, *grads = line(feed_forward, norm_two, cotangent, other_up, other_down)
    up_got, down_got = [swap(item, "core") for item in grads]
    output, res_grad, branch_grad, norm_two_grads = line(
        middle, residual, cotangent, ln2_gain, [mlp_a, mlp_b], [back_a, back_b]
    )

    def before_attention(attended, weights, grad):
        att_grad = dot(weights[2], grad, NT).astype(BF16).reshape(attended.shape)
        return att_grad, dot(attended.reshape(-1, rows), grad, NN).astype(BF16)


    quarter = up.shape[0] // 4

    def up_sum_of(terms, low, high):
        return add(*[item[low:high] for item in terms])

    def down_sum_of(terms, y, x, low=0, high=quarter):
        whole, by_y = terms[:2], terms[2:]
        whole = [item.reshape(2, 2, quarter, width)[y, x, low:high] for item in whole]
        return add(*whole, *[item.reshape(-1, quarter, width)[y, low:high] for item in by_y])

    def mlp_sum_first(up_terms, down_terms):
        return (
            up_sum_of(up_terms, 2 * quarter, 4 * quarter),
            jnp.stack([down_sum_of(down_terms, y, 1) for y in (0, 1)]),
        )

    up_terms, down_terms = (up_mine, up_got), (down_mine, down_got)
    sends = line(mlp_sum_first, up_terms, down_terms)
    up_terms += (swap(sends[0], "y"),)
    down_terms += (swap(sends[1], "x"),)

    def attend_back(saved, att_grad):
        return attend_backward(*saved[:3], att_grad, saved[3], place)

    def weight_grads(query_value_grad, key_grad, out_grad, norm):
        query_value = dot(query_value_grad.reshape(-1, rows), norm, NN).astype(BF16)
        keys = dot(key_grad.reshape(-1, rows), norm, NN).astype(BF16)
        sums = (
            query_value.reshape(2, 2, -1, width),
            keys.reshape(2, -1, width),
            out_grad.reshape(2, -1, width),
        )
        return sums, [item[1] for item in sums]

    def project_back(grads, weights):
        return dot(grads[0].reshape(-1, rows), weights[0], TN) + dot(
            grads[1].reshape(-1, rows), weights[1], TN
        )

    def attn_terms_of(mine, got, at):
        terms = [(mine[0][0, at], mine[1][0], mine[2][0]), (got[0][at], got[1], got[2])]
        first = at_y == at
        return [
            [item[0] for item in terms],
            [jnp.where(first, item[1], item[2]) for item in terms],
        ]

    def sum_other_y(mine, got):
        return jnp.stack([add(*terms) for terms in attn_terms_of(mine, got, 1)])

    def sum_this_y(mine, got, from_y):
        terms = attn_terms_of(mine, got, 0)
        return jnp.stack([add(*terms[i], from_y[i]) for i in (0, 1)])

    far_att, far_out = line(before_attention, far[2], far_w, branch_grad)
    far_grads = line(attend_back, far, far_att)
    far_mine, sends = line(weight_grads, *far_grads, far_out, norm_one)
    far_got = [swap(item, "core") for item in sends]
    near_att, near_out = line(before_attention, near[2], near_w, branch_grad)
    norm_one_grad = line(project_back, far_grads, far_w)
    far_y = swap(line(sum_other_y, far_mine, far_got), "y")

    def mlp_sum_second(up_terms, down_terms):
        return up_sum_of(up_terms, quarter, 2 * quarter), down_sum_of(down_terms, 1, 0)

    sends = line(mlp_sum_second, up_terms, down_terms)
    up_terms += (swap(sends[0], "x"),)
    down_y = swap(sends[1], "y")

    near_grads = line(attend_back, near, near_att)

    part = quarter // 4

    def mlp_sum_of_z(up_terms, down_terms, down_y, low, high):
        low, high = low * part, high * part
        return jnp.stack(
            [
                up_sum_of(up_terms, low, high),
                down_sum_of(down_terms + (jnp.stack([down_y, down_y]),), 0, 0, low, high),
            ]
        )

    mlp_terms = (up_terms, down_terms, down_y)
    mlp_z1 = swap(line(lambda *terms: mlp_sum_of_z(*terms, 2, 4), *mlp_terms), "z1")
    near_mine, sends = line(weight_grads, *near_grads, near_out, norm_one)
    near_got = [swap(item, "core") for item in sends]
    far_x = swap(line(sum_this_y, far_mine, far_got, far_y), "x")
    near_y = swap(line(sum_other_y, near_mine, near_got), "y")

    def finish(norm_one_grad, grads, weights):
        norm_one_grad = norm_one_grad + project_back(grads, weights)
        input_part, gain_grad, bias_grad = layer_norm_back(
            inputs.astype(F32), ln1_gain, norm_one_grad
        )
        parts = jnp.concatenate([gain_grad, bias_grad, norm_two_grads[:2]])
        return parts, (res_grad + input_part).astype(BF16)

    norm_sums, in_grad = line(finish, norm_one_grad, near_grads, near_w)

    mlp_send = line(
        lambda got, *terms: add(mlp_sum_of_z(*terms, 1, 2), got[:, part:]), mlp_z1, *mlp_terms
    )
    mlp_z2 = swap(mlp_send, "z2")

    def attn_sum_z(mine, got, from_y, from_x):
        from_x = from_x.reshape(2, -1, width)
        whole = sum_this_y(mine, got, from_y).astype(F32) + from_x
        return whole[:, : 2 * HEAD_DIM].astype(BF16), whole[:, 2 * HEAD_DIM :].astype(BF16)

    attn_mine, send = line(attn_sum_z, near_mine, near_got, near_y, far_x)
    attn_z1 = swap(send, "z1")
    got = swap(norm_sums, "core")

    def in_order(piece, y, core, both):
        return order(at_core, order(at_y, piece, y), order(at_y, core, both))

    mlp_sum = line(
        lambda got, other, *terms: add(mlp_sum_of_z(*terms, 0, 1), got[:, :part], other),
        mlp_z1,
        mlp_z2,
        *mlp_terms,
    )
    mlp_got = swap(mlp_sum, "y")
    norm_sums = line(jnp.add, norm_sums, got)
    got = swap(norm_sums, "y")
    attn_send = line(lambda mine, got: add(mine[:, HEAD_DIM:], got[:, HEAD_DIM:]), attn_mine, attn_z1)
    attn_z2 = swap(attn_send, "z2")
    mlp_sum = line(lambda mine, got, _: order(at_y, mine, got), mlp_sum, mlp_got, attn_z2)
    mlp_got = swap(mlp_sum, "core")
    norm_sums = line(jnp.add, norm_sums, got)
    got = swap(norm_sums, "x")
    attn_sum = line(
        lambda mine, got, other: add(mine[:, :HEAD_DIM], got[:, :HEAD_DIM], other),
        attn_mine,
        attn_z1,
        attn_z2,
    )
    attn_got = [
        lax.ppermute(attn_sum, "dp", [(i, i ^ mask) for i in range(4)]) for mask in (2, 1, 3)
    ]
    norm_sums = line(jnp.add, norm_sums, got)
    got = swap(norm_sums, "z1")
    mlp_sum = line(functools.partial(order, at_core), mlp_sum, mlp_got)
    up_sum, down_sum = line(
        lambda item: tuple(item.transpose(2, 1, 0, 3, 4).reshape(2, -1, width).astype(F32)), mlp_sum
    )
    norm_sums = line(jnp.add, norm_sums, got)
    got = swap(norm_sums, "z2")
    up_sum = line(jnp.transpose, up_sum)
    attn_sum = line(in_order, attn_sum, *attn_got)
    norm_sums = line(jnp.add, norm_sums, got)
    norm_sums = lax.dynamic_slice_in_dim(norm_sums, at_mp * (width // 8), width // 8, 1)
    attn_sum = attn_sum.transpose(1, 2, 0, 3, 4).reshape(4, local, width).astype(F32)
    return (
        output,
        in_grad,
        norm_sums[0],
        norm_sums[1],
        attn_sum[0].T,
        attn_sum[1].T,
        attn_sum[2].T,
        attn_sum[3],
        norm_sums[2],
        norm_sums[3],
        up_sum,
        down_sum,
    )


def on_any(
    mp_size,
    inputs,
    segments,
    ln1_gain,
    ln1_bias,
    w_query,
    w_key,
    w_value,
    w_output,
    ln2_gain,
    ln2_bias,
    w_up,
    w_down,
    cotangent,
):
    rows, width = inputs.shape
    seq_length = segments.shape[1]
    shared_by = seq_length // rows
    at_mp = lax.axis_index("mp")
    groups = [[start + i for i in range(shared_by)] for start in range(0, mp_size, shared_by)]

    def exchange(values, split, join):
        if shared_by == 1:
            return values
        return lax.all_to_all(values, "mp", split, join, axis_index_groups=groups, tiled=True)

    def gather(parts):
        return lax.all_gather(parts, "mp", axis=1, tiled=True)

    def reduce(parts):
        return lax.psum(lax.psum_scatter(parts, "mp", scatter_dimension=1, tiled=True), "dp")

    attn_w = gather(jnp.stack([w_query.T, w_value.T, w_key.T, w_output]))
    up, down = gather(jnp.stack([w_up.T, w_down]))
    project, w_out = attn_w[:3].reshape(3 * width, width), attn_w[3]

    segs = lax.dynamic_index_in_dim(segments, at_mp // shared_by, 0, keepdims=False)
    place = windows(segs) + (jnp.zeros((1,), jnp.int32), segs)
    resid_in = inputs.astype(F32)
    norm_one = layer_norm(resid_in, ln1_gain, ln1_bias).astype(BF16)
    projected = dot(project, norm_one, NT).astype(BF16).reshape(3, width, rows)
    projected = exchange(projected, 1, 2)
    query_value, keys = projected[None, :2], projected[2:]
    heads_out, lse = attend_forward(query_value, keys, place)
    attended = exchange(heads_out[0], 1, 0)
    residual = resid_in + dot(attended, w_out, TN)
    norm_two = layer_norm(residual, ln2_gain, ln2_bias).astype(BF16)
    mlp_branch, norm_two_grad, *mlp_grads = feed_forward(norm_two, cotangent, up, down)
    up_sum, down_sum = reduce(jnp.stack(mlp_grads)).astype(F32)

    output, res_grad, branch_grad, norm_two_grads = middle(
        residual, cotangent, ln2_gain, [mlp_branch], [norm_two_grad]
    )
    out_grad = dot(attended, branch_grad, NN).astype(BF16)
    att_grad = exchange(dot(w_out, branch_grad, NT).astype(BF16), 0, 1)
    query_value_grad, key_grad = attend_backward(
        query_value, keys, heads_out, att_grad[None], lse, place
    )
    proj_grad = exchange(jnp.concatenate([query_value_grad[0], key_grad]), 2, 1)
    proj_grad = proj_grad.reshape(3 * width, rows)
    project_grad = dot(proj_grad, norm_one, NN).astype(BF16).reshape(3, width, width)
    attn_sum = reduce(jnp.concatenate([project_grad, out_grad[None]])).astype(F32)
    input_part, gain_one_grad, bias_one_grad = layer_norm_back(
        resid_in, ln1_gain, dot(proj_grad, project, TN)
    )
    in_grad = (res_grad + input_part).astype(BF16)
    norm_parts = jnp.concatenate([gain_one_grad, bias_one_grad, norm_two_grads[:2]])
    norm_sums = lax.dynamic_slice_in_dim(
        lax.psum(norm_parts, ("dp", "mp")), at_mp * (width // mp_size), width // mp_size, 1
    )
    return (
        output,
        in_grad,
        norm_sums[0],
        norm_sums[1],
        attn_sum[0].T,
        attn_sum[2].T,
        attn_sum[1].T,
        attn_sum[3],
        norm_sums[2],
        norm_sums[3],
        up_sum.T,
        down_sum,
    )


def shards(dp_size, mp_size, inputs, segments, *rest):
    if dp_size == 4 and mp_size == 8 and inputs.shape[0] == segments.shape[1]:
        return on_cube(inputs, segments, *rest)
    return on_any(mp_size, inputs, segments, *rest)


def solution(mesh):
    return jax.shard_map(
        functools.partial(shards, mesh.shape["dp"], mesh.shape["mp"]),
        mesh=mesh,
        in_specs=(
            P(("dp", "mp"), None),
            P("dp", None),
            P(),
            P(),
            P(None, "mp"),
            P(None, "mp"),
            P(None, "mp"),
            P("mp", None),
            P(),
            P(),
            P(None, "mp"),
            P("mp", None),
            P(("dp", "mp"), None),
        ),
        out_specs=(
            P(("dp", "mp"), None),
            P(("dp", "mp"), None),
            P("mp"),
            P("mp"),
            P(None, "mp"),
            P(None, "mp"),
            P(None, "mp"),
            P("mp", None),
            P("mp"),
            P("mp"),
            P(None, "mp"),
            P("mp", None),
        ),
        check_vma=False,
    )
```

```python
import functools
import math

import jax
import jax.numpy as jnp
from jax import lax
from jax.experimental import pallas as pl
from jax.experimental.pallas import tpu as pltpu
from jax.sharding import PartitionSpec as P

HEAD_DIM = 48
PAIR = 2 * HEAD_DIM
IMAGES = 4
TILE = 128
norm_eps = 1e-06
negative_fill = -1e30
SCALE = HEAD_DIM ** (-0.5)
SCALE_LOG2 = SCALE * math.log2(math.e)
BF16 = jnp.bfloat16
F32 = jnp.float32


def layer_norm(values, gain, bias):
    center = jnp.mean(values, axis=-1, keepdims=True)
    shifted = values - center
    spread = jnp.mean(shifted * shifted, axis=-1, keepdims=True)
    return shifted * lax.rsqrt(spread + norm_eps) * gain + bias


def layer_norm_back(values, gain, grad):
    shifted = values - jnp.mean(values, axis=-1, keepdims=True)
    scale = lax.rsqrt(jnp.mean(shifted * shifted, axis=-1, keepdims=True) + norm_eps)
    unit = shifted * scale
    scaled = grad * gain
    back = scale * (
        scaled
        - jnp.mean(scaled, axis=-1, keepdims=True)
        - unit * jnp.mean(scaled * unit, axis=-1, keepdims=True)
    )
    return back, jnp.sum(grad * unit, axis=0, keepdims=True), jnp.sum(grad, axis=0, keepdims=True)


def dot(left, right, dims):
    return lax.dot_general(left, right, (dims, ((), ())), preferred_element_type=F32)


NN = ((1,), (0,))
NT = ((1,), (1,))
TN = ((0,), (0,))


def window_kinds(tiles):
    return tuple(n for n in (2, 3, 4, 5, 6) if n < tiles) + (tiles,)


def image_rows(segs, length):
    row = lax.broadcasted_iota(jnp.int32, (TILE - PAIR, length), 0)
    here = row == segs
    one_hot = jnp.where(here, 1.0, 0.0).astype(BF16)
    fill = jnp.where(jnp.logical_or(here, row >= IMAGES), 0.0, negative_fill).astype(BF16)
    return one_hot, fill


def side_by_side(pair, extra):
    blank = jnp.zeros((HEAD_DIM, TILE), BF16)
    left = jnp.concatenate([pair[:HEAD_DIM], blank, extra], axis=0)
    right = jnp.concatenate([blank, pair[HEAD_DIM:], extra], axis=0)
    return jnp.concatenate([left, right], axis=1)


def pair_places(ref):
    cores, count = ref.shape[0], ref.shape[1]
    return [(core, top) for core in range(cores) for top in range(0, count, PAIR)]


def attend_forward_kernel(
    first_ref, kind_ref, flip_ref, segs_ref, qv_ref, k_ref, out_ref, lse_ref, hot_ref, keys_ref, vals_ref
):
    length = k_ref.shape[-1]
    at_q = flip_ref[0]
    places = pair_places(k_ref)
    one_hot, fill = image_rows(segs_ref[...], length)
    hot_ref[...] = one_hot
    for j, (core, top) in enumerate(places):
        rows = slice(top, top + PAIR)
        keys_ref[j] = jnp.concatenate([k_ref[core, rows, :], fill], axis=0).T
        vals_ref[j] = jnp.concatenate(
            [qv_ref[core, 1 - at_q, rows, :], jnp.ones((16, length), BF16)], axis=0
        )

    def block(b, carry):
        at = pl.ds(pl.multiple_of(b * TILE, TILE), TILE)
        first = pl.multiple_of(first_ref[b] * TILE, TILE)

        def variant(tiles):
            span = pl.ds(first, tiles * TILE)
            scores = [
                dot(
                    keys_ref[j, span, :],
                    side_by_side(qv_ref[core, at_q, top : top + PAIR, at], hot_ref[:, at]),
                    NN,
                )
                for j, (core, top) in enumerate(places)
            ]
            for j, (core, top) in enumerate(places):
                most = jnp.max(scores[j], axis=0, keepdims=True)
                expo = jnp.exp2((scores[j] - most) * SCALE_LOG2).astype(BF16)
                mixed = dot(vals_ref[j, :, span], expo, NN)
                total = mixed[PAIR : PAIR + 1, :]
                inverse = 1.0 / total
                out_ref[core, top : top + HEAD_DIM, at] = (
                    mixed[:HEAD_DIM, :TILE] * inverse[:, :TILE]
                ).astype(BF16)
                out_ref[core, top + HEAD_DIM : top + PAIR, at] = (
                    mixed[HEAD_DIM:PAIR, TILE:] * inverse[:, TILE:]
                ).astype(BF16)
                lse_ref[j, pl.ds(b, 1), :] = most * SCALE_LOG2 + jnp.log2(total)

        for tiles in window_kinds(length // TILE):
            pl.when(kind_ref[b] == tiles)(functools.partial(variant, tiles))
        return carry

    lax.fori_loop(0, length // TILE, block, 0)


def attend_backward_kernel(
    first_ref,
    kind_ref,
    flip_ref,
    segs_ref,
    qv_ref,
    k_ref,
    att_ref,
    grad_ref,
    lse_ref,
    dqv_ref,
    dk_ref,
    hot_ref,
    keys_ref,
    vals_ref,
    queries_ref,
    grads_ref,
    key_sum_ref,
    val_sum_ref,
):
    length = k_ref.shape[-1]
    at_q = flip_ref[0]
    places = pair_places(k_ref)
    one_hot, fill = image_rows(segs_ref[...], length)
    hot_ref[...] = one_hot
    pad = jnp.zeros((TILE - PAIR, length), BF16)
    for j, (core, top) in enumerate(places):
        rows = slice(top, top + PAIR)
        keys_ref[j] = jnp.concatenate([k_ref[core, rows, :], fill], axis=0).T
        vals_ref[j] = jnp.concatenate([qv_ref[core, 1 - at_q, rows, :], pad], axis=0).T
        queries_ref[j] = jnp.concatenate([qv_ref[core, at_q, rows, :], pad], axis=0).T
        grads_ref[j] = jnp.concatenate([grad_ref[core, rows, :], pad], axis=0).T
    key_sum_ref[...] = jnp.zeros(key_sum_ref.shape, F32)
    val_sum_ref[...] = jnp.zeros(val_sum_ref.shape, F32)
    no_rows = jnp.zeros((TILE - PAIR, TILE), BF16)
    lane = lax.broadcasted_iota(jnp.int32, (TILE, TILE), 1)
    in_first = lane < HEAD_DIM

    def stacked(both):
        blank = jnp.zeros_like(both)
        return jnp.concatenate(
            [jnp.where(in_first, both, blank), jnp.where(in_first, blank, both)], axis=0
        )

    def block(b, carry):
        at = pl.ds(pl.multiple_of(b * TILE, TILE), TILE)
        first = pl.multiple_of(first_ref[b] * TILE, TILE)

        def variant(tiles):
            span = pl.ds(first, tiles * TILE)
            scores = [
                dot(
                    keys_ref[j, span, :],
                    side_by_side(qv_ref[core, at_q, top : top + PAIR, at], hot_ref[:, at]),
                    NN,
                )
                for j, (core, top) in enumerate(places)
            ]
            prob_grads = [
                dot(
                    vals_ref[j, span, :],
                    side_by_side(grad_ref[core, top : top + PAIR, at], no_rows),
                    NN,
                )
                for j, (core, top) in enumerate(places)
            ]
            for j, (core, top) in enumerate(places):
                rows = slice(top, top + PAIR)
                agree = grad_ref[core, rows, at].astype(F32) * att_ref[core, rows, at].astype(F32)
                delta = jnp.concatenate(
                    [
                        jnp.sum(agree[:HEAD_DIM], axis=0, keepdims=True),
                        jnp.sum(agree[HEAD_DIM:], axis=0, keepdims=True),
                    ],
                    axis=1,
                )
                probs = jnp.exp2(scores[j] * SCALE_LOG2 - lse_ref[j, pl.ds(b, 1), :])
                score_grad = (probs * (prob_grads[j] - delta)).astype(BF16)
                val_sum_ref[j, span, :] += dot(
                    probs.astype(BF16), stacked(grads_ref[j, at, :]), NN
                )
                key_sum_ref[j, span, :] += dot(score_grad, stacked(queries_ref[j, at, :]), NN)
                query_grad = dot(k_ref[core, rows, span], score_grad, NN) * SCALE
                dqv_ref[core, at_q, top : top + HEAD_DIM, at] = query_grad[
                    :HEAD_DIM, :TILE
                ].astype(BF16)
                dqv_ref[core, at_q, top + HEAD_DIM : top + PAIR, at] = query_grad[
                    HEAD_DIM:, TILE:
                ].astype(BF16)

        for tiles in window_kinds(length // TILE):
            pl.when(kind_ref[b] == tiles)(functools.partial(variant, tiles))
        return carry

    lax.fori_loop(0, length // TILE, block, 0)
    for j, (core, top) in enumerate(places):
        rows = slice(top, top + PAIR)
        dk_ref[core, rows, :] = (key_sum_ref[j] * SCALE).T[:PAIR].astype(BF16)
        dqv_ref[core, 1 - at_q, rows, :] = val_sum_ref[j].T[:PAIR].astype(BF16)


def windows(segs):
    length = segs.shape[0]
    tiles = length // TILE
    by_tile = segs.reshape(tiles, TILE)
    begin = jnp.sum(segs[None, :] < by_tile[:, :1], axis=1)
    end = jnp.sum(segs[None, :] <= by_tile[:, -1:], axis=1)
    first = begin // TILE
    need = (end + TILE - 1) // TILE - first
    kinds = jnp.asarray(window_kinds(tiles), jnp.int32)
    kind = jnp.min(jnp.where(kinds[None, :] >= need[:, None], kinds[None, :], tiles), axis=1)
    return jnp.minimum(first, tiles - kind).astype(jnp.int32), kind.astype(jnp.int32)


def attention_specs(keys):
    cores, count, length = keys.shape
    pairs = cores * count // PAIR
    step = pairs if pairs <= 4 else 4
    part = count * step // pairs
    rows = pl.BlockSpec((cores, part, length), lambda i, *_: (0, i, 0))
    two = pl.BlockSpec((cores, 2, part, length), lambda i, *_: (0, 0, i, 0))
    segs = pl.BlockSpec((1, length), lambda i, *_: (0, 0))
    lse = pl.BlockSpec((step, length // TILE, 2 * TILE), lambda i, *_: (i, 0, 0))
    return pairs, step, rows, two, segs, lse


def attend_forward(query_value, keys, place):
    first, kind, flip, segs = place
    length = segs.shape[0]
    pairs, step, rows, two, segs_spec, lse = attention_specs(keys)
    return pl.pallas_call(
        attend_forward_kernel,
        grid_spec=pltpu.PrefetchScalarGridSpec(
            num_scalar_prefetch=3,
            grid=(pairs // step,),
            in_specs=[segs_spec, two, rows],
            out_specs=[rows, lse],
            scratch_shapes=[
                pltpu.VMEM((TILE - PAIR, length), BF16),
                pltpu.VMEM((step, length, TILE), BF16),
                pltpu.VMEM((step, PAIR + 16, length), BF16),
            ],
        ),
        out_shape=[
            jax.ShapeDtypeStruct(keys.shape, BF16),
            jax.ShapeDtypeStruct((pairs, length // TILE, 2 * TILE), F32),
        ],
        compiler_params=pltpu.CompilerParams(vmem_limit_bytes=40 << 20),
        name="attend_forward",
    )(first, kind, flip, segs[None, :], query_value, keys)


def attend_backward(query_value, keys, attended, grad, lse, place):
    first, kind, flip, segs = place
    length = segs.shape[0]
    pairs, step, rows, two, segs_spec, lse_spec = attention_specs(keys)
    wide = pltpu.VMEM((step, length, TILE), BF16)
    total = pltpu.VMEM((step, length, TILE), F32)
    return pl.pallas_call(
        attend_backward_kernel,
        grid_spec=pltpu.PrefetchScalarGridSpec(
            num_scalar_prefetch=3,
            grid=(pairs // step,),
            in_specs=[segs_spec, two, rows, rows, rows, lse_spec],
            out_specs=[two, rows],
            scratch_shapes=[
                pltpu.VMEM((TILE - PAIR, length), BF16),
                wide,
                wide,
                wide,
                wide,
                total,
                total,
            ],
        ),
        out_shape=[
            jax.ShapeDtypeStruct(query_value.shape, BF16),
            jax.ShapeDtypeStruct(keys.shape, BF16),
        ],
        compiler_params=pltpu.CompilerParams(vmem_limit_bytes=40 << 20),
        name="attend_backward",
    )(first, kind, flip, segs[None, :], query_value, keys, attended, grad, lse)


def gelu_parts(values):
    below = 0.5 * (1.0 + lax.erf(values * (0.5 ** 0.5)))
    density = jnp.exp(values * values * -0.5) * ((2.0 * math.pi) ** -0.5)
    return values * below, below + values * density


def feed_forward_kernel(norm_ref, cot_ref, up_ref, down_ref, *refs):
    *earlier, mlp_ref, back_ref, up_grad_ref, down_grad_ref, sum_ref, act_ref, pre_ref = refs
    rows = norm_ref.shape[0]
    chunk = min(rows, 256)

    @pl.when(pl.program_id(0) == 0)
    def _():
        sum_ref[...] = jnp.zeros(sum_ref.shape, F32)
        back_ref[...] = jnp.zeros(back_ref.shape, F32)

    for start in range(0, rows, chunk):
        at = slice(start, start + chunk)
        pre_act = dot(norm_ref[at, :], up_ref[...], NT)
        act_grad = dot(cot_ref[at, :], down_ref[...], NT)
        activation, slope = gelu_parts(pre_act)
        activation = activation.astype(BF16)
        pre_grad = (act_grad * slope).astype(BF16)
        act_ref[at, :] = activation
        pre_ref[at, :] = pre_grad
        sum_ref[at, :] += dot(activation, down_ref[...], NN)
        back_ref[at, :] += dot(pre_grad, up_ref[...], NN)
    up_grad = dot(pre_ref[...], norm_ref[...], TN)
    down_grad = dot(act_ref[...], cot_ref[...], TN)
    if earlier:
        up_grad = up_grad + earlier[0][...].astype(F32)
        down_grad = down_grad + earlier[1][...].astype(F32)
    up_grad_ref[...] = up_grad.astype(BF16)
    down_grad_ref[...] = down_grad.astype(BF16)

    @pl.when(pl.program_id(0) == pl.num_programs(0) - 1)
    def _():
        mlp_ref[...] = sum_ref[...].astype(mlp_ref.dtype)


def feed_forward(norm, cot, up, down, earlier=(), kind=F32):
    rows, width = norm.shape
    hidden = up.shape[0]
    part = 512 if hidden % 512 == 0 else hidden
    whole = pl.BlockSpec((rows, width), lambda i: (0, 0))
    block = pl.BlockSpec((part, width), lambda i: (i, 0))
    grads = jax.ShapeDtypeStruct((hidden, width), BF16)
    return pl.pallas_call(
        feed_forward_kernel,
        grid=(hidden // part,),
        in_specs=[whole, whole, block, block] + [block] * len(earlier),
        out_specs=[whole, whole, block, block],
        out_shape=[
            jax.ShapeDtypeStruct((rows, width), kind),
            jax.ShapeDtypeStruct((rows, width), F32),
            grads,
            grads,
        ],
        scratch_shapes=[
            pltpu.VMEM((rows, width), F32),
            pltpu.VMEM((rows, part), BF16),
            pltpu.VMEM((rows, part), BF16),
        ],
        compiler_params=pltpu.CompilerParams(vmem_limit_bytes=58 << 20),
        name="feed_forward",
    )(norm, cot, up, down, *earlier)


def middle_kernel(parts, residual_ref, cot_ref, gain_ref, *refs):
    mlp_refs, back_refs = refs[:parts], refs[parts : 2 * parts]
    output_ref, res_grad_ref, branch_ref, norm_grad_ref = refs[2 * parts :]

    @pl.when(pl.program_id(0) == 0)
    def _():
        norm_grad_ref[...] = jnp.zeros(norm_grad_ref.shape, F32)

    residual = residual_ref[...]
    output_ref[...] = sum([ref[...].astype(F32) for ref in mlp_refs], residual).astype(BF16)
    grad = functools.reduce(jnp.add, [ref[...] for ref in back_refs])
    back, gain_grad, bias_grad = layer_norm_back(residual, gain_ref[...], grad)
    res_grad = cot_ref[...].astype(F32) + back
    res_grad_ref[...] = res_grad
    branch_ref[...] = res_grad.astype(BF16)
    norm_grad_ref[0:1, :] += gain_grad
    norm_grad_ref[1:2, :] += bias_grad


def middle(residual, cot, gain, mlps, backs):
    rows, width = residual.shape
    parts = len(mlps)
    step = 128
    block = pl.BlockSpec((step, width), lambda i: (i, 0))
    sums = jax.ShapeDtypeStruct((rows, width), F32)
    low = jax.ShapeDtypeStruct((rows, width), BF16)
    return pl.pallas_call(
        functools.partial(middle_kernel, parts),
        grid=(rows // step,),
        in_specs=[block, block, pl.BlockSpec((1, width), lambda i: (0, 0))] + [block] * (2 * parts),
        out_specs=[block, block, block, pl.BlockSpec((8, width), lambda i: (0, 0))],
        out_shape=[low, sums, low, jax.ShapeDtypeStruct((8, width), F32)],
        name="middle",
    )(residual, cot, gain[None, :], *mlps, *backs)


def add(*terms):
    return functools.reduce(jnp.add, [item.astype(F32) for item in terms]).astype(BF16)


def swap(values, axis):
    name, size, mask = {
        "core": ("dp", 4, 1),
        "y": ("dp", 4, 2),
        "x": ("mp", 8, 1),
        "z1": ("mp", 8, 2),
        "z2": ("mp", 8, 4),
        "z3": ("mp", 8, 6),
    }[axis]
    return lax.ppermute(values, name, [(i, i ^ mask) for i in range(size)])


def order(at, mine, other):
    return jnp.where(at == 0, jnp.stack([mine, other]), jnp.stack([other, mine]))


class Line:
    def __init__(self):
        self.last = ()

    def __call__(self, step, *args):
        args, _ = lax.optimization_barrier((args, self.last))
        result = step(*args)
        self.last = tuple(jax.tree.leaves(result))
        return result


def on_cube(
    inputs,
    segments,
    ln1_gain,
    ln1_bias,
    w_query,
    w_key,
    w_value,
    w_output,
    ln2_gain,
    ln2_bias,
    w_up,
    w_down,
    cotangent,
):
    rows, width = inputs.shape
    local = w_query.shape[1]
    at_dp, at_mp = lax.axis_index("dp"), lax.axis_index("mp")
    at_y, at_core = at_dp // 2, at_dp % 2
    line = Line()

    def pick(values, at):
        return lax.dynamic_index_in_dim(values, at, 0, keepdims=False)

    def cut_attention(query, key, value, out):
        kinds = jnp.stack([query.T, key.T, value.T, out]).reshape(2, 2, 2, HEAD_DIM, width)
        return pick(kinds.transpose(0, 2, 1, 3, 4).reshape(4, 2, HEAD_DIM, width), at_dp)

    def cut_mlp(up, down):
        pieces = jnp.stack([up.T, down]).reshape(2, 4, -1, width)
        return lax.dynamic_index_in_dim(pieces, at_dp, 1, keepdims=False)

    def join(*parts):
        return jnp.concatenate(parts, 0)

    along_z = ("z2", "z1", "z3")
    attn_piece = line(cut_attention, w_query, w_key, w_value, w_output)
    attn_z = [swap(attn_piece, axis) for axis in along_z]
    mlp_piece = line(cut_mlp, w_up, w_down)
    mlp_z = [swap(mlp_piece, axis) for axis in along_z]

    def begin(rows_in):
        return layer_norm(rows_in.astype(F32), ln1_gain, ln1_bias).astype(BF16)

    norm_one = line(begin, inputs)
    segs = pick(segments, at_mp)
    place = windows(segs) + (at_y.reshape(1), segs)
    place = line(lambda item: item, place)

    near_z = line(lambda *parts: jnp.stack(parts[:4]), attn_piece, *attn_z, mlp_z[1])
    near_got = swap(near_z, "y")
    far_z = swap(near_z, "x")
    near_y = line(lambda *parts: jnp.stack(parts[:2]), near_z, near_got, far_z, mlp_z[0])
    near_got = swap(near_y, "core")
    far_got = swap(far_z, "y")

    def both_cores(mine, other):
        query_value, key_out = [jnp.stack([mine[:, :, i], other[:, :, i]]) for i in (0, 1)]
        key, out = [
            lax.dynamic_index_in_dim(key_out, at, 1, keepdims=False).reshape(-1, width)
            for at in (at_y, 1 - at_y)
        ]
        return query_value.reshape(-1, width), key, out

    def project(weights, norm):
        query_value = dot(weights[0], norm, NT).astype(BF16).reshape(2, 2, -1, rows)
        return query_value, dot(weights[1], norm, NT).astype(BF16).reshape(2, -1, rows)

    def attend(query_value, keys):
        return attend_forward(query_value, keys, place)

    def branch(base, attended, weights):
        return base + dot(attended.reshape(-1, rows), weights[2], TN)

    def mlp_along_z(*parts):
        return [jnp.concatenate([item[i] for item in parts], 0) for i in (0, 1)]

    def mlp_second(up, up_got, down, down_got):
        return jnp.concatenate([up, up_got], 0), jnp.stack([down, down_got])

    near_w = line(both_cores, near_y, near_got)
    near = line(project, near_w, norm_one)
    up, down = line(mlp_along_z, mlp_piece, *mlp_z)
    up_got, down_got = swap(up, "x"), swap(down, "y")
    near += tuple(line(attend, *near))

    far_y = line(lambda *parts: jnp.stack(parts), far_z, far_got)
    far_got = swap(far_y, "core")
    up, down = line(mlp_second, up, up_got, down, down_got)
    up_got, down_got = swap(up, "y"), swap(down, "x")
    residual = line(branch, inputs.astype(F32), near[2], near_w)
    far_w = line(both_cores, far_y, far_got)
    far = line(project, far_w, norm_one)
    far += tuple(line(attend, *far))

    def second_norm(residual, attended, weights):
        residual = branch(residual, attended, weights)
        return residual, layer_norm(residual, ln2_gain, ln2_bias).astype(BF16)

    cot_other = swap(cotangent, "core")
    far_attended, cot_other = lax.optimization_barrier((far[2], cot_other))
    residual, norm_two = line(second_norm, residual, far_attended, far_w)
    norm_two_other = swap(norm_two, "core")

    def mlp_last(up, up_got, down, down_got):
        return jnp.concatenate([up, up_got], 0), jnp.concatenate([down, down_got], 1).reshape(-1, width)

    up, down = line(mlp_last, up, up_got, down, down_got)
    mlp_b, back_b, *grads = line(
        lambda *args: feed_forward(*args, kind=BF16), norm_two_other, cot_other, up, down
    )
    mlp_b, back_b = swap(mlp_b, "core"), swap(back_b, "core")
    mlp_a, back_a, up_grad, down_grad = line(feed_forward, norm_two, cotangent, up, down, grads)

    def before_attention(attended, weights, grad):
        att_grad = dot(weights[2], grad, NT).astype(BF16).reshape(attended.shape)
        return att_grad, dot(attended.reshape(-1, rows), grad, NN).astype(BF16)


    quarter = up.shape[0] // 4

    def up_sum_of(terms, low, high):
        return add(*[item[low:high] for item in terms])

    def down_sum_of(terms, y, x, low=0, high=quarter):
        whole = terms[0].reshape(2, 2, quarter, width)[y, x, low:high]
        return add(whole, *[item.reshape(-1, quarter, width)[y, low:high] for item in terms[1:]])

    def mlp_sum_first(up_terms, down_terms):
        return (
            up_sum_of(up_terms, 2 * quarter, 4 * quarter),
            jnp.stack([down_sum_of(down_terms, y, 1) for y in (0, 1)]),
        )

    up_terms, down_terms = (up_grad,), (down_grad,)
    sends = line(mlp_sum_first, up_terms, down_terms)
    up_terms += (swap(sends[0], "y"),)
    down_terms += (swap(sends[1], "x"),)

    def attend_back(saved, att_grad):
        return attend_backward(*saved[:3], att_grad, saved[3], place)

    def weight_grads(query_value_grad, key_grad, out_grad, norm):
        query_value = dot(query_value_grad.reshape(-1, rows), norm, NN).astype(BF16)
        keys = dot(key_grad.reshape(-1, rows), norm, NN).astype(BF16)
        sums = (
            query_value.reshape(2, 2, -1, width),
            keys.reshape(2, -1, width),
            out_grad.reshape(2, -1, width),
        )
        return sums, [item[1] for item in sums]

    def project_back(grads, weights):
        return dot(grads[0].reshape(-1, rows), weights[0], TN) + dot(
            grads[1].reshape(-1, rows), weights[1], TN
        )

    def attn_terms_of(mine, got, at):
        terms = [(mine[0][0, at], mine[1][0], mine[2][0]), (got[0][at], got[1], got[2])]
        first = at_y == at
        return [
            [item[0] for item in terms],
            [jnp.where(first, item[1], item[2]) for item in terms],
        ]

    def sum_other_y(mine, got):
        return jnp.stack([add(*terms) for terms in attn_terms_of(mine, got, 1)])

    def sum_this_y(mine, got, from_y):
        terms = attn_terms_of(mine, got, 0)
        return jnp.stack([add(*terms[i], from_y[i]) for i in (0, 1)])

    output, res_grad, branch_grad, norm_two_grads = line(
        middle, residual, cotangent, ln2_gain, [mlp_a, mlp_b], [back_a, back_b]
    )
    far_att, far_out = line(before_attention, far[2], far_w, branch_grad)
    far_grads = line(attend_back, far, far_att)
    far_mine, sends = line(weight_grads, *far_grads, far_out, norm_one)
    far_got = [swap(item, "core") for item in sends]
    near_att, near_out = line(before_attention, near[2], near_w, branch_grad)
    norm_one_grad = line(project_back, far_grads, far_w)
    far_y = swap(line(sum_other_y, far_mine, far_got), "y")

    def mlp_sum_second(up_terms, down_terms):
        return up_sum_of(up_terms, quarter, 2 * quarter), down_sum_of(down_terms, 1, 0)

    sends = line(mlp_sum_second, up_terms, down_terms)
    up_terms += (swap(sends[0], "x"),)
    down_y = swap(sends[1], "y")

    near_grads = line(attend_back, near, near_att)

    part = quarter // 4

    def mlp_sum_of_z(up_terms, down_terms, down_y, low, high):
        low, high = low * part, high * part
        return jnp.stack(
            [
                up_sum_of(up_terms, low, high),
                down_sum_of(down_terms + (jnp.stack([down_y, down_y]),), 0, 0, low, high),
            ]
        )

    mlp_terms = (up_terms, down_terms, down_y)
    mlp_z1 = swap(line(lambda *terms: mlp_sum_of_z(*terms, 2, 4), *mlp_terms), "z1")
    near_mine, sends = line(weight_grads, *near_grads, near_out, norm_one)
    near_got = [swap(item, "core") for item in sends]
    far_x = swap(line(sum_this_y, far_mine, far_got, far_y), "x")
    near_y = swap(line(sum_other_y, near_mine, near_got), "y")

    def finish(norm_one_grad, grads, weights):
        norm_one_grad = norm_one_grad + project_back(grads, weights)
        input_part, gain_grad, bias_grad = layer_norm_back(
            inputs.astype(F32), ln1_gain, norm_one_grad
        )
        parts = jnp.concatenate([gain_grad, bias_grad, norm_two_grads[:2]])
        return parts, (res_grad + input_part).astype(BF16)

    norm_sums, in_grad = line(finish, norm_one_grad, near_grads, near_w)

    mlp_send = line(
        lambda got, *terms: add(mlp_sum_of_z(*terms, 1, 2), got[:, part:]), mlp_z1, *mlp_terms
    )
    mlp_z2 = swap(mlp_send, "z2")

    def attn_sum_z(mine, got, from_y, from_x):
        from_x = from_x.reshape(2, -1, width)
        whole = sum_this_y(mine, got, from_y).astype(F32) + from_x
        return whole[:, : 2 * HEAD_DIM].astype(BF16), whole[:, 2 * HEAD_DIM :].astype(BF16)

    attn_mine, send = line(attn_sum_z, near_mine, near_got, near_y, far_x)
    attn_z1 = swap(send, "z1")
    got = swap(norm_sums, "core")

    def in_order(piece, y, core, both):
        return order(at_core, order(at_y, piece, y), order(at_y, core, both))

    mlp_sum = line(
        lambda got, other, *terms: add(mlp_sum_of_z(*terms, 0, 1), got[:, :part], other),
        mlp_z1,
        mlp_z2,
        *mlp_terms,
    )
    mlp_got = swap(mlp_sum, "y")
    norm_sums = line(jnp.add, norm_sums, got)
    got = swap(norm_sums, "y")
    attn_send = line(lambda mine, got: add(mine[:, HEAD_DIM:], got[:, HEAD_DIM:]), attn_mine, attn_z1)
    attn_z2 = swap(attn_send, "z2")
    mlp_sum = line(lambda mine, got, _: order(at_y, mine, got), mlp_sum, mlp_got, attn_z2)
    mlp_got = swap(mlp_sum, "core")
    norm_sums = line(jnp.add, norm_sums, got)
    got = swap(norm_sums, "x")
    attn_sum = line(
        lambda mine, got, other: add(mine[:, :HEAD_DIM], got[:, :HEAD_DIM], other),
        attn_mine,
        attn_z1,
        attn_z2,
    )
    attn_got = [
        lax.ppermute(attn_sum, "dp", [(i, i ^ mask) for i in range(4)]) for mask in (2, 1, 3)
    ]
    norm_sums = line(jnp.add, norm_sums, got)
    got = swap(norm_sums, "z1")
    mlp_sum = line(functools.partial(order, at_core), mlp_sum, mlp_got)
    up_sum, down_sum = line(
        lambda item: tuple(item.transpose(2, 1, 0, 3, 4).reshape(2, -1, width).astype(F32)), mlp_sum
    )
    norm_sums = line(jnp.add, norm_sums, got)
    got = swap(norm_sums, "z2")
    up_sum = line(jnp.transpose, up_sum)
    attn_sum = line(in_order, attn_sum, *attn_got)
    norm_sums = line(jnp.add, norm_sums, got)
    norm_sums = lax.dynamic_slice_in_dim(norm_sums, at_mp * (width // 8), width // 8, 1)
    attn_sum = attn_sum.transpose(1, 2, 0, 3, 4).reshape(4, local, width).astype(F32)
    return (
        output,
        in_grad,
        norm_sums[0],
        norm_sums[1],
        attn_sum[0].T,
        attn_sum[1].T,
        attn_sum[2].T,
        attn_sum[3],
        norm_sums[2],
        norm_sums[3],
        up_sum,
        down_sum,
    )


def on_any(
    mp_size,
    inputs,
    segments,
    ln1_gain,
    ln1_bias,
    w_query,
    w_key,
    w_value,
    w_output,
    ln2_gain,
    ln2_bias,
    w_up,
    w_down,
    cotangent,
):
    rows, width = inputs.shape
    seq_length = segments.shape[1]
    shared_by = seq_length // rows
    at_mp = lax.axis_index("mp")
    groups = [[start + i for i in range(shared_by)] for start in range(0, mp_size, shared_by)]

    def exchange(values, split, join):
        if shared_by == 1:
            return values
        return lax.all_to_all(values, "mp", split, join, axis_index_groups=groups, tiled=True)

    def gather(parts):
        return lax.all_gather(parts, "mp", axis=1, tiled=True)

    def reduce(parts):
        return lax.psum(lax.psum_scatter(parts, "mp", scatter_dimension=1, tiled=True), "dp")

    attn_w = gather(jnp.stack([w_query.T, w_value.T, w_key.T, w_output]))
    up, down = gather(jnp.stack([w_up.T, w_down]))
    project, w_out = attn_w[:3].reshape(3 * width, width), attn_w[3]

    segs = lax.dynamic_index_in_dim(segments, at_mp // shared_by, 0, keepdims=False)
    place = windows(segs) + (jnp.zeros((1,), jnp.int32), segs)
    resid_in = inputs.astype(F32)
    norm_one = layer_norm(resid_in, ln1_gain, ln1_bias).astype(BF16)
    projected = dot(project, norm_one, NT).astype(BF16).reshape(3, width, rows)
    projected = exchange(projected, 1, 2)
    query_value, keys = projected[None, :2], projected[2:]
    heads_out, lse = attend_forward(query_value, keys, place)
    attended = exchange(heads_out[0], 1, 0)
    residual = resid_in + dot(attended, w_out, TN)
    norm_two = layer_norm(residual, ln2_gain, ln2_bias).astype(BF16)
    mlp_branch, norm_two_grad, *mlp_grads = feed_forward(norm_two, cotangent, up, down)
    up_sum, down_sum = reduce(jnp.stack(mlp_grads)).astype(F32)

    output, res_grad, branch_grad, norm_two_grads = middle(
        residual, cotangent, ln2_gain, [mlp_branch], [norm_two_grad]
    )
    out_grad = dot(attended, branch_grad, NN).astype(BF16)
    att_grad = exchange(dot(w_out, branch_grad, NT).astype(BF16), 0, 1)
    query_value_grad, key_grad = attend_backward(
        query_value, keys, heads_out, att_grad[None], lse, place
    )
    proj_grad = exchange(jnp.concatenate([query_value_grad[0], key_grad]), 2, 1)
    proj_grad = proj_grad.reshape(3 * width, rows)
    project_grad = dot(proj_grad, norm_one, NN).astype(BF16).reshape(3, width, width)
    attn_sum = reduce(jnp.concatenate([project_grad, out_grad[None]])).astype(F32)
    input_part, gain_one_grad, bias_one_grad = layer_norm_back(
        resid_in, ln1_gain, dot(proj_grad, project, TN)
    )
    in_grad = (res_grad + input_part).astype(BF16)
    norm_parts = jnp.concatenate([gain_one_grad, bias_one_grad, norm_two_grads[:2]])
    norm_sums = lax.dynamic_slice_in_dim(
        lax.psum(norm_parts, ("dp", "mp")), at_mp * (width // mp_size), width // mp_size, 1
    )
    return (
        output,
        in_grad,
        norm_sums[0],
        norm_sums[1],
        attn_sum[0].T,
        attn_sum[2].T,
        attn_sum[1].T,
        attn_sum[3],
        norm_sums[2],
        norm_sums[3],
        up_sum.T,
        down_sum,
    )


def shards(dp_size, mp_size, inputs, segments, *rest):
    if dp_size == 4 and mp_size == 8 and inputs.shape[0] == segments.shape[1]:
        return on_cube(inputs, segments, *rest)
    return on_any(mp_size, inputs, segments, *rest)


def solution(mesh):
    return jax.shard_map(
        functools.partial(shards, mesh.shape["dp"], mesh.shape["mp"]),
        mesh=mesh,
        in_specs=(
            P(("dp", "mp"), None),
            P("dp", None),
            P(),
            P(),
            P(None, "mp"),
            P(None, "mp"),
            P(None, "mp"),
            P("mp", None),
            P(),
            P(),
            P(None, "mp"),
            P("mp", None),
            P(("dp", "mp"), None),
        ),
        out_specs=(
            P(("dp", "mp"), None),
            P(("dp", "mp"), None),
            P("mp"),
            P("mp"),
            P(None, "mp"),
            P(None, "mp"),
            P(None, "mp"),
            P("mp", None),
            P("mp"),
            P("mp"),
            P(None, "mp"),
            P("mp", None),
        ),
        check_vma=False,
    )
```

```python
import functools
import math

import jax
import jax.numpy as jnp
from jax import lax
from jax.experimental import pallas as pl
from jax.experimental.pallas import tpu as pltpu
from jax.sharding import PartitionSpec as P

HEAD_DIM = 48
PAIR = 2 * HEAD_DIM
IMAGES = 4
TILE = 128
norm_eps = 1e-06
negative_fill = -1e30
SCALE = HEAD_DIM ** (-0.5)
SCALE_LOG2 = SCALE * math.log2(math.e)
BF16 = jnp.bfloat16
F32 = jnp.float32


def layer_norm(values, gain, bias):
    center = jnp.mean(values, axis=-1, keepdims=True)
    shifted = values - center
    spread = jnp.mean(shifted * shifted, axis=-1, keepdims=True)
    return shifted * lax.rsqrt(spread + norm_eps) * gain + bias


def layer_norm_back(values, gain, grad):
    shifted = values - jnp.mean(values, axis=-1, keepdims=True)
    scale = lax.rsqrt(jnp.mean(shifted * shifted, axis=-1, keepdims=True) + norm_eps)
    unit = shifted * scale
    scaled = grad * gain
    back = scale * (
        scaled
        - jnp.mean(scaled, axis=-1, keepdims=True)
        - unit * jnp.mean(scaled * unit, axis=-1, keepdims=True)
    )
    return back, jnp.sum(grad * unit, axis=0, keepdims=True), jnp.sum(grad, axis=0, keepdims=True)


def dot(left, right, dims):
    return lax.dot_general(left, right, (dims, ((), ())), preferred_element_type=F32)


NN = ((1,), (0,))
NT = ((1,), (1,))
TN = ((0,), (0,))


def window_kinds(tiles):
    return tuple(n for n in (2, 3, 4, 5, 6) if n < tiles) + (tiles,)


def image_rows(segs, length):
    row = lax.broadcasted_iota(jnp.int32, (TILE - PAIR, length), 0)
    here = row == segs
    one_hot = jnp.where(here, 1.0, 0.0).astype(BF16)
    fill = jnp.where(jnp.logical_or(here, row >= IMAGES), 0.0, negative_fill).astype(BF16)
    return one_hot, fill


def side_by_side(pair, extra):
    blank = jnp.zeros((HEAD_DIM, TILE), BF16)
    left = jnp.concatenate([pair[:HEAD_DIM], blank, extra], axis=0)
    right = jnp.concatenate([blank, pair[HEAD_DIM:], extra], axis=0)
    return jnp.concatenate([left, right], axis=1)


def pair_places(ref):
    cores, count = ref.shape[0], ref.shape[1]
    return [(core, top) for core in range(cores) for top in range(0, count, PAIR)]


def attend_forward_kernel(
    first_ref, kind_ref, flip_ref, segs_ref, qv_ref, k_ref, out_ref, lse_ref, hot_ref, keys_ref, vals_ref
):
    length = k_ref.shape[-1]
    at_q = flip_ref[0]
    places = pair_places(k_ref)
    one_hot, fill = image_rows(segs_ref[...], length)
    hot_ref[...] = one_hot
    for j, (core, top) in enumerate(places):
        rows = slice(top, top + PAIR)
        keys_ref[j] = jnp.concatenate([k_ref[core, rows, :], fill], axis=0).T
        vals_ref[j] = jnp.concatenate(
            [qv_ref[core, 1 - at_q, rows, :], jnp.ones((16, length), BF16)], axis=0
        )

    def block(b, carry):
        at = pl.ds(pl.multiple_of(b * TILE, TILE), TILE)
        first = pl.multiple_of(first_ref[b] * TILE, TILE)

        def variant(tiles):
            span = pl.ds(first, tiles * TILE)
            scores = [
                dot(
                    keys_ref[j, span, :],
                    side_by_side(qv_ref[core, at_q, top : top + PAIR, at], hot_ref[:, at]),
                    NN,
                )
                for j, (core, top) in enumerate(places)
            ]
            for j, (core, top) in enumerate(places):
                most = jnp.max(scores[j], axis=0, keepdims=True)
                expo = jnp.exp2((scores[j] - most) * SCALE_LOG2).astype(BF16)
                mixed = dot(vals_ref[j, :, span], expo, NN)
                total = mixed[PAIR : PAIR + 1, :]
                inverse = 1.0 / total
                out_ref[core, top : top + HEAD_DIM, at] = (
                    mixed[:HEAD_DIM, :TILE] * inverse[:, :TILE]
                ).astype(BF16)
                out_ref[core, top + HEAD_DIM : top + PAIR, at] = (
                    mixed[HEAD_DIM:PAIR, TILE:] * inverse[:, TILE:]
                ).astype(BF16)
                lse_ref[j, pl.ds(b, 1), :] = most * SCALE_LOG2 + jnp.log2(total)

        for tiles in window_kinds(length // TILE):
            pl.when(kind_ref[b] == tiles)(functools.partial(variant, tiles))
        return carry

    lax.fori_loop(0, length // TILE, block, 0)


def attend_backward_kernel(
    first_ref,
    kind_ref,
    flip_ref,
    segs_ref,
    qv_ref,
    k_ref,
    att_ref,
    grad_ref,
    lse_ref,
    dqv_ref,
    dk_ref,
    hot_ref,
    keys_ref,
    vals_ref,
    queries_ref,
    grads_ref,
    key_sum_ref,
    val_sum_ref,
):
    length = k_ref.shape[-1]
    at_q = flip_ref[0]
    places = pair_places(k_ref)
    one_hot, fill = image_rows(segs_ref[...], length)
    hot_ref[...] = one_hot
    pad = jnp.zeros((TILE - PAIR, length), BF16)
    for j, (core, top) in enumerate(places):
        rows = slice(top, top + PAIR)
        keys_ref[j] = jnp.concatenate([k_ref[core, rows, :], fill], axis=0).T
        vals_ref[j] = jnp.concatenate([qv_ref[core, 1 - at_q, rows, :], pad], axis=0).T
        queries_ref[j] = jnp.concatenate([qv_ref[core, at_q, rows, :], pad], axis=0).T
        grads_ref[j] = jnp.concatenate([grad_ref[core, rows, :], pad], axis=0).T
    key_sum_ref[...] = jnp.zeros(key_sum_ref.shape, F32)
    val_sum_ref[...] = jnp.zeros(val_sum_ref.shape, F32)
    no_rows = jnp.zeros((TILE - PAIR, TILE), BF16)
    lane = lax.broadcasted_iota(jnp.int32, (TILE, TILE), 1)
    in_first = lane < HEAD_DIM

    def stacked(both):
        blank = jnp.zeros_like(both)
        return jnp.concatenate(
            [jnp.where(in_first, both, blank), jnp.where(in_first, blank, both)], axis=0
        )

    def block(b, carry):
        at = pl.ds(pl.multiple_of(b * TILE, TILE), TILE)
        first = pl.multiple_of(first_ref[b] * TILE, TILE)

        def variant(tiles):
            span = pl.ds(first, tiles * TILE)
            scores = [
                dot(
                    keys_ref[j, span, :],
                    side_by_side(qv_ref[core, at_q, top : top + PAIR, at], hot_ref[:, at]),
                    NN,
                )
                for j, (core, top) in enumerate(places)
            ]
            prob_grads = [
                dot(
                    vals_ref[j, span, :],
                    side_by_side(grad_ref[core, top : top + PAIR, at], no_rows),
                    NN,
                )
                for j, (core, top) in enumerate(places)
            ]
            for j, (core, top) in enumerate(places):
                rows = slice(top, top + PAIR)
                agree = grad_ref[core, rows, at].astype(F32) * att_ref[core, rows, at].astype(F32)
                delta = jnp.concatenate(
                    [
                        jnp.sum(agree[:HEAD_DIM], axis=0, keepdims=True),
                        jnp.sum(agree[HEAD_DIM:], axis=0, keepdims=True),
                    ],
                    axis=1,
                )
                probs = jnp.exp2(scores[j] * SCALE_LOG2 - lse_ref[j, pl.ds(b, 1), :])
                score_grad = (probs * (prob_grads[j] - delta)).astype(BF16)
                val_sum_ref[j, span, :] += dot(
                    probs.astype(BF16), stacked(grads_ref[j, at, :]), NN
                )
                key_sum_ref[j, span, :] += dot(score_grad, stacked(queries_ref[j, at, :]), NN)
                query_grad = dot(k_ref[core, rows, span], score_grad, NN) * SCALE
                dqv_ref[core, at_q, top : top + HEAD_DIM, at] = query_grad[
                    :HEAD_DIM, :TILE
                ].astype(BF16)
                dqv_ref[core, at_q, top + HEAD_DIM : top + PAIR, at] = query_grad[
                    HEAD_DIM:, TILE:
                ].astype(BF16)

        for tiles in window_kinds(length // TILE):
            pl.when(kind_ref[b] == tiles)(functools.partial(variant, tiles))
        return carry

    lax.fori_loop(0, length // TILE, block, 0)
    for j, (core, top) in enumerate(places):
        rows = slice(top, top + PAIR)
        dk_ref[core, rows, :] = (key_sum_ref[j] * SCALE).T[:PAIR].astype(BF16)
        dqv_ref[core, 1 - at_q, rows, :] = val_sum_ref[j].T[:PAIR].astype(BF16)


def windows(segs):
    length = segs.shape[0]
    tiles = length // TILE
    by_tile = segs.reshape(tiles, TILE)
    begin = jnp.sum(segs[None, :] < by_tile[:, :1], axis=1)
    end = jnp.sum(segs[None, :] <= by_tile[:, -1:], axis=1)
    first = begin // TILE
    need = (end + TILE - 1) // TILE - first
    kinds = jnp.asarray(window_kinds(tiles), jnp.int32)
    kind = jnp.min(jnp.where(kinds[None, :] >= need[:, None], kinds[None, :], tiles), axis=1)
    return jnp.minimum(first, tiles - kind).astype(jnp.int32), kind.astype(jnp.int32)


def attention_specs(keys):
    cores, count, length = keys.shape
    pairs = cores * count // PAIR
    step = pairs if pairs <= 4 else 4
    part = count * step // pairs
    rows = pl.BlockSpec((cores, part, length), lambda i, *_: (0, i, 0))
    two = pl.BlockSpec((cores, 2, part, length), lambda i, *_: (0, 0, i, 0))
    segs = pl.BlockSpec((1, length), lambda i, *_: (0, 0))
    lse = pl.BlockSpec((step, length // TILE, 2 * TILE), lambda i, *_: (i, 0, 0))
    return pairs, step, rows, two, segs, lse


def attend_forward(query_value, keys, place):
    first, kind, flip, segs = place
    length = segs.shape[0]
    pairs, step, rows, two, segs_spec, lse = attention_specs(keys)
    return pl.pallas_call(
        attend_forward_kernel,
        grid_spec=pltpu.PrefetchScalarGridSpec(
            num_scalar_prefetch=3,
            grid=(pairs // step,),
            in_specs=[segs_spec, two, rows],
            out_specs=[rows, lse],
            scratch_shapes=[
                pltpu.VMEM((TILE - PAIR, length), BF16),
                pltpu.VMEM((step, length, TILE), BF16),
                pltpu.VMEM((step, PAIR + 16, length), BF16),
            ],
        ),
        out_shape=[
            jax.ShapeDtypeStruct(keys.shape, BF16),
            jax.ShapeDtypeStruct((pairs, length // TILE, 2 * TILE), F32),
        ],
        compiler_params=pltpu.CompilerParams(vmem_limit_bytes=40 << 20),
        name="attend_forward",
    )(first, kind, flip, segs[None, :], query_value, keys)


def attend_backward(query_value, keys, attended, grad, lse, place):
    first, kind, flip, segs = place
    length = segs.shape[0]
    pairs, step, rows, two, segs_spec, lse_spec = attention_specs(keys)
    wide = pltpu.VMEM((step, length, TILE), BF16)
    total = pltpu.VMEM((step, length, TILE), F32)
    return pl.pallas_call(
        attend_backward_kernel,
        grid_spec=pltpu.PrefetchScalarGridSpec(
            num_scalar_prefetch=3,
            grid=(pairs // step,),
            in_specs=[segs_spec, two, rows, rows, rows, lse_spec],
            out_specs=[two, rows],
            scratch_shapes=[
                pltpu.VMEM((TILE - PAIR, length), BF16),
                wide,
                wide,
                wide,
                wide,
                total,
                total,
            ],
        ),
        out_shape=[
            jax.ShapeDtypeStruct(query_value.shape, BF16),
            jax.ShapeDtypeStruct(keys.shape, BF16),
        ],
        compiler_params=pltpu.CompilerParams(vmem_limit_bytes=40 << 20),
        name="attend_backward",
    )(first, kind, flip, segs[None, :], query_value, keys, attended, grad, lse)


def gelu_parts(values):
    below = 0.5 * (1.0 + lax.erf(values * (0.5 ** 0.5)))
    density = jnp.exp(values * values * -0.5) * ((2.0 * math.pi) ** -0.5)
    return values * below, below + values * density


def feed_forward_kernel(norm_ref, cot_ref, up_ref, down_ref, *refs):
    *earlier, mlp_ref, back_ref, up_grad_ref, down_grad_ref, sum_ref, act_ref, pre_ref = refs
    rows = norm_ref.shape[0]
    chunk = min(rows, 256)

    @pl.when(pl.program_id(0) == 0)
    def _():
        sum_ref[...] = jnp.zeros(sum_ref.shape, F32)
        back_ref[...] = jnp.zeros(back_ref.shape, F32)

    for start in range(0, rows, chunk):
        at = slice(start, start + chunk)
        pre_act = dot(norm_ref[at, :], up_ref[...], NT)
        act_grad = dot(cot_ref[at, :], down_ref[...], NT)
        activation, slope = gelu_parts(pre_act)
        activation = activation.astype(BF16)
        pre_grad = (act_grad * slope).astype(BF16)
        act_ref[at, :] = activation
        pre_ref[at, :] = pre_grad
        sum_ref[at, :] += dot(activation, down_ref[...], NN)
        back_ref[at, :] += dot(pre_grad, up_ref[...], NN)
    up_grad = dot(pre_ref[...], norm_ref[...], TN)
    down_grad = dot(act_ref[...], cot_ref[...], TN)
    if earlier:
        up_grad = up_grad + earlier[0][...].astype(F32)
        down_grad = down_grad + earlier[1][...].astype(F32)
    up_grad_ref[...] = up_grad.astype(BF16)
    down_grad_ref[...] = down_grad.astype(BF16)

    @pl.when(pl.program_id(0) == pl.num_programs(0) - 1)
    def _():
        mlp_ref[...] = sum_ref[...].astype(mlp_ref.dtype)


def feed_forward(norm, cot, up, down, earlier=(), kind=F32):
    rows, width = norm.shape
    hidden = up.shape[0]
    part = 512 if hidden % 512 == 0 else hidden
    whole = pl.BlockSpec((rows, width), lambda i: (0, 0))
    block = pl.BlockSpec((part, width), lambda i: (i, 0))
    grads = jax.ShapeDtypeStruct((hidden, width), BF16)
    return pl.pallas_call(
        feed_forward_kernel,
        grid=(hidden // part,),
        in_specs=[whole, whole, block, block] + [block] * len(earlier),
        out_specs=[whole, whole, block, block],
        out_shape=[
            jax.ShapeDtypeStruct((rows, width), kind),
            jax.ShapeDtypeStruct((rows, width), F32),
            grads,
            grads,
        ],
        scratch_shapes=[
            pltpu.VMEM((rows, width), F32),
            pltpu.VMEM((rows, part), BF16),
            pltpu.VMEM((rows, part), BF16),
        ],
        compiler_params=pltpu.CompilerParams(vmem_limit_bytes=58 << 20),
        name="feed_forward",
    )(norm, cot, up, down, *earlier)


def middle_kernel(parts, residual_ref, cot_ref, gain_ref, *refs):
    mlp_refs, back_refs = refs[:parts], refs[parts : 2 * parts]
    output_ref, res_grad_ref, branch_ref, norm_grad_ref = refs[2 * parts :]

    @pl.when(pl.program_id(0) == 0)
    def _():
        norm_grad_ref[...] = jnp.zeros(norm_grad_ref.shape, F32)

    residual = residual_ref[...]
    output_ref[...] = sum([ref[...].astype(F32) for ref in mlp_refs], residual).astype(BF16)
    grad = functools.reduce(jnp.add, [ref[...] for ref in back_refs])
    back, gain_grad, bias_grad = layer_norm_back(residual, gain_ref[...], grad)
    res_grad = cot_ref[...].astype(F32) + back
    res_grad_ref[...] = res_grad
    branch_ref[...] = res_grad.astype(BF16)
    norm_grad_ref[0:1, :] += gain_grad
    norm_grad_ref[1:2, :] += bias_grad


def middle(residual, cot, gain, mlps, backs):
    rows, width = residual.shape
    parts = len(mlps)
    step = 256
    block = pl.BlockSpec((step, width), lambda i: (i, 0))
    sums = jax.ShapeDtypeStruct((rows, width), F32)
    low = jax.ShapeDtypeStruct((rows, width), BF16)
    return pl.pallas_call(
        functools.partial(middle_kernel, parts),
        grid=(rows // step,),
        in_specs=[block, block, pl.BlockSpec((1, width), lambda i: (0, 0))] + [block] * (2 * parts),
        out_specs=[block, block, block, pl.BlockSpec((8, width), lambda i: (0, 0))],
        out_shape=[low, sums, low, jax.ShapeDtypeStruct((8, width), F32)],
        compiler_params=pltpu.CompilerParams(vmem_limit_bytes=40 << 20),
        name="middle",
    )(residual, cot, gain[None, :], *mlps, *backs)


def add(*terms):
    return functools.reduce(jnp.add, [item.astype(F32) for item in terms]).astype(BF16)


def swap(values, axis):
    name, size, mask = {
        "core": ("dp", 4, 1),
        "y": ("dp", 4, 2),
        "x": ("mp", 8, 1),
        "z1": ("mp", 8, 2),
        "z2": ("mp", 8, 4),
        "z3": ("mp", 8, 6),
    }[axis]
    return lax.ppermute(values, name, [(i, i ^ mask) for i in range(size)])


def order(at, mine, other):
    return jnp.where(at == 0, jnp.stack([mine, other]), jnp.stack([other, mine]))


class Line:
    def __init__(self):
        self.last = ()

    def __call__(self, step, *args):
        args, _ = lax.optimization_barrier((args, self.last))
        result = step(*args)
        self.last = tuple(jax.tree.leaves(result))
        return result


def on_cube(
    inputs,
    segments,
    ln1_gain,
    ln1_bias,
    w_query,
    w_key,
    w_value,
    w_output,
    ln2_gain,
    ln2_bias,
    w_up,
    w_down,
    cotangent,
):
    rows, width = inputs.shape
    local = w_query.shape[1]
    at_dp, at_mp = lax.axis_index("dp"), lax.axis_index("mp")
    at_y, at_core = at_dp // 2, at_dp % 2
    line = Line()

    def pick(values, at):
        return lax.dynamic_index_in_dim(values, at, 0, keepdims=False)

    def cut_attention(query, key, value, out):
        kinds = jnp.stack([query.T, key.T, value.T, out]).reshape(2, 2, 2, HEAD_DIM, width)
        return pick(kinds.transpose(0, 2, 1, 3, 4).reshape(4, 2, HEAD_DIM, width), at_dp)

    def cut_mlp(up, down):
        pieces = jnp.stack([up.T, down]).reshape(2, 4, -1, width)
        return lax.dynamic_index_in_dim(pieces, at_dp, 1, keepdims=False)

    def join(*parts):
        return jnp.concatenate(parts, 0)

    along_z = ("z2", "z1", "z3")
    attn_piece = line(cut_attention, w_query, w_key, w_value, w_output)
    attn_z = [swap(attn_piece, axis) for axis in along_z]
    mlp_piece = line(cut_mlp, w_up, w_down)
    mlp_z = [swap(mlp_piece, axis) for axis in along_z]

    def begin(rows_in):
        return layer_norm(rows_in.astype(F32), ln1_gain, ln1_bias).astype(BF16)

    norm_one = line(begin, inputs)
    segs = pick(segments, at_mp)
    place = windows(segs) + (at_y.reshape(1), segs)
    place = line(lambda item: item, place)

    near_z = line(lambda *parts: jnp.stack(parts[:4]), attn_piece, *attn_z, mlp_z[1])
    near_got = swap(near_z, "y")
    far_z = swap(near_z, "x")
    near_y = line(lambda *parts: jnp.stack(parts[:2]), near_z, near_got, far_z, mlp_z[0])
    near_got = swap(near_y, "core")
    far_got = swap(far_z, "y")

    def both_cores(mine, other):
        query_value, key_out = [jnp.stack([mine[:, :, i], other[:, :, i]]) for i in (0, 1)]
        key, out = [
            lax.dynamic_index_in_dim(key_out, at, 1, keepdims=False).reshape(-1, width)
            for at in (at_y, 1 - at_y)
        ]
        return query_value.reshape(-1, width), key, out

    def project(weights, norm):
        query_value = dot(weights[0], norm, NT).astype(BF16).reshape(2, 2, -1, rows)
        return query_value, dot(weights[1], norm, NT).astype(BF16).reshape(2, -1, rows)

    def attend(query_value, keys):
        return attend_forward(query_value, keys, place)

    def branch(base, attended, weights):
        return base + dot(attended.reshape(-1, rows), weights[2], TN)

    def mlp_along_z(*parts):
        return [jnp.concatenate([item[i] for item in parts], 0) for i in (0, 1)]

    def mlp_second(up, up_got, down, down_got):
        return jnp.concatenate([up, up_got], 0), jnp.stack([down, down_got])

    near_w = line(both_cores, near_y, near_got)
    near = line(project, near_w, norm_one)
    up, down = line(mlp_along_z, mlp_piece, *mlp_z)
    up_got, down_got = swap(up, "x"), swap(down, "y")
    near += tuple(line(attend, *near))

    far_y = line(lambda *parts: jnp.stack(parts), far_z, far_got)
    far_got = swap(far_y, "core")
    up, down = line(mlp_second, up, up_got, down, down_got)
    up_got, down_got = swap(up, "y"), swap(down, "x")
    residual = line(branch, inputs.astype(F32), near[2], near_w)
    far_w = line(both_cores, far_y, far_got)
    far = line(project, far_w, norm_one)
    far += tuple(line(attend, *far))

    def second_norm(residual, attended, weights):
        residual = branch(residual, attended, weights)
        return residual, layer_norm(residual, ln2_gain, ln2_bias).astype(BF16)

    cot_other = swap(cotangent, "core")
    far_attended, cot_other = lax.optimization_barrier((far[2], cot_other))
    residual, norm_two = line(second_norm, residual, far_attended, far_w)
    norm_two_other = swap(norm_two, "core")

    def mlp_last(up, up_got, down, down_got):
        return jnp.concatenate([up, up_got], 0), jnp.concatenate([down, down_got], 1).reshape(-1, width)

    up, down = line(mlp_last, up, up_got, down, down_got)
    mlp_b, back_b, *grads = line(
        lambda *args: feed_forward(*args, kind=BF16), norm_two_other, cot_other, up, down
    )
    mlp_b, back_b = swap(mlp_b, "core"), swap(back_b, "core")
    mlp_a, back_a, up_grad, down_grad = line(feed_forward, norm_two, cotangent, up, down, grads)

    def before_attention(attended, weights, grad):
        att_grad = dot(weights[2], grad, NT).astype(BF16).reshape(attended.shape)
        return att_grad, dot(attended.reshape(-1, rows), grad, NN).astype(BF16)


    quarter = up.shape[0] // 4

    def up_sum_of(terms, low, high):
        return add(*[item[low:high] for item in terms])

    def down_sum_of(terms, y, x, low=0, high=quarter):
        whole = terms[0].reshape(2, 2, quarter, width)[y, x, low:high]
        return add(whole, *[item.reshape(-1, quarter, width)[y, low:high] for item in terms[1:]])

    def mlp_sum_first(up_terms, down_terms):
        return (
            up_sum_of(up_terms, 2 * quarter, 4 * quarter),
            jnp.stack([down_sum_of(down_terms, y, 1) for y in (0, 1)]),
        )

    up_terms, down_terms = (up_grad,), (down_grad,)
    sends = line(mlp_sum_first, up_terms, down_terms)
    up_terms += (swap(sends[0], "y"),)
    down_terms += (swap(sends[1], "x"),)

    def attend_back(saved, att_grad):
        return attend_backward(*saved[:3], att_grad, saved[3], place)

    def weight_grads(query_value_grad, key_grad, out_grad, norm):
        query_value = dot(query_value_grad.reshape(-1, rows), norm, NN).astype(BF16)
        keys = dot(key_grad.reshape(-1, rows), norm, NN).astype(BF16)
        sums = (
            query_value.reshape(2, 2, -1, width),
            keys.reshape(2, -1, width),
            out_grad.reshape(2, -1, width),
        )
        return sums, [item[1] for item in sums]

    def project_back(grads, weights):
        return dot(grads[0].reshape(-1, rows), weights[0], TN) + dot(
            grads[1].reshape(-1, rows), weights[1], TN
        )

    def attn_terms_of(mine, got, at):
        terms = [(mine[0][0, at], mine[1][0], mine[2][0]), (got[0][at], got[1], got[2])]
        first = at_y == at
        return [
            [item[0] for item in terms],
            [jnp.where(first, item[1], item[2]) for item in terms],
        ]

    def sum_other_y(mine, got):
        return jnp.stack([add(*terms) for terms in attn_terms_of(mine, got, 1)])

    def sum_this_y(mine, got, from_y):
        terms = attn_terms_of(mine, got, 0)
        return jnp.stack([add(*terms[i], from_y[i]) for i in (0, 1)])

    output, res_grad, branch_grad, norm_two_grads = line(
        middle, residual, cotangent, ln2_gain, [mlp_a, mlp_b], [back_a, back_b]
    )
    far_att, far_out = line(before_attention, far[2], far_w, branch_grad)
    far_grads = line(attend_back, far, far_att)
    def mlp_sum_second(up_terms, down_terms):
        return up_sum_of(up_terms, quarter, 2 * quarter), down_sum_of(down_terms, 1, 0)

    sends = line(mlp_sum_second, up_terms, down_terms)
    up_terms += (swap(sends[0], "x"),)
    down_y = swap(sends[1], "y")

    far_mine, sends = line(weight_grads, *far_grads, far_out, norm_one)
    far_got = [swap(item, "core") for item in sends]
    near_att, near_out = line(before_attention, near[2], near_w, branch_grad)
    norm_one_grad = line(project_back, far_grads, far_w)
    far_y = swap(line(sum_other_y, far_mine, far_got), "y")

    part = quarter // 4

    def mlp_sum_of_z(up_terms, down_terms, down_y, low, high):
        low, high = low * part, high * part
        return jnp.stack(
            [
                up_sum_of(up_terms, low, high),
                down_sum_of(down_terms + (jnp.stack([down_y, down_y]),), 0, 0, low, high),
            ]
        )

    mlp_terms = (up_terms, down_terms, down_y)
    mlp_z1 = swap(line(lambda *terms: mlp_sum_of_z(*terms, 2, 4), *mlp_terms), "z1")
    near_grads = line(attend_back, near, near_att)
    mlp_send = line(
        lambda got, *terms: add(mlp_sum_of_z(*terms, 1, 2), got[:, part:]), mlp_z1, *mlp_terms
    )
    mlp_z2 = swap(mlp_send, "z2")
    near_mine, sends = line(weight_grads, *near_grads, near_out, norm_one)
    near_got = [swap(item, "core") for item in sends]
    far_x = swap(line(sum_this_y, far_mine, far_got, far_y), "x")
    near_y = swap(line(sum_other_y, near_mine, near_got), "y")

    def finish(norm_one_grad, grads, weights):
        norm_one_grad = norm_one_grad + project_back(grads, weights)
        input_part, gain_grad, bias_grad = layer_norm_back(
            inputs.astype(F32), ln1_gain, norm_one_grad
        )
        parts = jnp.concatenate([gain_grad, bias_grad, norm_two_grads[:2]])
        return parts, (res_grad + input_part).astype(BF16)

    norm_sums, in_grad = line(finish, norm_one_grad, near_grads, near_w)

    mlp_sum = line(
        lambda got, other, *terms: add(mlp_sum_of_z(*terms, 0, 1), got[:, :part], other),
        mlp_z1,
        mlp_z2,
        *mlp_terms,
    )
    mlp_got = swap(mlp_sum, "y")

    def attn_sum_z(mine, got, from_y, from_x):
        from_x = from_x.reshape(2, -1, width)
        whole = sum_this_y(mine, got, from_y).astype(F32) + from_x
        return whole[:, : 2 * HEAD_DIM].astype(BF16), whole[:, 2 * HEAD_DIM :].astype(BF16)

    attn_mine, send = line(attn_sum_z, near_mine, near_got, near_y, far_x)
    attn_z1 = swap(send, "z1")
    mlp_sum = line(functools.partial(order, at_y), mlp_sum, mlp_got)
    mlp_got = swap(mlp_sum, "core")
    got = swap(norm_sums, "core")

    def in_order(piece, y, core, both):
        return order(at_core, order(at_y, piece, y), order(at_y, core, both))

    norm_sums = line(jnp.add, norm_sums, got)
    got = swap(norm_sums, "y")
    attn_send = line(lambda mine, got: add(mine[:, HEAD_DIM:], got[:, HEAD_DIM:]), attn_mine, attn_z1)
    attn_z2 = swap(attn_send, "z2")
    norm_sums = line(jnp.add, norm_sums, got)
    got = swap(norm_sums, "x")
    attn_sum = line(
        lambda mine, got, other: add(mine[:, :HEAD_DIM], got[:, :HEAD_DIM], other),
        attn_mine,
        attn_z1,
        attn_z2,
    )
    attn_got = [
        lax.ppermute(attn_sum, "dp", [(i, i ^ mask) for i in range(4)]) for mask in (2, 1, 3)
    ]
    norm_sums = line(jnp.add, norm_sums, got)
    got = swap(norm_sums, "z1")
    mlp_sum = line(functools.partial(order, at_core), mlp_sum, mlp_got)
    up_sum, down_sum = line(
        lambda item: tuple(item.transpose(2, 1, 0, 3, 4).reshape(2, -1, width).astype(F32)), mlp_sum
    )
    norm_sums = line(jnp.add, norm_sums, got)
    got = swap(norm_sums, "z2")
    up_sum = line(jnp.transpose, up_sum)
    attn_sum = line(in_order, attn_sum, *attn_got)
    norm_sums = line(jnp.add, norm_sums, got)
    norm_sums = lax.dynamic_slice_in_dim(norm_sums, at_mp * (width // 8), width // 8, 1)
    attn_sum = attn_sum.transpose(1, 2, 0, 3, 4).reshape(4, local, width).astype(F32)
    return (
        output,
        in_grad,
        norm_sums[0],
        norm_sums[1],
        attn_sum[0].T,
        attn_sum[1].T,
        attn_sum[2].T,
        attn_sum[3],
        norm_sums[2],
        norm_sums[3],
        up_sum,
        down_sum,
    )


def on_any(
    mp_size,
    inputs,
    segments,
    ln1_gain,
    ln1_bias,
    w_query,
    w_key,
    w_value,
    w_output,
    ln2_gain,
    ln2_bias,
    w_up,
    w_down,
    cotangent,
):
    rows, width = inputs.shape
    seq_length = segments.shape[1]
    shared_by = seq_length // rows
    at_mp = lax.axis_index("mp")
    groups = [[start + i for i in range(shared_by)] for start in range(0, mp_size, shared_by)]

    def exchange(values, split, join):
        if shared_by == 1:
            return values
        return lax.all_to_all(values, "mp", split, join, axis_index_groups=groups, tiled=True)

    def gather(parts):
        return lax.all_gather(parts, "mp", axis=1, tiled=True)

    def reduce(parts):
        return lax.psum(lax.psum_scatter(parts, "mp", scatter_dimension=1, tiled=True), "dp")

    attn_w = gather(jnp.stack([w_query.T, w_value.T, w_key.T, w_output]))
    up, down = gather(jnp.stack([w_up.T, w_down]))
    project, w_out = attn_w[:3].reshape(3 * width, width), attn_w[3]

    segs = lax.dynamic_index_in_dim(segments, at_mp // shared_by, 0, keepdims=False)
    place = windows(segs) + (jnp.zeros((1,), jnp.int32), segs)
    resid_in = inputs.astype(F32)
    norm_one = layer_norm(resid_in, ln1_gain, ln1_bias).astype(BF16)
    projected = dot(project, norm_one, NT).astype(BF16).reshape(3, width, rows)
    projected = exchange(projected, 1, 2)
    query_value, keys = projected[None, :2], projected[2:]
    heads_out, lse = attend_forward(query_value, keys, place)
    attended = exchange(heads_out[0], 1, 0)
    residual = resid_in + dot(attended, w_out, TN)
    norm_two = layer_norm(residual, ln2_gain, ln2_bias).astype(BF16)
    mlp_branch, norm_two_grad, *mlp_grads = feed_forward(norm_two, cotangent, up, down)
    up_sum, down_sum = reduce(jnp.stack(mlp_grads)).astype(F32)

    output, res_grad, branch_grad, norm_two_grads = middle(
        residual, cotangent, ln2_gain, [mlp_branch], [norm_two_grad]
    )
    out_grad = dot(attended, branch_grad, NN).astype(BF16)
    att_grad = exchange(dot(w_out, branch_grad, NT).astype(BF16), 0, 1)
    query_value_grad, key_grad = attend_backward(
        query_value, keys, heads_out, att_grad[None], lse, place
    )
    proj_grad = exchange(jnp.concatenate([query_value_grad[0], key_grad]), 2, 1)
    proj_grad = proj_grad.reshape(3 * width, rows)
    project_grad = dot(proj_grad, norm_one, NN).astype(BF16).reshape(3, width, width)
    attn_sum = reduce(jnp.concatenate([project_grad, out_grad[None]])).astype(F32)
    input_part, gain_one_grad, bias_one_grad = layer_norm_back(
        resid_in, ln1_gain, dot(proj_grad, project, TN)
    )
    in_grad = (res_grad + input_part).astype(BF16)
    norm_parts = jnp.concatenate([gain_one_grad, bias_one_grad, norm_two_grads[:2]])
    norm_sums = lax.dynamic_slice_in_dim(
        lax.psum(norm_parts, ("dp", "mp")), at_mp * (width // mp_size), width // mp_size, 1
    )
    return (
        output,
        in_grad,
        norm_sums[0],
        norm_sums[1],
        attn_sum[0].T,
        attn_sum[2].T,
        attn_sum[1].T,
        attn_sum[3],
        norm_sums[2],
        norm_sums[3],
        up_sum.T,
        down_sum,
    )


def shards(dp_size, mp_size, inputs, segments, *rest):
    if dp_size == 4 and mp_size == 8 and inputs.shape[0] == segments.shape[1]:
        return on_cube(inputs, segments, *rest)
    return on_any(mp_size, inputs, segments, *rest)


def solution(mesh):
    return jax.shard_map(
        functools.partial(shards, mesh.shape["dp"], mesh.shape["mp"]),
        mesh=mesh,
        in_specs=(
            P(("dp", "mp"), None),
            P("dp", None),
            P(),
            P(),
            P(None, "mp"),
            P(None, "mp"),
            P(None, "mp"),
            P("mp", None),
            P(),
            P(),
            P(None, "mp"),
            P("mp", None),
            P(("dp", "mp"), None),
        ),
        out_specs=(
            P(("dp", "mp"), None),
            P(("dp", "mp"), None),
            P("mp"),
            P("mp"),
            P(None, "mp"),
            P(None, "mp"),
            P(None, "mp"),
            P("mp", None),
            P("mp"),
            P("mp"),
            P(None, "mp"),
            P("mp", None),
        ),
        check_vma=False,
    )
```

```python
import functools
import math

import jax
import jax.numpy as jnp
from jax import lax
from jax.experimental import pallas as pl
from jax.experimental.pallas import tpu as pltpu
from jax.sharding import PartitionSpec as P

HEAD_DIM = 48
PAIR = 2 * HEAD_DIM
IMAGES = 4
TILE = 128
norm_eps = 1e-06
negative_fill = -1e30
SCALE = HEAD_DIM ** (-0.5)
SCALE_LOG2 = SCALE * math.log2(math.e)
BF16 = jnp.bfloat16
F32 = jnp.float32


def layer_norm(values, gain, bias):
    center = jnp.mean(values, axis=-1, keepdims=True)
    shifted = values - center
    spread = jnp.mean(shifted * shifted, axis=-1, keepdims=True)
    return shifted * lax.rsqrt(spread + norm_eps) * gain + bias


def layer_norm_back(values, gain, grad):
    shifted = values - jnp.mean(values, axis=-1, keepdims=True)
    scale = lax.rsqrt(jnp.mean(shifted * shifted, axis=-1, keepdims=True) + norm_eps)
    unit = shifted * scale
    scaled = grad * gain
    back = scale * (
        scaled
        - jnp.mean(scaled, axis=-1, keepdims=True)
        - unit * jnp.mean(scaled * unit, axis=-1, keepdims=True)
    )
    return back, jnp.sum(grad * unit, axis=0, keepdims=True), jnp.sum(grad, axis=0, keepdims=True)


def dot(left, right, dims):
    return lax.dot_general(left, right, (dims, ((), ())), preferred_element_type=F32)


NN = ((1,), (0,))
NT = ((1,), (1,))
TN = ((0,), (0,))


def window_kinds(tiles):
    return tuple(n for n in (2, 3, 4, 5, 6) if n < tiles) + (tiles,)


def image_rows(segs, length):
    row = lax.broadcasted_iota(jnp.int32, (TILE - PAIR, length), 0)
    here = row == segs
    one_hot = jnp.where(here, 1.0, 0.0).astype(BF16)
    fill = jnp.where(jnp.logical_or(here, row >= IMAGES), 0.0, negative_fill).astype(BF16)
    return one_hot, fill


def side_by_side(pair, extra):
    blank = jnp.zeros((HEAD_DIM, TILE), BF16)
    left = jnp.concatenate([pair[:HEAD_DIM], blank, extra], axis=0)
    right = jnp.concatenate([blank, pair[HEAD_DIM:], extra], axis=0)
    return jnp.concatenate([left, right], axis=1)


def pair_places(ref):
    cores, count = ref.shape[0], ref.shape[1]
    return [(core, top) for core in range(cores) for top in range(0, count, PAIR)]


def attend_forward_kernel(
    first_ref, kind_ref, flip_ref, segs_ref, qv_ref, k_ref, out_ref, lse_ref, hot_ref, keys_ref, vals_ref
):
    length = k_ref.shape[-1]
    at_q = flip_ref[0]
    places = pair_places(k_ref)
    one_hot, fill = image_rows(segs_ref[...], length)
    hot_ref[...] = one_hot
    for j, (core, top) in enumerate(places):
        rows = slice(top, top + PAIR)
        keys_ref[j] = jnp.concatenate([k_ref[core, rows, :], fill], axis=0).T
        vals_ref[j] = jnp.concatenate(
            [qv_ref[core, 1 - at_q, rows, :], jnp.ones((16, length), BF16)], axis=0
        )

    def block(b, carry):
        at = pl.ds(pl.multiple_of(b * TILE, TILE), TILE)
        first = pl.multiple_of(first_ref[b] * TILE, TILE)

        def variant(tiles):
            span = pl.ds(first, tiles * TILE)
            scores = [
                dot(
                    keys_ref[j, span, :],
                    side_by_side(qv_ref[core, at_q, top : top + PAIR, at], hot_ref[:, at]),
                    NN,
                )
                for j, (core, top) in enumerate(places)
            ]
            for j, (core, top) in enumerate(places):
                most = jnp.max(scores[j], axis=0, keepdims=True)
                expo = jnp.exp2((scores[j] - most) * SCALE_LOG2).astype(BF16)
                mixed = dot(vals_ref[j, :, span], expo, NN)
                total = mixed[PAIR : PAIR + 1, :]
                inverse = 1.0 / total
                out_ref[core, top : top + HEAD_DIM, at] = (
                    mixed[:HEAD_DIM, :TILE] * inverse[:, :TILE]
                ).astype(BF16)
                out_ref[core, top + HEAD_DIM : top + PAIR, at] = (
                    mixed[HEAD_DIM:PAIR, TILE:] * inverse[:, TILE:]
                ).astype(BF16)
                lse_ref[j, pl.ds(b, 1), :] = most * SCALE_LOG2 + jnp.log2(total)

        for tiles in window_kinds(length // TILE):
            pl.when(kind_ref[b] == tiles)(functools.partial(variant, tiles))
        return carry

    lax.fori_loop(0, length // TILE, block, 0)


def attend_backward_kernel(
    first_ref,
    kind_ref,
    flip_ref,
    segs_ref,
    qv_ref,
    k_ref,
    att_ref,
    grad_ref,
    lse_ref,
    dqv_ref,
    dk_ref,
    hot_ref,
    keys_ref,
    vals_ref,
    queries_ref,
    grads_ref,
    key_sum_ref,
    val_sum_ref,
):
    length = k_ref.shape[-1]
    at_q = flip_ref[0]
    places = pair_places(k_ref)
    one_hot, fill = image_rows(segs_ref[...], length)
    hot_ref[...] = one_hot
    pad = jnp.zeros((TILE - PAIR, length), BF16)
    for j, (core, top) in enumerate(places):
        rows = slice(top, top + PAIR)
        keys_ref[j] = jnp.concatenate([k_ref[core, rows, :], fill], axis=0).T
        vals_ref[j] = jnp.concatenate([qv_ref[core, 1 - at_q, rows, :], pad], axis=0).T
        queries_ref[j] = jnp.concatenate([qv_ref[core, at_q, rows, :], pad], axis=0).T
        grads_ref[j] = jnp.concatenate([grad_ref[core, rows, :], pad], axis=0).T
    key_sum_ref[...] = jnp.zeros(key_sum_ref.shape, F32)
    val_sum_ref[...] = jnp.zeros(val_sum_ref.shape, F32)
    no_rows = jnp.zeros((TILE - PAIR, TILE), BF16)
    lane = lax.broadcasted_iota(jnp.int32, (TILE, TILE), 1)
    in_first = lane < HEAD_DIM

    def stacked(both):
        blank = jnp.zeros_like(both)
        return jnp.concatenate(
            [jnp.where(in_first, both, blank), jnp.where(in_first, blank, both)], axis=0
        )

    def block(b, carry):
        at = pl.ds(pl.multiple_of(b * TILE, TILE), TILE)
        first = pl.multiple_of(first_ref[b] * TILE, TILE)

        def variant(tiles):
            span = pl.ds(first, tiles * TILE)
            scores = [
                dot(
                    keys_ref[j, span, :],
                    side_by_side(qv_ref[core, at_q, top : top + PAIR, at], hot_ref[:, at]),
                    NN,
                )
                for j, (core, top) in enumerate(places)
            ]
            prob_grads = [
                dot(
                    vals_ref[j, span, :],
                    side_by_side(grad_ref[core, top : top + PAIR, at], no_rows),
                    NN,
                )
                for j, (core, top) in enumerate(places)
            ]
            for j, (core, top) in enumerate(places):
                rows = slice(top, top + PAIR)
                agree = grad_ref[core, rows, at].astype(F32) * att_ref[core, rows, at].astype(F32)
                delta = jnp.concatenate(
                    [
                        jnp.sum(agree[:HEAD_DIM], axis=0, keepdims=True),
                        jnp.sum(agree[HEAD_DIM:], axis=0, keepdims=True),
                    ],
                    axis=1,
                )
                probs = jnp.exp2(scores[j] * SCALE_LOG2 - lse_ref[j, pl.ds(b, 1), :])
                score_grad = (probs * (prob_grads[j] - delta)).astype(BF16)
                val_sum_ref[j, span, :] += dot(
                    probs.astype(BF16), stacked(grads_ref[j, at, :]), NN
                )
                key_sum_ref[j, span, :] += dot(score_grad, stacked(queries_ref[j, at, :]), NN)
                query_grad = dot(k_ref[core, rows, span], score_grad, NN) * SCALE
                dqv_ref[core, at_q, top : top + HEAD_DIM, at] = query_grad[
                    :HEAD_DIM, :TILE
                ].astype(BF16)
                dqv_ref[core, at_q, top + HEAD_DIM : top + PAIR, at] = query_grad[
                    HEAD_DIM:, TILE:
                ].astype(BF16)

        for tiles in window_kinds(length // TILE):
            pl.when(kind_ref[b] == tiles)(functools.partial(variant, tiles))
        return carry

    lax.fori_loop(0, length // TILE, block, 0)
    for j, (core, top) in enumerate(places):
        rows = slice(top, top + PAIR)
        dk_ref[core, rows, :] = (key_sum_ref[j] * SCALE).T[:PAIR].astype(BF16)
        dqv_ref[core, 1 - at_q, rows, :] = val_sum_ref[j].T[:PAIR].astype(BF16)


def windows(segs):
    length = segs.shape[0]
    tiles = length // TILE
    by_tile = segs.reshape(tiles, TILE)
    begin = jnp.sum(segs[None, :] < by_tile[:, :1], axis=1)
    end = jnp.sum(segs[None, :] <= by_tile[:, -1:], axis=1)
    first = begin // TILE
    need = (end + TILE - 1) // TILE - first
    kinds = jnp.asarray(window_kinds(tiles), jnp.int32)
    kind = jnp.min(jnp.where(kinds[None, :] >= need[:, None], kinds[None, :], tiles), axis=1)
    return jnp.minimum(first, tiles - kind).astype(jnp.int32), kind.astype(jnp.int32)


def attention_specs(keys):
    cores, count, length = keys.shape
    pairs = cores * count // PAIR
    step = pairs if pairs <= 4 else 4
    part = count * step // pairs
    rows = pl.BlockSpec((cores, part, length), lambda i, *_: (0, i, 0))
    two = pl.BlockSpec((cores, 2, part, length), lambda i, *_: (0, 0, i, 0))
    segs = pl.BlockSpec((1, length), lambda i, *_: (0, 0))
    lse = pl.BlockSpec((step, length // TILE, 2 * TILE), lambda i, *_: (i, 0, 0))
    return pairs, step, rows, two, segs, lse


def attend_forward(query_value, keys, place):
    first, kind, flip, segs = place
    length = segs.shape[0]
    pairs, step, rows, two, segs_spec, lse = attention_specs(keys)
    return pl.pallas_call(
        attend_forward_kernel,
        grid_spec=pltpu.PrefetchScalarGridSpec(
            num_scalar_prefetch=3,
            grid=(pairs // step,),
            in_specs=[segs_spec, two, rows],
            out_specs=[rows, lse],
            scratch_shapes=[
                pltpu.VMEM((TILE - PAIR, length), BF16),
                pltpu.VMEM((step, length, TILE), BF16),
                pltpu.VMEM((step, PAIR + 16, length), BF16),
            ],
        ),
        out_shape=[
            jax.ShapeDtypeStruct(keys.shape, BF16),
            jax.ShapeDtypeStruct((pairs, length // TILE, 2 * TILE), F32),
        ],
        compiler_params=pltpu.CompilerParams(vmem_limit_bytes=40 << 20),
        name="attend_forward",
    )(first, kind, flip, segs[None, :], query_value, keys)


def attend_backward(query_value, keys, attended, grad, lse, place):
    first, kind, flip, segs = place
    length = segs.shape[0]
    pairs, step, rows, two, segs_spec, lse_spec = attention_specs(keys)
    wide = pltpu.VMEM((step, length, TILE), BF16)
    total = pltpu.VMEM((step, length, TILE), F32)
    return pl.pallas_call(
        attend_backward_kernel,
        grid_spec=pltpu.PrefetchScalarGridSpec(
            num_scalar_prefetch=3,
            grid=(pairs // step,),
            in_specs=[segs_spec, two, rows, rows, rows, lse_spec],
            out_specs=[two, rows],
            scratch_shapes=[
                pltpu.VMEM((TILE - PAIR, length), BF16),
                wide,
                wide,
                wide,
                wide,
                total,
                total,
            ],
        ),
        out_shape=[
            jax.ShapeDtypeStruct(query_value.shape, BF16),
            jax.ShapeDtypeStruct(keys.shape, BF16),
        ],
        compiler_params=pltpu.CompilerParams(vmem_limit_bytes=40 << 20),
        name="attend_backward",
    )(first, kind, flip, segs[None, :], query_value, keys, attended, grad, lse)


def gelu_parts(values):
    below = 0.5 * (1.0 + lax.erf(values * (0.5 ** 0.5)))
    density = jnp.exp(values * values * -0.5) * ((2.0 * math.pi) ** -0.5)
    return values * below, below + values * density


def feed_forward_kernel(norm_ref, cot_ref, up_ref, down_ref, *refs):
    *earlier, mlp_ref, back_ref, up_grad_ref, down_grad_ref, sum_ref, act_ref, pre_ref = refs
    rows = norm_ref.shape[0]
    chunk = min(rows, 256)

    @pl.when(pl.program_id(0) == 0)
    def _():
        sum_ref[...] = jnp.zeros(sum_ref.shape, F32)
        back_ref[...] = jnp.zeros(back_ref.shape, F32)

    for start in range(0, rows, chunk):
        at = slice(start, start + chunk)
        pre_act = dot(norm_ref[at, :], up_ref[...], NT)
        act_grad = dot(cot_ref[at, :], down_ref[...], NT)
        activation, slope = gelu_parts(pre_act)
        activation = activation.astype(BF16)
        pre_grad = (act_grad * slope).astype(BF16)
        act_ref[at, :] = activation
        pre_ref[at, :] = pre_grad
        sum_ref[at, :] += dot(activation, down_ref[...], NN)
        back_ref[at, :] += dot(pre_grad, up_ref[...], NN)
    up_grad = dot(pre_ref[...], norm_ref[...], TN)
    down_grad = dot(act_ref[...], cot_ref[...], TN)
    if earlier:
        up_grad = up_grad + earlier[0][...].astype(F32)
        down_grad = down_grad + earlier[1][...].astype(F32)
    up_grad_ref[...] = up_grad.astype(BF16)
    down_grad_ref[...] = down_grad.astype(BF16)

    @pl.when(pl.program_id(0) == pl.num_programs(0) - 1)
    def _():
        mlp_ref[...] = sum_ref[...].astype(mlp_ref.dtype)


def feed_forward(norm, cot, up, down, earlier=(), kind=F32):
    rows, width = norm.shape
    hidden = up.shape[0]
    part = 512 if hidden % 512 == 0 else hidden
    whole = pl.BlockSpec((rows, width), lambda i: (0, 0))
    block = pl.BlockSpec((part, width), lambda i: (i, 0))
    grads = jax.ShapeDtypeStruct((hidden, width), BF16)
    return pl.pallas_call(
        feed_forward_kernel,
        grid=(hidden // part,),
        in_specs=[whole, whole, block, block] + [block] * len(earlier),
        out_specs=[whole, whole, block, block],
        out_shape=[
            jax.ShapeDtypeStruct((rows, width), kind),
            jax.ShapeDtypeStruct((rows, width), F32),
            grads,
            grads,
        ],
        scratch_shapes=[
            pltpu.VMEM((rows, width), F32),
            pltpu.VMEM((rows, part), BF16),
            pltpu.VMEM((rows, part), BF16),
        ],
        compiler_params=pltpu.CompilerParams(vmem_limit_bytes=58 << 20),
        name="feed_forward",
    )(norm, cot, up, down, *earlier)


def middle_kernel(parts, residual_ref, cot_ref, gain_ref, *refs):
    mlp_refs, back_refs = refs[:parts], refs[parts : 2 * parts]
    output_ref, res_grad_ref, branch_ref, norm_grad_ref = refs[2 * parts :]

    @pl.when(pl.program_id(0) == 0)
    def _():
        norm_grad_ref[...] = jnp.zeros(norm_grad_ref.shape, F32)

    residual = residual_ref[...]
    output_ref[...] = sum([ref[...].astype(F32) for ref in mlp_refs], residual).astype(BF16)
    grad = functools.reduce(jnp.add, [ref[...] for ref in back_refs])
    back, gain_grad, bias_grad = layer_norm_back(residual, gain_ref[...], grad)
    res_grad = cot_ref[...].astype(F32) + back
    res_grad_ref[...] = res_grad
    branch_ref[...] = res_grad.astype(BF16)
    norm_grad_ref[0:1, :] += gain_grad
    norm_grad_ref[1:2, :] += bias_grad


def middle(residual, cot, gain, mlps, backs):
    rows, width = residual.shape
    parts = len(mlps)
    step = 256
    block = pl.BlockSpec((step, width), lambda i: (i, 0))
    sums = jax.ShapeDtypeStruct((rows, width), F32)
    low = jax.ShapeDtypeStruct((rows, width), BF16)
    return pl.pallas_call(
        functools.partial(middle_kernel, parts),
        grid=(rows // step,),
        in_specs=[block, block, pl.BlockSpec((1, width), lambda i: (0, 0))] + [block] * (2 * parts),
        out_specs=[block, block, block, pl.BlockSpec((8, width), lambda i: (0, 0))],
        out_shape=[low, sums, low, jax.ShapeDtypeStruct((8, width), F32)],
        compiler_params=pltpu.CompilerParams(vmem_limit_bytes=40 << 20),
        name="middle",
    )(residual, cot, gain[None, :], *mlps, *backs)


def add(*terms):
    return functools.reduce(jnp.add, [item.astype(F32) for item in terms]).astype(BF16)


def swap(values, axis):
    name, size, mask = {
        "core": ("dp", 4, 1),
        "y": ("dp", 4, 2),
        "x": ("mp", 8, 1),
        "z1": ("mp", 8, 2),
        "z2": ("mp", 8, 4),
        "z3": ("mp", 8, 6),
    }[axis]
    return lax.ppermute(values, name, [(i, i ^ mask) for i in range(size)])


def order(at, mine, other):
    return jnp.where(at == 0, jnp.stack([mine, other]), jnp.stack([other, mine]))


class Line:
    def __init__(self):
        self.last = ()

    def __call__(self, step, *args):
        args, _ = lax.optimization_barrier((args, self.last))
        result = step(*args)
        self.last = tuple(jax.tree.leaves(result))
        return result


def on_cube(
    inputs,
    segments,
    ln1_gain,
    ln1_bias,
    w_query,
    w_key,
    w_value,
    w_output,
    ln2_gain,
    ln2_bias,
    w_up,
    w_down,
    cotangent,
):
    rows, width = inputs.shape
    local = w_query.shape[1]
    at_dp, at_mp = lax.axis_index("dp"), lax.axis_index("mp")
    at_y, at_core = at_dp // 2, at_dp % 2
    line = Line()

    def pick(values, at):
        return lax.dynamic_index_in_dim(values, at, 0, keepdims=False)

    def cut_attention(query, key, value, out):
        kinds = jnp.stack([query.T, key.T, value.T, out]).reshape(2, 2, 2, HEAD_DIM, width)
        return pick(kinds.transpose(0, 2, 1, 3, 4).reshape(4, 2, HEAD_DIM, width), at_dp)

    def cut_mlp(up, down):
        pieces = jnp.stack([up.T, down]).reshape(2, 4, -1, width)
        return lax.dynamic_index_in_dim(pieces, at_dp, 1, keepdims=False)

    def join(*parts):
        return jnp.concatenate(parts, 0)

    along_z = ("z2", "z1", "z3")
    attn_piece = line(cut_attention, w_query, w_key, w_value, w_output)
    attn_z = [swap(attn_piece, axis) for axis in along_z]
    mlp_piece = line(cut_mlp, w_up, w_down)
    mlp_z = [swap(mlp_piece, axis) for axis in along_z]

    def begin(rows_in):
        return layer_norm(rows_in.astype(F32), ln1_gain, ln1_bias).astype(BF16)

    norm_one = line(begin, inputs)
    segs = pick(segments, at_mp)
    place = windows(segs) + (at_y.reshape(1), segs)
    place = line(lambda item: item, place)

    near_z = line(lambda *parts: jnp.stack(parts[:4]), attn_piece, *attn_z, mlp_z[1])
    near_got = swap(near_z, "y")
    far_z = swap(near_z, "x")
    near_y = line(lambda *parts: jnp.stack(parts[:2]), near_z, near_got, far_z, mlp_z[0])
    near_got = swap(near_y, "core")
    far_got = swap(far_z, "y")

    def both_cores(mine, other):
        query_value, key_out = [jnp.stack([mine[:, :, i], other[:, :, i]]) for i in (0, 1)]
        key, out = [
            lax.dynamic_index_in_dim(key_out, at, 1, keepdims=False).reshape(-1, width)
            for at in (at_y, 1 - at_y)
        ]
        return query_value.reshape(-1, width), key, out

    def project(weights, norm):
        query_value = dot(weights[0], norm, NT).astype(BF16).reshape(2, 2, -1, rows)
        return query_value, dot(weights[1], norm, NT).astype(BF16).reshape(2, -1, rows)

    def attend(query_value, keys):
        return attend_forward(query_value, keys, place)

    def branch(base, attended, weights):
        return base + dot(attended.reshape(-1, rows), weights[2], TN)

    def mlp_along_z(*parts):
        return [jnp.concatenate([item[i] for item in parts], 0) for i in (0, 1)]

    def mlp_second(up, up_got, down, down_got):
        return jnp.concatenate([up, up_got], 0), jnp.stack([down, down_got])

    near_w = line(both_cores, near_y, near_got)
    near = line(project, near_w, norm_one)
    up, down = line(mlp_along_z, mlp_piece, *mlp_z)
    up_got, down_got = swap(up, "x"), swap(down, "y")
    near += tuple(line(attend, *near))

    far_y = line(lambda *parts: jnp.stack(parts), far_z, far_got)
    far_got = swap(far_y, "core")
    up, down = line(mlp_second, up, up_got, down, down_got)
    up_got, down_got = swap(up, "y"), swap(down, "x")
    residual = line(branch, inputs.astype(F32), near[2], near_w)
    far_w = line(both_cores, far_y, far_got)
    far = line(project, far_w, norm_one)
    far += tuple(line(attend, *far))

    def second_norm(residual, attended, weights):
        residual = branch(residual, attended, weights)
        return residual, layer_norm(residual, ln2_gain, ln2_bias).astype(BF16)

    cot_other = swap(cotangent, "core")
    far_attended, cot_other = lax.optimization_barrier((far[2], cot_other))
    residual, norm_two = line(second_norm, residual, far_attended, far_w)
    norm_two_other = swap(norm_two, "core")

    def mlp_last(up, up_got, down, down_got):
        return jnp.concatenate([up, up_got], 0), jnp.concatenate([down, down_got], 1).reshape(-1, width)

    up, down = line(mlp_last, up, up_got, down, down_got)
    mlp_b, back_b, *grads = line(
        lambda *args: feed_forward(*args, kind=BF16), norm_two_other, cot_other, up, down
    )
    mlp_b, back_b = swap(mlp_b, "core"), swap(back_b, "core")
    mlp_a, back_a, up_grad, down_grad = line(feed_forward, norm_two, cotangent, up, down, grads)

    def before_attention(attended, weights, grad):
        att_grad = dot(weights[2], grad, NT).astype(BF16).reshape(attended.shape)
        return att_grad, dot(attended.reshape(-1, rows), grad, NN).astype(BF16)


    quarter = up.shape[0] // 4

    def up_sum_of(terms, low, high):
        return add(*[item[low:high] for item in terms])

    def down_sum_of(terms, y, x, low=0, high=quarter):
        whole = terms[0].reshape(2, 2, quarter, width)[y, x, low:high]
        return add(whole, *[item.reshape(-1, quarter, width)[y, low:high] for item in terms[1:]])

    def mlp_sum_first(up_terms, down_terms):
        return (
            up_sum_of(up_terms, 2 * quarter, 4 * quarter),
            jnp.stack([down_sum_of(down_terms, y, 1) for y in (0, 1)]),
        )

    up_terms, down_terms = (up_grad,), (down_grad,)
    sends = line(mlp_sum_first, up_terms, down_terms)
    up_terms += (swap(sends[0], "y"),)
    down_terms += (swap(sends[1], "x"),)

    def attend_back(saved, att_grad):
        return attend_backward(*saved[:3], att_grad, saved[3], place)

    def weight_grads(query_value_grad, key_grad, out_grad, norm):
        query_value = dot(query_value_grad.reshape(-1, rows), norm, NN).astype(BF16)
        keys = dot(key_grad.reshape(-1, rows), norm, NN).astype(BF16)
        sums = (
            query_value.reshape(2, 2, -1, width),
            keys.reshape(2, -1, width),
            out_grad.reshape(2, -1, width),
        )
        return sums, [item[1] for item in sums]

    def project_back(grads, weights):
        return dot(grads[0].reshape(-1, rows), weights[0], TN) + dot(
            grads[1].reshape(-1, rows), weights[1], TN
        )

    def attn_terms_of(mine, got, at):
        terms = [(mine[0][0, at], mine[1][0], mine[2][0]), (got[0][at], got[1], got[2])]
        first = at_y == at
        return [
            [item[0] for item in terms],
            [jnp.where(first, item[1], item[2]) for item in terms],
        ]

    def sum_other_y(mine, got):
        return jnp.stack([add(*terms) for terms in attn_terms_of(mine, got, 1)])

    def sum_this_y(mine, got, from_y):
        terms = attn_terms_of(mine, got, 0)
        return jnp.stack([add(*terms[i], from_y[i]) for i in (0, 1)])

    output, res_grad, branch_grad, norm_two_grads = line(
        middle, residual, cotangent, ln2_gain, [mlp_a, mlp_b], [back_a, back_b]
    )
    far_att, far_out = line(before_attention, far[2], far_w, branch_grad)
    far_grads = line(attend_back, far, far_att)
    def mlp_sum_second(up_terms, down_terms):
        return up_sum_of(up_terms, quarter, 2 * quarter), down_sum_of(down_terms, 1, 0)

    sends = line(mlp_sum_second, up_terms, down_terms)
    up_terms += (swap(sends[0], "x"),)
    down_y = swap(sends[1], "y")

    far_mine, sends = line(weight_grads, *far_grads, far_out, norm_one)
    far_got = [swap(item, "core") for item in sends]
    near_att, near_out = line(before_attention, near[2], near_w, branch_grad)
    far_y = swap(line(sum_other_y, far_mine, far_got), "y")

    part = quarter // 4

    def mlp_sum_of_z(up_terms, down_terms, down_y, low, high):
        low, high = low * part, high * part
        return jnp.stack(
            [
                up_sum_of(up_terms, low, high),
                down_sum_of(down_terms + (jnp.stack([down_y, down_y]),), 0, 0, low, high),
            ]
        )

    mlp_terms = (up_terms, down_terms, down_y)
    near_grads = line(attend_back, near, near_att)
    mlp_z1 = swap(line(lambda *terms: mlp_sum_of_z(*terms, 2, 4), *mlp_terms), "z1")
    near_mine, sends = line(weight_grads, *near_grads, near_out, norm_one)
    near_got = [swap(item, "core") for item in sends]
    far_x = swap(line(sum_this_y, far_mine, far_got, far_y), "x")
    norm_one_grad = line(project_back, far_grads, far_w)
    near_y = swap(line(sum_other_y, near_mine, near_got), "y")

    def add_project_back(norm_one_grad, grads, weights):
        return norm_one_grad + project_back(grads, weights)

    def finish(norm_one_grad):
        input_part, gain_grad, bias_grad = layer_norm_back(
            inputs.astype(F32), ln1_gain, norm_one_grad
        )
        parts = jnp.concatenate([gain_grad, bias_grad, norm_two_grads[:2]])
        return parts, (res_grad + input_part).astype(BF16)

    norm_one_grad = line(add_project_back, norm_one_grad, near_grads, near_w)
    mlp_send = line(
        lambda got, *terms: add(mlp_sum_of_z(*terms, 1, 2), got[:, part:]), mlp_z1, *mlp_terms
    )
    mlp_z2 = swap(mlp_send, "z2")
    norm_sums, in_grad = line(finish, norm_one_grad)

    mlp_sum = line(
        lambda got, other, *terms: add(mlp_sum_of_z(*terms, 0, 1), got[:, :part], other),
        mlp_z1,
        mlp_z2,
        *mlp_terms,
    )
    mlp_got = swap(mlp_sum, "y")

    def attn_sum_z(mine, got, from_y, from_x):
        from_x = from_x.reshape(2, -1, width)
        whole = sum_this_y(mine, got, from_y).astype(F32) + from_x
        return whole[:, : 2 * HEAD_DIM].astype(BF16), whole[:, 2 * HEAD_DIM :].astype(BF16)

    attn_mine, send = line(attn_sum_z, near_mine, near_got, near_y, far_x)
    attn_z1 = swap(send, "z1")
    mlp_sum = line(functools.partial(order, at_y), mlp_sum, mlp_got)
    mlp_got = swap(mlp_sum, "core")
    got = swap(norm_sums, "core")

    def in_order(piece, y, core, both):
        return order(at_core, order(at_y, piece, y), order(at_y, core, both))

    norm_sums = line(jnp.add, norm_sums, got)
    got = swap(norm_sums, "y")
    attn_send = line(lambda mine, got: add(mine[:, HEAD_DIM:], got[:, HEAD_DIM:]), attn_mine, attn_z1)
    attn_z2 = swap(attn_send, "z2")
    norm_sums = line(jnp.add, norm_sums, got)
    got = swap(norm_sums, "x")
    attn_sum = line(
        lambda mine, got, other: add(mine[:, :HEAD_DIM], got[:, :HEAD_DIM], other),
        attn_mine,
        attn_z1,
        attn_z2,
    )
    attn_got = [
        lax.ppermute(attn_sum, "dp", [(i, i ^ mask) for i in range(4)]) for mask in (2, 1, 3)
    ]
    norm_sums = line(jnp.add, norm_sums, got)
    got = swap(norm_sums, "z1")
    mlp_sum = line(functools.partial(order, at_core), mlp_sum, mlp_got)
    up_sum, down_sum = line(
        lambda item: tuple(item.transpose(2, 1, 0, 3, 4).reshape(2, -1, width).astype(F32)), mlp_sum
    )
    norm_sums = line(jnp.add, norm_sums, got)
    got = swap(norm_sums, "z2")
    up_sum = line(jnp.transpose, up_sum)
    attn_sum = line(in_order, attn_sum, *attn_got)
    norm_sums = line(jnp.add, norm_sums, got)
    norm_sums = lax.dynamic_slice_in_dim(norm_sums, at_mp * (width // 8), width // 8, 1)
    attn_sum = attn_sum.transpose(1, 2, 0, 3, 4).reshape(4, local, width).astype(F32)
    return (
        output,
        in_grad,
        norm_sums[0],
        norm_sums[1],
        attn_sum[0].T,
        attn_sum[1].T,
        attn_sum[2].T,
        attn_sum[3],
        norm_sums[2],
        norm_sums[3],
        up_sum,
        down_sum,
    )


def on_any(
    mp_size,
    inputs,
    segments,
    ln1_gain,
    ln1_bias,
    w_query,
    w_key,
    w_value,
    w_output,
    ln2_gain,
    ln2_bias,
    w_up,
    w_down,
    cotangent,
):
    rows, width = inputs.shape
    seq_length = segments.shape[1]
    shared_by = seq_length // rows
    at_mp = lax.axis_index("mp")
    groups = [[start + i for i in range(shared_by)] for start in range(0, mp_size, shared_by)]

    def exchange(values, split, join):
        if shared_by == 1:
            return values
        return lax.all_to_all(values, "mp", split, join, axis_index_groups=groups, tiled=True)

    def gather(parts):
        return lax.all_gather(parts, "mp", axis=1, tiled=True)

    def reduce(parts):
        return lax.psum(lax.psum_scatter(parts, "mp", scatter_dimension=1, tiled=True), "dp")

    attn_w = gather(jnp.stack([w_query.T, w_value.T, w_key.T, w_output]))
    up, down = gather(jnp.stack([w_up.T, w_down]))
    project, w_out = attn_w[:3].reshape(3 * width, width), attn_w[3]

    segs = lax.dynamic_index_in_dim(segments, at_mp // shared_by, 0, keepdims=False)
    place = windows(segs) + (jnp.zeros((1,), jnp.int32), segs)
    resid_in = inputs.astype(F32)
    norm_one = layer_norm(resid_in, ln1_gain, ln1_bias).astype(BF16)
    projected = dot(project, norm_one, NT).astype(BF16).reshape(3, width, rows)
    projected = exchange(projected, 1, 2)
    query_value, keys = projected[None, :2], projected[2:]
    heads_out, lse = attend_forward(query_value, keys, place)
    attended = exchange(heads_out[0], 1, 0)
    residual = resid_in + dot(attended, w_out, TN)
    norm_two = layer_norm(residual, ln2_gain, ln2_bias).astype(BF16)
    mlp_branch, norm_two_grad, *mlp_grads = feed_forward(norm_two, cotangent, up, down)
    up_sum, down_sum = reduce(jnp.stack(mlp_grads)).astype(F32)

    output, res_grad, branch_grad, norm_two_grads = middle(
        residual, cotangent, ln2_gain, [mlp_branch], [norm_two_grad]
    )
    out_grad = dot(attended, branch_grad, NN).astype(BF16)
    att_grad = exchange(dot(w_out, branch_grad, NT).astype(BF16), 0, 1)
    query_value_grad, key_grad = attend_backward(
        query_value, keys, heads_out, att_grad[None], lse, place
    )
    proj_grad = exchange(jnp.concatenate([query_value_grad[0], key_grad]), 2, 1)
    proj_grad = proj_grad.reshape(3 * width, rows)
    project_grad = dot(proj_grad, norm_one, NN).astype(BF16).reshape(3, width, width)
    attn_sum = reduce(jnp.concatenate([project_grad, out_grad[None]])).astype(F32)
    input_part, gain_one_grad, bias_one_grad = layer_norm_back(
        resid_in, ln1_gain, dot(proj_grad, project, TN)
    )
    in_grad = (res_grad + input_part).astype(BF16)
    norm_parts = jnp.concatenate([gain_one_grad, bias_one_grad, norm_two_grads[:2]])
    norm_sums = lax.dynamic_slice_in_dim(
        lax.psum(norm_parts, ("dp", "mp")), at_mp * (width // mp_size), width // mp_size, 1
    )
    return (
        output,
        in_grad,
        norm_sums[0],
        norm_sums[1],
        attn_sum[0].T,
        attn_sum[2].T,
        attn_sum[1].T,
        attn_sum[3],
        norm_sums[2],
        norm_sums[3],
        up_sum.T,
        down_sum,
    )


def shards(dp_size, mp_size, inputs, segments, *rest):
    if dp_size == 4 and mp_size == 8 and inputs.shape[0] == segments.shape[1]:
        return on_cube(inputs, segments, *rest)
    return on_any(mp_size, inputs, segments, *rest)


def solution(mesh):
    return jax.shard_map(
        functools.partial(shards, mesh.shape["dp"], mesh.shape["mp"]),
        mesh=mesh,
        in_specs=(
            P(("dp", "mp"), None),
            P("dp", None),
            P(),
            P(),
            P(None, "mp"),
            P(None, "mp"),
            P(None, "mp"),
            P("mp", None),
            P(),
            P(),
            P(None, "mp"),
            P("mp", None),
            P(("dp", "mp"), None),
        ),
        out_specs=(
            P(("dp", "mp"), None),
            P(("dp", "mp"), None),
            P("mp"),
            P("mp"),
            P(None, "mp"),
            P(None, "mp"),
            P(None, "mp"),
            P("mp", None),
            P("mp"),
            P("mp"),
            P(None, "mp"),
            P("mp", None),
        ),
        check_vma=False,
    )
```

```python
import functools
import math

import jax
import jax.numpy as jnp
from jax import lax
from jax.experimental import pallas as pl
from jax.experimental.pallas import tpu as pltpu
from jax.sharding import PartitionSpec as P

HEAD_DIM = 48
PAIR = 2 * HEAD_DIM
IMAGES = 4
TILE = 128
norm_eps = 1e-06
negative_fill = -1e30
SCALE = HEAD_DIM ** (-0.5)
SCALE_LOG2 = SCALE * math.log2(math.e)
BF16 = jnp.bfloat16
F32 = jnp.float32


def layer_norm(values, gain, bias):
    center = jnp.mean(values, axis=-1, keepdims=True)
    shifted = values - center
    spread = jnp.mean(shifted * shifted, axis=-1, keepdims=True)
    return shifted * lax.rsqrt(spread + norm_eps) * gain + bias


def layer_norm_back(values, gain, grad):
    shifted = values - jnp.mean(values, axis=-1, keepdims=True)
    scale = lax.rsqrt(jnp.mean(shifted * shifted, axis=-1, keepdims=True) + norm_eps)
    unit = shifted * scale
    scaled = grad * gain
    back = scale * (
        scaled
        - jnp.mean(scaled, axis=-1, keepdims=True)
        - unit * jnp.mean(scaled * unit, axis=-1, keepdims=True)
    )
    return back, jnp.sum(grad * unit, axis=0, keepdims=True), jnp.sum(grad, axis=0, keepdims=True)


def dot(left, right, dims):
    return lax.dot_general(left, right, (dims, ((), ())), preferred_element_type=F32)


NN = ((1,), (0,))
NT = ((1,), (1,))
TN = ((0,), (0,))


def window_kinds(tiles):
    return tuple(n for n in (2, 3, 4, 5, 6) if n < tiles) + (tiles,)


def image_rows(segs, length):
    row = lax.broadcasted_iota(jnp.int32, (TILE - PAIR, length), 0)
    here = row == segs
    one_hot = jnp.where(here, 1.0, 0.0).astype(BF16)
    fill = jnp.where(jnp.logical_or(here, row >= IMAGES), 0.0, negative_fill).astype(BF16)
    return one_hot, fill


def side_by_side(pair, extra):
    blank = jnp.zeros((HEAD_DIM, TILE), BF16)
    left = jnp.concatenate([pair[:HEAD_DIM], blank, extra], axis=0)
    right = jnp.concatenate([blank, pair[HEAD_DIM:], extra], axis=0)
    return jnp.concatenate([left, right], axis=1)


def pair_places(ref):
    cores, count = ref.shape[0], ref.shape[1]
    return [(core, top) for core in range(cores) for top in range(0, count, PAIR)]


def attend_forward_kernel(
    first_ref, kind_ref, flip_ref, segs_ref, qv_ref, k_ref, out_ref, lse_ref, hot_ref, keys_ref, vals_ref
):
    length = k_ref.shape[-1]
    at_q = flip_ref[0]
    places = pair_places(k_ref)
    one_hot, fill = image_rows(segs_ref[...], length)
    hot_ref[...] = one_hot
    for j, (core, top) in enumerate(places):
        rows = slice(top, top + PAIR)
        keys_ref[j] = jnp.concatenate([k_ref[core, rows, :], fill], axis=0).T
        vals_ref[j] = jnp.concatenate(
            [qv_ref[core, 1 - at_q, rows, :], jnp.ones((16, length), BF16)], axis=0
        )

    def block(b, carry):
        at = pl.ds(pl.multiple_of(b * TILE, TILE), TILE)
        first = pl.multiple_of(first_ref[b] * TILE, TILE)

        def variant(tiles):
            span = pl.ds(first, tiles * TILE)
            scores = [
                dot(
                    keys_ref[j, span, :],
                    side_by_side(qv_ref[core, at_q, top : top + PAIR, at], hot_ref[:, at]),
                    NN,
                )
                for j, (core, top) in enumerate(places)
            ]
            for j, (core, top) in enumerate(places):
                most = jnp.max(scores[j], axis=0, keepdims=True)
                expo = jnp.exp2((scores[j] - most) * SCALE_LOG2).astype(BF16)
                mixed = dot(vals_ref[j, :, span], expo, NN)
                total = mixed[PAIR : PAIR + 1, :]
                inverse = 1.0 / total
                out_ref[core, top : top + HEAD_DIM, at] = (
                    mixed[:HEAD_DIM, :TILE] * inverse[:, :TILE]
                ).astype(BF16)
                out_ref[core, top + HEAD_DIM : top + PAIR, at] = (
                    mixed[HEAD_DIM:PAIR, TILE:] * inverse[:, TILE:]
                ).astype(BF16)
                lse_ref[j, pl.ds(b, 1), :] = most * SCALE_LOG2 + jnp.log2(total)

        for tiles in window_kinds(length // TILE):
            pl.when(kind_ref[b] == tiles)(functools.partial(variant, tiles))
        return carry

    lax.fori_loop(0, length // TILE, block, 0)


def attend_backward_kernel(
    first_ref,
    kind_ref,
    flip_ref,
    segs_ref,
    qv_ref,
    k_ref,
    att_ref,
    grad_ref,
    lse_ref,
    dqv_ref,
    dk_ref,
    hot_ref,
    keys_ref,
    vals_ref,
    queries_ref,
    grads_ref,
    key_sum_ref,
    val_sum_ref,
):
    length = k_ref.shape[-1]
    at_q = flip_ref[0]
    places = pair_places(k_ref)
    one_hot, fill = image_rows(segs_ref[...], length)
    hot_ref[...] = one_hot
    pad = jnp.zeros((TILE - PAIR, length), BF16)
    for j, (core, top) in enumerate(places):
        rows = slice(top, top + PAIR)
        keys_ref[j] = jnp.concatenate([k_ref[core, rows, :], fill], axis=0).T
        vals_ref[j] = jnp.concatenate([qv_ref[core, 1 - at_q, rows, :], pad], axis=0).T
        queries_ref[j] = jnp.concatenate([qv_ref[core, at_q, rows, :], pad], axis=0).T
        grads_ref[j] = jnp.concatenate([grad_ref[core, rows, :], pad], axis=0).T
    key_sum_ref[...] = jnp.zeros(key_sum_ref.shape, F32)
    val_sum_ref[...] = jnp.zeros(val_sum_ref.shape, F32)
    no_rows = jnp.zeros((TILE - PAIR, TILE), BF16)
    lane = lax.broadcasted_iota(jnp.int32, (TILE, TILE), 1)
    in_first = lane < HEAD_DIM

    def stacked(both):
        blank = jnp.zeros_like(both)
        return jnp.concatenate(
            [jnp.where(in_first, both, blank), jnp.where(in_first, blank, both)], axis=0
        )

    def block(b, carry):
        at = pl.ds(pl.multiple_of(b * TILE, TILE), TILE)
        first = pl.multiple_of(first_ref[b] * TILE, TILE)

        def variant(tiles):
            span = pl.ds(first, tiles * TILE)
            scores = [
                dot(
                    keys_ref[j, span, :],
                    side_by_side(qv_ref[core, at_q, top : top + PAIR, at], hot_ref[:, at]),
                    NN,
                )
                for j, (core, top) in enumerate(places)
            ]
            prob_grads = [
                dot(
                    vals_ref[j, span, :],
                    side_by_side(grad_ref[core, top : top + PAIR, at], no_rows),
                    NN,
                )
                for j, (core, top) in enumerate(places)
            ]
            for j, (core, top) in enumerate(places):
                rows = slice(top, top + PAIR)
                agree = grad_ref[core, rows, at].astype(F32) * att_ref[core, rows, at].astype(F32)
                delta = jnp.concatenate(
                    [
                        jnp.sum(agree[:HEAD_DIM], axis=0, keepdims=True),
                        jnp.sum(agree[HEAD_DIM:], axis=0, keepdims=True),
                    ],
                    axis=1,
                )
                probs = jnp.exp2(scores[j] * SCALE_LOG2 - lse_ref[j, pl.ds(b, 1), :])
                score_grad = (probs * (prob_grads[j] - delta)).astype(BF16)
                val_sum_ref[j, span, :] += dot(
                    probs.astype(BF16), stacked(grads_ref[j, at, :]), NN
                )
                key_sum_ref[j, span, :] += dot(score_grad, stacked(queries_ref[j, at, :]), NN)
                query_grad = dot(k_ref[core, rows, span], score_grad, NN) * SCALE
                dqv_ref[core, at_q, top : top + HEAD_DIM, at] = query_grad[
                    :HEAD_DIM, :TILE
                ].astype(BF16)
                dqv_ref[core, at_q, top + HEAD_DIM : top + PAIR, at] = query_grad[
                    HEAD_DIM:, TILE:
                ].astype(BF16)

        for tiles in window_kinds(length // TILE):
            pl.when(kind_ref[b] == tiles)(functools.partial(variant, tiles))
        return carry

    lax.fori_loop(0, length // TILE, block, 0)
    for j, (core, top) in enumerate(places):
        rows = slice(top, top + PAIR)
        dk_ref[core, rows, :] = (key_sum_ref[j] * SCALE).T[:PAIR].astype(BF16)
        dqv_ref[core, 1 - at_q, rows, :] = val_sum_ref[j].T[:PAIR].astype(BF16)


def windows(segs):
    length = segs.shape[0]
    tiles = length // TILE
    by_tile = segs.reshape(tiles, TILE)
    begin = jnp.sum(segs[None, :] < by_tile[:, :1], axis=1)
    end = jnp.sum(segs[None, :] <= by_tile[:, -1:], axis=1)
    first = begin // TILE
    need = (end + TILE - 1) // TILE - first
    kinds = jnp.asarray(window_kinds(tiles), jnp.int32)
    kind = jnp.min(jnp.where(kinds[None, :] >= need[:, None], kinds[None, :], tiles), axis=1)
    return jnp.minimum(first, tiles - kind).astype(jnp.int32), kind.astype(jnp.int32)


def attention_specs(keys):
    cores, count, length = keys.shape
    pairs = cores * count // PAIR
    step = pairs if pairs <= 4 else 4
    part = count * step // pairs
    rows = pl.BlockSpec((cores, part, length), lambda i, *_: (0, i, 0))
    two = pl.BlockSpec((cores, 2, part, length), lambda i, *_: (0, 0, i, 0))
    segs = pl.BlockSpec((1, length), lambda i, *_: (0, 0))
    lse = pl.BlockSpec((step, length // TILE, 2 * TILE), lambda i, *_: (i, 0, 0))
    return pairs, step, rows, two, segs, lse


def attend_forward(query_value, keys, place):
    first, kind, flip, segs = place
    length = segs.shape[0]
    pairs, step, rows, two, segs_spec, lse = attention_specs(keys)
    return pl.pallas_call(
        attend_forward_kernel,
        grid_spec=pltpu.PrefetchScalarGridSpec(
            num_scalar_prefetch=3,
            grid=(pairs // step,),
            in_specs=[segs_spec, two, rows],
            out_specs=[rows, lse],
            scratch_shapes=[
                pltpu.VMEM((TILE - PAIR, length), BF16),
                pltpu.VMEM((step, length, TILE), BF16),
                pltpu.VMEM((step, PAIR + 16, length), BF16),
            ],
        ),
        out_shape=[
            jax.ShapeDtypeStruct(keys.shape, BF16),
            jax.ShapeDtypeStruct((pairs, length // TILE, 2 * TILE), F32),
        ],
        compiler_params=pltpu.CompilerParams(vmem_limit_bytes=40 << 20),
        name="attend_forward",
    )(first, kind, flip, segs[None, :], query_value, keys)


def attend_backward(query_value, keys, attended, grad, lse, place):
    first, kind, flip, segs = place
    length = segs.shape[0]
    pairs, step, rows, two, segs_spec, lse_spec = attention_specs(keys)
    wide = pltpu.VMEM((step, length, TILE), BF16)
    total = pltpu.VMEM((step, length, TILE), F32)
    return pl.pallas_call(
        attend_backward_kernel,
        grid_spec=pltpu.PrefetchScalarGridSpec(
            num_scalar_prefetch=3,
            grid=(pairs // step,),
            in_specs=[segs_spec, two, rows, rows, rows, lse_spec],
            out_specs=[two, rows],
            scratch_shapes=[
                pltpu.VMEM((TILE - PAIR, length), BF16),
                wide,
                wide,
                wide,
                wide,
                total,
                total,
            ],
        ),
        out_shape=[
            jax.ShapeDtypeStruct(query_value.shape, BF16),
            jax.ShapeDtypeStruct(keys.shape, BF16),
        ],
        compiler_params=pltpu.CompilerParams(vmem_limit_bytes=40 << 20),
        name="attend_backward",
    )(first, kind, flip, segs[None, :], query_value, keys, attended, grad, lse)


def gelu_parts(values):
    below = 0.5 * (1.0 + lax.erf(values * (0.5 ** 0.5)))
    density = jnp.exp(values * values * -0.5) * ((2.0 * math.pi) ** -0.5)
    return values * below, below + values * density


def feed_forward_kernel(norm_ref, cot_ref, up_ref, down_ref, *refs):
    *earlier, mlp_ref, back_ref, up_grad_ref, down_grad_ref, sum_ref, act_ref, pre_ref = refs
    rows = norm_ref.shape[0]
    chunk = min(rows, 256)

    @pl.when(pl.program_id(0) == 0)
    def _():
        sum_ref[...] = jnp.zeros(sum_ref.shape, F32)
        back_ref[...] = jnp.zeros(back_ref.shape, F32)

    for start in range(0, rows, chunk):
        at = slice(start, start + chunk)
        pre_act = dot(norm_ref[at, :], up_ref[...], NT)
        act_grad = dot(cot_ref[at, :], down_ref[...], NT)
        activation, slope = gelu_parts(pre_act)
        activation = activation.astype(BF16)
        pre_grad = (act_grad * slope).astype(BF16)
        act_ref[at, :] = activation
        pre_ref[at, :] = pre_grad
        sum_ref[at, :] += dot(activation, down_ref[...], NN)
        back_ref[at, :] += dot(pre_grad, up_ref[...], NN)
    up_grad = dot(pre_ref[...], norm_ref[...], TN)
    down_grad = dot(act_ref[...], cot_ref[...], TN)
    if earlier:
        up_grad = up_grad + earlier[0][...].astype(F32)
        down_grad = down_grad + earlier[1][...].astype(F32)
    up_grad_ref[...] = up_grad.astype(BF16)
    down_grad_ref[...] = down_grad.astype(BF16)

    @pl.when(pl.program_id(0) == pl.num_programs(0) - 1)
    def _():
        mlp_ref[...] = sum_ref[...].astype(mlp_ref.dtype)


def feed_forward(norm, cot, up, down, earlier=(), kind=F32):
    rows, width = norm.shape
    hidden = up.shape[0]
    part = 512 if hidden % 512 == 0 else hidden
    whole = pl.BlockSpec((rows, width), lambda i: (0, 0))
    block = pl.BlockSpec((part, width), lambda i: (i, 0))
    grads = jax.ShapeDtypeStruct((hidden, width), BF16)
    return pl.pallas_call(
        feed_forward_kernel,
        grid=(hidden // part,),
        in_specs=[whole, whole, block, block] + [block] * len(earlier),
        out_specs=[whole, whole, block, block],
        out_shape=[
            jax.ShapeDtypeStruct((rows, width), kind),
            jax.ShapeDtypeStruct((rows, width), F32),
            grads,
            grads,
        ],
        scratch_shapes=[
            pltpu.VMEM((rows, width), F32),
            pltpu.VMEM((rows, part), BF16),
            pltpu.VMEM((rows, part), BF16),
        ],
        compiler_params=pltpu.CompilerParams(vmem_limit_bytes=58 << 20),
        name="feed_forward",
    )(norm, cot, up, down, *earlier)


def middle_kernel(parts, residual_ref, cot_ref, gain_ref, *refs):
    mlp_refs, back_refs = refs[:parts], refs[parts : 2 * parts]
    output_ref, res_grad_ref, branch_ref, norm_grad_ref = refs[2 * parts :]

    @pl.when(pl.program_id(0) == 0)
    def _():
        norm_grad_ref[...] = jnp.zeros(norm_grad_ref.shape, F32)

    residual = residual_ref[...]
    output_ref[...] = sum([ref[...].astype(F32) for ref in mlp_refs], residual).astype(BF16)
    grad = functools.reduce(jnp.add, [ref[...] for ref in back_refs])
    back, gain_grad, bias_grad = layer_norm_back(residual, gain_ref[...], grad)
    res_grad = cot_ref[...].astype(F32) + back
    res_grad_ref[...] = res_grad
    branch_ref[...] = res_grad.astype(BF16)
    norm_grad_ref[0:1, :] += gain_grad
    norm_grad_ref[1:2, :] += bias_grad


def middle(residual, cot, gain, mlps, backs):
    rows, width = residual.shape
    parts = len(mlps)
    step = 256
    block = pl.BlockSpec((step, width), lambda i: (i, 0))
    sums = jax.ShapeDtypeStruct((rows, width), F32)
    low = jax.ShapeDtypeStruct((rows, width), BF16)
    return pl.pallas_call(
        functools.partial(middle_kernel, parts),
        grid=(rows // step,),
        in_specs=[block, block, pl.BlockSpec((1, width), lambda i: (0, 0))] + [block] * (2 * parts),
        out_specs=[block, block, block, pl.BlockSpec((8, width), lambda i: (0, 0))],
        out_shape=[low, sums, low, jax.ShapeDtypeStruct((8, width), F32)],
        compiler_params=pltpu.CompilerParams(vmem_limit_bytes=40 << 20),
        name="middle",
    )(residual, cot, gain[None, :], *mlps, *backs)


def add(*terms):
    return functools.reduce(jnp.add, [item.astype(F32) for item in terms]).astype(BF16)


def swap(values, axis):
    name, size, mask = {
        "core": ("dp", 4, 1),
        "y": ("dp", 4, 2),
        "x": ("mp", 8, 1),
        "z1": ("mp", 8, 2),
        "z2": ("mp", 8, 4),
        "z3": ("mp", 8, 6),
    }[axis]
    return lax.ppermute(values, name, [(i, i ^ mask) for i in range(size)])


def order(at, mine, other):
    return jnp.where(at == 0, jnp.stack([mine, other]), jnp.stack([other, mine]))


class Line:
    def __init__(self):
        self.last = ()

    def __call__(self, step, *args):
        args, _ = lax.optimization_barrier((args, self.last))
        result = step(*args)
        self.last = tuple(jax.tree.leaves(result))
        return result


def on_cube(
    inputs,
    segments,
    ln1_gain,
    ln1_bias,
    w_query,
    w_key,
    w_value,
    w_output,
    ln2_gain,
    ln2_bias,
    w_up,
    w_down,
    cotangent,
):
    rows, width = inputs.shape
    local = w_query.shape[1]
    at_dp, at_mp = lax.axis_index("dp"), lax.axis_index("mp")
    at_y, at_core = at_dp // 2, at_dp % 2
    line = Line()

    def pick(values, at):
        return lax.dynamic_index_in_dim(values, at, 0, keepdims=False)

    def cut_attention(query, key, value, out):
        kinds = jnp.stack([query.T, key.T, value.T, out]).reshape(2, 2, 2, HEAD_DIM, width)
        return pick(kinds.transpose(0, 2, 1, 3, 4).reshape(4, 2, HEAD_DIM, width), at_dp)

    def cut_mlp(up, down):
        pieces = jnp.stack([up.T, down]).reshape(2, 4, -1, width)
        return lax.dynamic_index_in_dim(pieces, at_dp, 1, keepdims=False)

    def join(*parts):
        return jnp.concatenate(parts, 0)

    along_z = ("z2", "z1", "z3")
    attn_piece = line(cut_attention, w_query, w_key, w_value, w_output)
    attn_z = [swap(attn_piece, axis) for axis in along_z]
    mlp_piece = line(cut_mlp, w_up, w_down)
    mlp_z = [swap(mlp_piece, axis) for axis in along_z]

    def begin(rows_in):
        return layer_norm(rows_in.astype(F32), ln1_gain, ln1_bias).astype(BF16)

    norm_one = line(begin, inputs)
    segs = pick(segments, at_mp)
    place = windows(segs) + (at_y.reshape(1), segs)
    place = line(lambda item: item, place)

    near_z = line(lambda *parts: jnp.stack(parts[:4]), attn_piece, *attn_z, mlp_z[1])
    near_got = swap(near_z, "y")
    far_z = swap(near_z, "x")
    near_y = line(lambda *parts: jnp.stack(parts[:2]), near_z, near_got, far_z, mlp_z[0])
    near_got = swap(near_y, "core")
    far_got = swap(far_z, "y")

    def both_cores(mine, other):
        query_value, key_out = [jnp.stack([mine[:, :, i], other[:, :, i]]) for i in (0, 1)]
        key, out = [
            lax.dynamic_index_in_dim(key_out, at, 1, keepdims=False).reshape(-1, width)
            for at in (at_y, 1 - at_y)
        ]
        return query_value.reshape(-1, width), key, out

    def project(weights, norm):
        query_value = dot(weights[0], norm, NT).astype(BF16).reshape(2, 2, -1, rows)
        return query_value, dot(weights[1], norm, NT).astype(BF16).reshape(2, -1, rows)

    def attend(query_value, keys):
        return attend_forward(query_value, keys, place)

    def branch(base, attended, weights):
        return base + dot(attended.reshape(-1, rows), weights[2], TN)

    def mlp_along_z(*parts):
        return [jnp.concatenate([item[i] for item in parts], 0) for i in (0, 1)]

    def mlp_second(up, up_got, down, down_got):
        return jnp.concatenate([up, up_got], 0), jnp.stack([down, down_got])

    near_w = line(both_cores, near_y, near_got)
    near = line(project, near_w, norm_one)
    up, down = line(mlp_along_z, mlp_piece, *mlp_z)
    up_got, down_got = swap(up, "x"), swap(down, "y")
    near += tuple(line(attend, *near))

    far_y = line(lambda *parts: jnp.stack(parts), far_z, far_got)
    far_got = swap(far_y, "core")
    up, down = line(mlp_second, up, up_got, down, down_got)
    up_got, down_got = swap(up, "y"), swap(down, "x")
    residual = line(branch, inputs.astype(F32), near[2], near_w)
    far_w = line(both_cores, far_y, far_got)
    far = line(project, far_w, norm_one)
    far += tuple(line(attend, *far))

    def second_norm(residual, attended, weights):
        residual = branch(residual, attended, weights)
        return residual, layer_norm(residual, ln2_gain, ln2_bias).astype(BF16)

    cot_other = swap(cotangent, "core")
    far_attended, cot_other = lax.optimization_barrier((far[2], cot_other))
    residual, norm_two = line(second_norm, residual, far_attended, far_w)
    norm_two_other = swap(norm_two, "core")

    def mlp_last(up, up_got, down, down_got):
        return jnp.concatenate([up, up_got], 0), jnp.concatenate([down, down_got], 1).reshape(-1, width)

    up, down = line(mlp_last, up, up_got, down, down_got)
    mlp_b, back_b, *grads = line(
        lambda *args: feed_forward(*args, kind=BF16), norm_two_other, cot_other, up, down
    )
    mlp_b, back_b = swap(mlp_b, "core"), swap(back_b, "core")
    mlp_a, back_a, up_grad, down_grad = line(feed_forward, norm_two, cotangent, up, down, grads)

    def before_attention(attended, weights, grad):
        att_grad = dot(weights[2], grad, NT).astype(BF16).reshape(attended.shape)
        return att_grad, dot(attended.reshape(-1, rows), grad, NN).astype(BF16)


    quarter = up.shape[0] // 4

    def up_sum_of(terms, low, high):
        return add(*[item[low:high] for item in terms])

    def down_sum_of(terms, y, x, low=0, high=quarter):
        whole = terms[0].reshape(2, 2, quarter, width)[y, x, low:high]
        return add(whole, *[item.reshape(-1, quarter, width)[y, low:high] for item in terms[1:]])

    def mlp_sum_first(up_terms, down_terms):
        return (
            up_sum_of(up_terms, 2 * quarter, 4 * quarter),
            jnp.stack([down_sum_of(down_terms, y, 1) for y in (0, 1)]),
        )

    up_terms, down_terms = (up_grad,), (down_grad,)
    sends = line(mlp_sum_first, up_terms, down_terms)
    up_terms += (swap(sends[0], "y"),)
    down_terms += (swap(sends[1], "x"),)

    def attend_back(saved, att_grad):
        return attend_backward(*saved[:3], att_grad, saved[3], place)

    def weight_grads(query_value_grad, key_grad, out_grad, norm):
        query_value = dot(query_value_grad.reshape(-1, rows), norm, NN).astype(BF16)
        keys = dot(key_grad.reshape(-1, rows), norm, NN).astype(BF16)
        sums = (
            query_value.reshape(2, 2, -1, width),
            keys.reshape(2, -1, width),
            out_grad.reshape(2, -1, width),
        )
        return sums, [item[1] for item in sums]

    def project_back(grads, weights):
        return dot(grads[0].reshape(-1, rows), weights[0], TN) + dot(
            grads[1].reshape(-1, rows), weights[1], TN
        )

    def attn_terms_of(mine, got, at):
        terms = [(mine[0][0, at], mine[1][0], mine[2][0]), (got[0][at], got[1], got[2])]
        first = at_y == at
        return [
            [item[0] for item in terms],
            [jnp.where(first, item[1], item[2]) for item in terms],
        ]

    def sum_other_y(mine, got):
        return jnp.stack([add(*terms) for terms in attn_terms_of(mine, got, 1)])

    def sum_this_y(mine, got, from_y):
        terms = attn_terms_of(mine, got, 0)
        return jnp.stack([add(*terms[i], from_y[i]) for i in (0, 1)])

    output, res_grad, branch_grad, norm_two_grads = line(
        middle, residual, cotangent, ln2_gain, [mlp_a, mlp_b], [back_a, back_b]
    )
    far_att, far_out = line(before_attention, far[2], far_w, branch_grad)
    far_grads = line(attend_back, far, far_att)
    norm_one_grad = line(project_back, far_grads, far_w)
    far_mine, sends = line(weight_grads, *far_grads, far_out, norm_one)
    far_got = [swap(item, "core") for item in sends]
    def mlp_sum_second(up_terms, down_terms):
        return up_sum_of(up_terms, quarter, 2 * quarter), down_sum_of(down_terms, 1, 0)

    sends = line(mlp_sum_second, up_terms, down_terms)
    up_terms += (swap(sends[0], "x"),)
    down_y = swap(sends[1], "y")

    near_att, near_out = line(before_attention, near[2], near_w, branch_grad)
    far_y = swap(line(sum_other_y, far_mine, far_got), "y")

    part = quarter // 4

    def mlp_sum_of_z(up_terms, down_terms, down_y, low, high):
        low, high = low * part, high * part
        return jnp.stack(
            [
                up_sum_of(up_terms, low, high),
                down_sum_of(down_terms + (jnp.stack([down_y, down_y]),), 0, 0, low, high),
            ]
        )

    mlp_terms = (up_terms, down_terms, down_y)
    near_grads = line(attend_back, near, near_att)
    mlp_z1 = swap(line(lambda *terms: mlp_sum_of_z(*terms, 2, 4), *mlp_terms), "z1")
    near_mine, sends = line(weight_grads, *near_grads, near_out, norm_one)
    near_got = [swap(item, "core") for item in sends]
    far_x = swap(line(sum_this_y, far_mine, far_got, far_y), "x")
    near_y = swap(line(sum_other_y, near_mine, near_got), "y")

    def add_project_back(norm_one_grad, grads, weights):
        return norm_one_grad + project_back(grads, weights)

    def finish(norm_one_grad):
        input_part, gain_grad, bias_grad = layer_norm_back(
            inputs.astype(F32), ln1_gain, norm_one_grad
        )
        parts = jnp.concatenate([gain_grad, bias_grad, norm_two_grads[:2]])
        return parts, (res_grad + input_part).astype(BF16)

    norm_one_grad = line(add_project_back, norm_one_grad, near_grads, near_w)
    mlp_send = line(
        lambda got, *terms: add(mlp_sum_of_z(*terms, 1, 2), got[:, part:]), mlp_z1, *mlp_terms
    )
    mlp_z2 = swap(mlp_send, "z2")
    norm_sums, in_grad = line(finish, norm_one_grad)

    def attn_sum_z(mine, got, from_y, from_x):
        from_x = from_x.reshape(2, -1, width)
        whole = sum_this_y(mine, got, from_y).astype(F32) + from_x
        return whole[:, : 2 * HEAD_DIM].astype(BF16), whole[:, 2 * HEAD_DIM :].astype(BF16)

    attn_mine, send = line(attn_sum_z, near_mine, near_got, near_y, far_x)
    attn_z1 = swap(send, "z1")
    mlp_sum = line(
        lambda got, other, *terms: add(mlp_sum_of_z(*terms, 0, 1), got[:, :part], other),
        mlp_z1,
        mlp_z2,
        *mlp_terms,
    )
    mlp_got = swap(mlp_sum, "y")
    got = swap(norm_sums, "core")

    def in_order(piece, y, core, both):
        return order(at_core, order(at_y, piece, y), order(at_y, core, both))

    norm_sums = line(jnp.add, norm_sums, got)
    got = swap(norm_sums, "y")
    attn_send = line(lambda mine, got: add(mine[:, HEAD_DIM:], got[:, HEAD_DIM:]), attn_mine, attn_z1)
    attn_z2 = swap(attn_send, "z2")
    mlp_sum = line(lambda mine, got, _: order(at_y, mine, got), mlp_sum, mlp_got, attn_z2)
    mlp_got = swap(mlp_sum, "core")
    norm_sums = line(jnp.add, norm_sums, got)
    got = swap(norm_sums, "x")
    attn_sum = line(
        lambda mine, got, other: add(mine[:, :HEAD_DIM], got[:, :HEAD_DIM], other),
        attn_mine,
        attn_z1,
        attn_z2,
    )
    attn_got = [
        lax.ppermute(attn_sum, "dp", [(i, i ^ mask) for i in range(4)]) for mask in (2, 1, 3)
    ]
    norm_sums = line(jnp.add, norm_sums, got)
    got = swap(norm_sums, "z1")
    mlp_sum = line(functools.partial(order, at_core), mlp_sum, mlp_got)
    up_sum, down_sum = line(
        lambda item: tuple(item.transpose(2, 1, 0, 3, 4).reshape(2, -1, width).astype(F32)), mlp_sum
    )
    norm_sums = line(jnp.add, norm_sums, got)
    got = swap(norm_sums, "z2")
    up_sum = line(jnp.transpose, up_sum)
    attn_sum = line(in_order, attn_sum, *attn_got)
    norm_sums = line(jnp.add, norm_sums, got)
    norm_sums = lax.dynamic_slice_in_dim(norm_sums, at_mp * (width // 8), width // 8, 1)
    attn_sum = attn_sum.transpose(1, 2, 0, 3, 4).reshape(4, local, width).astype(F32)
    return (
        output,
        in_grad,
        norm_sums[0],
        norm_sums[1],
        attn_sum[0].T,
        attn_sum[1].T,
        attn_sum[2].T,
        attn_sum[3],
        norm_sums[2],
        norm_sums[3],
        up_sum,
        down_sum,
    )


def on_any(
    mp_size,
    inputs,
    segments,
    ln1_gain,
    ln1_bias,
    w_query,
    w_key,
    w_value,
    w_output,
    ln2_gain,
    ln2_bias,
    w_up,
    w_down,
    cotangent,
):
    rows, width = inputs.shape
    seq_length = segments.shape[1]
    shared_by = seq_length // rows
    at_mp = lax.axis_index("mp")
    groups = [[start + i for i in range(shared_by)] for start in range(0, mp_size, shared_by)]

    def exchange(values, split, join):
        if shared_by == 1:
            return values
        return lax.all_to_all(values, "mp", split, join, axis_index_groups=groups, tiled=True)

    def gather(parts):
        return lax.all_gather(parts, "mp", axis=1, tiled=True)

    def reduce(parts):
        return lax.psum(lax.psum_scatter(parts, "mp", scatter_dimension=1, tiled=True), "dp")

    attn_w = gather(jnp.stack([w_query.T, w_value.T, w_key.T, w_output]))
    up, down = gather(jnp.stack([w_up.T, w_down]))
    project, w_out = attn_w[:3].reshape(3 * width, width), attn_w[3]

    segs = lax.dynamic_index_in_dim(segments, at_mp // shared_by, 0, keepdims=False)
    place = windows(segs) + (jnp.zeros((1,), jnp.int32), segs)
    resid_in = inputs.astype(F32)
    norm_one = layer_norm(resid_in, ln1_gain, ln1_bias).astype(BF16)
    projected = dot(project, norm_one, NT).astype(BF16).reshape(3, width, rows)
    projected = exchange(projected, 1, 2)
    query_value, keys = projected[None, :2], projected[2:]
    heads_out, lse = attend_forward(query_value, keys, place)
    attended = exchange(heads_out[0], 1, 0)
    residual = resid_in + dot(attended, w_out, TN)
    norm_two = layer_norm(residual, ln2_gain, ln2_bias).astype(BF16)
    mlp_branch, norm_two_grad, *mlp_grads = feed_forward(norm_two, cotangent, up, down)
    up_sum, down_sum = reduce(jnp.stack(mlp_grads)).astype(F32)

    output, res_grad, branch_grad, norm_two_grads = middle(
        residual, cotangent, ln2_gain, [mlp_branch], [norm_two_grad]
    )
    out_grad = dot(attended, branch_grad, NN).astype(BF16)
    att_grad = exchange(dot(w_out, branch_grad, NT).astype(BF16), 0, 1)
    query_value_grad, key_grad = attend_backward(
        query_value, keys, heads_out, att_grad[None], lse, place
    )
    proj_grad = exchange(jnp.concatenate([query_value_grad[0], key_grad]), 2, 1)
    proj_grad = proj_grad.reshape(3 * width, rows)
    project_grad = dot(proj_grad, norm_one, NN).astype(BF16).reshape(3, width, width)
    attn_sum = reduce(jnp.concatenate([project_grad, out_grad[None]])).astype(F32)
    input_part, gain_one_grad, bias_one_grad = layer_norm_back(
        resid_in, ln1_gain, dot(proj_grad, project, TN)
    )
    in_grad = (res_grad + input_part).astype(BF16)
    norm_parts = jnp.concatenate([gain_one_grad, bias_one_grad, norm_two_grads[:2]])
    norm_sums = lax.dynamic_slice_in_dim(
        lax.psum(norm_parts, ("dp", "mp")), at_mp * (width // mp_size), width // mp_size, 1
    )
    return (
        output,
        in_grad,
        norm_sums[0],
        norm_sums[1],
        attn_sum[0].T,
        attn_sum[2].T,
        attn_sum[1].T,
        attn_sum[3],
        norm_sums[2],
        norm_sums[3],
        up_sum.T,
        down_sum,
    )


def shards(dp_size, mp_size, inputs, segments, *rest):
    if dp_size == 4 and mp_size == 8 and inputs.shape[0] == segments.shape[1]:
        return on_cube(inputs, segments, *rest)
    return on_any(mp_size, inputs, segments, *rest)


def solution(mesh):
    return jax.shard_map(
        functools.partial(shards, mesh.shape["dp"], mesh.shape["mp"]),
        mesh=mesh,
        in_specs=(
            P(("dp", "mp"), None),
            P("dp", None),
            P(),
            P(),
            P(None, "mp"),
            P(None, "mp"),
            P(None, "mp"),
            P("mp", None),
            P(),
            P(),
            P(None, "mp"),
            P("mp", None),
            P(("dp", "mp"), None),
        ),
        out_specs=(
            P(("dp", "mp"), None),
            P(("dp", "mp"), None),
            P("mp"),
            P("mp"),
            P(None, "mp"),
            P(None, "mp"),
            P(None, "mp"),
            P("mp", None),
            P("mp"),
            P("mp"),
            P(None, "mp"),
            P("mp", None),
        ),
        check_vma=False,
    )
```

```python
import functools
import math

import jax
import jax.numpy as jnp
from jax import lax
from jax.experimental import pallas as pl
from jax.experimental.pallas import tpu as pltpu
from jax.sharding import PartitionSpec as P

HEAD_DIM = 48
PAIR = 2 * HEAD_DIM
IMAGES = 4
TILE = 128
norm_eps = 1e-06
negative_fill = -1e30
SCALE = HEAD_DIM ** (-0.5)
SCALE_LOG2 = SCALE * math.log2(math.e)
BF16 = jnp.bfloat16
F32 = jnp.float32


def layer_norm(values, gain, bias):
    center = jnp.mean(values, axis=-1, keepdims=True)
    shifted = values - center
    spread = jnp.mean(shifted * shifted, axis=-1, keepdims=True)
    return shifted * lax.rsqrt(spread + norm_eps) * gain + bias


def layer_norm_back(values, gain, grad):
    shifted = values - jnp.mean(values, axis=-1, keepdims=True)
    scale = lax.rsqrt(jnp.mean(shifted * shifted, axis=-1, keepdims=True) + norm_eps)
    unit = shifted * scale
    scaled = grad * gain
    back = scale * (
        scaled
        - jnp.mean(scaled, axis=-1, keepdims=True)
        - unit * jnp.mean(scaled * unit, axis=-1, keepdims=True)
    )
    return back, jnp.sum(grad * unit, axis=0, keepdims=True), jnp.sum(grad, axis=0, keepdims=True)


def dot(left, right, dims):
    return lax.dot_general(left, right, (dims, ((), ())), preferred_element_type=F32)


NN = ((1,), (0,))
NT = ((1,), (1,))
TN = ((0,), (0,))


def window_kinds(tiles):
    return tuple(n for n in (2, 3, 4, 5, 6, 7) if n < tiles) + (tiles,)


def image_rows(segs, length):
    row = lax.broadcasted_iota(jnp.int32, (TILE - PAIR, length), 0)
    here = row == segs
    one_hot = jnp.where(here, 1.0, 0.0).astype(BF16)
    fill = jnp.where(jnp.logical_or(here, row >= IMAGES), 0.0, negative_fill).astype(BF16)
    return one_hot, fill


def side_by_side(pair, extra):
    blank = jnp.zeros((HEAD_DIM, TILE), BF16)
    left = jnp.concatenate([pair[:HEAD_DIM], blank, extra], axis=0)
    right = jnp.concatenate([blank, pair[HEAD_DIM:], extra], axis=0)
    return jnp.concatenate([left, right], axis=1)


def pair_places(ref):
    cores, count = ref.shape[0], ref.shape[1]
    return [(core, top) for core in range(cores) for top in range(0, count, PAIR)]


def attend_forward_kernel(
    first_ref, kind_ref, flip_ref, segs_ref, qv_ref, k_ref, out_ref, lse_ref, hot_ref, keys_ref, vals_ref
):
    length = k_ref.shape[-1]
    at_q = flip_ref[0]
    places = pair_places(k_ref)
    one_hot, fill = image_rows(segs_ref[...], length)
    hot_ref[...] = one_hot
    for j, (core, top) in enumerate(places):
        rows = slice(top, top + PAIR)
        keys_ref[j] = jnp.concatenate([k_ref[core, rows, :], fill], axis=0).T
        vals_ref[j] = jnp.concatenate(
            [qv_ref[core, 1 - at_q, rows, :], jnp.ones((16, length), BF16)], axis=0
        )

    def block(b, carry):
        at = pl.ds(pl.multiple_of(b * TILE, TILE), TILE)
        first = pl.multiple_of(first_ref[b] * TILE, TILE)

        def variant(tiles):
            span = pl.ds(first, tiles * TILE)
            scores = [
                dot(
                    keys_ref[j, span, :],
                    side_by_side(qv_ref[core, at_q, top : top + PAIR, at], hot_ref[:, at]),
                    NN,
                )
                for j, (core, top) in enumerate(places)
            ]
            for j, (core, top) in enumerate(places):
                most = jnp.max(scores[j], axis=0, keepdims=True)
                expo = jnp.exp2((scores[j] - most) * SCALE_LOG2).astype(BF16)
                mixed = dot(vals_ref[j, :, span], expo, NN)
                total = mixed[PAIR : PAIR + 1, :]
                inverse = 1.0 / total
                out_ref[core, top : top + HEAD_DIM, at] = (
                    mixed[:HEAD_DIM, :TILE] * inverse[:, :TILE]
                ).astype(BF16)
                out_ref[core, top + HEAD_DIM : top + PAIR, at] = (
                    mixed[HEAD_DIM:PAIR, TILE:] * inverse[:, TILE:]
                ).astype(BF16)
                lse_ref[j, pl.ds(b, 1), :] = most * SCALE_LOG2 + jnp.log2(total)

        for tiles in window_kinds(length // TILE):
            pl.when(kind_ref[b] == tiles)(functools.partial(variant, tiles))
        return carry

    lax.fori_loop(0, length // TILE, block, 0)


def attend_backward_kernel(
    first_ref,
    kind_ref,
    flip_ref,
    segs_ref,
    qv_ref,
    k_ref,
    att_ref,
    grad_ref,
    lse_ref,
    dqv_ref,
    dk_ref,
    hot_ref,
    keys_ref,
    vals_ref,
    queries_ref,
    grads_ref,
    key_sum_ref,
    val_sum_ref,
):
    length = k_ref.shape[-1]
    at_q = flip_ref[0]
    places = pair_places(k_ref)
    one_hot, fill = image_rows(segs_ref[...], length)
    hot_ref[...] = one_hot
    pad = jnp.zeros((TILE - PAIR, length), BF16)
    for j, (core, top) in enumerate(places):
        rows = slice(top, top + PAIR)
        keys_ref[j] = jnp.concatenate([k_ref[core, rows, :], fill], axis=0).T
        vals_ref[j] = jnp.concatenate([qv_ref[core, 1 - at_q, rows, :], pad], axis=0).T
        queries_ref[j] = jnp.concatenate([qv_ref[core, at_q, rows, :], pad], axis=0).T
        grads_ref[j] = jnp.concatenate([grad_ref[core, rows, :], pad], axis=0).T
    key_sum_ref[...] = jnp.zeros(key_sum_ref.shape, F32)
    val_sum_ref[...] = jnp.zeros(val_sum_ref.shape, F32)
    no_rows = jnp.zeros((TILE - PAIR, TILE), BF16)
    lane = lax.broadcasted_iota(jnp.int32, (TILE, TILE), 1)
    in_first = lane < HEAD_DIM

    def stacked(both):
        blank = jnp.zeros_like(both)
        return jnp.concatenate(
            [jnp.where(in_first, both, blank), jnp.where(in_first, blank, both)], axis=0
        )

    def block(b, carry):
        at = pl.ds(pl.multiple_of(b * TILE, TILE), TILE)
        first = pl.multiple_of(first_ref[b] * TILE, TILE)

        def variant(tiles):
            span = pl.ds(first, tiles * TILE)
            scores = [
                dot(
                    keys_ref[j, span, :],
                    side_by_side(qv_ref[core, at_q, top : top + PAIR, at], hot_ref[:, at]),
                    NN,
                )
                for j, (core, top) in enumerate(places)
            ]
            prob_grads = [
                dot(
                    vals_ref[j, span, :],
                    side_by_side(grad_ref[core, top : top + PAIR, at], no_rows),
                    NN,
                )
                for j, (core, top) in enumerate(places)
            ]
            for j, (core, top) in enumerate(places):
                rows = slice(top, top + PAIR)
                agree = grad_ref[core, rows, at].astype(F32) * att_ref[core, rows, at].astype(F32)
                delta = jnp.concatenate(
                    [
                        jnp.sum(agree[:HEAD_DIM], axis=0, keepdims=True),
                        jnp.sum(agree[HEAD_DIM:], axis=0, keepdims=True),
                    ],
                    axis=1,
                )
                probs = jnp.exp2(scores[j] * SCALE_LOG2 - lse_ref[j, pl.ds(b, 1), :])
                score_grad = (probs * (prob_grads[j] - delta)).astype(BF16)
                val_sum_ref[j, span, :] += dot(
                    probs.astype(BF16), stacked(grads_ref[j, at, :]), NN
                )
                key_sum_ref[j, span, :] += dot(score_grad, stacked(queries_ref[j, at, :]), NN)
                query_grad = dot(k_ref[core, rows, span], score_grad, NN) * SCALE
                dqv_ref[core, at_q, top : top + HEAD_DIM, at] = query_grad[
                    :HEAD_DIM, :TILE
                ].astype(BF16)
                dqv_ref[core, at_q, top + HEAD_DIM : top + PAIR, at] = query_grad[
                    HEAD_DIM:, TILE:
                ].astype(BF16)

        for tiles in window_kinds(length // TILE):
            pl.when(kind_ref[b] == tiles)(functools.partial(variant, tiles))
        return carry

    lax.fori_loop(0, length // TILE, block, 0)
    for j, (core, top) in enumerate(places):
        rows = slice(top, top + PAIR)
        dk_ref[core, rows, :] = (key_sum_ref[j] * SCALE).T[:PAIR].astype(BF16)
        dqv_ref[core, 1 - at_q, rows, :] = val_sum_ref[j].T[:PAIR].astype(BF16)


def windows(segs):
    length = segs.shape[0]
    tiles = length // TILE
    by_tile = segs.reshape(tiles, TILE)
    begin = jnp.sum(segs[None, :] < by_tile[:, :1], axis=1)
    end = jnp.sum(segs[None, :] <= by_tile[:, -1:], axis=1)
    first = begin // TILE
    need = (end + TILE - 1) // TILE - first
    kinds = jnp.asarray(window_kinds(tiles), jnp.int32)
    kind = jnp.min(jnp.where(kinds[None, :] >= need[:, None], kinds[None, :], tiles), axis=1)
    return jnp.minimum(first, tiles - kind).astype(jnp.int32), kind.astype(jnp.int32)


def attention_specs(keys):
    cores, count, length = keys.shape
    pairs = cores * count // PAIR
    step = pairs if pairs <= 4 else 4
    part = count * step // pairs
    rows = pl.BlockSpec((cores, part, length), lambda i, *_: (0, i, 0))
    two = pl.BlockSpec((cores, 2, part, length), lambda i, *_: (0, 0, i, 0))
    segs = pl.BlockSpec((1, length), lambda i, *_: (0, 0))
    lse = pl.BlockSpec((step, length // TILE, 2 * TILE), lambda i, *_: (i, 0, 0))
    return pairs, step, rows, two, segs, lse


def attend_forward(query_value, keys, place):
    first, kind, flip, segs = place
    length = segs.shape[0]
    pairs, step, rows, two, segs_spec, lse = attention_specs(keys)
    return pl.pallas_call(
        attend_forward_kernel,
        grid_spec=pltpu.PrefetchScalarGridSpec(
            num_scalar_prefetch=3,
            grid=(pairs // step,),
            in_specs=[segs_spec, two, rows],
            out_specs=[rows, lse],
            scratch_shapes=[
                pltpu.VMEM((TILE - PAIR, length), BF16),
                pltpu.VMEM((step, length, TILE), BF16),
                pltpu.VMEM((step, PAIR + 16, length), BF16),
            ],
        ),
        out_shape=[
            jax.ShapeDtypeStruct(keys.shape, BF16),
            jax.ShapeDtypeStruct((pairs, length // TILE, 2 * TILE), F32),
        ],
        compiler_params=pltpu.CompilerParams(vmem_limit_bytes=40 << 20),
        name="attend_forward",
    )(first, kind, flip, segs[None, :], query_value, keys)


def attend_backward(query_value, keys, attended, grad, lse, place):
    first, kind, flip, segs = place
    length = segs.shape[0]
    pairs, step, rows, two, segs_spec, lse_spec = attention_specs(keys)
    wide = pltpu.VMEM((step, length, TILE), BF16)
    total = pltpu.VMEM((step, length, TILE), F32)
    return pl.pallas_call(
        attend_backward_kernel,
        grid_spec=pltpu.PrefetchScalarGridSpec(
            num_scalar_prefetch=3,
            grid=(pairs // step,),
            in_specs=[segs_spec, two, rows, rows, rows, lse_spec],
            out_specs=[two, rows],
            scratch_shapes=[
                pltpu.VMEM((TILE - PAIR, length), BF16),
                wide,
                wide,
                wide,
                wide,
                total,
                total,
            ],
        ),
        out_shape=[
            jax.ShapeDtypeStruct(query_value.shape, BF16),
            jax.ShapeDtypeStruct(keys.shape, BF16),
        ],
        compiler_params=pltpu.CompilerParams(vmem_limit_bytes=40 << 20),
        name="attend_backward",
    )(first, kind, flip, segs[None, :], query_value, keys, attended, grad, lse)


def gelu_parts(values):
    below = 0.5 * (1.0 + lax.erf(values * (0.5 ** 0.5)))
    density = jnp.exp(values * values * -0.5) * ((2.0 * math.pi) ** -0.5)
    return values * below, below + values * density


def feed_forward_kernel(norm_ref, cot_ref, up_ref, down_ref, *refs):
    *earlier, mlp_ref, back_ref, up_grad_ref, down_grad_ref, act_ref, pre_ref = refs[:-1]
    sum_ref = mlp_ref if mlp_ref.dtype == F32 else refs[-1]
    rows = norm_ref.shape[0]
    chunk = min(rows, 256)

    @pl.when(pl.program_id(0) == 0)
    def _():
        sum_ref[...] = jnp.zeros(sum_ref.shape, F32)
        back_ref[...] = jnp.zeros(back_ref.shape, F32)

    for start in range(0, rows, chunk):
        at = slice(start, start + chunk)
        pre_act = dot(norm_ref[at, :], up_ref[...], NT)
        act_grad = dot(cot_ref[at, :], down_ref[...], NT)
        activation, slope = gelu_parts(pre_act)
        activation = activation.astype(BF16)
        pre_grad = (act_grad * slope).astype(BF16)
        act_ref[at, :] = activation
        pre_ref[at, :] = pre_grad
        sum_ref[at, :] += dot(activation, down_ref[...], NN)
        back_ref[at, :] += dot(pre_grad, up_ref[...], NN)
    up_grad = dot(pre_ref[...], norm_ref[...], TN)
    down_grad = dot(act_ref[...], cot_ref[...], TN)
    if earlier:
        up_grad = up_grad + earlier[0][...].astype(F32)
        down_grad = down_grad + earlier[1][...].astype(F32)
    up_grad_ref[...] = up_grad.astype(BF16)
    down_grad_ref[...] = down_grad.astype(BF16)

    if mlp_ref.dtype != F32:

        @pl.when(pl.program_id(0) == pl.num_programs(0) - 1)
        def _():
            mlp_ref[...] = sum_ref[...].astype(mlp_ref.dtype)


def feed_forward(norm, cot, up, down, earlier=(), kind=F32):
    rows, width = norm.shape
    hidden = up.shape[0]
    part = 512 if hidden % 512 == 0 else hidden
    whole = pl.BlockSpec((rows, width), lambda i: (0, 0))
    block = pl.BlockSpec((part, width), lambda i: (i, 0))
    grads = jax.ShapeDtypeStruct((hidden, width), BF16)
    return pl.pallas_call(
        feed_forward_kernel,
        grid=(hidden // part,),
        in_specs=[whole, whole, block, block] + [block] * len(earlier),
        out_specs=[whole, whole, block, block],
        out_shape=[
            jax.ShapeDtypeStruct((rows, width), kind),
            jax.ShapeDtypeStruct((rows, width), F32),
            grads,
            grads,
        ],
        scratch_shapes=[
            pltpu.VMEM((rows, part), BF16),
            pltpu.VMEM((rows, part), BF16),
            pltpu.VMEM((8, 128) if kind == F32 else (rows, width), F32),
        ],
        compiler_params=pltpu.CompilerParams(vmem_limit_bytes=58 << 20),
        name="feed_forward",
    )(norm, cot, up, down, *earlier)


def middle_kernel(parts, residual_ref, cot_ref, gain_ref, *refs):
    mlp_refs, back_refs = refs[:parts], refs[parts : 2 * parts]
    output_ref, res_grad_ref, branch_ref, norm_grad_ref = refs[2 * parts :]

    @pl.when(pl.program_id(0) == 0)
    def _():
        norm_grad_ref[...] = jnp.zeros(norm_grad_ref.shape, F32)

    residual = residual_ref[...]
    output_ref[...] = sum([ref[...].astype(F32) for ref in mlp_refs], residual).astype(BF16)
    grad = functools.reduce(jnp.add, [ref[...] for ref in back_refs])
    back, gain_grad, bias_grad = layer_norm_back(residual, gain_ref[...], grad)
    res_grad = cot_ref[...].astype(F32) + back
    res_grad_ref[...] = res_grad
    branch_ref[...] = res_grad.astype(BF16)
    norm_grad_ref[0:1, :] += gain_grad
    norm_grad_ref[1:2, :] += bias_grad


def middle(residual, cot, gain, mlps, backs):
    rows, width = residual.shape
    parts = len(mlps)
    step = 256
    block = pl.BlockSpec((step, width), lambda i: (i, 0))
    sums = jax.ShapeDtypeStruct((rows, width), F32)
    low = jax.ShapeDtypeStruct((rows, width), BF16)
    return pl.pallas_call(
        functools.partial(middle_kernel, parts),
        grid=(rows // step,),
        in_specs=[block, block, pl.BlockSpec((1, width), lambda i: (0, 0))] + [block] * (2 * parts),
        out_specs=[block, block, block, pl.BlockSpec((8, width), lambda i: (0, 0))],
        out_shape=[low, sums, low, jax.ShapeDtypeStruct((8, width), F32)],
        compiler_params=pltpu.CompilerParams(vmem_limit_bytes=40 << 20),
        name="middle",
    )(residual, cot, gain[None, :], *mlps, *backs)


def last_kernel(rows_ref, grad_ref, res_grad_ref, gain_ref, in_grad_ref, norm_grad_ref):
    @pl.when(pl.program_id(0) == 0)
    def _():
        norm_grad_ref[...] = jnp.zeros(norm_grad_ref.shape, F32)

    back, gain_grad, bias_grad = layer_norm_back(
        rows_ref[...].astype(F32), gain_ref[...], grad_ref[...]
    )
    in_grad_ref[...] = (res_grad_ref[...] + back).astype(BF16)
    norm_grad_ref[0:1, :] += gain_grad
    norm_grad_ref[1:2, :] += bias_grad


def last(rows_in, grad, res_grad, gain):
    rows, width = rows_in.shape
    step = 256
    block = pl.BlockSpec((step, width), lambda i: (i, 0))
    few = pl.BlockSpec((8, width), lambda i: (0, 0))
    return pl.pallas_call(
        last_kernel,
        grid=(rows // step,),
        in_specs=[block, block, block, pl.BlockSpec((1, width), lambda i: (0, 0))],
        out_specs=[block, few],
        out_shape=[
            jax.ShapeDtypeStruct((rows, width), BF16),
            jax.ShapeDtypeStruct((8, width), F32),
        ],
        compiler_params=pltpu.CompilerParams(vmem_limit_bytes=40 << 20),
        name="last",
    )(rows_in, grad, res_grad, gain[None, :])


def add(*terms):
    return functools.reduce(jnp.add, [item.astype(F32) for item in terms]).astype(BF16)


def swap(values, axis):
    name, size, mask = {
        "core": ("dp", 4, 1),
        "y": ("dp", 4, 2),
        "x": ("mp", 8, 1),
        "z1": ("mp", 8, 2),
        "z2": ("mp", 8, 4),
        "z3": ("mp", 8, 6),
    }[axis]
    return lax.ppermute(values, name, [(i, i ^ mask) for i in range(size)])


def order(at, mine, other):
    return jnp.where(at == 0, jnp.stack([mine, other]), jnp.stack([other, mine]))


class Line:
    def __init__(self):
        self.last = ()

    def __call__(self, step, *args):
        args, _ = lax.optimization_barrier((args, self.last))
        result = step(*args)
        self.last = tuple(jax.tree.leaves(result))
        return result


def on_cube(
    inputs,
    segments,
    ln1_gain,
    ln1_bias,
    w_query,
    w_key,
    w_value,
    w_output,
    ln2_gain,
    ln2_bias,
    w_up,
    w_down,
    cotangent,
):
    rows, width = inputs.shape
    local = w_query.shape[1]
    at_dp, at_mp = lax.axis_index("dp"), lax.axis_index("mp")
    at_y, at_core = at_dp // 2, at_dp % 2
    line = Line()

    def pick(values, at):
        return lax.dynamic_index_in_dim(values, at, 0, keepdims=False)

    def cut_attention(query, key, value, out):
        kinds = jnp.stack([query.T, key.T, value.T, out]).reshape(2, 2, 2, HEAD_DIM, width)
        return pick(kinds.transpose(0, 2, 1, 3, 4).reshape(4, 2, HEAD_DIM, width), at_dp)

    def cut_mlp(up, down):
        pieces = jnp.stack([up.T, down]).reshape(2, 4, -1, width)
        return lax.dynamic_index_in_dim(pieces, at_dp, 1, keepdims=False)

    def join(*parts):
        return jnp.concatenate(parts, 0)

    along_z = ("z2", "z1", "z3")
    attn_piece = line(cut_attention, w_query, w_key, w_value, w_output)
    attn_z = [swap(attn_piece, axis) for axis in along_z]
    mlp_piece = line(cut_mlp, w_up, w_down)
    mlp_z = [swap(mlp_piece, axis) for axis in along_z]

    def begin(rows_in):
        return layer_norm(rows_in.astype(F32), ln1_gain, ln1_bias).astype(BF16)

    norm_one = line(begin, inputs)
    segs = pick(segments, at_mp)
    place = windows(segs) + (at_y.reshape(1), segs)
    place = line(lambda item: item, place)

    near_z = line(lambda *parts: jnp.stack(parts[:4]), attn_piece, *attn_z, mlp_z[1])
    near_got = swap(near_z, "y")
    far_z = swap(near_z, "x")
    near_y = line(lambda *parts: jnp.stack(parts[:2]), near_z, near_got, far_z, mlp_z[0])
    near_got = swap(near_y, "core")
    far_got = swap(far_z, "y")

    def both_cores(mine, other):
        query_value, key_out = [jnp.stack([mine[:, :, i], other[:, :, i]]) for i in (0, 1)]
        key, out = [
            lax.dynamic_index_in_dim(key_out, at, 1, keepdims=False).reshape(-1, width)
            for at in (at_y, 1 - at_y)
        ]
        return query_value.reshape(-1, width), key, out

    def project(weights, norm):
        query_value = dot(weights[0], norm, NT).astype(BF16).reshape(2, 2, -1, rows)
        return query_value, dot(weights[1], norm, NT).astype(BF16).reshape(2, -1, rows)

    def attend(query_value, keys):
        return attend_forward(query_value, keys, place)

    def branch(base, attended, weights):
        return base + dot(attended.reshape(-1, rows), weights[2], TN)

    def mlp_along_z(*parts):
        return [jnp.concatenate([item[i] for item in parts], 0) for i in (0, 1)]

    def mlp_second(up, up_got, down, down_got):
        return jnp.concatenate([up, up_got], 0), jnp.stack([down, down_got])

    near_w = line(both_cores, near_y, near_got)
    near = line(project, near_w, norm_one)
    up, down = line(mlp_along_z, mlp_piece, *mlp_z)
    up_got, down_got = swap(up, "x"), swap(down, "y")
    near += tuple(line(attend, *near))

    far_y = line(lambda *parts: jnp.stack(parts), far_z, far_got)
    far_got = swap(far_y, "core")
    up, down = line(mlp_second, up, up_got, down, down_got)
    up_got, down_got = swap(up, "y"), swap(down, "x")
    residual = line(branch, inputs.astype(F32), near[2], near_w)
    far_w = line(both_cores, far_y, far_got)
    far = line(project, far_w, norm_one)
    far += tuple(line(attend, *far))

    def second_norm(residual, attended, weights):
        residual = branch(residual, attended, weights)
        return residual, layer_norm(residual, ln2_gain, ln2_bias).astype(BF16)

    cot_other = swap(cotangent, "core")
    far_attended, cot_other = lax.optimization_barrier((far[2], cot_other))
    residual, norm_two = line(second_norm, residual, far_attended, far_w)
    norm_two_other = swap(norm_two, "core")

    def mlp_last(up, up_got, down, down_got):
        return jnp.concatenate([up, up_got], 0), jnp.concatenate([down, down_got], 1).reshape(-1, width)

    up, down = line(mlp_last, up, up_got, down, down_got)
    mlp_b, back_b, *grads = line(
        lambda *args: feed_forward(*args, kind=BF16), norm_two_other, cot_other, up, down
    )
    mlp_b, back_b = swap(mlp_b, "core"), swap(back_b, "core")
    mlp_a, back_a, up_grad, down_grad = line(feed_forward, norm_two, cotangent, up, down, grads)

    def before_attention(attended, weights, grad):
        att_grad = dot(weights[2], grad, NT).astype(BF16).reshape(attended.shape)
        return att_grad, dot(attended.reshape(-1, rows), grad, NN).astype(BF16)


    quarter = up.shape[0] // 4

    def up_sum_of(terms, low, high):
        return add(*[item[low:high] for item in terms])

    def down_sum_of(terms, y, x, low=0, high=quarter):
        whole = terms[0].reshape(2, 2, quarter, width)[y, x, low:high]
        return add(whole, *[item.reshape(-1, quarter, width)[y, low:high] for item in terms[1:]])

    def mlp_sum_first(up_terms, down_terms):
        return (
            up_sum_of(up_terms, 2 * quarter, 4 * quarter),
            jnp.stack([down_sum_of(down_terms, y, 1) for y in (0, 1)]),
        )

    up_terms, down_terms = (up_grad,), (down_grad,)
    sends = line(mlp_sum_first, up_terms, down_terms)
    up_terms += (swap(sends[0], "y"),)
    down_terms += (swap(sends[1], "x"),)

    def attend_back(saved, att_grad):
        return attend_backward(*saved[:3], att_grad, saved[3], place)

    def weight_grads(query_value_grad, key_grad, out_grad, norm):
        query_value = dot(query_value_grad.reshape(-1, rows), norm, NN).astype(BF16)
        keys = dot(key_grad.reshape(-1, rows), norm, NN).astype(BF16)
        sums = (
            query_value.reshape(2, 2, -1, width),
            keys.reshape(2, -1, width),
            out_grad.reshape(2, -1, width),
        )
        return sums, [item[1] for item in sums]

    def project_back(grads, weights):
        return dot(grads[0].reshape(-1, rows), weights[0], TN) + dot(
            grads[1].reshape(-1, rows), weights[1], TN
        )

    def attn_terms_of(mine, got, at):
        terms = [(mine[0][0, at], mine[1][0], mine[2][0]), (got[0][at], got[1], got[2])]
        first = at_y == at
        return [
            [item[0] for item in terms],
            [jnp.where(first, item[1], item[2]) for item in terms],
        ]

    def sum_other_y(mine, got):
        return jnp.stack([add(*terms) for terms in attn_terms_of(mine, got, 1)])

    def sum_this_y(mine, got, from_y):
        terms = attn_terms_of(mine, got, 0)
        return jnp.stack([add(*terms[i], from_y[i]) for i in (0, 1)])

    output, res_grad, branch_grad, norm_two_grads = line(
        middle, residual, cotangent, ln2_gain, [mlp_a, mlp_b], [back_a, back_b]
    )
    far_att, far_out = line(before_attention, far[2], far_w, branch_grad)
    far_grads = line(attend_back, far, far_att)
    norm_one_grad = line(project_back, far_grads, far_w)
    far_mine, sends = line(weight_grads, *far_grads, far_out, norm_one)
    far_got = [swap(item, "core") for item in sends]
    def mlp_sum_second(up_terms, down_terms):
        return up_sum_of(up_terms, quarter, 2 * quarter), down_sum_of(down_terms, 1, 0)

    sends = line(mlp_sum_second, up_terms, down_terms)
    up_terms += (swap(sends[0], "x"),)
    down_y = swap(sends[1], "y")

    near_att, near_out = line(before_attention, near[2], near_w, branch_grad)
    far_y = swap(line(sum_other_y, far_mine, far_got), "y")

    part = quarter // 4

    def mlp_sum_of_z(up_terms, down_terms, down_y, low, high):
        low, high = low * part, high * part
        return jnp.stack(
            [
                up_sum_of(up_terms, low, high),
                down_sum_of(down_terms + (jnp.stack([down_y, down_y]),), 0, 0, low, high),
            ]
        )

    mlp_terms = (up_terms, down_terms, down_y)
    near_grads = line(attend_back, near, near_att)
    mlp_z1 = swap(line(lambda *terms: mlp_sum_of_z(*terms, 2, 4), *mlp_terms), "z1")
    near_mine, sends = line(weight_grads, *near_grads, near_out, norm_one)
    near_got = [swap(item, "core") for item in sends]
    far_x = swap(line(sum_this_y, far_mine, far_got, far_y), "x")
    near_y = swap(line(sum_other_y, near_mine, near_got), "y")

    def add_project_back(norm_one_grad, grads, weights):
        return norm_one_grad + project_back(grads, weights)

    def finish(norm_one_grad):
        in_grad, norm_one_grads = last(inputs, norm_one_grad, res_grad, ln1_gain)
        return jnp.concatenate([norm_one_grads[:2], norm_two_grads[:2]]), in_grad

    norm_one_grad = line(add_project_back, norm_one_grad, near_grads, near_w)
    mlp_send = line(
        lambda got, *terms: add(mlp_sum_of_z(*terms, 1, 2), got[:, part:]), mlp_z1, *mlp_terms
    )
    mlp_z2 = swap(mlp_send, "z2")
    norm_sums, in_grad = line(finish, norm_one_grad)

    def attn_sum_z(mine, got, from_y, from_x):
        from_x = from_x.reshape(2, -1, width)
        whole = sum_this_y(mine, got, from_y).astype(F32) + from_x
        return [whole[:, at * HEAD_DIM : (at + 1) * HEAD_DIM].astype(BF16) for at in range(4)]

    attn_mine, *sends = line(attn_sum_z, near_mine, near_got, near_y, far_x)
    attn_z = [swap(item, axis) for item, axis in zip(sends, along_z)]
    mlp_sum = line(
        lambda got, other, *terms: add(mlp_sum_of_z(*terms, 0, 1), got[:, :part], other),
        mlp_z1,
        mlp_z2,
        *mlp_terms,
    )
    mlp_got = swap(mlp_sum, "y")
    got = swap(norm_sums, "core")

    def in_order(piece, y, core, both):
        return order(at_core, order(at_y, piece, y), order(at_y, core, both))

    norm_sums = line(jnp.add, norm_sums, got)
    got = swap(norm_sums, "y")
    norm_sums = line(jnp.add, norm_sums, got)
    got = swap(norm_sums, "x")
    attn_sum = line(add, attn_mine, *attn_z)
    attn_got = [
        lax.ppermute(attn_sum, "dp", [(i, i ^ mask) for i in range(4)]) for mask in (2, 1, 3)
    ]
    norm_sums = line(jnp.add, norm_sums, got)
    got = swap(norm_sums, "z1")
    attn_sum = line(in_order, attn_sum, *attn_got)
    mlp_sum = line(functools.partial(order, at_y), mlp_sum, mlp_got)
    mlp_got = swap(mlp_sum, "core")
    attn_sum = line(
        lambda item: item.transpose(1, 2, 0, 3, 4).reshape(4, local, width).astype(F32), attn_sum
    )
    norm_sums = line(jnp.add, norm_sums, got)
    got = swap(norm_sums, "z2")
    attn_sums = line(lambda item: (item[0].T, item[1].T, item[2].T, item[3]), attn_sum)
    mlp_sum = line(functools.partial(order, at_core), mlp_sum, mlp_got)
    up_sum, down_sum = line(
        lambda item: tuple(item.transpose(2, 1, 0, 3, 4).reshape(2, -1, width).astype(F32)), mlp_sum
    )
    up_sum = line(jnp.transpose, up_sum)
    norm_sums = line(jnp.add, norm_sums, got)
    norm_sums = lax.dynamic_slice_in_dim(norm_sums, at_mp * (width // 8), width // 8, 1)
    return (
        output,
        in_grad,
        norm_sums[0],
        norm_sums[1],
        *attn_sums,
        norm_sums[2],
        norm_sums[3],
        up_sum,
        down_sum,
    )


def on_any(
    mp_size,
    inputs,
    segments,
    ln1_gain,
    ln1_bias,
    w_query,
    w_key,
    w_value,
    w_output,
    ln2_gain,
    ln2_bias,
    w_up,
    w_down,
    cotangent,
):
    rows, width = inputs.shape
    seq_length = segments.shape[1]
    shared_by = seq_length // rows
    at_mp = lax.axis_index("mp")
    groups = [[start + i for i in range(shared_by)] for start in range(0, mp_size, shared_by)]

    def exchange(values, split, join):
        if shared_by == 1:
            return values
        return lax.all_to_all(values, "mp", split, join, axis_index_groups=groups, tiled=True)

    def gather(parts):
        return lax.all_gather(parts, "mp", axis=1, tiled=True)

    def reduce(parts):
        return lax.psum(lax.psum_scatter(parts, "mp", scatter_dimension=1, tiled=True), "dp")

    attn_w = gather(jnp.stack([w_query.T, w_value.T, w_key.T, w_output]))
    up, down = gather(jnp.stack([w_up.T, w_down]))
    project, w_out = attn_w[:3].reshape(3 * width, width), attn_w[3]

    segs = lax.dynamic_index_in_dim(segments, at_mp // shared_by, 0, keepdims=False)
    place = windows(segs) + (jnp.zeros((1,), jnp.int32), segs)
    resid_in = inputs.astype(F32)
    norm_one = layer_norm(resid_in, ln1_gain, ln1_bias).astype(BF16)
    projected = dot(project, norm_one, NT).astype(BF16).reshape(3, width, rows)
    projected = exchange(projected, 1, 2)
    query_value, keys = projected[None, :2], projected[2:]
    heads_out, lse = attend_forward(query_value, keys, place)
    attended = exchange(heads_out[0], 1, 0)
    residual = resid_in + dot(attended, w_out, TN)
    norm_two = layer_norm(residual, ln2_gain, ln2_bias).astype(BF16)
    mlp_branch, norm_two_grad, *mlp_grads = feed_forward(norm_two, cotangent, up, down)
    up_sum, down_sum = reduce(jnp.stack(mlp_grads)).astype(F32)

    output, res_grad, branch_grad, norm_two_grads = middle(
        residual, cotangent, ln2_gain, [mlp_branch], [norm_two_grad]
    )
    out_grad = dot(attended, branch_grad, NN).astype(BF16)
    att_grad = exchange(dot(w_out, branch_grad, NT).astype(BF16), 0, 1)
    query_value_grad, key_grad = attend_backward(
        query_value, keys, heads_out, att_grad[None], lse, place
    )
    proj_grad = exchange(jnp.concatenate([query_value_grad[0], key_grad]), 2, 1)
    proj_grad = proj_grad.reshape(3 * width, rows)
    project_grad = dot(proj_grad, norm_one, NN).astype(BF16).reshape(3, width, width)
    attn_sum = reduce(jnp.concatenate([project_grad, out_grad[None]])).astype(F32)
    in_grad, norm_one_grads = last(inputs, dot(proj_grad, project, TN), res_grad, ln1_gain)
    norm_parts = jnp.concatenate([norm_one_grads[:2], norm_two_grads[:2]])
    norm_sums = lax.dynamic_slice_in_dim(
        lax.psum(norm_parts, ("dp", "mp")), at_mp * (width // mp_size), width // mp_size, 1
    )
    return (
        output,
        in_grad,
        norm_sums[0],
        norm_sums[1],
        attn_sum[0].T,
        attn_sum[2].T,
        attn_sum[1].T,
        attn_sum[3],
        norm_sums[2],
        norm_sums[3],
        up_sum.T,
        down_sum,
    )


def shards(dp_size, mp_size, inputs, segments, *rest):
    if dp_size == 4 and mp_size == 8 and inputs.shape[0] == segments.shape[1]:
        return on_cube(inputs, segments, *rest)
    return on_any(mp_size, inputs, segments, *rest)


def solution(mesh):
    return jax.shard_map(
        functools.partial(shards, mesh.shape["dp"], mesh.shape["mp"]),
        mesh=mesh,
        in_specs=(
            P(("dp", "mp"), None),
            P("dp", None),
            P(),
            P(),
            P(None, "mp"),
            P(None, "mp"),
            P(None, "mp"),
            P("mp", None),
            P(),
            P(),
            P(None, "mp"),
            P("mp", None),
            P(("dp", "mp"), None),
        ),
        out_specs=(
            P(("dp", "mp"), None),
            P(("dp", "mp"), None),
            P("mp"),
            P("mp"),
            P(None, "mp"),
            P(None, "mp"),
            P(None, "mp"),
            P("mp", None),
            P("mp"),
            P("mp"),
            P(None, "mp"),
            P("mp", None),
        ),
        check_vma=False,
    )
```

```python
import functools
import math

import jax
import jax.numpy as jnp
from jax import lax
from jax.experimental import pallas as pl
from jax.experimental.pallas import tpu as pltpu
from jax.sharding import PartitionSpec as P

HEAD_DIM = 48
PAIR = 2 * HEAD_DIM
IMAGES = 4
TILE = 128
norm_eps = 1e-06
negative_fill = -1e30
SCALE = HEAD_DIM ** (-0.5)
SCALE_LOG2 = SCALE * math.log2(math.e)
BF16 = jnp.bfloat16
F32 = jnp.float32


def layer_norm(values, gain, bias):
    center = jnp.mean(values, axis=-1, keepdims=True)
    shifted = values - center
    spread = jnp.mean(shifted * shifted, axis=-1, keepdims=True)
    return shifted * lax.rsqrt(spread + norm_eps) * gain + bias


def layer_norm_back(values, gain, grad):
    shifted = values - jnp.mean(values, axis=-1, keepdims=True)
    scale = lax.rsqrt(jnp.mean(shifted * shifted, axis=-1, keepdims=True) + norm_eps)
    unit = shifted * scale
    scaled = grad * gain
    back = scale * (
        scaled
        - jnp.mean(scaled, axis=-1, keepdims=True)
        - unit * jnp.mean(scaled * unit, axis=-1, keepdims=True)
    )
    return back, jnp.sum(grad * unit, axis=0, keepdims=True), jnp.sum(grad, axis=0, keepdims=True)


def dot(left, right, dims):
    return lax.dot_general(left, right, (dims, ((), ())), preferred_element_type=F32)


NN = ((1,), (0,))
NT = ((1,), (1,))
TN = ((0,), (0,))


def window_kinds(tiles):
    return tuple(n for n in (2, 3, 4, 5, 6, 7) if n < tiles) + (tiles,)


def image_rows(segs, length):
    row = lax.broadcasted_iota(jnp.int32, (TILE - PAIR, length), 0)
    here = row == segs
    one_hot = jnp.where(here, 1.0, 0.0).astype(BF16)
    fill = jnp.where(jnp.logical_or(here, row >= IMAGES), 0.0, negative_fill).astype(BF16)
    return one_hot, fill


def side_by_side(pair, extra):
    blank = jnp.zeros((HEAD_DIM, TILE), BF16)
    left = jnp.concatenate([pair[:HEAD_DIM], blank, extra], axis=0)
    right = jnp.concatenate([blank, pair[HEAD_DIM:], extra], axis=0)
    return jnp.concatenate([left, right], axis=1)


def pair_places(ref):
    cores, count = ref.shape[0], ref.shape[1]
    return [(core, top) for core in range(cores) for top in range(0, count, PAIR)]


def attend_forward_kernel(
    first_ref, kind_ref, flip_ref, segs_ref, qv_ref, k_ref, out_ref, lse_ref, hot_ref, keys_ref, vals_ref
):
    length = k_ref.shape[-1]
    at_q = flip_ref[0]
    places = pair_places(k_ref)
    one_hot, fill = image_rows(segs_ref[...], length)
    hot_ref[...] = one_hot
    for j, (core, top) in enumerate(places):
        rows = slice(top, top + PAIR)
        keys_ref[j] = jnp.concatenate([k_ref[core, rows, :], fill], axis=0).T
        vals_ref[j] = jnp.concatenate(
            [qv_ref[core, 1 - at_q, rows, :], jnp.ones((16, length), BF16)], axis=0
        )

    def block(b, carry):
        at = pl.ds(pl.multiple_of(b * TILE, TILE), TILE)
        first = pl.multiple_of(first_ref[b] * TILE, TILE)

        def variant(tiles):
            span = pl.ds(first, tiles * TILE)
            scores = [
                dot(
                    keys_ref[j, span, :],
                    side_by_side(qv_ref[core, at_q, top : top + PAIR, at], hot_ref[:, at]),
                    NN,
                )
                for j, (core, top) in enumerate(places)
            ]
            for j, (core, top) in enumerate(places):
                most = jnp.max(scores[j], axis=0, keepdims=True)
                expo = jnp.exp2((scores[j] - most) * SCALE_LOG2).astype(BF16)
                mixed = dot(vals_ref[j, :, span], expo, NN)
                total = mixed[PAIR : PAIR + 1, :]
                inverse = 1.0 / total
                out_ref[core, top : top + HEAD_DIM, at] = (
                    mixed[:HEAD_DIM, :TILE] * inverse[:, :TILE]
                ).astype(BF16)
                out_ref[core, top + HEAD_DIM : top + PAIR, at] = (
                    mixed[HEAD_DIM:PAIR, TILE:] * inverse[:, TILE:]
                ).astype(BF16)
                lse_ref[j, pl.ds(b, 1), :] = most * SCALE_LOG2 + jnp.log2(total)

        for tiles in window_kinds(length // TILE):
            pl.when(kind_ref[b] == tiles)(functools.partial(variant, tiles))
        return carry

    lax.fori_loop(0, length // TILE, block, 0)


def attend_backward_kernel(
    first_ref,
    kind_ref,
    flip_ref,
    segs_ref,
    qv_ref,
    k_ref,
    att_ref,
    grad_ref,
    lse_ref,
    dqv_ref,
    dk_ref,
    hot_ref,
    keys_ref,
    vals_ref,
    queries_ref,
    grads_ref,
    key_sum_ref,
    val_sum_ref,
):
    length = k_ref.shape[-1]
    at_q = flip_ref[0]
    places = pair_places(k_ref)
    one_hot, fill = image_rows(segs_ref[...], length)
    hot_ref[...] = one_hot
    pad = jnp.zeros((TILE - PAIR, length), BF16)
    for j, (core, top) in enumerate(places):
        rows = slice(top, top + PAIR)
        keys_ref[j] = jnp.concatenate([k_ref[core, rows, :], fill], axis=0).T
        vals_ref[j] = jnp.concatenate([qv_ref[core, 1 - at_q, rows, :], pad], axis=0).T
        queries_ref[j] = jnp.concatenate([qv_ref[core, at_q, rows, :], pad], axis=0).T
        grads_ref[j] = jnp.concatenate([grad_ref[core, rows, :], pad], axis=0).T
    key_sum_ref[...] = jnp.zeros(key_sum_ref.shape, F32)
    val_sum_ref[...] = jnp.zeros(val_sum_ref.shape, F32)
    no_rows = jnp.zeros((TILE - PAIR, TILE), BF16)
    lane = lax.broadcasted_iota(jnp.int32, (TILE, TILE), 1)
    in_first = lane < HEAD_DIM

    def stacked(both):
        blank = jnp.zeros_like(both)
        return jnp.concatenate(
            [jnp.where(in_first, both, blank), jnp.where(in_first, blank, both)], axis=0
        )

    def block(b, carry):
        at = pl.ds(pl.multiple_of(b * TILE, TILE), TILE)
        first = pl.multiple_of(first_ref[b] * TILE, TILE)

        def variant(tiles):
            span = pl.ds(first, tiles * TILE)
            scores = [
                dot(
                    keys_ref[j, span, :],
                    side_by_side(qv_ref[core, at_q, top : top + PAIR, at], hot_ref[:, at]),
                    NN,
                )
                for j, (core, top) in enumerate(places)
            ]
            prob_grads = [
                dot(
                    vals_ref[j, span, :],
                    side_by_side(grad_ref[core, top : top + PAIR, at], no_rows),
                    NN,
                )
                for j, (core, top) in enumerate(places)
            ]
            for j, (core, top) in enumerate(places):
                rows = slice(top, top + PAIR)
                agree = grad_ref[core, rows, at].astype(F32) * att_ref[core, rows, at].astype(F32)
                delta = jnp.concatenate(
                    [
                        jnp.sum(agree[:HEAD_DIM], axis=0, keepdims=True),
                        jnp.sum(agree[HEAD_DIM:], axis=0, keepdims=True),
                    ],
                    axis=1,
                )
                probs = jnp.exp2(scores[j] * SCALE_LOG2 - lse_ref[j, pl.ds(b, 1), :])
                score_grad = (probs * (prob_grads[j] - delta)).astype(BF16)
                val_sum_ref[j, span, :] += dot(
                    probs.astype(BF16), stacked(grads_ref[j, at, :]), NN
                )
                key_sum_ref[j, span, :] += dot(score_grad, stacked(queries_ref[j, at, :]), NN)
                query_grad = dot(k_ref[core, rows, span], score_grad, NN) * SCALE
                dqv_ref[core, at_q, top : top + HEAD_DIM, at] = query_grad[
                    :HEAD_DIM, :TILE
                ].astype(BF16)
                dqv_ref[core, at_q, top + HEAD_DIM : top + PAIR, at] = query_grad[
                    HEAD_DIM:, TILE:
                ].astype(BF16)

        for tiles in window_kinds(length // TILE):
            pl.when(kind_ref[b] == tiles)(functools.partial(variant, tiles))
        return carry

    lax.fori_loop(0, length // TILE, block, 0)
    for j, (core, top) in enumerate(places):
        rows = slice(top, top + PAIR)
        dk_ref[core, rows, :] = (key_sum_ref[j] * SCALE).T[:PAIR].astype(BF16)
        dqv_ref[core, 1 - at_q, rows, :] = val_sum_ref[j].T[:PAIR].astype(BF16)


def windows(segs):
    length = segs.shape[0]
    tiles = length // TILE
    by_tile = segs.reshape(tiles, TILE)
    begin = jnp.sum(segs[None, :] < by_tile[:, :1], axis=1)
    end = jnp.sum(segs[None, :] <= by_tile[:, -1:], axis=1)
    first = begin // TILE
    need = (end + TILE - 1) // TILE - first
    kinds = jnp.asarray(window_kinds(tiles), jnp.int32)
    kind = jnp.min(jnp.where(kinds[None, :] >= need[:, None], kinds[None, :], tiles), axis=1)
    return jnp.minimum(first, tiles - kind).astype(jnp.int32), kind.astype(jnp.int32)


def attention_specs(keys):
    cores, count, length = keys.shape
    pairs = cores * count // PAIR
    step = pairs if pairs <= 4 else 4
    part = count * step // pairs
    rows = pl.BlockSpec((cores, part, length), lambda i, *_: (0, i, 0))
    two = pl.BlockSpec((cores, 2, part, length), lambda i, *_: (0, 0, i, 0))
    segs = pl.BlockSpec((1, length), lambda i, *_: (0, 0))
    lse = pl.BlockSpec((step, length // TILE, 2 * TILE), lambda i, *_: (i, 0, 0))
    return pairs, step, rows, two, segs, lse


def attend_forward(query_value, keys, place):
    first, kind, flip, segs = place
    length = segs.shape[0]
    pairs, step, rows, two, segs_spec, lse = attention_specs(keys)
    return pl.pallas_call(
        attend_forward_kernel,
        grid_spec=pltpu.PrefetchScalarGridSpec(
            num_scalar_prefetch=3,
            grid=(pairs // step,),
            in_specs=[segs_spec, two, rows],
            out_specs=[rows, lse],
            scratch_shapes=[
                pltpu.VMEM((TILE - PAIR, length), BF16),
                pltpu.VMEM((step, length, TILE), BF16),
                pltpu.VMEM((step, PAIR + 16, length), BF16),
            ],
        ),
        out_shape=[
            jax.ShapeDtypeStruct(keys.shape, BF16),
            jax.ShapeDtypeStruct((pairs, length // TILE, 2 * TILE), F32),
        ],
        compiler_params=pltpu.CompilerParams(vmem_limit_bytes=40 << 20),
        name="attend_forward",
    )(first, kind, flip, segs[None, :], query_value, keys)


def attend_backward(query_value, keys, attended, grad, lse, place):
    first, kind, flip, segs = place
    length = segs.shape[0]
    pairs, step, rows, two, segs_spec, lse_spec = attention_specs(keys)
    wide = pltpu.VMEM((step, length, TILE), BF16)
    total = pltpu.VMEM((step, length, TILE), F32)
    return pl.pallas_call(
        attend_backward_kernel,
        grid_spec=pltpu.PrefetchScalarGridSpec(
            num_scalar_prefetch=3,
            grid=(pairs // step,),
            in_specs=[segs_spec, two, rows, rows, rows, lse_spec],
            out_specs=[two, rows],
            scratch_shapes=[
                pltpu.VMEM((TILE - PAIR, length), BF16),
                wide,
                wide,
                wide,
                wide,
                total,
                total,
            ],
        ),
        out_shape=[
            jax.ShapeDtypeStruct(query_value.shape, BF16),
            jax.ShapeDtypeStruct(keys.shape, BF16),
        ],
        compiler_params=pltpu.CompilerParams(vmem_limit_bytes=40 << 20),
        name="attend_backward",
    )(first, kind, flip, segs[None, :], query_value, keys, attended, grad, lse)


def gelu_parts(values):
    below = 0.5 * (1.0 + lax.erf(values * (0.5 ** 0.5)))
    density = jnp.exp(values * values * -0.5) * ((2.0 * math.pi) ** -0.5)
    return values * below, below + values * density


def feed_forward_kernel(norm_ref, cot_ref, up_ref, down_ref, *refs):
    *earlier, mlp_ref, back_ref, up_grad_ref, down_grad_ref, act_ref, pre_ref = refs[:-1]
    sum_ref = mlp_ref if mlp_ref.dtype == F32 else refs[-1]
    rows = norm_ref.shape[0]
    chunk = min(rows, 256)

    @pl.when(pl.program_id(0) == 0)
    def _():
        sum_ref[...] = jnp.zeros(sum_ref.shape, F32)
        back_ref[...] = jnp.zeros(back_ref.shape, F32)

    for start in range(0, rows, chunk):
        at = slice(start, start + chunk)
        pre_act = dot(norm_ref[at, :], up_ref[...], NT)
        act_grad = dot(cot_ref[at, :], down_ref[...], NT)
        activation, slope = gelu_parts(pre_act)
        activation = activation.astype(BF16)
        pre_grad = (act_grad * slope).astype(BF16)
        act_ref[at, :] = activation
        pre_ref[at, :] = pre_grad
        sum_ref[at, :] += dot(activation, down_ref[...], NN)
        back_ref[at, :] += dot(pre_grad, up_ref[...], NN)
    up_grad = dot(pre_ref[...], norm_ref[...], TN)
    down_grad = dot(act_ref[...], cot_ref[...], TN)
    if earlier:
        up_grad = up_grad + earlier[0][...].astype(F32)
        down_grad = down_grad + earlier[1][...].astype(F32)
    up_grad_ref[...] = up_grad.astype(BF16)
    down_grad_ref[...] = down_grad.astype(BF16)

    if mlp_ref.dtype != F32:

        @pl.when(pl.program_id(0) == pl.num_programs(0) - 1)
        def _():
            mlp_ref[...] = sum_ref[...].astype(mlp_ref.dtype)


def feed_forward(norm, cot, up, down, earlier=(), kind=F32):
    rows, width = norm.shape
    hidden = up.shape[0]
    part = 512 if hidden % 512 == 0 else hidden
    whole = pl.BlockSpec((rows, width), lambda i: (0, 0))
    block = pl.BlockSpec((part, width), lambda i: (i, 0))
    grads = jax.ShapeDtypeStruct((hidden, width), BF16)
    return pl.pallas_call(
        feed_forward_kernel,
        grid=(hidden // part,),
        in_specs=[whole, whole, block, block] + [block] * len(earlier),
        out_specs=[whole, whole, block, block],
        out_shape=[
            jax.ShapeDtypeStruct((rows, width), kind),
            jax.ShapeDtypeStruct((rows, width), F32),
            grads,
            grads,
        ],
        scratch_shapes=[
            pltpu.VMEM((rows, part), BF16),
            pltpu.VMEM((rows, part), BF16),
            pltpu.VMEM((8, 128) if kind == F32 else (rows, width), F32),
        ],
        compiler_params=pltpu.CompilerParams(vmem_limit_bytes=58 << 20),
        name="feed_forward",
    )(norm, cot, up, down, *earlier)


def middle_kernel(parts, residual_ref, cot_ref, gain_ref, *refs):
    mlp_refs, back_refs = refs[:parts], refs[parts : 2 * parts]
    output_ref, res_grad_ref, branch_ref, norm_grad_ref = refs[2 * parts :]

    @pl.when(pl.program_id(0) == 0)
    def _():
        norm_grad_ref[...] = jnp.zeros(norm_grad_ref.shape, F32)

    residual = residual_ref[...]
    output_ref[...] = sum([ref[...].astype(F32) for ref in mlp_refs], residual).astype(BF16)
    grad = functools.reduce(jnp.add, [ref[...] for ref in back_refs])
    back, gain_grad, bias_grad = layer_norm_back(residual, gain_ref[...], grad)
    res_grad = cot_ref[...].astype(F32) + back
    res_grad_ref[...] = res_grad
    branch_ref[...] = res_grad.astype(BF16)
    norm_grad_ref[0:1, :] += gain_grad
    norm_grad_ref[1:2, :] += bias_grad


def middle(residual, cot, gain, mlps, backs):
    rows, width = residual.shape
    parts = len(mlps)
    step = 256
    block = pl.BlockSpec((step, width), lambda i: (i, 0))
    sums = jax.ShapeDtypeStruct((rows, width), F32)
    low = jax.ShapeDtypeStruct((rows, width), BF16)
    return pl.pallas_call(
        functools.partial(middle_kernel, parts),
        grid=(rows // step,),
        in_specs=[block, block, pl.BlockSpec((1, width), lambda i: (0, 0))] + [block] * (2 * parts),
        out_specs=[block, block, block, pl.BlockSpec((8, width), lambda i: (0, 0))],
        out_shape=[low, sums, low, jax.ShapeDtypeStruct((8, width), F32)],
        compiler_params=pltpu.CompilerParams(vmem_limit_bytes=40 << 20),
        name="middle",
    )(residual, cot, gain[None, :], *mlps, *backs)


def last_kernel(rows_ref, grad_ref, res_grad_ref, gain_ref, in_grad_ref, norm_grad_ref):
    @pl.when(pl.program_id(0) == 0)
    def _():
        norm_grad_ref[...] = jnp.zeros(norm_grad_ref.shape, F32)

    back, gain_grad, bias_grad = layer_norm_back(
        rows_ref[...].astype(F32), gain_ref[...], grad_ref[...]
    )
    in_grad_ref[...] = (res_grad_ref[...] + back).astype(BF16)
    norm_grad_ref[0:1, :] += gain_grad
    norm_grad_ref[1:2, :] += bias_grad


def last(rows_in, grad, res_grad, gain):
    rows, width = rows_in.shape
    step = 256
    block = pl.BlockSpec((step, width), lambda i: (i, 0))
    few = pl.BlockSpec((8, width), lambda i: (0, 0))
    return pl.pallas_call(
        last_kernel,
        grid=(rows // step,),
        in_specs=[block, block, block, pl.BlockSpec((1, width), lambda i: (0, 0))],
        out_specs=[block, few],
        out_shape=[
            jax.ShapeDtypeStruct((rows, width), BF16),
            jax.ShapeDtypeStruct((8, width), F32),
        ],
        compiler_params=pltpu.CompilerParams(vmem_limit_bytes=40 << 20),
        name="last",
    )(rows_in, grad, res_grad, gain[None, :])


def add(*terms):
    return functools.reduce(jnp.add, [item.astype(F32) for item in terms]).astype(BF16)


def swap(values, axis):
    name, size, mask = {
        "core": ("dp", 4, 1),
        "y": ("dp", 4, 2),
        "x": ("mp", 8, 1),
        "z1": ("mp", 8, 2),
        "z2": ("mp", 8, 4),
        "z3": ("mp", 8, 6),
    }[axis]
    return lax.ppermute(values, name, [(i, i ^ mask) for i in range(size)])


def order(at, mine, other):
    return jnp.where(at == 0, jnp.stack([mine, other]), jnp.stack([other, mine]))


class Line:
    def __init__(self):
        self.last = ()

    def __call__(self, step, *args):
        args, _ = lax.optimization_barrier((args, self.last))
        result = step(*args)
        self.last = tuple(jax.tree.leaves(result))
        return result


def on_cube(
    inputs,
    segments,
    ln1_gain,
    ln1_bias,
    w_query,
    w_key,
    w_value,
    w_output,
    ln2_gain,
    ln2_bias,
    w_up,
    w_down,
    cotangent,
):
    rows, width = inputs.shape
    local = w_query.shape[1]
    at_dp, at_mp = lax.axis_index("dp"), lax.axis_index("mp")
    at_y, at_core = at_dp // 2, at_dp % 2
    line = Line()

    def pick(values, at):
        return lax.dynamic_index_in_dim(values, at, 0, keepdims=False)

    def cut_attention(query, key, value, out):
        kinds = jnp.stack([query.T, key.T, value.T, out]).reshape(2, 2, 2, HEAD_DIM, width)
        return pick(kinds.transpose(0, 2, 1, 3, 4).reshape(4, 2, HEAD_DIM, width), at_dp)

    def cut_mlp(up, down):
        pieces = jnp.stack([up.T, down]).reshape(2, 4, -1, width)
        return lax.dynamic_index_in_dim(pieces, at_dp, 1, keepdims=False)

    def join(*parts):
        return jnp.concatenate(parts, 0)

    along_z = ("z2", "z1", "z3")
    attn_piece = line(cut_attention, w_query, w_key, w_value, w_output)
    attn_z = [swap(attn_piece, axis) for axis in along_z]
    mlp_piece = line(cut_mlp, w_up, w_down)
    mlp_z = [swap(mlp_piece, axis) for axis in along_z]

    def begin(rows_in):
        return layer_norm(rows_in.astype(F32), ln1_gain, ln1_bias).astype(BF16)

    norm_one = line(begin, inputs)
    segs = pick(segments, at_mp)
    place = windows(segs) + (at_y.reshape(1), segs)
    place = line(lambda item: item, place)

    near_z = line(lambda *parts: jnp.stack(parts[:4]), attn_piece, *attn_z, mlp_z[1])
    near_got = swap(near_z, "y")
    far_z = swap(near_z, "x")
    near_y = line(lambda *parts: jnp.stack(parts[:2]), near_z, near_got, far_z, mlp_z[0])
    near_got = swap(near_y, "core")
    far_got = swap(far_z, "y")

    def both_cores(mine, other):
        query_value, key_out = [jnp.stack([mine[:, :, i], other[:, :, i]]) for i in (0, 1)]
        key, out = [
            lax.dynamic_index_in_dim(key_out, at, 1, keepdims=False).reshape(-1, width)
            for at in (at_y, 1 - at_y)
        ]
        return query_value.reshape(-1, width), key, out

    def project(weights, norm):
        query_value = dot(weights[0], norm, NT).astype(BF16).reshape(2, 2, -1, rows)
        return query_value, dot(weights[1], norm, NT).astype(BF16).reshape(2, -1, rows)

    def attend(query_value, keys):
        return attend_forward(query_value, keys, place)

    def branch(base, attended, weights):
        return base + dot(attended.reshape(-1, rows), weights[2], TN)

    def mlp_along_z(*parts):
        return [jnp.concatenate([item[i] for item in parts], 0) for i in (0, 1)]

    def mlp_second(up, up_got, down, down_got):
        return jnp.concatenate([up, up_got], 0), jnp.stack([down, down_got])

    near_w = line(both_cores, near_y, near_got)
    near = line(project, near_w, norm_one)
    up, down = line(mlp_along_z, mlp_piece, *mlp_z)
    up_got, down_got = swap(up, "x"), swap(down, "y")
    near += tuple(line(attend, *near))

    far_y = line(lambda *parts: jnp.stack(parts), far_z, far_got)
    far_got = swap(far_y, "core")
    up, down = line(mlp_second, up, up_got, down, down_got)
    up_got, down_got = swap(up, "y"), swap(down, "x")
    residual = line(branch, inputs.astype(F32), near[2], near_w)
    far_w = line(both_cores, far_y, far_got)
    far = line(project, far_w, norm_one)
    far += tuple(line(attend, *far))

    def second_norm(residual, attended, weights):
        residual = branch(residual, attended, weights)
        return residual, layer_norm(residual, ln2_gain, ln2_bias).astype(BF16)

    cot_other = swap(cotangent, "core")
    far_attended, cot_other = lax.optimization_barrier((far[2], cot_other))
    residual, norm_two = line(second_norm, residual, far_attended, far_w)
    norm_two_other = swap(norm_two, "core")

    def mlp_last(up, up_got, down, down_got):
        return jnp.concatenate([up, up_got], 0), jnp.concatenate([down, down_got], 1).reshape(-1, width)

    up, down = line(mlp_last, up, up_got, down, down_got)
    mlp_b, back_b, *grads = line(
        lambda *args: feed_forward(*args, kind=BF16), norm_two_other, cot_other, up, down
    )
    mlp_b, back_b = swap(mlp_b, "core"), swap(back_b, "core")
    mlp_a, back_a, up_grad, down_grad = line(feed_forward, norm_two, cotangent, up, down, grads)

    def before_attention(attended, weights, grad):
        att_grad = dot(weights[2], grad, NT).astype(BF16).reshape(attended.shape)
        return att_grad, dot(attended.reshape(-1, rows), grad, NN).astype(BF16)


    quarter = up.shape[0] // 4

    def up_sum_of(terms, low, high):
        return add(*[item[low:high] for item in terms])

    def down_sum_of(terms, y, x, low=0, high=quarter):
        whole = terms[0].reshape(2, 2, quarter, width)[y, x, low:high]
        return add(whole, *[item.reshape(-1, quarter, width)[y, low:high] for item in terms[1:]])

    def mlp_sum_first(up_terms, down_terms):
        return (
            up_sum_of(up_terms, 2 * quarter, 4 * quarter),
            jnp.stack([down_sum_of(down_terms, y, 1) for y in (0, 1)]),
        )

    up_terms, down_terms = (up_grad,), (down_grad,)
    sends = line(mlp_sum_first, up_terms, down_terms)
    up_terms += (swap(sends[0], "y"),)
    down_terms += (swap(sends[1], "x"),)

    def attend_back(saved, att_grad):
        return attend_backward(*saved[:3], att_grad, saved[3], place)

    def weight_grads(query_value_grad, key_grad, out_grad, norm):
        query_value = dot(query_value_grad.reshape(-1, rows), norm, NN).astype(BF16)
        keys = dot(key_grad.reshape(-1, rows), norm, NN).astype(BF16)
        sums = (
            query_value.reshape(2, 2, -1, width),
            keys.reshape(2, -1, width),
            out_grad.reshape(2, -1, width),
        )
        return sums, [item[1] for item in sums]

    def project_back(grads, weights):
        return dot(grads[0].reshape(-1, rows), weights[0], TN) + dot(
            grads[1].reshape(-1, rows), weights[1], TN
        )

    def attn_terms_of(mine, got, at):
        terms = [(mine[0][0, at], mine[1][0], mine[2][0]), (got[0][at], got[1], got[2])]
        first = at_y == at
        return [
            [item[0] for item in terms],
            [jnp.where(first, item[1], item[2]) for item in terms],
        ]

    def sum_other_y(mine, got):
        return jnp.stack([add(*terms) for terms in attn_terms_of(mine, got, 1)])

    def sum_this_y(mine, got, from_y):
        terms = attn_terms_of(mine, got, 0)
        return jnp.stack([add(*terms[i], from_y[i]) for i in (0, 1)])

    output, res_grad, branch_grad, norm_two_grads = line(
        middle, residual, cotangent, ln2_gain, [mlp_a, mlp_b], [back_a, back_b]
    )
    far_att, far_out = line(before_attention, far[2], far_w, branch_grad)
    far_grads = line(attend_back, far, far_att)
    norm_one_grad = line(project_back, far_grads, far_w)
    far_mine, sends = line(weight_grads, *far_grads, far_out, norm_one)
    far_got = [swap(item, "core") for item in sends]
    def mlp_sum_second(up_terms, down_terms):
        return up_sum_of(up_terms, quarter, 2 * quarter), down_sum_of(down_terms, 1, 0)

    sends = line(mlp_sum_second, up_terms, down_terms)
    up_terms += (swap(sends[0], "x"),)
    down_y = swap(sends[1], "y")

    near_att, near_out = line(before_attention, near[2], near_w, branch_grad)
    far_y = swap(line(sum_other_y, far_mine, far_got), "y")

    part = quarter // 4

    def mlp_sum_of_z(up_terms, down_terms, down_y, low, high):
        low, high = low * part, high * part
        return jnp.stack(
            [
                up_sum_of(up_terms, low, high),
                down_sum_of(down_terms + (jnp.stack([down_y, down_y]),), 0, 0, low, high),
            ]
        )

    mlp_terms = (up_terms, down_terms, down_y)
    near_grads = line(attend_back, near, near_att)
    sends = line(lambda *terms: [mlp_sum_of_z(*terms, at, at + 1) for at in (1, 2, 3)], *mlp_terms)
    mlp_z = [swap(item, axis) for item, axis in zip(sends, along_z)]
    near_mine, sends = line(weight_grads, *near_grads, near_out, norm_one)
    near_got = [swap(item, "core") for item in sends]
    far_send = line(lambda *args: sum_this_y(*args[:3]), far_mine, far_got, far_y, mlp_z[1])
    far_x = swap(far_send, "x")
    near_y = swap(line(sum_other_y, near_mine, near_got), "y")

    def add_project_back(norm_one_grad, grads, weights):
        return norm_one_grad + project_back(grads, weights)

    def finish(norm_one_grad):
        in_grad, norm_one_grads = last(inputs, norm_one_grad, res_grad, ln1_gain)
        return jnp.concatenate([norm_one_grads[:2], norm_two_grads[:2]]), in_grad

    norm_one_grad = line(
        lambda *args: add_project_back(*args[:3]), norm_one_grad, near_grads, near_w, mlp_z[0]
    )
    norm_sums, in_grad = line(finish, norm_one_grad)

    def attn_sum_z(mine, got, from_y, from_x):
        from_x = from_x.reshape(2, -1, width)
        whole = sum_this_y(mine, got, from_y).astype(F32) + from_x
        return [whole[:, at * HEAD_DIM : (at + 1) * HEAD_DIM].astype(BF16) for at in range(4)]

    attn_mine, *sends = line(attn_sum_z, near_mine, near_got, near_y, far_x)
    attn_z = [swap(item, axis) for item, axis in zip(sends, along_z)]
    got = swap(norm_sums, "core")
    mlp_sum = line(
        lambda others, *terms: add(mlp_sum_of_z(*terms, 0, 1), *others), mlp_z, *mlp_terms
    )
    mlp_got = swap(mlp_sum, "y")

    def in_order(piece, y, core, both):
        return order(at_core, order(at_y, piece, y), order(at_y, core, both))

    norm_sums = line(jnp.add, norm_sums, got)
    got = swap(norm_sums, "y")
    attn_sum = line(lambda _, *terms: add(*terms), mlp_got, attn_mine, *attn_z)
    attn_got = [
        lax.ppermute(attn_sum, "dp", [(i, i ^ mask) for i in range(4)]) for mask in (2, 1, 3)
    ]
    mlp_sum = line(functools.partial(order, at_y), mlp_sum, mlp_got)
    mlp_got = swap(mlp_sum, "core")
    norm_sums = line(jnp.add, norm_sums, got)
    got = swap(norm_sums, "x")
    attn_sum = line(in_order, attn_sum, *attn_got)
    attn_sum = line(
        lambda item: item.transpose(1, 2, 0, 3, 4).reshape(4, local, width).astype(F32), attn_sum
    )
    norm_sums = line(jnp.add, norm_sums, got)
    got = swap(norm_sums, "z1")
    attn_sums = line(lambda item: (item[0].T, item[1].T, item[2].T, item[3]), attn_sum)
    mlp_sum = line(functools.partial(order, at_core), mlp_sum, mlp_got)
    norm_sums = line(jnp.add, norm_sums, got)
    got = swap(norm_sums, "z2")
    up_sum, down_sum = line(
        lambda item: tuple(item.transpose(2, 1, 0, 3, 4).reshape(2, -1, width).astype(F32)), mlp_sum
    )
    up_sum = line(jnp.transpose, up_sum)
    norm_sums = line(jnp.add, norm_sums, got)
    norm_sums = lax.dynamic_slice_in_dim(norm_sums, at_mp * (width // 8), width // 8, 1)
    return (
        output,
        in_grad,
        norm_sums[0],
        norm_sums[1],
        *attn_sums,
        norm_sums[2],
        norm_sums[3],
        up_sum,
        down_sum,
    )


def on_any(
    mp_size,
    inputs,
    segments,
    ln1_gain,
    ln1_bias,
    w_query,
    w_key,
    w_value,
    w_output,
    ln2_gain,
    ln2_bias,
    w_up,
    w_down,
    cotangent,
):
    rows, width = inputs.shape
    seq_length = segments.shape[1]
    shared_by = seq_length // rows
    at_mp = lax.axis_index("mp")
    groups = [[start + i for i in range(shared_by)] for start in range(0, mp_size, shared_by)]

    def exchange(values, split, join):
        if shared_by == 1:
            return values
        return lax.all_to_all(values, "mp", split, join, axis_index_groups=groups, tiled=True)

    def gather(parts):
        return lax.all_gather(parts, "mp", axis=1, tiled=True)

    def reduce(parts):
        return lax.psum(lax.psum_scatter(parts, "mp", scatter_dimension=1, tiled=True), "dp")

    attn_w = gather(jnp.stack([w_query.T, w_value.T, w_key.T, w_output]))
    up, down = gather(jnp.stack([w_up.T, w_down]))
    project, w_out = attn_w[:3].reshape(3 * width, width), attn_w[3]

    segs = lax.dynamic_index_in_dim(segments, at_mp // shared_by, 0, keepdims=False)
    place = windows(segs) + (jnp.zeros((1,), jnp.int32), segs)
    resid_in = inputs.astype(F32)
    norm_one = layer_norm(resid_in, ln1_gain, ln1_bias).astype(BF16)
    projected = dot(project, norm_one, NT).astype(BF16).reshape(3, width, rows)
    projected = exchange(projected, 1, 2)
    query_value, keys = projected[None, :2], projected[2:]
    heads_out, lse = attend_forward(query_value, keys, place)
    attended = exchange(heads_out[0], 1, 0)
    residual = resid_in + dot(attended, w_out, TN)
    norm_two = layer_norm(residual, ln2_gain, ln2_bias).astype(BF16)
    mlp_branch, norm_two_grad, *mlp_grads = feed_forward(norm_two, cotangent, up, down)
    up_sum, down_sum = reduce(jnp.stack(mlp_grads)).astype(F32)

    output, res_grad, branch_grad, norm_two_grads = middle(
        residual, cotangent, ln2_gain, [mlp_branch], [norm_two_grad]
    )
    out_grad = dot(attended, branch_grad, NN).astype(BF16)
    att_grad = exchange(dot(w_out, branch_grad, NT).astype(BF16), 0, 1)
    query_value_grad, key_grad = attend_backward(
        query_value, keys, heads_out, att_grad[None], lse, place
    )
    proj_grad = exchange(jnp.concatenate([query_value_grad[0], key_grad]), 2, 1)
    proj_grad = proj_grad.reshape(3 * width, rows)
    project_grad = dot(proj_grad, norm_one, NN).astype(BF16).reshape(3, width, width)
    attn_sum = reduce(jnp.concatenate([project_grad, out_grad[None]])).astype(F32)
    in_grad, norm_one_grads = last(inputs, dot(proj_grad, project, TN), res_grad, ln1_gain)
    norm_parts = jnp.concatenate([norm_one_grads[:2], norm_two_grads[:2]])
    norm_sums = lax.dynamic_slice_in_dim(
        lax.psum(norm_parts, ("dp", "mp")), at_mp * (width // mp_size), width // mp_size, 1
    )
    return (
        output,
        in_grad,
        norm_sums[0],
        norm_sums[1],
        attn_sum[0].T,
        attn_sum[2].T,
        attn_sum[1].T,
        attn_sum[3],
        norm_sums[2],
        norm_sums[3],
        up_sum.T,
        down_sum,
    )


def shards(dp_size, mp_size, inputs, segments, *rest):
    if dp_size == 4 and mp_size == 8 and inputs.shape[0] == segments.shape[1]:
        return on_cube(inputs, segments, *rest)
    return on_any(mp_size, inputs, segments, *rest)


def solution(mesh):
    return jax.shard_map(
        functools.partial(shards, mesh.shape["dp"], mesh.shape["mp"]),
        mesh=mesh,
        in_specs=(
            P(("dp", "mp"), None),
            P("dp", None),
            P(),
            P(),
            P(None, "mp"),
            P(None, "mp"),
            P(None, "mp"),
            P("mp", None),
            P(),
            P(),
            P(None, "mp"),
            P("mp", None),
            P(("dp", "mp"), None),
        ),
        out_specs=(
            P(("dp", "mp"), None),
            P(("dp", "mp"), None),
            P("mp"),
            P("mp"),
            P(None, "mp"),
            P(None, "mp"),
            P(None, "mp"),
            P("mp", None),
            P("mp"),
            P("mp"),
            P(None, "mp"),
            P("mp", None),
        ),
        check_vma=False,
    )
```

```python
import functools
import math

import jax
import jax.numpy as jnp
from jax import lax
from jax.experimental import pallas as pl
from jax.experimental.pallas import tpu as pltpu
from jax.sharding import PartitionSpec as P

HEAD_DIM = 48
PAIR = 2 * HEAD_DIM
IMAGES = 4
TILE = 128
norm_eps = 1e-06
negative_fill = -1e30
SCALE = HEAD_DIM ** (-0.5)
SCALE_LOG2 = SCALE * math.log2(math.e)
BF16 = jnp.bfloat16
F32 = jnp.float32


def layer_norm(values, gain, bias):
    center = jnp.mean(values, axis=-1, keepdims=True)
    shifted = values - center
    spread = jnp.mean(shifted * shifted, axis=-1, keepdims=True)
    return shifted * lax.rsqrt(spread + norm_eps) * gain + bias


def layer_norm_back(values, gain, grad):
    shifted = values - jnp.mean(values, axis=-1, keepdims=True)
    scale = lax.rsqrt(jnp.mean(shifted * shifted, axis=-1, keepdims=True) + norm_eps)
    unit = shifted * scale
    scaled = grad * gain
    back = scale * (
        scaled
        - jnp.mean(scaled, axis=-1, keepdims=True)
        - unit * jnp.mean(scaled * unit, axis=-1, keepdims=True)
    )
    return back, jnp.sum(grad * unit, axis=0, keepdims=True), jnp.sum(grad, axis=0, keepdims=True)


def dot(left, right, dims):
    return lax.dot_general(left, right, (dims, ((), ())), preferred_element_type=F32)


NN = ((1,), (0,))
NT = ((1,), (1,))
TN = ((0,), (0,))


def window_kinds(tiles):
    return tuple(n for n in (2, 3, 4, 5, 6, 7) if n < tiles) + (tiles,)


def image_rows(segs, length):
    row = lax.broadcasted_iota(jnp.int32, (TILE - PAIR, length), 0)
    here = row == segs
    one_hot = jnp.where(here, 1.0, 0.0).astype(BF16)
    fill = jnp.where(jnp.logical_or(here, row >= IMAGES), 0.0, negative_fill).astype(BF16)
    return one_hot, fill


def side_by_side(pair, extra):
    blank = jnp.zeros((HEAD_DIM, TILE), BF16)
    left = jnp.concatenate([pair[:HEAD_DIM], blank, extra], axis=0)
    right = jnp.concatenate([blank, pair[HEAD_DIM:], extra], axis=0)
    return jnp.concatenate([left, right], axis=1)


def pair_places(ref):
    cores, count = ref.shape[0], ref.shape[1]
    return [(core, top) for core in range(cores) for top in range(0, count, PAIR)]


def attend_forward_kernel(
    first_ref, kind_ref, flip_ref, segs_ref, qv_ref, k_ref, out_ref, lse_ref, hot_ref, keys_ref, vals_ref
):
    length = k_ref.shape[-1]
    at_q = flip_ref[0]
    places = pair_places(k_ref)
    one_hot, fill = image_rows(segs_ref[...], length)
    hot_ref[...] = one_hot
    for j, (core, top) in enumerate(places):
        rows = slice(top, top + PAIR)
        keys_ref[j] = jnp.concatenate([k_ref[core, rows, :], fill], axis=0).T
        vals_ref[j] = jnp.concatenate(
            [qv_ref[core, 1 - at_q, rows, :], jnp.ones((16, length), BF16)], axis=0
        )

    def block(b, carry):
        at = pl.ds(pl.multiple_of(b * TILE, TILE), TILE)
        first = pl.multiple_of(first_ref[b] * TILE, TILE)

        def variant(tiles):
            span = pl.ds(first, tiles * TILE)
            scores = [
                dot(
                    keys_ref[j, span, :],
                    side_by_side(qv_ref[core, at_q, top : top + PAIR, at], hot_ref[:, at]),
                    NN,
                )
                for j, (core, top) in enumerate(places)
            ]
            for j, (core, top) in enumerate(places):
                most = jnp.max(scores[j], axis=0, keepdims=True)
                expo = jnp.exp2((scores[j] - most) * SCALE_LOG2).astype(BF16)
                mixed = dot(vals_ref[j, :, span], expo, NN)
                total = mixed[PAIR : PAIR + 1, :]
                inverse = 1.0 / total
                out_ref[core, top : top + HEAD_DIM, at] = (
                    mixed[:HEAD_DIM, :TILE] * inverse[:, :TILE]
                ).astype(BF16)
                out_ref[core, top + HEAD_DIM : top + PAIR, at] = (
                    mixed[HEAD_DIM:PAIR, TILE:] * inverse[:, TILE:]
                ).astype(BF16)
                lse_ref[j, pl.ds(b, 1), :] = most * SCALE_LOG2 + jnp.log2(total)

        for tiles in window_kinds(length // TILE):
            pl.when(kind_ref[b] == tiles)(functools.partial(variant, tiles))
        return carry

    lax.fori_loop(0, length // TILE, block, 0)


def attend_backward_kernel(
    first_ref,
    kind_ref,
    flip_ref,
    segs_ref,
    qv_ref,
    k_ref,
    att_ref,
    grad_ref,
    lse_ref,
    dqv_ref,
    dk_ref,
    hot_ref,
    keys_ref,
    vals_ref,
    queries_ref,
    grads_ref,
    key_sum_ref,
    val_sum_ref,
):
    length = k_ref.shape[-1]
    at_q = flip_ref[0]
    places = pair_places(k_ref)
    one_hot, fill = image_rows(segs_ref[...], length)
    hot_ref[...] = one_hot
    pad = jnp.zeros((TILE - PAIR, length), BF16)
    for j, (core, top) in enumerate(places):
        rows = slice(top, top + PAIR)
        keys_ref[j] = jnp.concatenate([k_ref[core, rows, :], fill], axis=0).T
        vals_ref[j] = jnp.concatenate([qv_ref[core, 1 - at_q, rows, :], pad], axis=0).T
        queries_ref[j] = jnp.concatenate([qv_ref[core, at_q, rows, :], pad], axis=0).T
        grads_ref[j] = jnp.concatenate([grad_ref[core, rows, :], pad], axis=0).T
    key_sum_ref[...] = jnp.zeros(key_sum_ref.shape, F32)
    val_sum_ref[...] = jnp.zeros(val_sum_ref.shape, F32)
    no_rows = jnp.zeros((TILE - PAIR, TILE), BF16)
    lane = lax.broadcasted_iota(jnp.int32, (TILE, TILE), 1)
    in_first = lane < HEAD_DIM

    def stacked(both):
        blank = jnp.zeros_like(both)
        return jnp.concatenate(
            [jnp.where(in_first, both, blank), jnp.where(in_first, blank, both)], axis=0
        )

    def block(b, carry):
        at = pl.ds(pl.multiple_of(b * TILE, TILE), TILE)
        first = pl.multiple_of(first_ref[b] * TILE, TILE)

        def variant(tiles):
            span = pl.ds(first, tiles * TILE)
            scores = [
                dot(
                    keys_ref[j, span, :],
                    side_by_side(qv_ref[core, at_q, top : top + PAIR, at], hot_ref[:, at]),
                    NN,
                )
                for j, (core, top) in enumerate(places)
            ]
            prob_grads = [
                dot(
                    vals_ref[j, span, :],
                    side_by_side(grad_ref[core, top : top + PAIR, at], no_rows),
                    NN,
                )
                for j, (core, top) in enumerate(places)
            ]
            for j, (core, top) in enumerate(places):
                rows = slice(top, top + PAIR)
                agree = grad_ref[core, rows, at].astype(F32) * att_ref[core, rows, at].astype(F32)
                delta = jnp.concatenate(
                    [
                        jnp.sum(agree[:HEAD_DIM], axis=0, keepdims=True),
                        jnp.sum(agree[HEAD_DIM:], axis=0, keepdims=True),
                    ],
                    axis=1,
                )
                probs = jnp.exp2(scores[j] * SCALE_LOG2 - lse_ref[j, pl.ds(b, 1), :])
                score_grad = (probs * (prob_grads[j] - delta)).astype(BF16)
                val_sum_ref[j, span, :] += dot(
                    probs.astype(BF16), stacked(grads_ref[j, at, :]), NN
                )
                key_sum_ref[j, span, :] += dot(score_grad, stacked(queries_ref[j, at, :]), NN)
                query_grad = dot(k_ref[core, rows, span], score_grad, NN) * SCALE
                dqv_ref[core, at_q, top : top + HEAD_DIM, at] = query_grad[
                    :HEAD_DIM, :TILE
                ].astype(BF16)
                dqv_ref[core, at_q, top + HEAD_DIM : top + PAIR, at] = query_grad[
                    HEAD_DIM:, TILE:
                ].astype(BF16)

        for tiles in window_kinds(length // TILE):
            pl.when(kind_ref[b] == tiles)(functools.partial(variant, tiles))
        return carry

    lax.fori_loop(0, length // TILE, block, 0)
    for j, (core, top) in enumerate(places):
        rows = slice(top, top + PAIR)
        dk_ref[core, rows, :] = (key_sum_ref[j] * SCALE).T[:PAIR].astype(BF16)
        dqv_ref[core, 1 - at_q, rows, :] = val_sum_ref[j].T[:PAIR].astype(BF16)


def windows(segs):
    length = segs.shape[0]
    tiles = length // TILE
    by_tile = segs.reshape(tiles, TILE)
    begin = jnp.sum(segs[None, :] < by_tile[:, :1], axis=1)
    end = jnp.sum(segs[None, :] <= by_tile[:, -1:], axis=1)
    first = begin // TILE
    need = (end + TILE - 1) // TILE - first
    kinds = jnp.asarray(window_kinds(tiles), jnp.int32)
    kind = jnp.min(jnp.where(kinds[None, :] >= need[:, None], kinds[None, :], tiles), axis=1)
    return jnp.minimum(first, tiles - kind).astype(jnp.int32), kind.astype(jnp.int32)


def attention_specs(keys):
    cores, count, length = keys.shape
    pairs = cores * count // PAIR
    step = pairs if pairs <= 4 else 4
    part = count * step // pairs
    rows = pl.BlockSpec((cores, part, length), lambda i, *_: (0, i, 0))
    two = pl.BlockSpec((cores, 2, part, length), lambda i, *_: (0, 0, i, 0))
    segs = pl.BlockSpec((1, length), lambda i, *_: (0, 0))
    lse = pl.BlockSpec((step, length // TILE, 2 * TILE), lambda i, *_: (i, 0, 0))
    return pairs, step, rows, two, segs, lse


def attend_forward(query_value, keys, place):
    first, kind, flip, segs = place
    length = segs.shape[0]
    pairs, step, rows, two, segs_spec, lse = attention_specs(keys)
    return pl.pallas_call(
        attend_forward_kernel,
        grid_spec=pltpu.PrefetchScalarGridSpec(
            num_scalar_prefetch=3,
            grid=(pairs // step,),
            in_specs=[segs_spec, two, rows],
            out_specs=[rows, lse],
            scratch_shapes=[
                pltpu.VMEM((TILE - PAIR, length), BF16),
                pltpu.VMEM((step, length, TILE), BF16),
                pltpu.VMEM((step, PAIR + 16, length), BF16),
            ],
        ),
        out_shape=[
            jax.ShapeDtypeStruct(keys.shape, BF16),
            jax.ShapeDtypeStruct((pairs, length // TILE, 2 * TILE), F32),
        ],
        compiler_params=pltpu.CompilerParams(vmem_limit_bytes=40 << 20),
        name="attend_forward",
    )(first, kind, flip, segs[None, :], query_value, keys)


def attend_backward(query_value, keys, attended, grad, lse, place):
    first, kind, flip, segs = place
    length = segs.shape[0]
    pairs, step, rows, two, segs_spec, lse_spec = attention_specs(keys)
    wide = pltpu.VMEM((step, length, TILE), BF16)
    total = pltpu.VMEM((step, length, TILE), F32)
    return pl.pallas_call(
        attend_backward_kernel,
        grid_spec=pltpu.PrefetchScalarGridSpec(
            num_scalar_prefetch=3,
            grid=(pairs // step,),
            in_specs=[segs_spec, two, rows, rows, rows, lse_spec],
            out_specs=[two, rows],
            scratch_shapes=[
                pltpu.VMEM((TILE - PAIR, length), BF16),
                wide,
                wide,
                wide,
                wide,
                total,
                total,
            ],
        ),
        out_shape=[
            jax.ShapeDtypeStruct(query_value.shape, BF16),
            jax.ShapeDtypeStruct(keys.shape, BF16),
        ],
        compiler_params=pltpu.CompilerParams(vmem_limit_bytes=40 << 20),
        name="attend_backward",
    )(first, kind, flip, segs[None, :], query_value, keys, attended, grad, lse)


def gelu_parts(values):
    below = 0.5 * (1.0 + lax.erf(values * (0.5 ** 0.5)))
    density = jnp.exp(values * values * -0.5) * ((2.0 * math.pi) ** -0.5)
    return values * below, below + values * density


def feed_forward_kernel(norm_ref, cot_ref, up_ref, down_ref, *refs):
    *earlier, mlp_ref, back_ref, up_grad_ref, down_grad_ref, act_ref, pre_ref = refs[:-1]
    sum_ref = mlp_ref if mlp_ref.dtype == F32 else refs[-1]
    rows = norm_ref.shape[0]
    chunk = min(rows, 256)

    @pl.when(pl.program_id(0) == 0)
    def _():
        sum_ref[...] = jnp.zeros(sum_ref.shape, F32)
        back_ref[...] = jnp.zeros(back_ref.shape, F32)

    for start in range(0, rows, chunk):
        at = slice(start, start + chunk)
        pre_act = dot(norm_ref[at, :], up_ref[...], NT)
        act_grad = dot(cot_ref[at, :], down_ref[...], NT)
        activation, slope = gelu_parts(pre_act)
        activation = activation.astype(BF16)
        pre_grad = (act_grad * slope).astype(BF16)
        act_ref[at, :] = activation
        pre_ref[at, :] = pre_grad
        sum_ref[at, :] += dot(activation, down_ref[...], NN)
        back_ref[at, :] += dot(pre_grad, up_ref[...], NN)
    up_grad = dot(pre_ref[...], norm_ref[...], TN)
    down_grad = dot(act_ref[...], cot_ref[...], TN)
    if earlier:
        up_grad = up_grad + earlier[0][...].astype(F32)
        down_grad = down_grad + earlier[1][...].astype(F32)
    up_grad_ref[...] = up_grad.astype(BF16)
    down_grad_ref[...] = down_grad.astype(BF16)

    if mlp_ref.dtype != F32:

        @pl.when(pl.program_id(0) == pl.num_programs(0) - 1)
        def _():
            mlp_ref[...] = sum_ref[...].astype(mlp_ref.dtype)


def feed_forward(norm, cot, up, down, earlier=(), kind=F32):
    rows, width = norm.shape
    hidden = up.shape[0]
    part = 512 if hidden % 512 == 0 else hidden
    whole = pl.BlockSpec((rows, width), lambda i: (0, 0))
    block = pl.BlockSpec((part, width), lambda i: (i, 0))
    grads = jax.ShapeDtypeStruct((hidden, width), BF16)
    return pl.pallas_call(
        feed_forward_kernel,
        grid=(hidden // part,),
        in_specs=[whole, whole, block, block] + [block] * len(earlier),
        out_specs=[whole, whole, block, block],
        out_shape=[
            jax.ShapeDtypeStruct((rows, width), kind),
            jax.ShapeDtypeStruct((rows, width), F32),
            grads,
            grads,
        ],
        scratch_shapes=[
            pltpu.VMEM((rows, part), BF16),
            pltpu.VMEM((rows, part), BF16),
            pltpu.VMEM((8, 128) if kind == F32 else (rows, width), F32),
        ],
        compiler_params=pltpu.CompilerParams(vmem_limit_bytes=58 << 20),
        name="feed_forward",
    )(norm, cot, up, down, *earlier)


def middle_kernel(parts, residual_ref, cot_ref, gain_ref, *refs):
    mlp_refs, back_refs = refs[:parts], refs[parts : 2 * parts]
    output_ref, res_grad_ref, branch_ref, norm_grad_ref = refs[2 * parts :]

    @pl.when(pl.program_id(0) == 0)
    def _():
        norm_grad_ref[...] = jnp.zeros(norm_grad_ref.shape, F32)

    residual = residual_ref[...]
    output_ref[...] = sum([ref[...].astype(F32) for ref in mlp_refs], residual).astype(BF16)
    grad = functools.reduce(jnp.add, [ref[...] for ref in back_refs])
    back, gain_grad, bias_grad = layer_norm_back(residual, gain_ref[...], grad)
    res_grad = cot_ref[...].astype(F32) + back
    res_grad_ref[...] = res_grad
    branch_ref[...] = res_grad.astype(BF16)
    norm_grad_ref[0:1, :] += gain_grad
    norm_grad_ref[1:2, :] += bias_grad


def middle(residual, cot, gain, mlps, backs):
    rows, width = residual.shape
    parts = len(mlps)
    step = 256
    block = pl.BlockSpec((step, width), lambda i: (i, 0))
    sums = jax.ShapeDtypeStruct((rows, width), F32)
    low = jax.ShapeDtypeStruct((rows, width), BF16)
    return pl.pallas_call(
        functools.partial(middle_kernel, parts),
        grid=(rows // step,),
        in_specs=[block, block, pl.BlockSpec((1, width), lambda i: (0, 0))] + [block] * (2 * parts),
        out_specs=[block, block, block, pl.BlockSpec((8, width), lambda i: (0, 0))],
        out_shape=[low, sums, low, jax.ShapeDtypeStruct((8, width), F32)],
        compiler_params=pltpu.CompilerParams(vmem_limit_bytes=40 << 20),
        name="middle",
    )(residual, cot, gain[None, :], *mlps, *backs)


def last_kernel(rows_ref, grad_ref, res_grad_ref, gain_ref, in_grad_ref, norm_grad_ref):
    @pl.when(pl.program_id(0) == 0)
    def _():
        norm_grad_ref[...] = jnp.zeros(norm_grad_ref.shape, F32)

    back, gain_grad, bias_grad = layer_norm_back(
        rows_ref[...].astype(F32), gain_ref[...], grad_ref[...]
    )
    in_grad_ref[...] = (res_grad_ref[...] + back).astype(BF16)
    norm_grad_ref[0:1, :] += gain_grad
    norm_grad_ref[1:2, :] += bias_grad


def last(rows_in, grad, res_grad, gain):
    rows, width = rows_in.shape
    step = 256
    block = pl.BlockSpec((step, width), lambda i: (i, 0))
    few = pl.BlockSpec((8, width), lambda i: (0, 0))
    return pl.pallas_call(
        last_kernel,
        grid=(rows // step,),
        in_specs=[block, block, block, pl.BlockSpec((1, width), lambda i: (0, 0))],
        out_specs=[block, few],
        out_shape=[
            jax.ShapeDtypeStruct((rows, width), BF16),
            jax.ShapeDtypeStruct((8, width), F32),
        ],
        compiler_params=pltpu.CompilerParams(vmem_limit_bytes=40 << 20),
        name="last",
    )(rows_in, grad, res_grad, gain[None, :])


def add(*terms):
    return functools.reduce(jnp.add, [item.astype(F32) for item in terms]).astype(BF16)


def swap(values, axis):
    name, size, mask = {
        "core": ("dp", 4, 1),
        "y": ("dp", 4, 2),
        "x": ("mp", 8, 1),
        "z1": ("mp", 8, 2),
        "z2": ("mp", 8, 4),
        "z3": ("mp", 8, 6),
    }[axis]
    return lax.ppermute(values, name, [(i, i ^ mask) for i in range(size)])


def order(at, mine, other):
    return jnp.where(at == 0, jnp.stack([mine, other]), jnp.stack([other, mine]))


class Line:
    def __init__(self):
        self.last = ()

    def __call__(self, step, *args):
        args, _ = lax.optimization_barrier((args, self.last))
        result = step(*args)
        self.last = tuple(jax.tree.leaves(result))
        return result


def on_cube(
    inputs,
    segments,
    ln1_gain,
    ln1_bias,
    w_query,
    w_key,
    w_value,
    w_output,
    ln2_gain,
    ln2_bias,
    w_up,
    w_down,
    cotangent,
):
    rows, width = inputs.shape
    local = w_query.shape[1]
    at_dp, at_mp = lax.axis_index("dp"), lax.axis_index("mp")
    at_y, at_core = at_dp // 2, at_dp % 2
    line = Line()

    def pick(values, at):
        return lax.dynamic_index_in_dim(values, at, 0, keepdims=False)

    def cut_attention(query, key, value, out):
        kinds = jnp.stack([query.T, key.T, value.T, out]).reshape(2, 2, 2, HEAD_DIM, width)
        return pick(kinds.transpose(0, 2, 1, 3, 4).reshape(4, 2, HEAD_DIM, width), at_dp)

    def cut_mlp(up, down):
        pieces = jnp.stack([up.T, down]).reshape(2, 4, -1, width)
        return lax.dynamic_index_in_dim(pieces, at_dp, 1, keepdims=False)

    def join(*parts):
        return jnp.concatenate(parts, 0)

    along_z = ("z2", "z1", "z3")
    attn_piece = line(cut_attention, w_query, w_key, w_value, w_output)
    attn_z = [swap(attn_piece, axis) for axis in along_z]
    mlp_piece = line(cut_mlp, w_up, w_down)
    mlp_z = [swap(mlp_piece, axis) for axis in along_z]

    def begin(rows_in):
        return layer_norm(rows_in.astype(F32), ln1_gain, ln1_bias).astype(BF16)

    norm_one = line(begin, inputs)
    segs = pick(segments, at_mp)
    place = windows(segs) + (at_y.reshape(1), segs)
    place = line(lambda item: item, place)

    near_z = line(lambda *parts: jnp.stack(parts[:4]), attn_piece, *attn_z, mlp_z[1])
    near_got = swap(near_z, "y")
    far_z = swap(near_z, "x")
    near_y = line(lambda *parts: jnp.stack(parts[:2]), near_z, near_got, far_z, mlp_z[0])
    near_got = swap(near_y, "core")
    far_got = swap(far_z, "y")

    def both_cores(mine, other):
        query_value, key_out = [jnp.stack([mine[:, :, i], other[:, :, i]]) for i in (0, 1)]
        key, out = [
            lax.dynamic_index_in_dim(key_out, at, 1, keepdims=False).reshape(-1, width)
            for at in (at_y, 1 - at_y)
        ]
        return query_value.reshape(-1, width), key, out

    def project(weights, norm):
        query_value = dot(weights[0], norm, NT).astype(BF16).reshape(2, 2, -1, rows)
        return query_value, dot(weights[1], norm, NT).astype(BF16).reshape(2, -1, rows)

    def attend(query_value, keys):
        return attend_forward(query_value, keys, place)

    def branch(base, attended, weights):
        return base + dot(attended.reshape(-1, rows), weights[2], TN)

    def mlp_along_z(*parts):
        return [jnp.concatenate([item[i] for item in parts], 0) for i in (0, 1)]

    def mlp_second(up, up_got, down, down_got):
        return jnp.concatenate([up, up_got], 0), jnp.stack([down, down_got])

    near_w = line(both_cores, near_y, near_got)
    near = line(project, near_w, norm_one)
    up, down = line(mlp_along_z, mlp_piece, *mlp_z)
    up_got, down_got = swap(up, "x"), swap(down, "y")
    near += tuple(line(attend, *near))

    far_y = line(lambda *parts: jnp.stack(parts), far_z, far_got)
    far_got = swap(far_y, "core")
    up, down = line(mlp_second, up, up_got, down, down_got)
    up_got, down_got = swap(up, "y"), swap(down, "x")
    residual = line(branch, inputs.astype(F32), near[2], near_w)
    far_w = line(both_cores, far_y, far_got)
    far = line(project, far_w, norm_one)
    far += tuple(line(attend, *far))

    def second_norm(residual, attended, weights):
        residual = branch(residual, attended, weights)
        return residual, layer_norm(residual, ln2_gain, ln2_bias).astype(BF16)

    cot_other = swap(cotangent, "core")
    far_attended, cot_other = lax.optimization_barrier((far[2], cot_other))
    residual, norm_two = line(second_norm, residual, far_attended, far_w)
    norm_two_other = swap(norm_two, "core")

    def mlp_last(up, up_got, down, down_got):
        return jnp.concatenate([up, up_got], 0), jnp.concatenate([down, down_got], 1).reshape(-1, width)

    up, down = line(mlp_last, up, up_got, down, down_got)
    mlp_b, back_b, *grads = line(
        lambda *args: feed_forward(*args, kind=BF16), norm_two_other, cot_other, up, down
    )
    mlp_b, back_b = swap(mlp_b, "core"), swap(back_b, "core")
    mlp_a, back_a, up_grad, down_grad = line(feed_forward, norm_two, cotangent, up, down, grads)

    def before_attention(attended, weights, grad):
        att_grad = dot(weights[2], grad, NT).astype(BF16).reshape(attended.shape)
        return att_grad, dot(attended.reshape(-1, rows), grad, NN).astype(BF16)


    quarter = up.shape[0] // 4

    def up_sum_of(terms, low, high):
        return add(*[item[low:high] for item in terms])

    def down_sum_of(terms, y, x, low=0, high=quarter):
        whole = terms[0].reshape(2, 2, quarter, width)[y, x, low:high]
        return add(whole, *[item.reshape(-1, quarter, width)[y, low:high] for item in terms[1:]])

    def mlp_sum_first(up_terms, down_terms):
        return (
            up_sum_of(up_terms, 2 * quarter, 4 * quarter),
            jnp.stack([down_sum_of(down_terms, y, 1) for y in (0, 1)]),
        )

    up_terms, down_terms = (up_grad,), (down_grad,)
    sends = line(mlp_sum_first, up_terms, down_terms)
    up_terms += (swap(sends[0], "y"),)
    down_terms += (swap(sends[1], "x"),)

    def attend_back(saved, att_grad):
        return attend_backward(*saved[:3], att_grad, saved[3], place)

    def weight_grads(query_value_grad, key_grad, out_grad, norm):
        query_value = dot(query_value_grad.reshape(-1, rows), norm, NN).astype(BF16)
        keys = dot(key_grad.reshape(-1, rows), norm, NN).astype(BF16)
        sums = (
            query_value.reshape(2, 2, -1, width),
            keys.reshape(2, -1, width),
            out_grad.reshape(2, -1, width),
        )
        return sums, [item[1] for item in sums]

    def project_back(grads, weights):
        return dot(grads[0].reshape(-1, rows), weights[0], TN) + dot(
            grads[1].reshape(-1, rows), weights[1], TN
        )

    def attn_terms_of(mine, got, at):
        terms = [(mine[0][0, at], mine[1][0], mine[2][0]), (got[0][at], got[1], got[2])]
        first = at_y == at
        return [
            [item[0] for item in terms],
            [jnp.where(first, item[1], item[2]) for item in terms],
        ]

    def sum_other_y(mine, got):
        return jnp.stack([add(*terms) for terms in attn_terms_of(mine, got, 1)])

    def sum_this_y(mine, got, from_y):
        terms = attn_terms_of(mine, got, 0)
        return jnp.stack([add(*terms[i], from_y[i]) for i in (0, 1)])

    output, res_grad, branch_grad, norm_two_grads = line(
        middle, residual, cotangent, ln2_gain, [mlp_a, mlp_b], [back_a, back_b]
    )
    far_att, far_out = line(before_attention, far[2], far_w, branch_grad)
    far_grads = line(attend_back, far, far_att)
    far_mine, sends = line(weight_grads, *far_grads, far_out, norm_one)
    far_got = [swap(item, "core") for item in sends]
    def mlp_sum_second(up_terms, down_terms):
        return up_sum_of(up_terms, quarter, 2 * quarter), down_sum_of(down_terms, 1, 0)

    sends = line(mlp_sum_second, up_terms, down_terms)
    up_terms += (swap(sends[0], "x"),)
    down_y = swap(sends[1], "y")

    norm_one_grad = line(project_back, far_grads, far_w)
    near_att, near_out = line(before_attention, near[2], near_w, branch_grad)
    far_y = swap(line(sum_other_y, far_mine, far_got), "y")

    part = quarter // 4

    def mlp_sum_of_z(up_terms, down_terms, down_y, low, high):
        low, high = low * part, high * part
        return jnp.stack(
            [
                up_sum_of(up_terms, low, high),
                down_sum_of(down_terms + (jnp.stack([down_y, down_y]),), 0, 0, low, high),
            ]
        )

    mlp_terms = (up_terms, down_terms, down_y)
    mlp_z1 = swap(line(lambda *terms: mlp_sum_of_z(*terms, 2, 4), *mlp_terms), "z1")
    near_grads = line(attend_back, near, near_att)
    mlp_send = line(
        lambda got, *terms: add(mlp_sum_of_z(*terms, 1, 2), got[:, part:]), mlp_z1, *mlp_terms
    )
    mlp_z2 = swap(mlp_send, "z2")
    near_mine, sends = line(weight_grads, *near_grads, near_out, norm_one)
    near_got = [swap(item, "core") for item in sends]
    far_x = swap(line(sum_this_y, far_mine, far_got, far_y), "x")
    near_y = swap(line(sum_other_y, near_mine, near_got), "y")

    def add_project_back(norm_one_grad, grads, weights):
        return norm_one_grad + project_back(grads, weights)

    def finish(norm_one_grad):
        in_grad, norm_one_grads = last(inputs, norm_one_grad, res_grad, ln1_gain)
        return jnp.concatenate([norm_one_grads[:2], norm_two_grads[:2]]), in_grad

    norm_one_grad = line(add_project_back, norm_one_grad, near_grads, near_w)
    norm_sums, in_grad = line(finish, norm_one_grad)
    got = swap(norm_sums, "core")

    mlp_sum = line(
        lambda got, other, *terms: add(mlp_sum_of_z(*terms, 0, 1), got[:, :part], other),
        mlp_z1,
        mlp_z2,
        *mlp_terms,
    )
    mlp_got = swap(mlp_sum, "y")
    norm_sums = line(jnp.add, norm_sums, got)
    got = swap(norm_sums, "y")

    def attn_sum_z(mine, got, from_y, from_x):
        from_x = from_x.reshape(2, -1, width)
        whole = sum_this_y(mine, got, from_y).astype(F32) + from_x
        return [whole[:, at * HEAD_DIM : (at + 1) * HEAD_DIM].astype(BF16) for at in range(4)]

    attn_mine, *sends = line(attn_sum_z, near_mine, near_got, near_y, far_x)
    attn_z = [swap(item, axis) for item, axis in zip(sends, along_z)]

    def in_order(piece, y, core, both):
        return order(at_core, order(at_y, piece, y), order(at_y, core, both))

    norm_sums = line(jnp.add, norm_sums, got)
    got = swap(norm_sums, "x")
    attn_sum = line(lambda _, *terms: add(*terms), mlp_got, attn_mine, *attn_z)
    attn_got = [
        lax.ppermute(attn_sum, "dp", [(i, i ^ mask) for i in range(4)]) for mask in (2, 1, 3)
    ]
    norm_sums = line(jnp.add, norm_sums, got)
    got = swap(norm_sums, "z1")
    mlp_sum = line(functools.partial(order, at_y), mlp_sum, mlp_got)
    mlp_got = swap(mlp_sum, "core")
    norm_sums = line(jnp.add, norm_sums, got)
    got = swap(norm_sums, "z2")
    attn_sum = line(in_order, attn_sum, *attn_got)
    attn_sum = line(
        lambda item: item.transpose(1, 2, 0, 3, 4).reshape(4, local, width).astype(F32), attn_sum
    )
    attn_sums = line(lambda item: (item[0].T, item[1].T, item[2].T, item[3]), attn_sum)
    norm_sums = line(jnp.add, norm_sums, got)
    mlp_sum = line(functools.partial(order, at_core), mlp_sum, mlp_got)
    up_sum, down_sum = line(
        lambda item: tuple(item.transpose(2, 1, 0, 3, 4).reshape(2, -1, width).astype(F32)), mlp_sum
    )
    up_sum = line(jnp.transpose, up_sum)
    norm_sums = lax.dynamic_slice_in_dim(norm_sums, at_mp * (width // 8), width // 8, 1)
    return (
        output,
        in_grad,
        norm_sums[0],
        norm_sums[1],
        *attn_sums,
        norm_sums[2],
        norm_sums[3],
        up_sum,
        down_sum,
    )


def on_any(
    mp_size,
    inputs,
    segments,
    ln1_gain,
    ln1_bias,
    w_query,
    w_key,
    w_value,
    w_output,
    ln2_gain,
    ln2_bias,
    w_up,
    w_down,
    cotangent,
):
    rows, width = inputs.shape
    seq_length = segments.shape[1]
    shared_by = seq_length // rows
    at_mp = lax.axis_index("mp")
    groups = [[start + i for i in range(shared_by)] for start in range(0, mp_size, shared_by)]

    def exchange(values, split, join):
        if shared_by == 1:
            return values
        return lax.all_to_all(values, "mp", split, join, axis_index_groups=groups, tiled=True)

    def gather(parts):
        return lax.all_gather(parts, "mp", axis=1, tiled=True)

    def reduce(parts):
        return lax.psum(lax.psum_scatter(parts, "mp", scatter_dimension=1, tiled=True), "dp")

    attn_w = gather(jnp.stack([w_query.T, w_value.T, w_key.T, w_output]))
    up, down = gather(jnp.stack([w_up.T, w_down]))
    project, w_out = attn_w[:3].reshape(3 * width, width), attn_w[3]

    segs = lax.dynamic_index_in_dim(segments, at_mp // shared_by, 0, keepdims=False)
    place = windows(segs) + (jnp.zeros((1,), jnp.int32), segs)
    resid_in = inputs.astype(F32)
    norm_one = layer_norm(resid_in, ln1_gain, ln1_bias).astype(BF16)
    projected = dot(project, norm_one, NT).astype(BF16).reshape(3, width, rows)
    projected = exchange(projected, 1, 2)
    query_value, keys = projected[None, :2], projected[2:]
    heads_out, lse = attend_forward(query_value, keys, place)
    attended = exchange(heads_out[0], 1, 0)
    residual = resid_in + dot(attended, w_out, TN)
    norm_two = layer_norm(residual, ln2_gain, ln2_bias).astype(BF16)
    mlp_branch, norm_two_grad, *mlp_grads = feed_forward(norm_two, cotangent, up, down)
    up_sum, down_sum = reduce(jnp.stack(mlp_grads)).astype(F32)

    output, res_grad, branch_grad, norm_two_grads = middle(
        residual, cotangent, ln2_gain, [mlp_branch], [norm_two_grad]
    )
    out_grad = dot(attended, branch_grad, NN).astype(BF16)
    att_grad = exchange(dot(w_out, branch_grad, NT).astype(BF16), 0, 1)
    query_value_grad, key_grad = attend_backward(
        query_value, keys, heads_out, att_grad[None], lse, place
    )
    proj_grad = exchange(jnp.concatenate([query_value_grad[0], key_grad]), 2, 1)
    proj_grad = proj_grad.reshape(3 * width, rows)
    project_grad = dot(proj_grad, norm_one, NN).astype(BF16).reshape(3, width, width)
    attn_sum = reduce(jnp.concatenate([project_grad, out_grad[None]])).astype(F32)
    in_grad, norm_one_grads = last(inputs, dot(proj_grad, project, TN), res_grad, ln1_gain)
    norm_parts = jnp.concatenate([norm_one_grads[:2], norm_two_grads[:2]])
    norm_sums = lax.dynamic_slice_in_dim(
        lax.psum(norm_parts, ("dp", "mp")), at_mp * (width // mp_size), width // mp_size, 1
    )
    return (
        output,
        in_grad,
        norm_sums[0],
        norm_sums[1],
        attn_sum[0].T,
        attn_sum[2].T,
        attn_sum[1].T,
        attn_sum[3],
        norm_sums[2],
        norm_sums[3],
        up_sum.T,
        down_sum,
    )


def shards(dp_size, mp_size, inputs, segments, *rest):
    if dp_size == 4 and mp_size == 8 and inputs.shape[0] == segments.shape[1]:
        return on_cube(inputs, segments, *rest)
    return on_any(mp_size, inputs, segments, *rest)


def solution(mesh):
    return jax.shard_map(
        functools.partial(shards, mesh.shape["dp"], mesh.shape["mp"]),
        mesh=mesh,
        in_specs=(
            P(("dp", "mp"), None),
            P("dp", None),
            P(),
            P(),
            P(None, "mp"),
            P(None, "mp"),
            P(None, "mp"),
            P("mp", None),
            P(),
            P(),
            P(None, "mp"),
            P("mp", None),
            P(("dp", "mp"), None),
        ),
        out_specs=(
            P(("dp", "mp"), None),
            P(("dp", "mp"), None),
            P("mp"),
            P("mp"),
            P(None, "mp"),
            P(None, "mp"),
            P(None, "mp"),
            P("mp", None),
            P("mp"),
            P("mp"),
            P(None, "mp"),
            P("mp", None),
        ),
        check_vma=False,
    )
```

```python
import functools
import math

import jax
import jax.numpy as jnp
from jax import lax
from jax.experimental import pallas as pl
from jax.experimental.pallas import tpu as pltpu
from jax.sharding import PartitionSpec as P

HEAD_DIM = 48
PAIR = 2 * HEAD_DIM
IMAGES = 4
TILE = 128
norm_eps = 1e-06
negative_fill = -1e30
SCALE = HEAD_DIM ** (-0.5)
SCALE_LOG2 = SCALE * math.log2(math.e)
BF16 = jnp.bfloat16
F32 = jnp.float32


def layer_norm(values, gain, bias):
    center = jnp.mean(values, axis=-1, keepdims=True)
    shifted = values - center
    spread = jnp.mean(shifted * shifted, axis=-1, keepdims=True)
    return shifted * lax.rsqrt(spread + norm_eps) * gain + bias


def layer_norm_back(values, gain, grad):
    shifted = values - jnp.mean(values, axis=-1, keepdims=True)
    scale = lax.rsqrt(jnp.mean(shifted * shifted, axis=-1, keepdims=True) + norm_eps)
    unit = shifted * scale
    scaled = grad * gain
    back = scale * (
        scaled
        - jnp.mean(scaled, axis=-1, keepdims=True)
        - unit * jnp.mean(scaled * unit, axis=-1, keepdims=True)
    )
    return back, jnp.sum(grad * unit, axis=0, keepdims=True), jnp.sum(grad, axis=0, keepdims=True)


def dot(left, right, dims):
    return lax.dot_general(left, right, (dims, ((), ())), preferred_element_type=F32)


NN = ((1,), (0,))
NT = ((1,), (1,))
TN = ((0,), (0,))


def window_kinds(tiles):
    return tuple(n for n in (2, 3, 4, 5, 6, 7) if n < tiles) + (tiles,)


def image_rows(segs, length):
    row = lax.broadcasted_iota(jnp.int32, (TILE - PAIR, length), 0)
    here = row == segs
    one_hot = jnp.where(here, 1.0, 0.0).astype(BF16)
    fill = jnp.where(jnp.logical_or(here, row >= IMAGES), 0.0, negative_fill).astype(BF16)
    return one_hot, fill


def side_by_side(pair, extra):
    blank = jnp.zeros((HEAD_DIM, TILE), BF16)
    left = jnp.concatenate([pair[:HEAD_DIM], blank, extra], axis=0)
    right = jnp.concatenate([blank, pair[HEAD_DIM:], extra], axis=0)
    return jnp.concatenate([left, right], axis=1)


def pair_places(ref):
    cores, count = ref.shape[0], ref.shape[1]
    return [(core, top) for core in range(cores) for top in range(0, count, PAIR)]


def attend_forward_kernel(
    first_ref, kind_ref, flip_ref, segs_ref, qv_ref, k_ref, out_ref, lse_ref, hot_ref, keys_ref, vals_ref
):
    length = k_ref.shape[-1]
    at_q = flip_ref[0]
    places = pair_places(k_ref)
    one_hot, fill = image_rows(segs_ref[...], length)
    hot_ref[...] = one_hot
    for j, (core, top) in enumerate(places):
        rows = slice(top, top + PAIR)
        keys_ref[j] = jnp.concatenate([k_ref[core, rows, :], fill], axis=0).T
        vals_ref[j] = jnp.concatenate(
            [qv_ref[core, 1 - at_q, rows, :], jnp.ones((16, length), BF16)], axis=0
        )

    def block(b, carry):
        at = pl.ds(pl.multiple_of(b * TILE, TILE), TILE)
        first = pl.multiple_of(first_ref[b] * TILE, TILE)

        def variant(tiles):
            span = pl.ds(first, tiles * TILE)
            scores = [
                dot(
                    keys_ref[j, span, :],
                    side_by_side(qv_ref[core, at_q, top : top + PAIR, at], hot_ref[:, at]),
                    NN,
                )
                for j, (core, top) in enumerate(places)
            ]
            for j, (core, top) in enumerate(places):
                most = jnp.max(scores[j], axis=0, keepdims=True)
                expo = jnp.exp2((scores[j] - most) * SCALE_LOG2).astype(BF16)
                mixed = dot(vals_ref[j, :, span], expo, NN)
                total = mixed[PAIR : PAIR + 1, :]
                inverse = 1.0 / total
                out_ref[core, top : top + HEAD_DIM, at] = (
                    mixed[:HEAD_DIM, :TILE] * inverse[:, :TILE]
                ).astype(BF16)
                out_ref[core, top + HEAD_DIM : top + PAIR, at] = (
                    mixed[HEAD_DIM:PAIR, TILE:] * inverse[:, TILE:]
                ).astype(BF16)
                lse_ref[j, pl.ds(b, 1), :] = most * SCALE_LOG2 + jnp.log2(total)

        for tiles in window_kinds(length // TILE):
            pl.when(kind_ref[b] == tiles)(functools.partial(variant, tiles))
        return carry

    lax.fori_loop(0, length // TILE, block, 0)


def attend_backward_kernel(
    first_ref,
    kind_ref,
    flip_ref,
    segs_ref,
    qv_ref,
    k_ref,
    att_ref,
    grad_ref,
    lse_ref,
    dqv_ref,
    dk_ref,
    hot_ref,
    keys_ref,
    vals_ref,
    queries_ref,
    grads_ref,
    key_sum_ref,
    val_sum_ref,
):
    length = k_ref.shape[-1]
    at_q = flip_ref[0]
    places = pair_places(k_ref)
    one_hot, fill = image_rows(segs_ref[...], length)
    hot_ref[...] = one_hot
    pad = jnp.zeros((TILE - PAIR, length), BF16)
    for j, (core, top) in enumerate(places):
        rows = slice(top, top + PAIR)
        keys_ref[j] = jnp.concatenate([k_ref[core, rows, :], fill], axis=0).T
        vals_ref[j] = jnp.concatenate([qv_ref[core, 1 - at_q, rows, :], pad], axis=0).T
        queries_ref[j] = jnp.concatenate([qv_ref[core, at_q, rows, :], pad], axis=0).T
        grads_ref[j] = jnp.concatenate([grad_ref[core, rows, :], pad], axis=0).T
    key_sum_ref[...] = jnp.zeros(key_sum_ref.shape, F32)
    val_sum_ref[...] = jnp.zeros(val_sum_ref.shape, F32)
    no_rows = jnp.zeros((TILE - PAIR, TILE), BF16)
    lane = lax.broadcasted_iota(jnp.int32, (TILE, TILE), 1)
    in_first = lane < HEAD_DIM

    def stacked(both):
        blank = jnp.zeros_like(both)
        return jnp.concatenate(
            [jnp.where(in_first, both, blank), jnp.where(in_first, blank, both)], axis=0
        )

    def block(b, carry):
        at = pl.ds(pl.multiple_of(b * TILE, TILE), TILE)
        first = pl.multiple_of(first_ref[b] * TILE, TILE)

        def variant(tiles):
            span = pl.ds(first, tiles * TILE)
            scores = [
                dot(
                    keys_ref[j, span, :],
                    side_by_side(qv_ref[core, at_q, top : top + PAIR, at], hot_ref[:, at]),
                    NN,
                )
                for j, (core, top) in enumerate(places)
            ]
            prob_grads = [
                dot(
                    vals_ref[j, span, :],
                    side_by_side(grad_ref[core, top : top + PAIR, at], no_rows),
                    NN,
                )
                for j, (core, top) in enumerate(places)
            ]
            for j, (core, top) in enumerate(places):
                rows = slice(top, top + PAIR)
                agree = grad_ref[core, rows, at].astype(F32) * att_ref[core, rows, at].astype(F32)
                delta = jnp.concatenate(
                    [
                        jnp.sum(agree[:HEAD_DIM], axis=0, keepdims=True),
                        jnp.sum(agree[HEAD_DIM:], axis=0, keepdims=True),
                    ],
                    axis=1,
                )
                probs = jnp.exp2(scores[j] * SCALE_LOG2 - lse_ref[j, pl.ds(b, 1), :])
                score_grad = (probs * (prob_grads[j] - delta)).astype(BF16)
                val_sum_ref[j, span, :] += dot(
                    probs.astype(BF16), stacked(grads_ref[j, at, :]), NN
                )
                key_sum_ref[j, span, :] += dot(score_grad, stacked(queries_ref[j, at, :]), NN)
                query_grad = dot(k_ref[core, rows, span], score_grad, NN) * SCALE
                dqv_ref[core, at_q, top : top + HEAD_DIM, at] = query_grad[
                    :HEAD_DIM, :TILE
                ].astype(BF16)
                dqv_ref[core, at_q, top + HEAD_DIM : top + PAIR, at] = query_grad[
                    HEAD_DIM:, TILE:
                ].astype(BF16)

        for tiles in window_kinds(length // TILE):
            pl.when(kind_ref[b] == tiles)(functools.partial(variant, tiles))
        return carry

    lax.fori_loop(0, length // TILE, block, 0)
    for j, (core, top) in enumerate(places):
        rows = slice(top, top + PAIR)
        dk_ref[core, rows, :] = (key_sum_ref[j] * SCALE).T[:PAIR].astype(BF16)
        dqv_ref[core, 1 - at_q, rows, :] = val_sum_ref[j].T[:PAIR].astype(BF16)


def windows(segs):
    length = segs.shape[0]
    tiles = length // TILE
    by_tile = segs.reshape(tiles, TILE)
    begin = jnp.sum(segs[None, :] < by_tile[:, :1], axis=1)
    end = jnp.sum(segs[None, :] <= by_tile[:, -1:], axis=1)
    first = begin // TILE
    need = (end + TILE - 1) // TILE - first
    kinds = jnp.asarray(window_kinds(tiles), jnp.int32)
    kind = jnp.min(jnp.where(kinds[None, :] >= need[:, None], kinds[None, :], tiles), axis=1)
    return jnp.minimum(first, tiles - kind).astype(jnp.int32), kind.astype(jnp.int32)


def attention_specs(keys):
    cores, count, length = keys.shape
    pairs = cores * count // PAIR
    step = pairs if pairs <= 4 else 4
    part = count * step // pairs
    rows = pl.BlockSpec((cores, part, length), lambda i, *_: (0, i, 0))
    two = pl.BlockSpec((cores, 2, part, length), lambda i, *_: (0, 0, i, 0))
    segs = pl.BlockSpec((1, length), lambda i, *_: (0, 0))
    lse = pl.BlockSpec((step, length // TILE, 2 * TILE), lambda i, *_: (i, 0, 0))
    return pairs, step, rows, two, segs, lse


def attend_forward(query_value, keys, place):
    first, kind, flip, segs = place
    length = segs.shape[0]
    pairs, step, rows, two, segs_spec, lse = attention_specs(keys)
    return pl.pallas_call(
        attend_forward_kernel,
        grid_spec=pltpu.PrefetchScalarGridSpec(
            num_scalar_prefetch=3,
            grid=(pairs // step,),
            in_specs=[segs_spec, two, rows],
            out_specs=[rows, lse],
            scratch_shapes=[
                pltpu.VMEM((TILE - PAIR, length), BF16),
                pltpu.VMEM((step, length, TILE), BF16),
                pltpu.VMEM((step, PAIR + 16, length), BF16),
            ],
        ),
        out_shape=[
            jax.ShapeDtypeStruct(keys.shape, BF16),
            jax.ShapeDtypeStruct((pairs, length // TILE, 2 * TILE), F32),
        ],
        compiler_params=pltpu.CompilerParams(vmem_limit_bytes=40 << 20),
        name="attend_forward",
    )(first, kind, flip, segs[None, :], query_value, keys)


def attend_backward(query_value, keys, attended, grad, lse, place):
    first, kind, flip, segs = place
    length = segs.shape[0]
    pairs, step, rows, two, segs_spec, lse_spec = attention_specs(keys)
    wide = pltpu.VMEM((step, length, TILE), BF16)
    total = pltpu.VMEM((step, length, TILE), F32)
    return pl.pallas_call(
        attend_backward_kernel,
        grid_spec=pltpu.PrefetchScalarGridSpec(
            num_scalar_prefetch=3,
            grid=(pairs // step,),
            in_specs=[segs_spec, two, rows, rows, rows, lse_spec],
            out_specs=[two, rows],
            scratch_shapes=[
                pltpu.VMEM((TILE - PAIR, length), BF16),
                wide,
                wide,
                wide,
                wide,
                total,
                total,
            ],
        ),
        out_shape=[
            jax.ShapeDtypeStruct(query_value.shape, BF16),
            jax.ShapeDtypeStruct(keys.shape, BF16),
        ],
        compiler_params=pltpu.CompilerParams(vmem_limit_bytes=40 << 20),
        name="attend_backward",
    )(first, kind, flip, segs[None, :], query_value, keys, attended, grad, lse)


def gelu_parts(values):
    below = 0.5 * (1.0 + lax.erf(values * (0.5 ** 0.5)))
    density = jnp.exp(values * values * -0.5) * ((2.0 * math.pi) ** -0.5)
    return values * below, below + values * density


def feed_forward_kernel(norm_ref, cot_ref, up_ref, down_ref, *refs):
    *earlier, mlp_ref, back_ref, up_grad_ref, down_grad_ref, act_ref, pre_ref = refs[:-1]
    sum_ref = mlp_ref if mlp_ref.dtype == F32 else refs[-1]
    rows = norm_ref.shape[0]
    chunk = min(rows, 256)

    @pl.when(pl.program_id(0) == 0)
    def _():
        sum_ref[...] = jnp.zeros(sum_ref.shape, F32)
        back_ref[...] = jnp.zeros(back_ref.shape, F32)

    for start in range(0, rows, chunk):
        at = slice(start, start + chunk)
        pre_act = dot(norm_ref[at, :], up_ref[...], NT)
        act_grad = dot(cot_ref[at, :], down_ref[...], NT)
        activation, slope = gelu_parts(pre_act)
        activation = activation.astype(BF16)
        pre_grad = (act_grad * slope).astype(BF16)
        act_ref[at, :] = activation
        pre_ref[at, :] = pre_grad
        sum_ref[at, :] += dot(activation, down_ref[...], NN)
        back_ref[at, :] += dot(pre_grad, up_ref[...], NN)
    up_grad = dot(pre_ref[...], norm_ref[...], TN)
    down_grad = dot(act_ref[...], cot_ref[...], TN)
    if earlier:
        up_grad = up_grad + earlier[0][...].astype(F32)
        down_grad = down_grad + earlier[1][...].astype(F32)
    up_grad_ref[...] = up_grad.astype(BF16)
    down_grad_ref[...] = down_grad.astype(BF16)

    if mlp_ref.dtype != F32:

        @pl.when(pl.program_id(0) == pl.num_programs(0) - 1)
        def _():
            mlp_ref[...] = sum_ref[...].astype(mlp_ref.dtype)


def feed_forward(norm, cot, up, down, earlier=(), kind=F32):
    rows, width = norm.shape
    hidden = up.shape[0]
    part = 512 if hidden % 512 == 0 else hidden
    whole = pl.BlockSpec((rows, width), lambda i: (0, 0))
    block = pl.BlockSpec((part, width), lambda i: (i, 0))
    grads = jax.ShapeDtypeStruct((hidden, width), BF16)
    return pl.pallas_call(
        feed_forward_kernel,
        grid=(hidden // part,),
        in_specs=[whole, whole, block, block] + [block] * len(earlier),
        out_specs=[whole, whole, block, block],
        out_shape=[
            jax.ShapeDtypeStruct((rows, width), kind),
            jax.ShapeDtypeStruct((rows, width), F32),
            grads,
            grads,
        ],
        scratch_shapes=[
            pltpu.VMEM((rows, part), BF16),
            pltpu.VMEM((rows, part), BF16),
            pltpu.VMEM((8, 128) if kind == F32 else (rows, width), F32),
        ],
        compiler_params=pltpu.CompilerParams(vmem_limit_bytes=58 << 20),
        name="feed_forward",
    )(norm, cot, up, down, *earlier)


def middle_kernel(parts, residual_ref, cot_ref, gain_ref, *refs):
    mlp_refs, back_refs = refs[:parts], refs[parts : 2 * parts]
    output_ref, res_grad_ref, branch_ref, norm_grad_ref = refs[2 * parts :]

    @pl.when(pl.program_id(0) == 0)
    def _():
        norm_grad_ref[...] = jnp.zeros(norm_grad_ref.shape, F32)

    residual = residual_ref[...]
    output_ref[...] = sum([ref[...].astype(F32) for ref in mlp_refs], residual).astype(BF16)
    grad = functools.reduce(jnp.add, [ref[...] for ref in back_refs])
    back, gain_grad, bias_grad = layer_norm_back(residual, gain_ref[...], grad)
    res_grad = cot_ref[...].astype(F32) + back
    res_grad_ref[...] = res_grad
    branch_ref[...] = res_grad.astype(BF16)
    norm_grad_ref[0:1, :] += gain_grad
    norm_grad_ref[1:2, :] += bias_grad


def middle(residual, cot, gain, mlps, backs):
    rows, width = residual.shape
    parts = len(mlps)
    step = 256
    block = pl.BlockSpec((step, width), lambda i: (i, 0))
    sums = jax.ShapeDtypeStruct((rows, width), F32)
    low = jax.ShapeDtypeStruct((rows, width), BF16)
    return pl.pallas_call(
        functools.partial(middle_kernel, parts),
        grid=(rows // step,),
        in_specs=[block, block, pl.BlockSpec((1, width), lambda i: (0, 0))] + [block] * (2 * parts),
        out_specs=[block, block, block, pl.BlockSpec((8, width), lambda i: (0, 0))],
        out_shape=[low, sums, low, jax.ShapeDtypeStruct((8, width), F32)],
        compiler_params=pltpu.CompilerParams(vmem_limit_bytes=40 << 20),
        name="middle",
    )(residual, cot, gain[None, :], *mlps, *backs)


def last_kernel(rows_ref, grad_ref, res_grad_ref, gain_ref, in_grad_ref, norm_grad_ref):
    @pl.when(pl.program_id(0) == 0)
    def _():
        norm_grad_ref[...] = jnp.zeros(norm_grad_ref.shape, F32)

    back, gain_grad, bias_grad = layer_norm_back(
        rows_ref[...].astype(F32), gain_ref[...], grad_ref[...]
    )
    in_grad_ref[...] = (res_grad_ref[...] + back).astype(BF16)
    norm_grad_ref[0:1, :] += gain_grad
    norm_grad_ref[1:2, :] += bias_grad


def last(rows_in, grad, res_grad, gain):
    rows, width = rows_in.shape
    step = 256
    block = pl.BlockSpec((step, width), lambda i: (i, 0))
    few = pl.BlockSpec((8, width), lambda i: (0, 0))
    return pl.pallas_call(
        last_kernel,
        grid=(rows // step,),
        in_specs=[block, block, block, pl.BlockSpec((1, width), lambda i: (0, 0))],
        out_specs=[block, few],
        out_shape=[
            jax.ShapeDtypeStruct((rows, width), BF16),
            jax.ShapeDtypeStruct((8, width), F32),
        ],
        compiler_params=pltpu.CompilerParams(vmem_limit_bytes=40 << 20),
        name="last",
    )(rows_in, grad, res_grad, gain[None, :])


def add(*terms):
    return functools.reduce(jnp.add, [item.astype(F32) for item in terms]).astype(BF16)


def swap(values, axis):
    name, size, mask = {
        "core": ("dp", 4, 1),
        "y": ("dp", 4, 2),
        "x": ("mp", 8, 1),
        "z1": ("mp", 8, 2),
        "z2": ("mp", 8, 4),
        "z3": ("mp", 8, 6),
    }[axis]
    return lax.ppermute(values, name, [(i, i ^ mask) for i in range(size)])


def order(at, mine, other):
    return jnp.where(at == 0, jnp.stack([mine, other]), jnp.stack([other, mine]))


class Line:
    def __init__(self):
        self.last = ()

    def __call__(self, step, *args):
        args, _ = lax.optimization_barrier((args, self.last))
        result = step(*args)
        self.last = tuple(jax.tree.leaves(result))
        return result


def on_cube(
    inputs,
    segments,
    ln1_gain,
    ln1_bias,
    w_query,
    w_key,
    w_value,
    w_output,
    ln2_gain,
    ln2_bias,
    w_up,
    w_down,
    cotangent,
):
    rows, width = inputs.shape
    local = w_query.shape[1]
    at_dp, at_mp = lax.axis_index("dp"), lax.axis_index("mp")
    at_y, at_core = at_dp // 2, at_dp % 2
    line = Line()

    def pick(values, at):
        return lax.dynamic_index_in_dim(values, at, 0, keepdims=False)

    def cut_attention(query, key, value, out):
        kinds = jnp.stack([query.T, key.T, value.T, out]).reshape(2, 2, 2, HEAD_DIM, width)
        return pick(kinds.transpose(0, 2, 1, 3, 4).reshape(4, 2, HEAD_DIM, width), at_dp)

    def cut_mlp(up, down):
        pieces = jnp.stack([up.T, down]).reshape(2, 4, -1, width)
        return lax.dynamic_index_in_dim(pieces, at_dp, 1, keepdims=False)

    def join(*parts):
        return jnp.concatenate(parts, 0)

    along_z = ("z2", "z1", "z3")
    attn_piece = line(cut_attention, w_query, w_key, w_value, w_output)
    attn_z = [swap(attn_piece, axis) for axis in along_z]
    mlp_piece = line(cut_mlp, w_up, w_down)
    mlp_z = [swap(mlp_piece, axis) for axis in along_z]

    def begin(rows_in):
        return layer_norm(rows_in.astype(F32), ln1_gain, ln1_bias).astype(BF16)

    norm_one = line(begin, inputs)
    segs = pick(segments, at_mp)
    place = windows(segs) + (at_y.reshape(1), segs)
    place = line(lambda item: item, place)

    near_z = line(lambda *parts: jnp.stack(parts[:4]), attn_piece, *attn_z, mlp_z[1])
    near_got = swap(near_z, "y")
    far_z = swap(near_z, "x")
    near_y = line(lambda *parts: jnp.stack(parts[:2]), near_z, near_got, far_z, mlp_z[0])
    near_got = swap(near_y, "core")
    far_got = swap(far_z, "y")

    def both_cores(mine, other):
        query_value, key_out = [jnp.stack([mine[:, :, i], other[:, :, i]]) for i in (0, 1)]
        key, out = [
            lax.dynamic_index_in_dim(key_out, at, 1, keepdims=False).reshape(-1, width)
            for at in (at_y, 1 - at_y)
        ]
        return query_value.reshape(-1, width), key, out

    def project(weights, norm):
        query_value = dot(weights[0], norm, NT).astype(BF16).reshape(2, 2, -1, rows)
        return query_value, dot(weights[1], norm, NT).astype(BF16).reshape(2, -1, rows)

    def attend(query_value, keys):
        return attend_forward(query_value, keys, place)

    def branch(base, attended, weights):
        return base + dot(attended.reshape(-1, rows), weights[2], TN)

    def mlp_along_z(*parts):
        return [jnp.concatenate([item[i] for item in parts], 0) for i in (0, 1)]

    def mlp_second(up, up_got, down, down_got):
        return jnp.concatenate([up, up_got], 0), jnp.stack([down, down_got])

    near_w = line(both_cores, near_y, near_got)
    near = line(project, near_w, norm_one)
    up, down = line(mlp_along_z, mlp_piece, *mlp_z)
    up_got, down_got = swap(up, "x"), swap(down, "y")
    near += tuple(line(attend, *near))

    far_y = line(lambda *parts: jnp.stack(parts), far_z, far_got)
    far_got = swap(far_y, "core")
    up, down = line(mlp_second, up, up_got, down, down_got)
    up_got, down_got = swap(up, "y"), swap(down, "x")
    residual = line(branch, inputs.astype(F32), near[2], near_w)
    far_w = line(both_cores, far_y, far_got)
    far = line(project, far_w, norm_one)
    far += tuple(line(attend, *far))

    def second_norm(residual, attended, weights):
        residual = branch(residual, attended, weights)
        return residual, layer_norm(residual, ln2_gain, ln2_bias).astype(BF16)

    cot_other = swap(cotangent, "core")
    far_attended, cot_other = lax.optimization_barrier((far[2], cot_other))
    residual, norm_two = line(second_norm, residual, far_attended, far_w)
    norm_two_other = swap(norm_two, "core")

    def mlp_last(up, up_got, down, down_got):
        return jnp.concatenate([up, up_got], 0), jnp.concatenate([down, down_got], 1).reshape(-1, width)

    up, down = line(mlp_last, up, up_got, down, down_got)
    mlp_b, back_b, *grads = line(
        lambda *args: feed_forward(*args, kind=BF16), norm_two_other, cot_other, up, down
    )
    mlp_b, back_b = swap(mlp_b, "core"), swap(back_b, "core")
    mlp_a, back_a, up_grad, down_grad = line(feed_forward, norm_two, cotangent, up, down, grads)

    def before_attention(attended, weights, grad):
        att_grad = dot(weights[2], grad, NT).astype(BF16).reshape(attended.shape)
        return att_grad, dot(attended.reshape(-1, rows), grad, NN).astype(BF16)


    quarter = up.shape[0] // 4

    def up_sum_of(terms, low, high):
        return add(*[item[low:high] for item in terms])

    def down_sum_of(terms, y, x, low=0, high=quarter):
        whole = terms[0].reshape(2, 2, quarter, width)[y, x, low:high]
        return add(whole, *[item.reshape(-1, quarter, width)[y, low:high] for item in terms[1:]])

    def mlp_sum_first(up_terms, down_terms):
        return (
            up_sum_of(up_terms, 2 * quarter, 4 * quarter),
            jnp.stack([down_sum_of(down_terms, y, 1) for y in (0, 1)]),
        )

    up_terms, down_terms = (up_grad,), (down_grad,)
    sends = line(mlp_sum_first, up_terms, down_terms)
    up_terms += (swap(sends[0], "y"),)
    down_terms += (swap(sends[1], "x"),)

    def attend_back(saved, att_grad):
        return attend_backward(*saved[:3], att_grad, saved[3], place)

    def weight_grads(query_value_grad, key_grad, out_grad, norm):
        query_value = dot(query_value_grad.reshape(-1, rows), norm, NN).astype(BF16)
        keys = dot(key_grad.reshape(-1, rows), norm, NN).astype(BF16)
        sums = (
            query_value.reshape(2, 2, -1, width),
            keys.reshape(2, -1, width),
            out_grad.reshape(2, -1, width),
        )
        return sums, [item[1] for item in sums]

    def project_back(grads, weights):
        return dot(grads[0].reshape(-1, rows), weights[0], TN) + dot(
            grads[1].reshape(-1, rows), weights[1], TN
        )

    def attn_terms_of(mine, got, at):
        terms = [(mine[0][0, at], mine[1][0], mine[2][0]), (got[0][at], got[1], got[2])]
        first = at_y == at
        return [
            [item[0] for item in terms],
            [jnp.where(first, item[1], item[2]) for item in terms],
        ]

    def sum_other_y(mine, got):
        return jnp.stack([add(*terms) for terms in attn_terms_of(mine, got, 1)])

    def sum_this_y(mine, got, from_y):
        terms = attn_terms_of(mine, got, 0)
        return jnp.stack([add(*terms[i], from_y[i]) for i in (0, 1)])

    output, res_grad, branch_grad, norm_two_grads = line(
        middle, residual, cotangent, ln2_gain, [mlp_a, mlp_b], [back_a, back_b]
    )
    far_att, far_out = line(before_attention, far[2], far_w, branch_grad)
    far_grads = line(attend_back, far, far_att)
    far_mine, sends = line(weight_grads, *far_grads, far_out, norm_one)
    far_got = [swap(item, "core") for item in sends]
    def mlp_sum_second(up_terms, down_terms):
        return up_sum_of(up_terms, quarter, 2 * quarter), down_sum_of(down_terms, 1, 0)

    sends = line(mlp_sum_second, up_terms, down_terms)
    up_terms += (swap(sends[0], "x"),)
    down_y = swap(sends[1], "y")

    norm_one_grad = line(project_back, far_grads, far_w)
    near_att, near_out = line(before_attention, near[2], near_w, branch_grad)
    far_y = swap(line(sum_other_y, far_mine, far_got), "y")

    part = quarter // 4

    def mlp_sum_of_z(up_terms, down_terms, down_y, low, high):
        low, high = low * part, high * part
        return jnp.stack(
            [
                up_sum_of(up_terms, low, high),
                down_sum_of(down_terms + (jnp.stack([down_y, down_y]),), 0, 0, low, high),
            ]
        )

    mlp_terms = (up_terms, down_terms, down_y)
    mlp_z1 = swap(line(lambda *terms: mlp_sum_of_z(*terms, 2, 4), *mlp_terms), "z1")
    near_grads = line(attend_back, near, near_att)
    mlp_send = line(
        lambda got, *terms: add(mlp_sum_of_z(*terms, 1, 2), got[:, part:]), mlp_z1, *mlp_terms
    )
    mlp_z2 = swap(mlp_send, "z2")
    near_mine, sends = line(weight_grads, *near_grads, near_out, norm_one)
    near_got = [swap(item, "core") for item in sends]
    far_x = swap(line(sum_this_y, far_mine, far_got, far_y), "x")
    near_y = swap(line(sum_other_y, near_mine, near_got), "y")

    def add_project_back(norm_one_grad, grads, weights):
        return norm_one_grad + project_back(grads, weights)

    def finish(norm_one_grad):
        in_grad, norm_one_grads = last(inputs, norm_one_grad, res_grad, ln1_gain)
        return jnp.concatenate([norm_one_grads[:2], norm_two_grads[:2]]), in_grad

    norm_one_grad = line(add_project_back, norm_one_grad, near_grads, near_w)
    norm_sums, in_grad = line(finish, norm_one_grad)
    got = swap(norm_sums, "core")

    mlp_sum = line(
        lambda got, other, *terms: add(mlp_sum_of_z(*terms, 0, 1), got[:, :part], other),
        mlp_z1,
        mlp_z2,
        *mlp_terms,
    )
    mlp_got = swap(mlp_sum, "y")
    norm_sums = line(jnp.add, norm_sums, got)
    got = swap(norm_sums, "x")

    def attn_sum_z(mine, got, from_y, from_x):
        from_x = from_x.reshape(2, -1, width)
        whole = sum_this_y(mine, got, from_y).astype(F32) + from_x
        return [whole[:, at * HEAD_DIM : (at + 1) * HEAD_DIM].astype(BF16) for at in range(4)]

    attn_mine, *sends = line(attn_sum_z, near_mine, near_got, near_y, far_x)
    attn_z = [swap(item, axis) for item, axis in zip(sends, along_z)]

    def in_order(piece, y, core, both):
        return order(at_core, order(at_y, piece, y), order(at_y, core, both))

    norm_sums = line(jnp.add, norm_sums, got)
    got = swap(norm_sums, "z1")
    norm_sums = line(jnp.add, norm_sums, got)
    got = swap(norm_sums, "z2")
    attn_sum = line(lambda _, *terms: add(*terms), mlp_got, attn_mine, *attn_z)
    attn_got = [
        lax.ppermute(attn_sum, "dp", [(i, i ^ mask) for i in range(4)]) for mask in (2, 1, 3)
    ]
    mlp_sum = line(functools.partial(order, at_y), mlp_sum, mlp_got)
    mlp_got = swap(mlp_sum, "core")
    norm_sums = line(jnp.add, norm_sums, got)
    got = swap(norm_sums, "y")
    attn_sum = line(in_order, attn_sum, *attn_got)
    attn_sum = line(
        lambda item: item.transpose(1, 2, 0, 3, 4).reshape(4, local, width).astype(F32), attn_sum
    )
    attn_sums = line(lambda item: (item[0].T, item[1].T, item[2].T, item[3]), attn_sum)
    mlp_sum = line(functools.partial(order, at_core), mlp_sum, mlp_got)
    up_sum, down_sum = line(
        lambda item: tuple(item.transpose(2, 1, 0, 3, 4).reshape(2, -1, width).astype(F32)), mlp_sum
    )
    up_sum = line(jnp.transpose, up_sum)
    norm_sums = line(jnp.add, norm_sums, got)
    norm_sums = lax.dynamic_slice_in_dim(norm_sums, at_mp * (width // 8), width // 8, 1)
    return (
        output,
        in_grad,
        norm_sums[0],
        norm_sums[1],
        *attn_sums,
        norm_sums[2],
        norm_sums[3],
        up_sum,
        down_sum,
    )


def on_any(
    mp_size,
    inputs,
    segments,
    ln1_gain,
    ln1_bias,
    w_query,
    w_key,
    w_value,
    w_output,
    ln2_gain,
    ln2_bias,
    w_up,
    w_down,
    cotangent,
):
    rows, width = inputs.shape
    seq_length = segments.shape[1]
    shared_by = seq_length // rows
    at_mp = lax.axis_index("mp")
    groups = [[start + i for i in range(shared_by)] for start in range(0, mp_size, shared_by)]

    def exchange(values, split, join):
        if shared_by == 1:
            return values
        return lax.all_to_all(values, "mp", split, join, axis_index_groups=groups, tiled=True)

    def gather(parts):
        return lax.all_gather(parts, "mp", axis=1, tiled=True)

    def reduce(parts):
        return lax.psum(lax.psum_scatter(parts, "mp", scatter_dimension=1, tiled=True), "dp")

    attn_w = gather(jnp.stack([w_query.T, w_value.T, w_key.T, w_output]))
    up, down = gather(jnp.stack([w_up.T, w_down]))
    project, w_out = attn_w[:3].reshape(3 * width, width), attn_w[3]

    segs = lax.dynamic_index_in_dim(segments, at_mp // shared_by, 0, keepdims=False)
    place = windows(segs) + (jnp.zeros((1,), jnp.int32), segs)
    resid_in = inputs.astype(F32)
    norm_one = layer_norm(resid_in, ln1_gain, ln1_bias).astype(BF16)
    projected = dot(project, norm_one, NT).astype(BF16).reshape(3, width, rows)
    projected = exchange(projected, 1, 2)
    query_value, keys = projected[None, :2], projected[2:]
    heads_out, lse = attend_forward(query_value, keys, place)
    attended = exchange(heads_out[0], 1, 0)
    residual = resid_in + dot(attended, w_out, TN)
    norm_two = layer_norm(residual, ln2_gain, ln2_bias).astype(BF16)
    mlp_branch, norm_two_grad, *mlp_grads = feed_forward(norm_two, cotangent, up, down)
    up_sum, down_sum = reduce(jnp.stack(mlp_grads)).astype(F32)

    output, res_grad, branch_grad, norm_two_grads = middle(
        residual, cotangent, ln2_gain, [mlp_branch], [norm_two_grad]
    )
    out_grad = dot(attended, branch_grad, NN).astype(BF16)
    att_grad = exchange(dot(w_out, branch_grad, NT).astype(BF16), 0, 1)
    query_value_grad, key_grad = attend_backward(
        query_value, keys, heads_out, att_grad[None], lse, place
    )
    proj_grad = exchange(jnp.concatenate([query_value_grad[0], key_grad]), 2, 1)
    proj_grad = proj_grad.reshape(3 * width, rows)
    project_grad = dot(proj_grad, norm_one, NN).astype(BF16).reshape(3, width, width)
    attn_sum = reduce(jnp.concatenate([project_grad, out_grad[None]])).astype(F32)
    in_grad, norm_one_grads = last(inputs, dot(proj_grad, project, TN), res_grad, ln1_gain)
    norm_parts = jnp.concatenate([norm_one_grads[:2], norm_two_grads[:2]])
    norm_sums = lax.dynamic_slice_in_dim(
        lax.psum(norm_parts, ("dp", "mp")), at_mp * (width // mp_size), width // mp_size, 1
    )
    return (
        output,
        in_grad,
        norm_sums[0],
        norm_sums[1],
        attn_sum[0].T,
        attn_sum[2].T,
        attn_sum[1].T,
        attn_sum[3],
        norm_sums[2],
        norm_sums[3],
        up_sum.T,
        down_sum,
    )


def shards(dp_size, mp_size, inputs, segments, *rest):
    if dp_size == 4 and mp_size == 8 and inputs.shape[0] == segments.shape[1]:
        return on_cube(inputs, segments, *rest)
    return on_any(mp_size, inputs, segments, *rest)


def solution(mesh):
    return jax.shard_map(
        functools.partial(shards, mesh.shape["dp"], mesh.shape["mp"]),
        mesh=mesh,
        in_specs=(
            P(("dp", "mp"), None),
            P("dp", None),
            P(),
            P(),
            P(None, "mp"),
            P(None, "mp"),
            P(None, "mp"),
            P("mp", None),
            P(),
            P(),
            P(None, "mp"),
            P("mp", None),
            P(("dp", "mp"), None),
        ),
        out_specs=(
            P(("dp", "mp"), None),
            P(("dp", "mp"), None),
            P("mp"),
            P("mp"),
            P(None, "mp"),
            P(None, "mp"),
            P(None, "mp"),
            P("mp", None),
            P("mp"),
            P("mp"),
            P(None, "mp"),
            P("mp", None),
        ),
        check_vma=False,
    )
```

```python
import functools
import math

import jax
import jax.numpy as jnp
from jax import lax
from jax.experimental import pallas as pl
from jax.experimental.pallas import tpu as pltpu
from jax.sharding import PartitionSpec as P

HEAD_DIM = 48
PAIR = 2 * HEAD_DIM
IMAGES = 4
TILE = 128
norm_eps = 1e-06
negative_fill = -1e30
SCALE = HEAD_DIM ** (-0.5)
SCALE_LOG2 = SCALE * math.log2(math.e)
BF16 = jnp.bfloat16
F32 = jnp.float32


def layer_norm(values, gain, bias):
    center = jnp.mean(values, axis=-1, keepdims=True)
    shifted = values - center
    spread = jnp.mean(shifted * shifted, axis=-1, keepdims=True)
    return shifted * lax.rsqrt(spread + norm_eps) * gain + bias


def layer_norm_back(values, gain, grad):
    shifted = values - jnp.mean(values, axis=-1, keepdims=True)
    scale = lax.rsqrt(jnp.mean(shifted * shifted, axis=-1, keepdims=True) + norm_eps)
    unit = shifted * scale
    scaled = grad * gain
    back = scale * (
        scaled
        - jnp.mean(scaled, axis=-1, keepdims=True)
        - unit * jnp.mean(scaled * unit, axis=-1, keepdims=True)
    )
    return back, jnp.sum(grad * unit, axis=0, keepdims=True), jnp.sum(grad, axis=0, keepdims=True)


def dot(left, right, dims):
    return lax.dot_general(left, right, (dims, ((), ())), preferred_element_type=F32)


NN = ((1,), (0,))
NT = ((1,), (1,))
TN = ((0,), (0,))


def window_kinds(tiles):
    return tuple(n for n in (2, 3, 4, 5, 6, 7) if n < tiles) + (tiles,)


def image_rows(segs, length):
    row = lax.broadcasted_iota(jnp.int32, (TILE - PAIR, length), 0)
    here = row == segs
    one_hot = jnp.where(here, 1.0, 0.0).astype(BF16)
    fill = jnp.where(jnp.logical_or(here, row >= IMAGES), 0.0, negative_fill).astype(BF16)
    return one_hot, fill


def side_by_side(pair, extra):
    blank = jnp.zeros((HEAD_DIM, TILE), BF16)
    left = jnp.concatenate([pair[:HEAD_DIM], blank, extra], axis=0)
    right = jnp.concatenate([blank, pair[HEAD_DIM:], extra], axis=0)
    return jnp.concatenate([left, right], axis=1)


def pair_places(ref):
    cores, count = ref.shape[0], ref.shape[1]
    return [(core, top) for core in range(cores) for top in range(0, count, PAIR)]


def attend_forward_kernel(
    first_ref, kind_ref, flip_ref, segs_ref, qv_ref, k_ref, out_ref, lse_ref, hot_ref, keys_ref, vals_ref
):
    length = k_ref.shape[-1]
    at_q = flip_ref[0]
    places = pair_places(k_ref)
    one_hot, fill = image_rows(segs_ref[...], length)
    hot_ref[...] = one_hot
    for j, (core, top) in enumerate(places):
        rows = slice(top, top + PAIR)
        keys_ref[j] = jnp.concatenate([k_ref[core, rows, :], fill], axis=0).T
        vals_ref[j] = jnp.concatenate(
            [qv_ref[core, 1 - at_q, rows, :], jnp.ones((16, length), BF16)], axis=0
        )

    def block(b, carry):
        at = pl.ds(pl.multiple_of(b * TILE, TILE), TILE)
        first = pl.multiple_of(first_ref[b] * TILE, TILE)

        def variant(tiles):
            span = pl.ds(first, tiles * TILE)
            scores = [
                dot(
                    keys_ref[j, span, :],
                    side_by_side(qv_ref[core, at_q, top : top + PAIR, at], hot_ref[:, at]),
                    NN,
                )
                for j, (core, top) in enumerate(places)
            ]
            for j, (core, top) in enumerate(places):
                most = jnp.max(scores[j], axis=0, keepdims=True)
                expo = jnp.exp2((scores[j] - most) * SCALE_LOG2).astype(BF16)
                mixed = dot(vals_ref[j, :, span], expo, NN)
                total = mixed[PAIR : PAIR + 1, :]
                inverse = 1.0 / total
                out_ref[core, top : top + HEAD_DIM, at] = (
                    mixed[:HEAD_DIM, :TILE] * inverse[:, :TILE]
                ).astype(BF16)
                out_ref[core, top + HEAD_DIM : top + PAIR, at] = (
                    mixed[HEAD_DIM:PAIR, TILE:] * inverse[:, TILE:]
                ).astype(BF16)
                lse_ref[j, pl.ds(b, 1), :] = most * SCALE_LOG2 + jnp.log2(total)

        for tiles in window_kinds(length // TILE):
            pl.when(kind_ref[b] == tiles)(functools.partial(variant, tiles))
        return carry

    lax.fori_loop(0, length // TILE, block, 0)


def attend_backward_kernel(
    first_ref,
    kind_ref,
    flip_ref,
    segs_ref,
    qv_ref,
    k_ref,
    att_ref,
    grad_ref,
    lse_ref,
    dqv_ref,
    dk_ref,
    hot_ref,
    keys_ref,
    vals_ref,
    queries_ref,
    grads_ref,
    key_sum_ref,
    val_sum_ref,
):
    length = k_ref.shape[-1]
    at_q = flip_ref[0]
    places = pair_places(k_ref)
    one_hot, fill = image_rows(segs_ref[...], length)
    hot_ref[...] = one_hot
    pad = jnp.zeros((TILE - PAIR, length), BF16)
    for j, (core, top) in enumerate(places):
        rows = slice(top, top + PAIR)
        keys_ref[j] = jnp.concatenate([k_ref[core, rows, :], fill], axis=0).T
        vals_ref[j] = jnp.concatenate([qv_ref[core, 1 - at_q, rows, :], pad], axis=0).T
        queries_ref[j] = jnp.concatenate([qv_ref[core, at_q, rows, :], pad], axis=0).T
        grads_ref[j] = jnp.concatenate([grad_ref[core, rows, :], pad], axis=0).T
    key_sum_ref[...] = jnp.zeros(key_sum_ref.shape, F32)
    val_sum_ref[...] = jnp.zeros(val_sum_ref.shape, F32)
    no_rows = jnp.zeros((TILE - PAIR, TILE), BF16)
    lane = lax.broadcasted_iota(jnp.int32, (TILE, TILE), 1)
    in_first = lane < HEAD_DIM

    def stacked(both):
        blank = jnp.zeros_like(both)
        return jnp.concatenate(
            [jnp.where(in_first, both, blank), jnp.where(in_first, blank, both)], axis=0
        )

    def block(b, carry):
        at = pl.ds(pl.multiple_of(b * TILE, TILE), TILE)
        first = pl.multiple_of(first_ref[b] * TILE, TILE)

        def variant(tiles):
            span = pl.ds(first, tiles * TILE)
            scores = [
                dot(
                    keys_ref[j, span, :],
                    side_by_side(qv_ref[core, at_q, top : top + PAIR, at], hot_ref[:, at]),
                    NN,
                )
                for j, (core, top) in enumerate(places)
            ]
            prob_grads = [
                dot(
                    vals_ref[j, span, :],
                    side_by_side(grad_ref[core, top : top + PAIR, at], no_rows),
                    NN,
                )
                for j, (core, top) in enumerate(places)
            ]
            for j, (core, top) in enumerate(places):
                rows = slice(top, top + PAIR)
                agree = grad_ref[core, rows, at].astype(F32) * att_ref[core, rows, at].astype(F32)
                delta = jnp.concatenate(
                    [
                        jnp.sum(agree[:HEAD_DIM], axis=0, keepdims=True),
                        jnp.sum(agree[HEAD_DIM:], axis=0, keepdims=True),
                    ],
                    axis=1,
                )
                probs = jnp.exp2(scores[j] * SCALE_LOG2 - lse_ref[j, pl.ds(b, 1), :])
                score_grad = (probs * (prob_grads[j] - delta)).astype(BF16)
                val_sum_ref[j, span, :] += dot(
                    probs.astype(BF16), stacked(grads_ref[j, at, :]), NN
                )
                key_sum_ref[j, span, :] += dot(score_grad, stacked(queries_ref[j, at, :]), NN)
                query_grad = dot(k_ref[core, rows, span], score_grad, NN) * SCALE
                dqv_ref[core, at_q, top : top + HEAD_DIM, at] = query_grad[
                    :HEAD_DIM, :TILE
                ].astype(BF16)
                dqv_ref[core, at_q, top + HEAD_DIM : top + PAIR, at] = query_grad[
                    HEAD_DIM:, TILE:
                ].astype(BF16)

        for tiles in window_kinds(length // TILE):
            pl.when(kind_ref[b] == tiles)(functools.partial(variant, tiles))
        return carry

    lax.fori_loop(0, length // TILE, block, 0)
    for j, (core, top) in enumerate(places):
        rows = slice(top, top + PAIR)
        dk_ref[core, rows, :] = (key_sum_ref[j] * SCALE).T[:PAIR].astype(BF16)
        dqv_ref[core, 1 - at_q, rows, :] = val_sum_ref[j].T[:PAIR].astype(BF16)


def windows(segs):
    length = segs.shape[0]
    tiles = length // TILE
    by_tile = segs.reshape(tiles, TILE)
    begin = jnp.sum(segs[None, :] < by_tile[:, :1], axis=1)
    end = jnp.sum(segs[None, :] <= by_tile[:, -1:], axis=1)
    first = begin // TILE
    need = (end + TILE - 1) // TILE - first
    kinds = jnp.asarray(window_kinds(tiles), jnp.int32)
    kind = jnp.min(jnp.where(kinds[None, :] >= need[:, None], kinds[None, :], tiles), axis=1)
    return jnp.minimum(first, tiles - kind).astype(jnp.int32), kind.astype(jnp.int32)


def attention_specs(keys):
    cores, count, length = keys.shape
    pairs = cores * count // PAIR
    step = pairs if pairs <= 4 else 4
    part = count * step // pairs
    rows = pl.BlockSpec((cores, part, length), lambda i, *_: (0, i, 0))
    two = pl.BlockSpec((cores, 2, part, length), lambda i, *_: (0, 0, i, 0))
    segs = pl.BlockSpec((1, length), lambda i, *_: (0, 0))
    lse = pl.BlockSpec((step, length // TILE, 2 * TILE), lambda i, *_: (i, 0, 0))
    return pairs, step, rows, two, segs, lse


def attend_forward(query_value, keys, place):
    first, kind, flip, segs = place
    length = segs.shape[0]
    pairs, step, rows, two, segs_spec, lse = attention_specs(keys)
    return pl.pallas_call(
        attend_forward_kernel,
        grid_spec=pltpu.PrefetchScalarGridSpec(
            num_scalar_prefetch=3,
            grid=(pairs // step,),
            in_specs=[segs_spec, two, rows],
            out_specs=[rows, lse],
            scratch_shapes=[
                pltpu.VMEM((TILE - PAIR, length), BF16),
                pltpu.VMEM((step, length, TILE), BF16),
                pltpu.VMEM((step, PAIR + 16, length), BF16),
            ],
        ),
        out_shape=[
            jax.ShapeDtypeStruct(keys.shape, BF16),
            jax.ShapeDtypeStruct((pairs, length // TILE, 2 * TILE), F32),
        ],
        compiler_params=pltpu.CompilerParams(vmem_limit_bytes=40 << 20),
        name="attend_forward",
    )(first, kind, flip, segs[None, :], query_value, keys)


def attend_backward(query_value, keys, attended, grad, lse, place):
    first, kind, flip, segs = place
    length = segs.shape[0]
    pairs, step, rows, two, segs_spec, lse_spec = attention_specs(keys)
    wide = pltpu.VMEM((step, length, TILE), BF16)
    total = pltpu.VMEM((step, length, TILE), F32)
    return pl.pallas_call(
        attend_backward_kernel,
        grid_spec=pltpu.PrefetchScalarGridSpec(
            num_scalar_prefetch=3,
            grid=(pairs // step,),
            in_specs=[segs_spec, two, rows, rows, rows, lse_spec],
            out_specs=[two, rows],
            scratch_shapes=[
                pltpu.VMEM((TILE - PAIR, length), BF16),
                wide,
                wide,
                wide,
                wide,
                total,
                total,
            ],
        ),
        out_shape=[
            jax.ShapeDtypeStruct(query_value.shape, BF16),
            jax.ShapeDtypeStruct(keys.shape, BF16),
        ],
        compiler_params=pltpu.CompilerParams(vmem_limit_bytes=40 << 20),
        name="attend_backward",
    )(first, kind, flip, segs[None, :], query_value, keys, attended, grad, lse)


def gelu_parts(values):
    below = 0.5 * (1.0 + lax.erf(values * (0.5 ** 0.5)))
    density = jnp.exp(values * values * -0.5) * ((2.0 * math.pi) ** -0.5)
    return values * below, below + values * density


def feed_forward_kernel(norm_ref, cot_ref, up_ref, down_ref, *refs):
    *earlier, mlp_ref, back_ref, up_grad_ref, down_grad_ref, act_ref, pre_ref = refs[:-1]
    sum_ref = mlp_ref if mlp_ref.dtype == F32 else refs[-1]
    rows = norm_ref.shape[0]
    chunk = min(rows, 256)

    @pl.when(pl.program_id(0) == 0)
    def _():
        sum_ref[...] = jnp.zeros(sum_ref.shape, F32)
        back_ref[...] = jnp.zeros(back_ref.shape, F32)

    for start in range(0, rows, chunk):
        at = slice(start, start + chunk)
        pre_act = dot(norm_ref[at, :], up_ref[...], NT)
        act_grad = dot(cot_ref[at, :], down_ref[...], NT)
        activation, slope = gelu_parts(pre_act)
        activation = activation.astype(BF16)
        pre_grad = (act_grad * slope).astype(BF16)
        act_ref[at, :] = activation
        pre_ref[at, :] = pre_grad
        sum_ref[at, :] += dot(activation, down_ref[...], NN)
        back_ref[at, :] += dot(pre_grad, up_ref[...], NN)
    up_grad = dot(pre_ref[...], norm_ref[...], TN)
    down_grad = dot(act_ref[...], cot_ref[...], TN)
    if earlier:
        up_grad = up_grad + earlier[0][...].astype(F32)
        down_grad = down_grad + earlier[1][...].astype(F32)
    up_grad_ref[...] = up_grad.astype(BF16)
    down_grad_ref[...] = down_grad.astype(BF16)

    if mlp_ref.dtype != F32:

        @pl.when(pl.program_id(0) == pl.num_programs(0) - 1)
        def _():
            mlp_ref[...] = sum_ref[...].astype(mlp_ref.dtype)


def feed_forward(norm, cot, up, down, earlier=(), kind=F32):
    rows, width = norm.shape
    hidden = up.shape[0]
    part = 512 if hidden % 512 == 0 else hidden
    whole = pl.BlockSpec((rows, width), lambda i: (0, 0))
    block = pl.BlockSpec((part, width), lambda i: (i, 0))
    grads = jax.ShapeDtypeStruct((hidden, width), BF16)
    return pl.pallas_call(
        feed_forward_kernel,
        grid=(hidden // part,),
        in_specs=[whole, whole, block, block] + [block] * len(earlier),
        out_specs=[whole, whole, block, block],
        out_shape=[
            jax.ShapeDtypeStruct((rows, width), kind),
            jax.ShapeDtypeStruct((rows, width), F32),
            grads,
            grads,
        ],
        scratch_shapes=[
            pltpu.VMEM((rows, part), BF16),
            pltpu.VMEM((rows, part), BF16),
            pltpu.VMEM((8, 128) if kind == F32 else (rows, width), F32),
        ],
        compiler_params=pltpu.CompilerParams(vmem_limit_bytes=58 << 20),
        name="feed_forward",
    )(norm, cot, up, down, *earlier)


def middle_kernel(parts, residual_ref, cot_ref, gain_ref, *refs):
    mlp_refs, back_refs = refs[:parts], refs[parts : 2 * parts]
    output_ref, res_grad_ref, branch_ref, norm_grad_ref = refs[2 * parts :]

    @pl.when(pl.program_id(0) == 0)
    def _():
        norm_grad_ref[...] = jnp.zeros(norm_grad_ref.shape, F32)

    residual = residual_ref[...]
    output_ref[...] = sum([ref[...].astype(F32) for ref in mlp_refs], residual).astype(BF16)
    grad = functools.reduce(jnp.add, [ref[...] for ref in back_refs])
    back, gain_grad, bias_grad = layer_norm_back(residual, gain_ref[...], grad)
    res_grad = cot_ref[...].astype(F32) + back
    res_grad_ref[...] = res_grad
    branch_ref[...] = res_grad.astype(BF16)
    norm_grad_ref[0:1, :] += gain_grad
    norm_grad_ref[1:2, :] += bias_grad


def middle(residual, cot, gain, mlps, backs):
    rows, width = residual.shape
    parts = len(mlps)
    step = 256
    block = pl.BlockSpec((step, width), lambda i: (i, 0))
    sums = jax.ShapeDtypeStruct((rows, width), F32)
    low = jax.ShapeDtypeStruct((rows, width), BF16)
    return pl.pallas_call(
        functools.partial(middle_kernel, parts),
        grid=(rows // step,),
        in_specs=[block, block, pl.BlockSpec((1, width), lambda i: (0, 0))] + [block] * (2 * parts),
        out_specs=[block, block, block, pl.BlockSpec((8, width), lambda i: (0, 0))],
        out_shape=[low, sums, low, jax.ShapeDtypeStruct((8, width), F32)],
        compiler_params=pltpu.CompilerParams(vmem_limit_bytes=40 << 20),
        name="middle",
    )(residual, cot, gain[None, :], *mlps, *backs)


def last_kernel(rows_ref, grad_ref, res_grad_ref, gain_ref, in_grad_ref, norm_grad_ref):
    @pl.when(pl.program_id(0) == 0)
    def _():
        norm_grad_ref[...] = jnp.zeros(norm_grad_ref.shape, F32)

    back, gain_grad, bias_grad = layer_norm_back(
        rows_ref[...].astype(F32), gain_ref[...], grad_ref[...]
    )
    in_grad_ref[...] = (res_grad_ref[...] + back).astype(BF16)
    norm_grad_ref[0:1, :] += gain_grad
    norm_grad_ref[1:2, :] += bias_grad


def last(rows_in, grad, res_grad, gain):
    rows, width = rows_in.shape
    step = 256
    block = pl.BlockSpec((step, width), lambda i: (i, 0))
    few = pl.BlockSpec((8, width), lambda i: (0, 0))
    return pl.pallas_call(
        last_kernel,
        grid=(rows // step,),
        in_specs=[block, block, block, pl.BlockSpec((1, width), lambda i: (0, 0))],
        out_specs=[block, few],
        out_shape=[
            jax.ShapeDtypeStruct((rows, width), BF16),
            jax.ShapeDtypeStruct((8, width), F32),
        ],
        compiler_params=pltpu.CompilerParams(vmem_limit_bytes=40 << 20),
        name="last",
    )(rows_in, grad, res_grad, gain[None, :])


def add(*terms):
    return functools.reduce(jnp.add, [item.astype(F32) for item in terms]).astype(BF16)


def swap(values, axis):
    name, size, mask = {
        "core": ("dp", 4, 1),
        "y": ("dp", 4, 2),
        "x": ("mp", 8, 1),
        "z1": ("mp", 8, 2),
        "z2": ("mp", 8, 4),
        "z3": ("mp", 8, 6),
    }[axis]
    return lax.ppermute(values, name, [(i, i ^ mask) for i in range(size)])


def order(at, mine, other):
    return jnp.where(at == 0, jnp.stack([mine, other]), jnp.stack([other, mine]))


class Line:
    def __init__(self):
        self.last = ()

    def __call__(self, step, *args):
        args, _ = lax.optimization_barrier((args, self.last))
        result = step(*args)
        self.last = tuple(jax.tree.leaves(result))
        return result


def on_cube(
    inputs,
    segments,
    ln1_gain,
    ln1_bias,
    w_query,
    w_key,
    w_value,
    w_output,
    ln2_gain,
    ln2_bias,
    w_up,
    w_down,
    cotangent,
):
    rows, width = inputs.shape
    local = w_query.shape[1]
    at_dp, at_mp = lax.axis_index("dp"), lax.axis_index("mp")
    at_y, at_core = at_dp // 2, at_dp % 2
    line = Line()

    def pick(values, at):
        return lax.dynamic_index_in_dim(values, at, 0, keepdims=False)

    def cut_attention(query, key, value, out):
        kinds = jnp.stack([query.T, key.T, value.T, out]).reshape(2, 2, 2, HEAD_DIM, width)
        return pick(kinds.transpose(0, 2, 1, 3, 4).reshape(4, 2, HEAD_DIM, width), at_dp)

    def cut_mlp(up, down):
        pieces = jnp.stack([up.T, down]).reshape(2, 4, -1, width)
        return lax.dynamic_index_in_dim(pieces, at_dp, 1, keepdims=False)

    def join(*parts):
        return jnp.concatenate(parts, 0)

    along_z = ("z2", "z1", "z3")
    attn_piece = line(cut_attention, w_query, w_key, w_value, w_output)
    attn_z = [swap(attn_piece, axis) for axis in along_z]
    mlp_piece = line(cut_mlp, w_up, w_down)
    mlp_z = [swap(mlp_piece, axis) for axis in along_z]

    def begin(rows_in):
        return layer_norm(rows_in.astype(F32), ln1_gain, ln1_bias).astype(BF16)

    norm_one = line(begin, inputs)
    segs = pick(segments, at_mp)
    place = windows(segs) + (at_y.reshape(1), segs)
    place = line(lambda item: item, place)

    near_z = line(lambda *parts: jnp.stack(parts), attn_piece, *attn_z)
    near_got = swap(near_z, "y")
    far_z = swap(near_z, "x")
    near_y = line(lambda *parts: jnp.stack(parts[:2]), near_z, near_got, far_z, *mlp_z[:2])
    near_got = swap(near_y, "core")
    far_got = swap(far_z, "y")

    def both_cores(mine, other):
        query_value, key_out = [jnp.stack([mine[:, :, i], other[:, :, i]]) for i in (0, 1)]
        key, out = [
            lax.dynamic_index_in_dim(key_out, at, 1, keepdims=False).reshape(-1, width)
            for at in (at_y, 1 - at_y)
        ]
        return query_value.reshape(-1, width), key, out

    def project(weights, norm):
        query_value = dot(weights[0], norm, NT).astype(BF16).reshape(2, 2, -1, rows)
        return query_value, dot(weights[1], norm, NT).astype(BF16).reshape(2, -1, rows)

    def attend(query_value, keys):
        return attend_forward(query_value, keys, place)

    def branch(base, attended, weights):
        return base + dot(attended.reshape(-1, rows), weights[2], TN)

    def mlp_along_z(*parts):
        return [jnp.concatenate([item[i] for item in parts], 0) for i in (0, 1)]

    def mlp_second(up, up_got, down, down_got):
        return jnp.concatenate([up, up_got], 0), jnp.stack([down, down_got])

    near_w = line(both_cores, near_y, near_got)
    near = line(project, near_w, norm_one)
    up, down = line(mlp_along_z, mlp_piece, *mlp_z)
    up_got, down_got = swap(up, "x"), swap(down, "y")
    near += tuple(line(attend, *near))

    far_y = line(lambda *parts: jnp.stack(parts), far_z, far_got)
    far_got = swap(far_y, "core")
    up, down = line(mlp_second, up, up_got, down, down_got)
    up_got, down_got = swap(up, "y"), swap(down, "x")
    residual = line(branch, inputs.astype(F32), near[2], near_w)
    far_w = line(both_cores, far_y, far_got)
    far = line(project, far_w, norm_one)
    far += tuple(line(attend, *far))

    def second_norm(residual, attended, weights):
        residual = branch(residual, attended, weights)
        return residual, layer_norm(residual, ln2_gain, ln2_bias).astype(BF16)

    cot_other = swap(cotangent, "core")
    far_attended, cot_other = lax.optimization_barrier((far[2], cot_other))
    residual, norm_two = line(second_norm, residual, far_attended, far_w)
    norm_two_other = swap(norm_two, "core")

    def mlp_last(up, up_got, down, down_got):
        return jnp.concatenate([up, up_got], 0), jnp.concatenate([down, down_got], 1).reshape(-1, width)

    up, down = line(mlp_last, up, up_got, down, down_got)
    mlp_b, back_b, *grads = line(
        lambda *args: feed_forward(*args, kind=BF16), norm_two_other, cot_other, up, down
    )
    mlp_b, back_b = swap(mlp_b, "core"), swap(back_b, "core")
    mlp_a, back_a, up_grad, down_grad = line(feed_forward, norm_two, cotangent, up, down, grads)

    def before_attention(attended, weights, grad):
        att_grad = dot(weights[2], grad, NT).astype(BF16).reshape(attended.shape)
        return att_grad, dot(attended.reshape(-1, rows), grad, NN).astype(BF16)


    quarter = up.shape[0] // 4

    def up_sum_of(terms, low, high):
        return add(*[item[low:high] for item in terms])

    def down_sum_of(terms, y, x, low=0, high=quarter):
        whole = terms[0].reshape(2, 2, quarter, width)[y, x, low:high]
        return add(whole, *[item.reshape(-1, quarter, width)[y, low:high] for item in terms[1:]])

    def mlp_sum_first(up_terms, down_terms):
        return (
            up_sum_of(up_terms, 2 * quarter, 4 * quarter),
            jnp.stack([down_sum_of(down_terms, y, 1) for y in (0, 1)]),
        )

    up_terms, down_terms = (up_grad,), (down_grad,)
    sends = line(mlp_sum_first, up_terms, down_terms)
    up_terms += (swap(sends[0], "y"),)
    down_terms += (swap(sends[1], "x"),)

    def attend_back(saved, att_grad):
        return attend_backward(*saved[:3], att_grad, saved[3], place)

    def weight_grads(query_value_grad, key_grad, out_grad, norm):
        query_value = dot(query_value_grad.reshape(-1, rows), norm, NN).astype(BF16)
        keys = dot(key_grad.reshape(-1, rows), norm, NN).astype(BF16)
        sums = (
            query_value.reshape(2, 2, -1, width),
            keys.reshape(2, -1, width),
            out_grad.reshape(2, -1, width),
        )
        return sums, [item[1] for item in sums]

    def project_back(grads, weights):
        return dot(grads[0].reshape(-1, rows), weights[0], TN) + dot(
            grads[1].reshape(-1, rows), weights[1], TN
        )

    def attn_terms_of(mine, got, at):
        terms = [(mine[0][0, at], mine[1][0], mine[2][0]), (got[0][at], got[1], got[2])]
        first = at_y == at
        return [
            [item[0] for item in terms],
            [jnp.where(first, item[1], item[2]) for item in terms],
        ]

    def sum_other_y(mine, got):
        return jnp.stack([add(*terms) for terms in attn_terms_of(mine, got, 1)])

    def sum_this_y(mine, got, from_y):
        terms = attn_terms_of(mine, got, 0)
        return jnp.stack([add(*terms[i], from_y[i]) for i in (0, 1)])

    output, res_grad, branch_grad, norm_two_grads = line(
        middle, residual, cotangent, ln2_gain, [mlp_a, mlp_b], [back_a, back_b]
    )
    far_att, far_out = line(before_attention, far[2], far_w, branch_grad)
    far_grads = line(attend_back, far, far_att)
    far_mine, sends = line(weight_grads, *far_grads, far_out, norm_one)
    far_got = [swap(item, "core") for item in sends]
    def mlp_sum_second(up_terms, down_terms):
        return up_sum_of(up_terms, quarter, 2 * quarter), down_sum_of(down_terms, 1, 0)

    sends = line(mlp_sum_second, up_terms, down_terms)
    up_terms += (swap(sends[0], "x"),)
    down_y = swap(sends[1], "y")

    norm_one_grad = line(project_back, far_grads, far_w)
    near_att, near_out = line(before_attention, near[2], near_w, branch_grad)
    far_y = swap(line(sum_other_y, far_mine, far_got), "y")

    part = quarter // 4

    def mlp_sum_of_z(up_terms, down_terms, down_y, low, high):
        low, high = low * part, high * part
        return jnp.stack(
            [
                up_sum_of(up_terms, low, high),
                down_sum_of(down_terms + (jnp.stack([down_y, down_y]),), 0, 0, low, high),
            ]
        )

    mlp_terms = (up_terms, down_terms, down_y)
    mlp_z1 = swap(line(lambda *terms: mlp_sum_of_z(*terms, 2, 4), *mlp_terms), "z1")
    near_grads = line(attend_back, near, near_att)
    mlp_send = line(
        lambda got, *terms: add(mlp_sum_of_z(*terms, 1, 2), got[:, part:]), mlp_z1, *mlp_terms
    )
    mlp_z2 = swap(mlp_send, "z2")
    near_mine, sends = line(weight_grads, *near_grads, near_out, norm_one)
    near_got = [swap(item, "core") for item in sends]
    far_x = swap(line(sum_this_y, far_mine, far_got, far_y), "x")
    near_y = swap(line(sum_other_y, near_mine, near_got), "y")

    def add_project_back(norm_one_grad, grads, weights):
        return norm_one_grad + project_back(grads, weights)

    def finish(norm_one_grad):
        in_grad, norm_one_grads = last(inputs, norm_one_grad, res_grad, ln1_gain)
        return jnp.concatenate([norm_one_grads[:2], norm_two_grads[:2]]), in_grad

    norm_one_grad = line(add_project_back, norm_one_grad, near_grads, near_w)
    norm_sums, in_grad = line(finish, norm_one_grad)
    got = swap(norm_sums, "core")

    mlp_sum = line(
        lambda got, other, *terms: add(mlp_sum_of_z(*terms, 0, 1), got[:, :part], other),
        mlp_z1,
        mlp_z2,
        *mlp_terms,
    )
    mlp_got = swap(mlp_sum, "y")
    norm_sums = line(jnp.add, norm_sums, got)
    got = swap(norm_sums, "x")

    def attn_sum_z(mine, got, from_y, from_x):
        from_x = from_x.reshape(2, -1, width)
        whole = sum_this_y(mine, got, from_y).astype(F32) + from_x
        return [whole[:, at * HEAD_DIM : (at + 1) * HEAD_DIM].astype(BF16) for at in range(4)]

    attn_mine, *sends = line(attn_sum_z, near_mine, near_got, near_y, far_x)
    attn_z = [swap(item, axis) for item, axis in zip(sends, along_z)]

    def in_order(piece, y, core, both):
        return order(at_core, order(at_y, piece, y), order(at_y, core, both))

    norm_sums = line(jnp.add, norm_sums, got)
    got = swap(norm_sums, "z1")
    norm_sums = line(jnp.add, norm_sums, got)
    got = swap(norm_sums, "z2")
    attn_sum = line(lambda _, *terms: add(*terms), mlp_got, attn_mine, *attn_z)
    attn_got = [
        lax.ppermute(attn_sum, "dp", [(i, i ^ mask) for i in range(4)]) for mask in (2, 1, 3)
    ]
    mlp_sum = line(functools.partial(order, at_y), mlp_sum, mlp_got)
    mlp_got = swap(mlp_sum, "core")
    norm_sums = line(jnp.add, norm_sums, got)
    got = swap(norm_sums, "y")
    attn_sum = line(in_order, attn_sum, *attn_got)
    attn_sum = line(
        lambda item: item.transpose(1, 2, 0, 3, 4).reshape(4, local, width).astype(F32), attn_sum
    )
    attn_sums = line(lambda item: (item[0].T, item[1].T, item[2].T, item[3]), attn_sum)
    mlp_sum = line(functools.partial(order, at_core), mlp_sum, mlp_got)
    up_sum, down_sum = line(
        lambda item: tuple(item.transpose(2, 1, 0, 3, 4).reshape(2, -1, width).astype(F32)), mlp_sum
    )
    up_sum = line(jnp.transpose, up_sum)
    norm_sums = line(jnp.add, norm_sums, got)
    norm_sums = lax.dynamic_slice_in_dim(norm_sums, at_mp * (width // 8), width // 8, 1)
    return (
        output,
        in_grad,
        norm_sums[0],
        norm_sums[1],
        *attn_sums,
        norm_sums[2],
        norm_sums[3],
        up_sum,
        down_sum,
    )


def on_any(
    mp_size,
    inputs,
    segments,
    ln1_gain,
    ln1_bias,
    w_query,
    w_key,
    w_value,
    w_output,
    ln2_gain,
    ln2_bias,
    w_up,
    w_down,
    cotangent,
):
    rows, width = inputs.shape
    seq_length = segments.shape[1]
    shared_by = seq_length // rows
    at_mp = lax.axis_index("mp")
    groups = [[start + i for i in range(shared_by)] for start in range(0, mp_size, shared_by)]

    def exchange(values, split, join):
        if shared_by == 1:
            return values
        return lax.all_to_all(values, "mp", split, join, axis_index_groups=groups, tiled=True)

    def gather(parts):
        return lax.all_gather(parts, "mp", axis=1, tiled=True)

    def reduce(parts):
        return lax.psum(lax.psum_scatter(parts, "mp", scatter_dimension=1, tiled=True), "dp")

    attn_w = gather(jnp.stack([w_query.T, w_value.T, w_key.T, w_output]))
    up, down = gather(jnp.stack([w_up.T, w_down]))
    project, w_out = attn_w[:3].reshape(3 * width, width), attn_w[3]

    segs = lax.dynamic_index_in_dim(segments, at_mp // shared_by, 0, keepdims=False)
    place = windows(segs) + (jnp.zeros((1,), jnp.int32), segs)
    resid_in = inputs.astype(F32)
    norm_one = layer_norm(resid_in, ln1_gain, ln1_bias).astype(BF16)
    projected = dot(project, norm_one, NT).astype(BF16).reshape(3, width, rows)
    projected = exchange(projected, 1, 2)
    query_value, keys = projected[None, :2], projected[2:]
    heads_out, lse = attend_forward(query_value, keys, place)
    attended = exchange(heads_out[0], 1, 0)
    residual = resid_in + dot(attended, w_out, TN)
    norm_two = layer_norm(residual, ln2_gain, ln2_bias).astype(BF16)
    mlp_branch, norm_two_grad, *mlp_grads = feed_forward(norm_two, cotangent, up, down)
    up_sum, down_sum = reduce(jnp.stack(mlp_grads)).astype(F32)

    output, res_grad, branch_grad, norm_two_grads = middle(
        residual, cotangent, ln2_gain, [mlp_branch], [norm_two_grad]
    )
    out_grad = dot(attended, branch_grad, NN).astype(BF16)
    att_grad = exchange(dot(w_out, branch_grad, NT).astype(BF16), 0, 1)
    query_value_grad, key_grad = attend_backward(
        query_value, keys, heads_out, att_grad[None], lse, place
    )
    proj_grad = exchange(jnp.concatenate([query_value_grad[0], key_grad]), 2, 1)
    proj_grad = proj_grad.reshape(3 * width, rows)
    project_grad = dot(proj_grad, norm_one, NN).astype(BF16).reshape(3, width, width)
    attn_sum = reduce(jnp.concatenate([project_grad, out_grad[None]])).astype(F32)
    in_grad, norm_one_grads = last(inputs, dot(proj_grad, project, TN), res_grad, ln1_gain)
    norm_parts = jnp.concatenate([norm_one_grads[:2], norm_two_grads[:2]])
    norm_sums = lax.dynamic_slice_in_dim(
        lax.psum(norm_parts, ("dp", "mp")), at_mp * (width // mp_size), width // mp_size, 1
    )
    return (
        output,
        in_grad,
        norm_sums[0],
        norm_sums[1],
        attn_sum[0].T,
        attn_sum[2].T,
        attn_sum[1].T,
        attn_sum[3],
        norm_sums[2],
        norm_sums[3],
        up_sum.T,
        down_sum,
    )


def shards(dp_size, mp_size, inputs, segments, *rest):
    if dp_size == 4 and mp_size == 8 and inputs.shape[0] == segments.shape[1]:
        return on_cube(inputs, segments, *rest)
    return on_any(mp_size, inputs, segments, *rest)


def solution(mesh):
    return jax.shard_map(
        functools.partial(shards, mesh.shape["dp"], mesh.shape["mp"]),
        mesh=mesh,
        in_specs=(
            P(("dp", "mp"), None),
            P("dp", None),
            P(),
            P(),
            P(None, "mp"),
            P(None, "mp"),
            P(None, "mp"),
            P("mp", None),
            P(),
            P(),
            P(None, "mp"),
            P("mp", None),
            P(("dp", "mp"), None),
        ),
        out_specs=(
            P(("dp", "mp"), None),
            P(("dp", "mp"), None),
            P("mp"),
            P("mp"),
            P(None, "mp"),
            P(None, "mp"),
            P(None, "mp"),
            P("mp", None),
            P("mp"),
            P("mp"),
            P(None, "mp"),
            P("mp", None),
        ),
        check_vma=False,
    )
```

```python
import functools
import math

import jax
import jax.numpy as jnp
from jax import lax
from jax.experimental import pallas as pl
from jax.experimental.pallas import tpu as pltpu
from jax.sharding import PartitionSpec as P

HEAD_DIM = 48
PAIR = 2 * HEAD_DIM
IMAGES = 4
TILE = 128
norm_eps = 1e-06
negative_fill = -1e30
SCALE = HEAD_DIM ** (-0.5)
SCALE_LOG2 = SCALE * math.log2(math.e)
BF16 = jnp.bfloat16
F32 = jnp.float32


def layer_norm(values, gain, bias):
    center = jnp.mean(values, axis=-1, keepdims=True)
    shifted = values - center
    spread = jnp.mean(shifted * shifted, axis=-1, keepdims=True)
    return shifted * lax.rsqrt(spread + norm_eps) * gain + bias


def layer_norm_back(values, gain, grad):
    shifted = values - jnp.mean(values, axis=-1, keepdims=True)
    scale = lax.rsqrt(jnp.mean(shifted * shifted, axis=-1, keepdims=True) + norm_eps)
    unit = shifted * scale
    scaled = grad * gain
    back = scale * (
        scaled
        - jnp.mean(scaled, axis=-1, keepdims=True)
        - unit * jnp.mean(scaled * unit, axis=-1, keepdims=True)
    )
    return back, jnp.sum(grad * unit, axis=0, keepdims=True), jnp.sum(grad, axis=0, keepdims=True)


def dot(left, right, dims):
    return lax.dot_general(left, right, (dims, ((), ())), preferred_element_type=F32)


NN = ((1,), (0,))
NT = ((1,), (1,))
TN = ((0,), (0,))


def window_kinds(tiles):
    return tuple(n for n in (2, 3, 4, 5, 6, 7) if n < tiles) + (tiles,)


def image_rows(segs, length):
    row = lax.broadcasted_iota(jnp.int32, (TILE - PAIR, length), 0)
    here = row == segs
    one_hot = jnp.where(here, 1.0, 0.0).astype(BF16)
    fill = jnp.where(jnp.logical_or(here, row >= IMAGES), 0.0, negative_fill).astype(BF16)
    return one_hot, fill


def side_by_side(pair, extra):
    blank = jnp.zeros((HEAD_DIM, TILE), BF16)
    left = jnp.concatenate([pair[:HEAD_DIM], blank, extra], axis=0)
    right = jnp.concatenate([blank, pair[HEAD_DIM:], extra], axis=0)
    return jnp.concatenate([left, right], axis=1)


def pair_places(ref):
    cores, count = ref.shape[0], ref.shape[1]
    return [(core, top) for core in range(cores) for top in range(0, count, PAIR)]


def attend_forward_kernel(
    first_ref, kind_ref, flip_ref, segs_ref, qv_ref, k_ref, out_ref, lse_ref, hot_ref, keys_ref, vals_ref
):
    length = k_ref.shape[-1]
    at_q = flip_ref[0]
    places = pair_places(k_ref)
    one_hot, fill = image_rows(segs_ref[...], length)
    hot_ref[...] = one_hot
    for j, (core, top) in enumerate(places):
        rows = slice(top, top + PAIR)
        keys_ref[j] = jnp.concatenate([k_ref[core, rows, :], fill], axis=0).T
        vals_ref[j] = jnp.concatenate(
            [qv_ref[core, 1 - at_q, rows, :], jnp.ones((16, length), BF16)], axis=0
        )

    def block(b, carry):
        at = pl.ds(pl.multiple_of(b * TILE, TILE), TILE)
        first = pl.multiple_of(first_ref[b] * TILE, TILE)

        def variant(tiles):
            span = pl.ds(first, tiles * TILE)
            scores = [
                dot(
                    keys_ref[j, span, :],
                    side_by_side(qv_ref[core, at_q, top : top + PAIR, at], hot_ref[:, at]),
                    NN,
                )
                for j, (core, top) in enumerate(places)
            ]
            for j, (core, top) in enumerate(places):
                most = jnp.max(scores[j], axis=0, keepdims=True)
                expo = jnp.exp2((scores[j] - most) * SCALE_LOG2).astype(BF16)
                mixed = dot(vals_ref[j, :, span], expo, NN)
                total = mixed[PAIR : PAIR + 1, :]
                inverse = 1.0 / total
                out_ref[core, top : top + HEAD_DIM, at] = (
                    mixed[:HEAD_DIM, :TILE] * inverse[:, :TILE]
                ).astype(BF16)
                out_ref[core, top + HEAD_DIM : top + PAIR, at] = (
                    mixed[HEAD_DIM:PAIR, TILE:] * inverse[:, TILE:]
                ).astype(BF16)
                lse_ref[j, pl.ds(b, 1), :] = most * SCALE_LOG2 + jnp.log2(total)

        for tiles in window_kinds(length // TILE):
            pl.when(kind_ref[b] == tiles)(functools.partial(variant, tiles))
        return carry

    lax.fori_loop(0, length // TILE, block, 0)


def attend_backward_kernel(
    first_ref,
    kind_ref,
    flip_ref,
    segs_ref,
    qv_ref,
    k_ref,
    att_ref,
    grad_ref,
    lse_ref,
    dqv_ref,
    dk_ref,
    hot_ref,
    keys_ref,
    vals_ref,
    queries_ref,
    grads_ref,
    key_sum_ref,
    val_sum_ref,
):
    length = k_ref.shape[-1]
    at_q = flip_ref[0]
    places = pair_places(k_ref)
    one_hot, fill = image_rows(segs_ref[...], length)
    hot_ref[...] = one_hot
    pad = jnp.zeros((TILE - PAIR, length), BF16)
    for j, (core, top) in enumerate(places):
        rows = slice(top, top + PAIR)
        keys_ref[j] = jnp.concatenate([k_ref[core, rows, :], fill], axis=0).T
        vals_ref[j] = jnp.concatenate([qv_ref[core, 1 - at_q, rows, :], pad], axis=0).T
        queries_ref[j] = jnp.concatenate([qv_ref[core, at_q, rows, :], pad], axis=0).T
        grads_ref[j] = jnp.concatenate([grad_ref[core, rows, :], pad], axis=0).T
    key_sum_ref[...] = jnp.zeros(key_sum_ref.shape, F32)
    val_sum_ref[...] = jnp.zeros(val_sum_ref.shape, F32)
    no_rows = jnp.zeros((TILE - PAIR, TILE), BF16)
    lane = lax.broadcasted_iota(jnp.int32, (TILE, TILE), 1)
    in_first = lane < HEAD_DIM

    def stacked(both):
        blank = jnp.zeros_like(both)
        return jnp.concatenate(
            [jnp.where(in_first, both, blank), jnp.where(in_first, blank, both)], axis=0
        )

    def block(b, carry):
        at = pl.ds(pl.multiple_of(b * TILE, TILE), TILE)
        first = pl.multiple_of(first_ref[b] * TILE, TILE)

        def variant(tiles):
            span = pl.ds(first, tiles * TILE)
            scores = [
                dot(
                    keys_ref[j, span, :],
                    side_by_side(qv_ref[core, at_q, top : top + PAIR, at], hot_ref[:, at]),
                    NN,
                )
                for j, (core, top) in enumerate(places)
            ]
            prob_grads = [
                dot(
                    vals_ref[j, span, :],
                    side_by_side(grad_ref[core, top : top + PAIR, at], no_rows),
                    NN,
                )
                for j, (core, top) in enumerate(places)
            ]
            for j, (core, top) in enumerate(places):
                rows = slice(top, top + PAIR)
                agree = grad_ref[core, rows, at].astype(F32) * att_ref[core, rows, at].astype(F32)
                delta = jnp.concatenate(
                    [
                        jnp.sum(agree[:HEAD_DIM], axis=0, keepdims=True),
                        jnp.sum(agree[HEAD_DIM:], axis=0, keepdims=True),
                    ],
                    axis=1,
                )
                probs = jnp.exp2(scores[j] * SCALE_LOG2 - lse_ref[j, pl.ds(b, 1), :])
                score_grad = (probs * (prob_grads[j] - delta)).astype(BF16)
                val_sum_ref[j, span, :] += dot(
                    probs.astype(BF16), stacked(grads_ref[j, at, :]), NN
                )
                key_sum_ref[j, span, :] += dot(score_grad, stacked(queries_ref[j, at, :]), NN)
                query_grad = dot(k_ref[core, rows, span], score_grad, NN) * SCALE
                dqv_ref[core, at_q, top : top + HEAD_DIM, at] = query_grad[
                    :HEAD_DIM, :TILE
                ].astype(BF16)
                dqv_ref[core, at_q, top + HEAD_DIM : top + PAIR, at] = query_grad[
                    HEAD_DIM:, TILE:
                ].astype(BF16)

        for tiles in window_kinds(length // TILE):
            pl.when(kind_ref[b] == tiles)(functools.partial(variant, tiles))
        return carry

    lax.fori_loop(0, length // TILE, block, 0)
    for j, (core, top) in enumerate(places):
        rows = slice(top, top + PAIR)
        dk_ref[core, rows, :] = (key_sum_ref[j] * SCALE).T[:PAIR].astype(BF16)
        dqv_ref[core, 1 - at_q, rows, :] = val_sum_ref[j].T[:PAIR].astype(BF16)


def windows(segs):
    length = segs.shape[0]
    tiles = length // TILE
    by_tile = segs.reshape(tiles, TILE)
    begin = jnp.sum(segs[None, :] < by_tile[:, :1], axis=1)
    end = jnp.sum(segs[None, :] <= by_tile[:, -1:], axis=1)
    first = begin // TILE
    need = (end + TILE - 1) // TILE - first
    kinds = jnp.asarray(window_kinds(tiles), jnp.int32)
    kind = jnp.min(jnp.where(kinds[None, :] >= need[:, None], kinds[None, :], tiles), axis=1)
    return jnp.minimum(first, tiles - kind).astype(jnp.int32), kind.astype(jnp.int32)


def attention_specs(keys):
    cores, count, length = keys.shape
    pairs = cores * count // PAIR
    step = pairs if pairs <= 4 else 4
    part = count * step // pairs
    rows = pl.BlockSpec((cores, part, length), lambda i, *_: (0, i, 0))
    two = pl.BlockSpec((cores, 2, part, length), lambda i, *_: (0, 0, i, 0))
    segs = pl.BlockSpec((1, length), lambda i, *_: (0, 0))
    lse = pl.BlockSpec((step, length // TILE, 2 * TILE), lambda i, *_: (i, 0, 0))
    return pairs, step, rows, two, segs, lse


def attend_forward(query_value, keys, place):
    first, kind, flip, segs = place
    length = segs.shape[0]
    pairs, step, rows, two, segs_spec, lse = attention_specs(keys)
    return pl.pallas_call(
        attend_forward_kernel,
        grid_spec=pltpu.PrefetchScalarGridSpec(
            num_scalar_prefetch=3,
            grid=(pairs // step,),
            in_specs=[segs_spec, two, rows],
            out_specs=[rows, lse],
            scratch_shapes=[
                pltpu.VMEM((TILE - PAIR, length), BF16),
                pltpu.VMEM((step, length, TILE), BF16),
                pltpu.VMEM((step, PAIR + 16, length), BF16),
            ],
        ),
        out_shape=[
            jax.ShapeDtypeStruct(keys.shape, BF16),
            jax.ShapeDtypeStruct((pairs, length // TILE, 2 * TILE), F32),
        ],
        compiler_params=pltpu.CompilerParams(vmem_limit_bytes=40 << 20),
        name="attend_forward",
    )(first, kind, flip, segs[None, :], query_value, keys)


def attend_backward(query_value, keys, attended, grad, lse, place):
    first, kind, flip, segs = place
    length = segs.shape[0]
    pairs, step, rows, two, segs_spec, lse_spec = attention_specs(keys)
    wide = pltpu.VMEM((step, length, TILE), BF16)
    total = pltpu.VMEM((step, length, TILE), F32)
    return pl.pallas_call(
        attend_backward_kernel,
        grid_spec=pltpu.PrefetchScalarGridSpec(
            num_scalar_prefetch=3,
            grid=(pairs // step,),
            in_specs=[segs_spec, two, rows, rows, rows, lse_spec],
            out_specs=[two, rows],
            scratch_shapes=[
                pltpu.VMEM((TILE - PAIR, length), BF16),
                wide,
                wide,
                wide,
                wide,
                total,
                total,
            ],
        ),
        out_shape=[
            jax.ShapeDtypeStruct(query_value.shape, BF16),
            jax.ShapeDtypeStruct(keys.shape, BF16),
        ],
        compiler_params=pltpu.CompilerParams(vmem_limit_bytes=40 << 20),
        name="attend_backward",
    )(first, kind, flip, segs[None, :], query_value, keys, attended, grad, lse)


def gelu_parts(values):
    below = 0.5 * (1.0 + lax.erf(values * (0.5 ** 0.5)))
    density = jnp.exp(values * values * -0.5) * ((2.0 * math.pi) ** -0.5)
    return values * below, below + values * density


def feed_forward_kernel(norm_ref, cot_ref, up_ref, down_ref, *refs):
    *earlier, mlp_ref, back_ref, up_grad_ref, down_grad_ref, act_ref, pre_ref = refs[:-1]
    sum_ref = mlp_ref if mlp_ref.dtype == F32 else refs[-1]
    rows = norm_ref.shape[0]
    chunk = min(rows, 256)

    @pl.when(pl.program_id(0) == 0)
    def _():
        sum_ref[...] = jnp.zeros(sum_ref.shape, F32)
        back_ref[...] = jnp.zeros(back_ref.shape, F32)

    for start in range(0, rows, chunk):
        at = slice(start, start + chunk)
        pre_act = dot(norm_ref[at, :], up_ref[...], NT)
        act_grad = dot(cot_ref[at, :], down_ref[...], NT)
        activation, slope = gelu_parts(pre_act)
        activation = activation.astype(BF16)
        pre_grad = (act_grad * slope).astype(BF16)
        act_ref[at, :] = activation
        pre_ref[at, :] = pre_grad
        sum_ref[at, :] += dot(activation, down_ref[...], NN)
        back_ref[at, :] += dot(pre_grad, up_ref[...], NN)
    up_grad = dot(pre_ref[...], norm_ref[...], TN)
    down_grad = dot(act_ref[...], cot_ref[...], TN)
    if earlier:
        up_grad = up_grad + earlier[0][...].astype(F32)
        down_grad = down_grad + earlier[1][...].astype(F32)
    up_grad_ref[...] = up_grad.astype(BF16)
    down_grad_ref[...] = down_grad.astype(BF16)

    if mlp_ref.dtype != F32:

        @pl.when(pl.program_id(0) == pl.num_programs(0) - 1)
        def _():
            mlp_ref[...] = sum_ref[...].astype(mlp_ref.dtype)


def feed_forward(norm, cot, up, down, earlier=(), kind=F32):
    rows, width = norm.shape
    hidden = up.shape[0]
    part = 512 if hidden % 512 == 0 else hidden
    whole = pl.BlockSpec((rows, width), lambda i: (0, 0))
    block = pl.BlockSpec((part, width), lambda i: (i, 0))
    grads = jax.ShapeDtypeStruct((hidden, width), BF16)
    return pl.pallas_call(
        feed_forward_kernel,
        grid=(hidden // part,),
        in_specs=[whole, whole, block, block] + [block] * len(earlier),
        out_specs=[whole, whole, block, block],
        out_shape=[
            jax.ShapeDtypeStruct((rows, width), kind),
            jax.ShapeDtypeStruct((rows, width), F32),
            grads,
            grads,
        ],
        scratch_shapes=[
            pltpu.VMEM((rows, part), BF16),
            pltpu.VMEM((rows, part), BF16),
            pltpu.VMEM((8, 128) if kind == F32 else (rows, width), F32),
        ],
        compiler_params=pltpu.CompilerParams(vmem_limit_bytes=58 << 20),
        name="feed_forward",
    )(norm, cot, up, down, *earlier)


def middle_kernel(parts, residual_ref, cot_ref, gain_ref, *refs):
    mlp_refs, back_refs = refs[:parts], refs[parts : 2 * parts]
    output_ref, res_grad_ref, branch_ref, norm_grad_ref = refs[2 * parts :]

    @pl.when(pl.program_id(0) == 0)
    def _():
        norm_grad_ref[...] = jnp.zeros(norm_grad_ref.shape, F32)

    residual = residual_ref[...]
    output_ref[...] = sum([ref[...].astype(F32) for ref in mlp_refs], residual).astype(BF16)
    grad = functools.reduce(jnp.add, [ref[...] for ref in back_refs])
    back, gain_grad, bias_grad = layer_norm_back(residual, gain_ref[...], grad)
    res_grad = cot_ref[...].astype(F32) + back
    res_grad_ref[...] = res_grad
    branch_ref[...] = res_grad.astype(BF16)
    norm_grad_ref[0:1, :] += gain_grad
    norm_grad_ref[1:2, :] += bias_grad


def middle(residual, cot, gain, mlps, backs):
    rows, width = residual.shape
    parts = len(mlps)
    step = 256
    block = pl.BlockSpec((step, width), lambda i: (i, 0))
    sums = jax.ShapeDtypeStruct((rows, width), F32)
    low = jax.ShapeDtypeStruct((rows, width), BF16)
    return pl.pallas_call(
        functools.partial(middle_kernel, parts),
        grid=(rows // step,),
        in_specs=[block, block, pl.BlockSpec((1, width), lambda i: (0, 0))] + [block] * (2 * parts),
        out_specs=[block, block, block, pl.BlockSpec((8, width), lambda i: (0, 0))],
        out_shape=[low, sums, low, jax.ShapeDtypeStruct((8, width), F32)],
        compiler_params=pltpu.CompilerParams(vmem_limit_bytes=40 << 20),
        name="middle",
    )(residual, cot, gain[None, :], *mlps, *backs)


def last_kernel(rows_ref, grad_ref, res_grad_ref, gain_ref, in_grad_ref, norm_grad_ref):
    @pl.when(pl.program_id(0) == 0)
    def _():
        norm_grad_ref[...] = jnp.zeros(norm_grad_ref.shape, F32)

    back, gain_grad, bias_grad = layer_norm_back(
        rows_ref[...].astype(F32), gain_ref[...], grad_ref[...]
    )
    in_grad_ref[...] = (res_grad_ref[...] + back).astype(BF16)
    norm_grad_ref[0:1, :] += gain_grad
    norm_grad_ref[1:2, :] += bias_grad


def last(rows_in, grad, res_grad, gain):
    rows, width = rows_in.shape
    step = 256
    block = pl.BlockSpec((step, width), lambda i: (i, 0))
    few = pl.BlockSpec((8, width), lambda i: (0, 0))
    return pl.pallas_call(
        last_kernel,
        grid=(rows // step,),
        in_specs=[block, block, block, pl.BlockSpec((1, width), lambda i: (0, 0))],
        out_specs=[block, few],
        out_shape=[
            jax.ShapeDtypeStruct((rows, width), BF16),
            jax.ShapeDtypeStruct((8, width), F32),
        ],
        compiler_params=pltpu.CompilerParams(vmem_limit_bytes=40 << 20),
        name="last",
    )(rows_in, grad, res_grad, gain[None, :])


def add(*terms):
    return functools.reduce(jnp.add, [item.astype(F32) for item in terms]).astype(BF16)


def swap(values, axis):
    name, size, mask = {
        "core": ("dp", 4, 1),
        "y": ("dp", 4, 2),
        "x": ("mp", 8, 1),
        "z1": ("mp", 8, 2),
        "z2": ("mp", 8, 4),
        "z3": ("mp", 8, 6),
    }[axis]
    return lax.ppermute(values, name, [(i, i ^ mask) for i in range(size)])


def order(at, mine, other):
    return jnp.where(at == 0, jnp.stack([mine, other]), jnp.stack([other, mine]))


class Line:
    def __init__(self):
        self.last = ()

    def __call__(self, step, *args):
        args, _ = lax.optimization_barrier((args, self.last))
        result = step(*args)
        self.last = tuple(jax.tree.leaves(result))
        return result


def on_cube(
    inputs,
    segments,
    ln1_gain,
    ln1_bias,
    w_query,
    w_key,
    w_value,
    w_output,
    ln2_gain,
    ln2_bias,
    w_up,
    w_down,
    cotangent,
):
    rows, width = inputs.shape
    local = w_query.shape[1]
    at_dp, at_mp = lax.axis_index("dp"), lax.axis_index("mp")
    at_y, at_core = at_dp // 2, at_dp % 2
    line = Line()

    def pick(values, at):
        return lax.dynamic_index_in_dim(values, at, 0, keepdims=False)

    def cut_attention(query, key, value, out):
        kinds = jnp.stack([query.T, key.T, value.T, out]).reshape(2, 2, 2, HEAD_DIM, width)
        return pick(kinds.transpose(0, 2, 1, 3, 4).reshape(4, 2, HEAD_DIM, width), at_dp)

    def cut_mlp(up, down):
        pieces = jnp.stack([up.T, down]).reshape(2, 4, -1, width)
        return lax.dynamic_index_in_dim(pieces, at_dp, 1, keepdims=False)

    def join(*parts):
        return jnp.concatenate(parts, 0)

    along_z = ("z2", "z1", "z3")
    attn_piece = line(cut_attention, w_query, w_key, w_value, w_output)
    attn_z = [swap(attn_piece, axis) for axis in along_z]
    mlp_piece = line(cut_mlp, w_up, w_down)
    mlp_z = [swap(mlp_piece, axis) for axis in along_z]

    def begin(rows_in):
        return layer_norm(rows_in.astype(F32), ln1_gain, ln1_bias).astype(BF16)

    norm_one = line(begin, inputs)
    segs = pick(segments, at_mp)
    place = windows(segs) + (at_y.reshape(1), segs)
    place = line(lambda item: item, place)

    near_z = line(lambda *parts: jnp.stack(parts), attn_piece, *attn_z)
    near_got = swap(near_z, "y")
    far_z = swap(near_z, "x")
    near_y = line(lambda *parts: jnp.stack(parts[:2]), near_z, near_got, far_z, mlp_z[0])
    near_got = swap(near_y, "core")
    far_got = swap(far_z, "y")

    def both_cores(mine, other):
        query_value, key_out = [jnp.stack([mine[:, :, i], other[:, :, i]]) for i in (0, 1)]
        key, out = [
            lax.dynamic_index_in_dim(key_out, at, 1, keepdims=False).reshape(-1, width)
            for at in (at_y, 1 - at_y)
        ]
        return query_value.reshape(-1, width), key, out

    def project(weights, norm):
        query_value = dot(weights[0], norm, NT).astype(BF16).reshape(2, 2, -1, rows)
        return query_value, dot(weights[1], norm, NT).astype(BF16).reshape(2, -1, rows)

    def attend(query_value, keys):
        return attend_forward(query_value, keys, place)

    def branch(base, attended, weights):
        return base + dot(attended.reshape(-1, rows), weights[2], TN)

    def mlp_along_z(*parts):
        return [jnp.concatenate([item[i] for item in parts], 0) for i in (0, 1)]

    def mlp_second(up, up_got, down, down_got):
        return jnp.concatenate([up, up_got], 0), jnp.stack([down, down_got])

    near_w = line(both_cores, near_y, near_got)
    near = line(project, near_w, norm_one)
    up, down = line(mlp_along_z, mlp_piece, *mlp_z)
    up_got, down_got = swap(up, "x"), swap(down, "y")
    near += tuple(line(attend, *near))

    far_y = line(lambda *parts: jnp.stack(parts), far_z, far_got)
    far_got = swap(far_y, "core")
    up, down = line(mlp_second, up, up_got, down, down_got)
    up_got, down_got = swap(up, "y"), swap(down, "x")
    residual = line(branch, inputs.astype(F32), near[2], near_w)
    far_w = line(both_cores, far_y, far_got)
    far = line(project, far_w, norm_one)
    far += tuple(line(attend, *far))

    def second_norm(residual, attended, weights):
        residual = branch(residual, attended, weights)
        return residual, layer_norm(residual, ln2_gain, ln2_bias).astype(BF16)

    cot_other = swap(cotangent, "core")
    far_attended, cot_other = lax.optimization_barrier((far[2], cot_other))
    residual, norm_two = line(second_norm, residual, far_attended, far_w)
    norm_two_other = swap(norm_two, "core")

    def mlp_last(up, up_got, down, down_got):
        return jnp.concatenate([up, up_got], 0), jnp.concatenate([down, down_got], 1).reshape(-1, width)

    up, down = line(mlp_last, up, up_got, down, down_got)
    mlp_b, back_b, *grads = line(
        lambda *args: feed_forward(*args, kind=BF16), norm_two_other, cot_other, up, down
    )
    mlp_b, back_b = swap(mlp_b, "core"), swap(back_b, "core")
    mlp_a, back_a, up_grad, down_grad = line(feed_forward, norm_two, cotangent, up, down, grads)

    def before_attention(attended, weights, grad):
        att_grad = dot(weights[2], grad, NT).astype(BF16).reshape(attended.shape)
        return att_grad, dot(attended.reshape(-1, rows), grad, NN).astype(BF16)


    quarter = up.shape[0] // 4

    def up_sum_of(terms, low, high):
        return add(*[item[low:high] for item in terms])

    def down_sum_of(terms, y, x, low=0, high=quarter):
        whole = terms[0].reshape(2, 2, quarter, width)[y, x, low:high]
        return add(whole, *[item.reshape(-1, quarter, width)[y, low:high] for item in terms[1:]])

    def mlp_sum_first(up_terms, down_terms):
        return (
            up_sum_of(up_terms, 2 * quarter, 4 * quarter),
            jnp.stack([down_sum_of(down_terms, y, 1) for y in (0, 1)]),
        )

    up_terms, down_terms = (up_grad,), (down_grad,)
    sends = line(mlp_sum_first, up_terms, down_terms)
    up_terms += (swap(sends[0], "y"),)
    down_terms += (swap(sends[1], "x"),)

    def attend_back(saved, att_grad):
        return attend_backward(*saved[:3], att_grad, saved[3], place)

    def weight_grads(query_value_grad, key_grad, out_grad, norm):
        query_value = dot(query_value_grad.reshape(-1, rows), norm, NN).astype(BF16)
        keys = dot(key_grad.reshape(-1, rows), norm, NN).astype(BF16)
        sums = (
            query_value.reshape(2, 2, -1, width),
            keys.reshape(2, -1, width),
            out_grad.reshape(2, -1, width),
        )
        return sums, [item[1] for item in sums]

    def project_back(grads, weights):
        return dot(grads[0].reshape(-1, rows), weights[0], TN) + dot(
            grads[1].reshape(-1, rows), weights[1], TN
        )

    def attn_terms_of(mine, got, at):
        terms = [(mine[0][0, at], mine[1][0], mine[2][0]), (got[0][at], got[1], got[2])]
        first = at_y == at
        return [
            [item[0] for item in terms],
            [jnp.where(first, item[1], item[2]) for item in terms],
        ]

    def sum_other_y(mine, got):
        return jnp.stack([add(*terms) for terms in attn_terms_of(mine, got, 1)])

    def sum_this_y(mine, got, from_y):
        terms = attn_terms_of(mine, got, 0)
        return jnp.stack([add(*terms[i], from_y[i]) for i in (0, 1)])

    output, res_grad, branch_grad, norm_two_grads = line(
        middle, residual, cotangent, ln2_gain, [mlp_a, mlp_b], [back_a, back_b]
    )
    far_att, far_out = line(before_attention, far[2], far_w, branch_grad)
    far_grads = line(attend_back, far, far_att)
    far_mine, sends = line(weight_grads, *far_grads, far_out, norm_one)
    far_got = [swap(item, "core") for item in sends]
    def mlp_sum_second(up_terms, down_terms):
        return up_sum_of(up_terms, quarter, 2 * quarter), down_sum_of(down_terms, 1, 0)

    sends = line(mlp_sum_second, up_terms, down_terms)
    up_terms += (swap(sends[0], "x"),)
    down_y = swap(sends[1], "y")

    norm_one_grad = line(project_back, far_grads, far_w)
    near_att, near_out = line(before_attention, near[2], near_w, branch_grad)
    far_y = swap(line(sum_other_y, far_mine, far_got), "y")

    part = quarter // 4

    def mlp_sum_of_z(up_terms, down_terms, down_y, low, high):
        low, high = low * part, high * part
        return jnp.stack(
            [
                up_sum_of(up_terms, low, high),
                down_sum_of(down_terms + (jnp.stack([down_y, down_y]),), 0, 0, low, high),
            ]
        )

    mlp_terms = (up_terms, down_terms, down_y)
    mlp_z1 = swap(line(lambda *terms: mlp_sum_of_z(*terms, 2, 4), *mlp_terms), "z1")
    near_grads = line(attend_back, near, near_att)
    mlp_send = line(
        lambda got, *terms: add(mlp_sum_of_z(*terms, 1, 2), got[:, part:]), mlp_z1, *mlp_terms
    )
    mlp_z2 = swap(mlp_send, "z2")
    near_mine, sends = line(weight_grads, *near_grads, near_out, norm_one)
    near_got = [swap(item, "core") for item in sends]
    far_x = swap(line(sum_this_y, far_mine, far_got, far_y), "x")
    near_y = swap(line(sum_other_y, near_mine, near_got), "y")

    def add_project_back(norm_one_grad, grads, weights):
        return norm_one_grad + project_back(grads, weights)

    def finish(norm_one_grad):
        in_grad, norm_one_grads = last(inputs, norm_one_grad, res_grad, ln1_gain)
        return jnp.concatenate([norm_one_grads[:2], norm_two_grads[:2]]), in_grad

    norm_one_grad = line(add_project_back, norm_one_grad, near_grads, near_w)
    norm_sums, in_grad = line(finish, norm_one_grad)
    got = swap(norm_sums, "core")

    mlp_sum = line(
        lambda got, other, *terms: add(mlp_sum_of_z(*terms, 0, 1), got[:, :part], other),
        mlp_z1,
        mlp_z2,
        *mlp_terms,
    )
    mlp_got = swap(mlp_sum, "y")
    norm_sums = line(jnp.add, norm_sums, got)
    got = swap(norm_sums, "x")

    def attn_sum_z(mine, got, from_y, from_x):
        from_x = from_x.reshape(2, -1, width)
        whole = sum_this_y(mine, got, from_y).astype(F32) + from_x
        return [whole[:, at * HEAD_DIM : (at + 1) * HEAD_DIM].astype(BF16) for at in range(4)]

    attn_mine, *sends = line(attn_sum_z, near_mine, near_got, near_y, far_x)
    attn_z = [swap(item, axis) for item, axis in zip(sends, along_z)]

    def in_order(piece, y, core, both):
        return order(at_core, order(at_y, piece, y), order(at_y, core, both))

    norm_sums = line(jnp.add, norm_sums, got)
    got = swap(norm_sums, "z1")
    norm_sums = line(jnp.add, norm_sums, got)
    got = swap(norm_sums, "z2")
    attn_sum = line(lambda _, *terms: add(*terms), mlp_got, attn_mine, *attn_z)
    attn_got = [
        lax.ppermute(attn_sum, "dp", [(i, i ^ mask) for i in range(4)]) for mask in (2, 1, 3)
    ]
    mlp_sum = line(functools.partial(order, at_y), mlp_sum, mlp_got)
    mlp_got = swap(mlp_sum, "core")
    norm_sums = line(jnp.add, norm_sums, got)
    got = swap(norm_sums, "y")
    attn_sum = line(in_order, attn_sum, *attn_got)
    attn_sum = line(
        lambda item: item.transpose(1, 2, 0, 3, 4).reshape(4, local, width).astype(F32), attn_sum
    )
    attn_sums = line(lambda item: (item[0].T, item[1].T, item[2].T, item[3]), attn_sum)
    mlp_sum = line(functools.partial(order, at_core), mlp_sum, mlp_got)
    up_sum, down_sum = line(
        lambda item: tuple(item.transpose(2, 1, 0, 3, 4).reshape(2, -1, width).astype(F32)), mlp_sum
    )
    up_sum = line(jnp.transpose, up_sum)
    norm_sums = line(jnp.add, norm_sums, got)
    norm_sums = lax.dynamic_slice_in_dim(norm_sums, at_mp * (width // 8), width // 8, 1)
    return (
        output,
        in_grad,
        norm_sums[0],
        norm_sums[1],
        *attn_sums,
        norm_sums[2],
        norm_sums[3],
        up_sum,
        down_sum,
    )


def on_any(
    mp_size,
    inputs,
    segments,
    ln1_gain,
    ln1_bias,
    w_query,
    w_key,
    w_value,
    w_output,
    ln2_gain,
    ln2_bias,
    w_up,
    w_down,
    cotangent,
):
    rows, width = inputs.shape
    seq_length = segments.shape[1]
    shared_by = seq_length // rows
    at_mp = lax.axis_index("mp")
    groups = [[start + i for i in range(shared_by)] for start in range(0, mp_size, shared_by)]

    def exchange(values, split, join):
        if shared_by == 1:
            return values
        return lax.all_to_all(values, "mp", split, join, axis_index_groups=groups, tiled=True)

    def gather(parts):
        return lax.all_gather(parts, "mp", axis=1, tiled=True)

    def reduce(parts):
        return lax.psum(lax.psum_scatter(parts, "mp", scatter_dimension=1, tiled=True), "dp")

    attn_w = gather(jnp.stack([w_query.T, w_value.T, w_key.T, w_output]))
    up, down = gather(jnp.stack([w_up.T, w_down]))
    project, w_out = attn_w[:3].reshape(3 * width, width), attn_w[3]

    segs = lax.dynamic_index_in_dim(segments, at_mp // shared_by, 0, keepdims=False)
    place = windows(segs) + (jnp.zeros((1,), jnp.int32), segs)
    resid_in = inputs.astype(F32)
    norm_one = layer_norm(resid_in, ln1_gain, ln1_bias).astype(BF16)
    projected = dot(project, norm_one, NT).astype(BF16).reshape(3, width, rows)
    projected = exchange(projected, 1, 2)
    query_value, keys = projected[None, :2], projected[2:]
    heads_out, lse = attend_forward(query_value, keys, place)
    attended = exchange(heads_out[0], 1, 0)
    residual = resid_in + dot(attended, w_out, TN)
    norm_two = layer_norm(residual, ln2_gain, ln2_bias).astype(BF16)
    mlp_branch, norm_two_grad, *mlp_grads = feed_forward(norm_two, cotangent, up, down)
    up_sum, down_sum = reduce(jnp.stack(mlp_grads)).astype(F32)

    output, res_grad, branch_grad, norm_two_grads = middle(
        residual, cotangent, ln2_gain, [mlp_branch], [norm_two_grad]
    )
    out_grad = dot(attended, branch_grad, NN).astype(BF16)
    att_grad = exchange(dot(w_out, branch_grad, NT).astype(BF16), 0, 1)
    query_value_grad, key_grad = attend_backward(
        query_value, keys, heads_out, att_grad[None], lse, place
    )
    proj_grad = exchange(jnp.concatenate([query_value_grad[0], key_grad]), 2, 1)
    proj_grad = proj_grad.reshape(3 * width, rows)
    project_grad = dot(proj_grad, norm_one, NN).astype(BF16).reshape(3, width, width)
    attn_sum = reduce(jnp.concatenate([project_grad, out_grad[None]])).astype(F32)
    in_grad, norm_one_grads = last(inputs, dot(proj_grad, project, TN), res_grad, ln1_gain)
    norm_parts = jnp.concatenate([norm_one_grads[:2], norm_two_grads[:2]])
    norm_sums = lax.dynamic_slice_in_dim(
        lax.psum(norm_parts, ("dp", "mp")), at_mp * (width // mp_size), width // mp_size, 1
    )
    return (
        output,
        in_grad,
        norm_sums[0],
        norm_sums[1],
        attn_sum[0].T,
        attn_sum[2].T,
        attn_sum[1].T,
        attn_sum[3],
        norm_sums[2],
        norm_sums[3],
        up_sum.T,
        down_sum,
    )


def shards(dp_size, mp_size, inputs, segments, *rest):
    if dp_size == 4 and mp_size == 8 and inputs.shape[0] == segments.shape[1]:
        return on_cube(inputs, segments, *rest)
    return on_any(mp_size, inputs, segments, *rest)


def solution(mesh):
    return jax.shard_map(
        functools.partial(shards, mesh.shape["dp"], mesh.shape["mp"]),
        mesh=mesh,
        in_specs=(
            P(("dp", "mp"), None),
            P("dp", None),
            P(),
            P(),
            P(None, "mp"),
            P(None, "mp"),
            P(None, "mp"),
            P("mp", None),
            P(),
            P(),
            P(None, "mp"),
            P("mp", None),
            P(("dp", "mp"), None),
        ),
        out_specs=(
            P(("dp", "mp"), None),
            P(("dp", "mp"), None),
            P("mp"),
            P("mp"),
            P(None, "mp"),
            P(None, "mp"),
            P(None, "mp"),
            P("mp", None),
            P("mp"),
            P("mp"),
            P(None, "mp"),
            P("mp", None),
        ),
        check_vma=False,
    )
```
